32 devices in a mesh: ctx: 8 (over z, x), fsdp: 4 (over y, core).
Axes of the slice: x: 2, y: 2, z: 4, core: 2. Of those that a mesh axis runs over, the one named last changes fastest.
Arguments:
- inputs: bfloat16 [16384, 2304], P(('ctx', 'fsdp')), may hold values from -6 to 6
- cotangent: bfloat16 [16384, 2304], P(('ctx', 'fsdp')), may hold values from -6 to 6
- block_ids: int32 [64], replicated, may hold values from 0 to 63, as said below
- positions: int32 [16384], P(('ctx', 'fsdp')), may hold values from 0 to 8191, as said below
- attn_in: bfloat16 [2304, 4096], P('fsdp', 'ctx'), may hold values from -1 to 1
- attn_out: bfloat16 [2304, 2048], P('fsdp', 'ctx'), may hold values from -0.125 to 0.125
- mlp_in: bfloat16 [2304, 18432], P('fsdp', 'ctx'), may hold values from -0.125 to 0.125
- mlp_out: bfloat16 [2304, 9216], P('fsdp', 'ctx'), may hold values from -0.0625 to 0.0625
- gains: bfloat16 [2304, 4], P('fsdp'), may hold values from 0.5 to 1.5
Outputs:
- output: bfloat16 [16384, 2304], P(('ctx', 'fsdp'))
- grad_input: float32 [16384, 2304], P(('ctx', 'fsdp'))
- grad_attn_in: float32 [2304, 4096], P('fsdp', 'ctx')
- grad_attn_out: float32 [2304, 2048], P('fsdp', 'ctx')
- grad_mlp_in: float32 [2304, 18432], P('fsdp', 'ctx')
- grad_mlp_out: float32 [2304, 9216], P('fsdp', 'ctx')
- grad_gains: float32 [2304, 4], P('fsdp')
The draws below stay inside these ranges and needn't reach their ends.
Inputs may be any that keep to these rules, and one draw needn't show every extreme that they name: `block_ids`: slots 2 i and 2 i + 1 hold the two blocks dealt to device i: blocks b and 31 - b of one sequence, in either order; each block of the 2 sequences is dealt once; an entry is sequence * 32 + block. `positions`: row r holds position 256 * (id mod 32) + r mod 256, with id = block_ids[r // 256].
All inputs are finite; a program needn't handle non-finite values.
Results may differ from the reference program's by a relative error of at most 0.02.
Values may be sent and summed in bfloat16 or wider, within the bound.
No kernel may reach another device: no remote copies, remote signals or barrier semaphores. Data moves between devices by JAX's collectives and lax.ppermute only.
A program may use at most 640 MiB of HBM per device.

```python
import jax
import jax.numpy as jnp
from jax import lax

D = 2304
QUERY_HEADS = 8
KEY_VALUE_HEADS = 4
HEAD_SIZE = 256
FF = 9216
LOOKBACK_SPAN = 4096
SEQUENCE_COUNT = 2
TOKENS = 16384
SEQUENCE_TOKENS = 8192
BLK = 256
NBLK = 32
DEVICES = 32


def deal_blocks(key):
    half_count = NBLK // 2
    visit_order = jax.random.permutation(jax.random.fold_in(key, 101), DEVICES).astype(jnp.int32)
    flipped = jax.random.randint(jax.random.fold_in(key, 102), (DEVICES,), 0, 2).astype(jnp.int32)
    sequence = visit_order // half_count
    lower = visit_order % half_count
    early_block = sequence * NBLK + lower
    late_block = sequence * NBLK + NBLK - 1 - lower
    leading = jnp.where(flipped == 1, late_block, early_block)
    trailing = jnp.where(flipped == 1, early_block, late_block)
    return jnp.stack([leading, trailing], axis=1).reshape(2 * DEVICES).astype(jnp.int32)


def draw_block_ids(key, part):
    table = deal_blocks(key)
    return table


def draw_positions(key, part):
    table = deal_blocks(key)
    row_index = jnp.arange(TOKENS, dtype=jnp.int32)
    owner_ids = table[row_index // BLK]
    return (owner_ids % NBLK * BLK + row_index % BLK).astype(jnp.int32)


def draw_attn_in(key, part):
    key = jax.random.fold_in(key, 3)
    column_total = QUERY_HEADS * HEAD_SIZE + 2 * KEY_VALUE_HEADS * HEAD_SIZE
    column_number = jnp.arange(column_total, dtype=jnp.int32)
    column_factor = jnp.where(column_number < (QUERY_HEADS + KEY_VALUE_HEADS) * HEAD_SIZE, 1.7, 1.0).astype(jnp.float32)
    raw_draw = jax.random.truncated_normal(key, -6.0, 6.0, (D, column_total), jnp.float32)
    scaled = raw_draw * column_factor[None, :] * D ** (-0.5)
    return jnp.clip(scaled, -1.0, 1.0).astype(jnp.bfloat16)


def block_scale(stream_key, dims, pieces, smallest, top_value):
    factor_of, own = 1.0, jax.random.fold_in(stream_key, 6)
    for position, blocks in pieces:
        heights = jnp.exp(jax.random.uniform(jax.random.fold_in(own, position), (blocks,), jnp.float32, smallest / len(pieces), top_value / len(pieces)))
        factor_of = factor_of * jnp.repeat(heights, dims[position] // blocks).reshape([-1 if axis == position else 1 for axis in range(len(dims))])
    return factor_of


def normal_values(key, extent, width, reach, shards=(), kind=jnp.bfloat16):
    entries = jax.random.normal(key, extent, jnp.float32) * width
    if len(shards) > 0:
        entries = block_scale(key, extent, shards, -0.22, 0.18) * entries
    return jnp.clip(entries, min=-reach, max=reach).astype(kind)


def setup_inputs(seed: int = 0) -> dict:
    seeds = jax.random.split(jax.random.key(seed), 10)
    return {
        "inputs": normal_values(seeds[0], (TOKENS, D), 1.0, 6.0, ((0, 32),)),
        "cotangent": normal_values(seeds[1], (TOKENS, D), 1.0, 6.0, ((0, 32),)),
        "block_ids": draw_block_ids(jax.random.fold_in(seeds[9], 71), 0),
        "positions": draw_positions(jax.random.fold_in(seeds[9], 71), 0),
        "attn_in": draw_attn_in(jax.random.fold_in(seeds[9], 71), 0),
        "attn_out": normal_values(seeds[5], (D, QUERY_HEADS * HEAD_SIZE), (QUERY_HEADS * HEAD_SIZE) ** -0.5, 0.125, ((0, 4), (1, 8))),
        "mlp_in": normal_values(seeds[6], (D, 2 * FF), D ** -0.5, 0.125, ((0, 4), (1, 8))),
        "mlp_out": normal_values(seeds[7], (D, FF), FF ** -0.5, 0.0625, ((0, 4), (1, 8))),
        "gains": jnp.clip(1.0 + 0.1 * jax.random.normal(seeds[8], (D, 4), jnp.float32), 0.5, 1.5).astype(jnp.bfloat16),
    }


EPSILON = 1e-06
SOFT_CAP = 50.0
ROPE_BASE = 10000.0
HIGHEST_PRECISION = lax.Precision.HIGHEST

@jax.custom_vjp
def low(v):
    return lax.optimization_barrier(v.astype(jnp.bfloat16)).astype(jnp.float32)

@jax.custom_vjp
def low_back(v):
    return v

def low_keep(v):
    return (low(v), None)

def low_pass(kept, grad):
    return (grad,)

def back_keep(v):
    return (v, None)

def back_low(kept, grad):
    return (low(grad),)
low.defvjp(low_keep, low_pass)
low_back.defvjp(back_keep, back_low)

def inverse_rms(values):
    return lax.rsqrt(lax.optimization_barrier(jnp.mean(values * values, axis=-1, keepdims=True)) + EPSILON)

def rotary_tables(positions):
    half_width = HEAD_SIZE // 2
    frequency = ROPE_BASE ** (-2.0 * jnp.arange(half_width, dtype=jnp.float32) / HEAD_SIZE)
    angles = positions.astype(jnp.float32)[:, None] * frequency[None, :]
    return (jnp.cos(angles)[:, None, :], jnp.sin(angles)[:, None, :])

def apply_rotation(values, cosine_table, sine_lookup):
    half_width = values.shape[-1] // 2
    first_half = values[..., :half_width]
    second_half = values[..., half_width:]
    return jnp.concatenate([first_half * cosine_table - second_half * sine_lookup, second_half * cosine_table + first_half * sine_lookup], axis=-1)

def attention(query_head_rows, key_head_rows, value_head_rows, positions, block_ids):
    head_cluster = QUERY_HEADS // KEY_VALUE_HEADS
    row_index = jnp.arange(TOKENS, dtype=jnp.int32)
    owner_ids = block_ids[row_index // BLK]
    place = (owner_ids // NBLK * SEQUENCE_TOKENS + owner_ids % NBLK * BLK + row_index % BLK).astype(jnp.int32)
    visit_order = jnp.zeros((TOKENS,), jnp.int32).at[place].set(row_index)
    sequence_queries = query_head_rows[visit_order].reshape(SEQUENCE_COUNT, SEQUENCE_TOKENS, KEY_VALUE_HEADS, head_cluster, HEAD_SIZE)
    sequence_keys = key_head_rows[visit_order].reshape(SEQUENCE_COUNT, SEQUENCE_TOKENS, KEY_VALUE_HEADS, HEAD_SIZE)
    sequence_values = value_head_rows[visit_order].reshape(SEQUENCE_COUNT, SEQUENCE_TOKENS, KEY_VALUE_HEADS, HEAD_SIZE)
    seq_pos = positions[visit_order].reshape(SEQUENCE_COUNT, SEQUENCE_TOKENS).astype(jnp.int32)
    key_padded_rows = jnp.concatenate([jnp.zeros((SEQUENCE_COUNT, LOOKBACK_SPAN, KEY_VALUE_HEADS, HEAD_SIZE), jnp.float32), sequence_keys], axis=1)
    value_padded_rows = jnp.concatenate([jnp.zeros((SEQUENCE_COUNT, LOOKBACK_SPAN, KEY_VALUE_HEADS, HEAD_SIZE), jnp.float32), sequence_values], axis=1)
    padded_pos = jnp.concatenate([jnp.full((SEQUENCE_COUNT, LOOKBACK_SPAN), -2 * (SEQUENCE_TOKENS + LOOKBACK_SPAN), jnp.int32), seq_pos], axis=1)
    block_span_size = min(512, SEQUENCE_TOKENS)
    block_count = SEQUENCE_TOKENS // block_span_size
    zeroth_index = jnp.int32(0)

    def one_block(block_index):
        selector = (block_index // block_count).astype(jnp.int32)
        first_row_index = (block_index % block_count * block_span_size).astype(jnp.int32)
        query_tile_block = lax.dynamic_slice(sequence_queries, (selector, first_row_index, zeroth_index, zeroth_index, zeroth_index), (1, block_span_size, KEY_VALUE_HEADS, head_cluster, HEAD_SIZE))[0]
        key_tile_block = lax.dynamic_slice(key_padded_rows, (selector, first_row_index, zeroth_index, zeroth_index), (1, block_span_size + LOOKBACK_SPAN, KEY_VALUE_HEADS, HEAD_SIZE))[0]
        value_tile_block = lax.dynamic_slice(value_padded_rows, (selector, first_row_index, zeroth_index, zeroth_index), (1, block_span_size + LOOKBACK_SPAN, KEY_VALUE_HEADS, HEAD_SIZE))[0]
        query_pos = lax.dynamic_slice(seq_pos, (selector, first_row_index), (1, block_span_size))[0]
        key_pos = lax.dynamic_slice(padded_pos, (selector, first_row_index), (1, block_span_size + LOOKBACK_SPAN))[0]
        raw_scores = low_back(jnp.einsum('qhgd,khd->hgqk', query_tile_block, key_tile_block, precision=HIGHEST_PRECISION) * HEAD_SIZE ** (-0.5))
        capped = SOFT_CAP * jnp.tanh(raw_scores / SOFT_CAP)
        spacing = query_pos[:, None] - key_pos[None, :]
        live_pairs = (spacing >= 0) & (spacing < LOOKBACK_SPAN)
        weights = jnp.where(live_pairs, jnp.exp(capped), 0.0)
        totals = lax.optimization_barrier(jnp.sum(weights, axis=-1))
        summed = low_back(jnp.einsum('hgqk,khd->qhgd', low(weights), value_tile_block, precision=HIGHEST_PRECISION))
        attended = summed / jnp.transpose(totals, (2, 0, 1))[..., None]
        return attended.reshape(block_span_size, QUERY_HEADS * HEAD_SIZE)
    blocks = lax.map(jax.checkpoint(one_block), jnp.arange(SEQUENCE_COUNT * block_count, dtype=jnp.int32))
    return blocks.reshape(TOKENS, QUERY_HEADS * HEAD_SIZE)[place]

def layer(source, attn_in, attn_out, mlp_in, mlp_out, gains, positions, block_ids):
    query_span_width = QUERY_HEADS * HEAD_SIZE
    key_span_width = KEY_VALUE_HEADS * HEAD_SIZE
    lowered_in = low(source * inverse_rms(source) * gains[:, 0])
    projected_rows = low_back(jnp.dot(lowered_in, attn_in, precision=HIGHEST_PRECISION))
    cosine_table, sine_lookup = rotary_tables(positions)
    query_head_rows = low(apply_rotation(projected_rows[:, :query_span_width].reshape(-1, QUERY_HEADS, HEAD_SIZE), cosine_table, sine_lookup))
    key_head_rows = low(apply_rotation(projected_rows[:, query_span_width:query_span_width + key_span_width].reshape(-1, KEY_VALUE_HEADS, HEAD_SIZE), cosine_table, sine_lookup))
    value_head_rows = low(projected_rows[:, query_span_width + key_span_width:].reshape(-1, KEY_VALUE_HEADS, HEAD_SIZE))
    attended = attention(query_head_rows, key_head_rows, value_head_rows, positions, block_ids)
    attended_low = low(low_back(attended))
    branch = low_back(jnp.dot(attended_low, attn_out.T, precision=HIGHEST_PRECISION))
    middle = source + branch * inverse_rms(branch) * gains[:, 1]
    lowered_mid = low(middle * inverse_rms(middle) * gains[:, 2])
    gate_up = low_back(jnp.dot(lowered_mid, mlp_in, precision=HIGHEST_PRECISION))
    hidden = low(jax.nn.gelu(gate_up[:, :FF], approximate=True) * gate_up[:, FF:])
    down_branch = low_back(jnp.dot(hidden, mlp_out.T, precision=HIGHEST_PRECISION))
    return middle + down_branch * inverse_rms(down_branch) * gains[:, 3]

def reference(inputs, cotangent, block_ids, positions, attn_in, attn_out, mlp_in, mlp_out, gains):

    def forward(source, w_attn_in, w_attn_out, w_mlp_in, w_mlp_out, w_gains):
        return layer(source, w_attn_in, w_attn_out, w_mlp_in, w_mlp_out, w_gains, positions, block_ids)
    result, pullback = jax.vjp(forward, inputs.astype(jnp.float32), attn_in.astype(jnp.float32), attn_out.astype(jnp.float32), mlp_in.astype(jnp.float32), mlp_out.astype(jnp.float32), gains.astype(jnp.float32))
    grads = pullback(cotangent.astype(jnp.float32))
    return (result.astype(jnp.bfloat16), grads[0], grads[1], grads[2], grads[3], grads[4], grads[5])
```

```python
import functools
import math

import jax
import jax.numpy as jnp
from jax import lax
from jax.experimental import pallas as pl
from jax.experimental.pallas import tpu as pltpu
from jax.sharding import PartitionSpec as P

QUERY_HEADS = 8
KEY_VALUE_HEADS = 4
HEAD_SIZE = 256
LOOKBACK_SPAN = 4096
SEQUENCE_COUNT = 2


EPSILON = 1e-06
SOFT_CAP = 50.0
ROPE_BASE = 10000.0
AXES = ("ctx", "fsdp")
PLANE = 8
CORE, SIDE, ACROSS = 1, 2, 4
TANH_SCALE = HEAD_SIZE ** (-0.5) / SOFT_CAP
EXP2_SCALE = SOFT_CAP * math.log2(math.e)
VMEM_BYTES = 56 * 1024 * 1024


def inverse_rms(values):
    return lax.rsqrt(jnp.mean(values * values, axis=-1, keepdims=True) + EPSILON)


def norm_back(values, inverse, scale, upstream):
    scaled = upstream * scale
    through = inverse * scaled - values * inverse**3 * jnp.mean(
        scaled * values, axis=-1, keepdims=True
    )
    return (through, jnp.sum(upstream * values * inverse, axis=0))


def rotary_tables(positions):
    half_width = HEAD_SIZE // 2
    frequency = ROPE_BASE ** (-2.0 * jnp.arange(half_width, dtype=jnp.float32) / HEAD_SIZE)
    angles = positions.astype(jnp.float32)[:, None] * frequency[None, :]
    return (jnp.cos(angles), jnp.sin(angles))


def rotate(values, cosine, sine):
    half_width = values.shape[-1] // 2
    first_half = values[..., :half_width]
    second_half = values[..., half_width:]
    return jnp.concatenate(
        [
            first_half * cosine - second_half * sine,
            second_half * cosine + first_half * sine,
        ],
        axis=-1,
    )


def dot(left, right, left_axis, right_axis):
    return lax.dot_general(
        left,
        right,
        (((left_axis,), (right_axis,)), ((), ())),
        preferred_element_type=jnp.float32,
    )


def swap(values, mask):
    count = lax.axis_size(AXES)
    return lax.ppermute(values, AXES, [(i, i ^ mask) for i in range(count)])


def shift(values):
    count = lax.axis_size(AXES)
    return lax.ppermute(values, AXES, [(i, (i + PLANE) % count) for i in range(count)])


def pick(stacked, index):
    return lax.dynamic_index_in_dim(stacked, index, 0, keepdims=False)


def scatter_plane(stacked, place):
    received = [pick(stacked, place)]
    for mask in range(1, PLANE):
        received.append(swap(pick(stacked, place ^ mask), mask))
    return received


def ordered(received, place):
    stacked = jnp.stack(received)
    return jnp.stack([pick(stacked, place ^ j) for j in range(len(received))])


def gather_plane(rows):
    half = rows.shape[0] // 2
    low, high = rows[:half], rows[half:]
    other = swap(rows, CORE)
    across_low = swap(low, ACROSS)
    side_high = swap(high, SIDE)
    first = jnp.concatenate([across_low, side_high])
    first_other = swap(first, CORE)
    side_lows = swap(jnp.concatenate([low, across_low]), SIDE)
    across_highs = swap(jnp.concatenate([high, side_high]), ACROSS)
    second = jnp.concatenate([side_lows, across_highs])
    second_other = swap(second, CORE)
    return [
        jnp.concatenate([rows, other]),
        jnp.concatenate([first, first_other]),
        second,
        second_other,
    ]


def reduce_plane(groups):
    wide = lambda v: v.astype(jnp.float32)
    low = jnp.bfloat16
    own, first, second, second_other = groups
    rows = own.shape[0] // 2
    half = rows // 2
    second_sum = (wide(second) + wide(swap(second_other.astype(low), CORE))).astype(low)
    from_side = swap(second_sum[:rows], SIDE)
    from_across = swap(second_sum[rows:], ACROSS)
    first_sum = wide(first[:rows]) + wide(swap(first[rows:].astype(low), CORE))
    own_sum = wide(own[:rows]) + wide(swap(own[rows:].astype(low), CORE))
    across_low = (first_sum[:half] + wide(from_side[half:])).astype(low)
    side_high = (first_sum[half:] + wide(from_across[half:])).astype(low)
    got_low = swap(across_low, ACROSS)
    got_high = swap(side_high, SIDE)
    return jnp.concatenate(
        [
            own_sum[:half] + wide(from_side[:half]) + wide(got_low),
            own_sum[half:] + wide(from_across[:half]) + wide(got_high),
        ]
    )


def pair_lists(query_ids, key_ids, blocks_per_seq, span_blocks):
    query_seq, query_at = query_ids // blocks_per_seq, query_ids % blocks_per_seq
    key_seq, key_at = key_ids // blocks_per_seq, key_ids % blocks_per_seq
    distance = (query_at[:, None] - key_at[None, :]).reshape(-1)
    same = (query_seq[:, None] == key_seq[None, :]).reshape(-1)
    whole = same & (distance > 0) & (distance < span_blocks)
    edged = same & ((distance == 0) | (distance == span_blocks))
    count_whole = jnp.sum(whole.astype(jnp.int32))
    count_edged = jnp.sum(edged.astype(jnp.int32))
    place = jnp.where(
        whole,
        jnp.cumsum(whole.astype(jnp.int32)) - 1,
        jnp.where(edged, count_whole + jnp.cumsum(edged.astype(jnp.int32)) - 1, -1),
    )
    total = distance.shape[0]
    code = jnp.arange(total, dtype=jnp.int32) * 2 + (distance == span_blocks).astype(jnp.int32)
    hit = place[:, None] == jnp.arange(total, dtype=jnp.int32)[None, :]
    entries = jnp.sum(jnp.where(hit, code[:, None], 0), axis=0)
    return jnp.concatenate([jnp.stack([count_whole, count_edged]), entries]).astype(jnp.int32)


def run_pairs(list_ref, row, key_count, unroll, visit):
    whole = list_ref[row, 0]
    edged = list_ref[row, 1]

    def decode(position):
        code = list_ref[row, 2 + position]
        pair = code // 2
        return pair // key_count, pair % key_count, code % 2

    def several(step, carry):
        found = [decode(step * unroll + i) for i in range(unroll)]
        visit([f[0] for f in found], [f[1] for f in found], None)
        return carry

    def single(position, carry):
        i, j, _ = decode(position)
        visit([i], [j], None)
        return carry

    def masked(position, carry):
        i, j, far = decode(position)
        visit([i], [j], far)
        return carry

    groups = whole // unroll
    lax.fori_loop(0, groups, several, 0)
    lax.fori_loop(groups * unroll, whole, single, 0)
    lax.fori_loop(whole, whole + edged, masked, 0)


def attend_kernel(first, unroll, list_ref, query_hbm, own_hbm, other_hbm, *rest):
    if first:
        state_hbm = None
        out_hbm, query, own, other, state, sems = rest
    else:
        state_hbm, out_hbm, query, own, other, state, sems = rest
    copies = [
        pltpu.make_async_copy(query_hbm, query, sems.at[0]),
        pltpu.make_async_copy(own_hbm, own, sems.at[1]),
        pltpu.make_async_copy(other_hbm, other, sems.at[2]),
    ]
    if not first:
        copies.append(pltpu.make_async_copy(state_hbm, state, sems.at[3]))
    for copy in copies:
        copy.start()
    if first:
        state[...] = jnp.zeros_like(state)
    for copy in copies:
        copy.wait()
    rows = query.shape[1]
    lane = lax.broadcasted_iota(jnp.int32, (rows, 128), 1)

    def visit_in(keys):
        def visit(query_at, key_at, far):
            scores = [
                dot(query[i], keys[j, :, :HEAD_SIZE], 1, 1) for i, j in zip(query_at, key_at)
            ]
            for i, j, score in zip(query_at, key_at, scores):
                weights = jnp.exp2(EXP2_SCALE * jnp.tanh(score * TANH_SCALE))
                if far is not None:
                    spacing = (
                        lax.broadcasted_iota(jnp.int32, weights.shape, 0)
                        - lax.broadcasted_iota(jnp.int32, weights.shape, 1)
                        + far * LOOKBACK_SPAN
                    )
                    live = (spacing >= 0) & (spacing < LOOKBACK_SPAN)
                    weights = jnp.where(live, weights, 0.0)
                if rows % 128 == 0:
                    part = weights[:, :128]
                    for k in range(1, rows // 128):
                        part = part + weights[:, k * 128 : (k + 1) * 128]
                else:
                    part = jnp.where(lane == 0, jnp.sum(weights, axis=1, keepdims=True), 0.0)
                state[i, :, HEAD_SIZE:] += part
                state[i, :, :HEAD_SIZE] += dot(
                    weights.astype(jnp.bfloat16), keys[j, :, HEAD_SIZE:], 1, 0
                )

        return visit

    key_count = own.shape[0]
    run_pairs(list_ref, 0, key_count, unroll, visit_in(own))
    run_pairs(list_ref, 1, key_count, unroll, visit_in(other))
    out = pltpu.make_async_copy(state, out_hbm, sems.at[4])
    out.start()
    out.wait()


def attend(lists, query, own, other, state):
    first = state is None
    blocks, rows, _ = query.shape
    shape = (blocks, rows, HEAD_SIZE + 128)
    operands = (query, own, other) if first else (query, own, other, state)
    return pl.pallas_call(
        functools.partial(attend_kernel, first, 4),
        out_shape=jax.ShapeDtypeStruct(shape, jnp.float32),
        grid_spec=pltpu.PrefetchScalarGridSpec(
            num_scalar_prefetch=1,
            grid=(1,),
            in_specs=[pl.BlockSpec(memory_space=pl.ANY)] * len(operands),
            out_specs=pl.BlockSpec(memory_space=pl.ANY),
            scratch_shapes=[
                pltpu.VMEM(query.shape, jnp.bfloat16),
                pltpu.VMEM(own.shape, jnp.bfloat16),
                pltpu.VMEM(other.shape, jnp.bfloat16),
                pltpu.VMEM(shape, jnp.float32),
                pltpu.SemaphoreType.DMA((5,)),
            ],
        ),
        compiler_params=pltpu.CompilerParams(vmem_limit_bytes=VMEM_BYTES),
        cost_estimate=pl.CostEstimate(
            flops=60 * 4 * rows * rows * HEAD_SIZE,
            bytes_accessed=14 * 1024 * 1024,
            transcendentals=60 * 2 * rows * rows,
        ),
    )(lists, *operands)


def attend_back_kernel(
    first,
    unroll,
    list_ref,
    query_hbm,
    grad_hbm,
    term_hbm,
    own_hbm,
    other_hbm,
    *rest,
):
    if first:
        state_hbm = None
    else:
        state_hbm, *rest = rest
    (
        out_hbm,
        own_out_hbm,
        other_out_hbm,
        query,
        grad,
        term,
        own,
        other,
        state,
        own_grad,
        other_grad,
        own_low,
        other_low,
        sems,
    ) = rest
    copies = [
        pltpu.make_async_copy(query_hbm, query, sems.at[0]),
        pltpu.make_async_copy(grad_hbm, grad, sems.at[1]),
        pltpu.make_async_copy(term_hbm, term, sems.at[2]),
        pltpu.make_async_copy(own_hbm, own, sems.at[3]),
        pltpu.make_async_copy(other_hbm, other, sems.at[4]),
    ]
    if not first:
        copies.append(pltpu.make_async_copy(state_hbm, state, sems.at[5]))
    for copy in copies:
        copy.start()
    if first:
        state[...] = jnp.zeros_like(state)
    own_grad[...] = jnp.zeros_like(own_grad)
    other_grad[...] = jnp.zeros_like(other_grad)
    for copy in copies:
        copy.wait()

    def visit_in(keys, key_grad):
        def visit(query_at, key_at, far):
            scores = []
            slopes = []
            for i, j in zip(query_at, key_at):
                scores.append(dot(keys[j, :, :HEAD_SIZE], query[i], 1, 1))
                slopes.append(dot(keys[j, :, HEAD_SIZE:], grad[i], 1, 1))
            for i, j, score, slope in zip(query_at, key_at, scores, slopes):
                bent = jnp.tanh(score * TANH_SCALE)
                weights = jnp.exp2(EXP2_SCALE * bent)
                if far is not None:
                    spacing = (
                        lax.broadcasted_iota(jnp.int32, weights.shape, 1)
                        - lax.broadcasted_iota(jnp.int32, weights.shape, 0)
                        + far * LOOKBACK_SPAN
                    )
                    live = (spacing >= 0) & (spacing < LOOKBACK_SPAN)
                    weights = jnp.where(live, weights, 0.0)
                grad_scores = (
                    (slope + term[i]) * (weights * (1.0 - bent * bent))
                ).astype(jnp.bfloat16)
                key_grad[j, :, :HEAD_SIZE] += dot(grad_scores, query[i], 1, 0)
                key_grad[j, :, HEAD_SIZE:] += dot(weights.astype(jnp.bfloat16), grad[i], 1, 0)
                state[i] += dot(grad_scores, keys[j, :, :HEAD_SIZE], 0, 0)

        return visit

    key_count = own.shape[0]
    run_pairs(list_ref, 1, key_count, unroll, visit_in(other, other_grad))
    other_low[...] = other_grad[...].astype(jnp.bfloat16)
    other_out = pltpu.make_async_copy(other_low, other_out_hbm, sems.at[6])
    other_out.start()
    run_pairs(list_ref, 0, key_count, unroll, visit_in(own, own_grad))
    own_low[...] = own_grad[...].astype(jnp.bfloat16)
    own_out = pltpu.make_async_copy(own_low, own_out_hbm, sems.at[7])
    own_out.start()
    out = pltpu.make_async_copy(state, out_hbm, sems.at[8])
    out.start()
    other_out.wait()
    own_out.wait()
    out.wait()


def attend_back(lists, query, grad, term, own, other, state):
    first = state is None
    blocks, rows, _ = query.shape
    operands = (query, grad, term, own, other)
    if not first:
        operands = operands + (state,)
    return pl.pallas_call(
        functools.partial(attend_back_kernel, first, 2),
        out_shape=[
            jax.ShapeDtypeStruct(query.shape, jnp.float32),
            jax.ShapeDtypeStruct(own.shape, jnp.bfloat16),
            jax.ShapeDtypeStruct(other.shape, jnp.bfloat16),
        ],
        grid_spec=pltpu.PrefetchScalarGridSpec(
            num_scalar_prefetch=1,
            grid=(1,),
            in_specs=[pl.BlockSpec(memory_space=pl.ANY)] * len(operands),
            out_specs=[pl.BlockSpec(memory_space=pl.ANY)] * 3,
            scratch_shapes=[
                pltpu.VMEM(query.shape, jnp.bfloat16),
                pltpu.VMEM(query.shape, jnp.bfloat16),
                pltpu.VMEM(term.shape, jnp.float32),
                pltpu.VMEM(own.shape, jnp.bfloat16),
                pltpu.VMEM(other.shape, jnp.bfloat16),
                pltpu.VMEM(query.shape, jnp.float32),
                pltpu.VMEM(own.shape, jnp.float32),
                pltpu.VMEM(other.shape, jnp.float32),
                pltpu.VMEM(own.shape, jnp.bfloat16),
                pltpu.VMEM(other.shape, jnp.bfloat16),
                pltpu.SemaphoreType.DMA((9,)),
            ],
        ),
        compiler_params=pltpu.CompilerParams(vmem_limit_bytes=VMEM_BYTES),
        cost_estimate=pl.CostEstimate(
            flops=60 * 10 * rows * rows * HEAD_SIZE,
            bytes_accessed=24 * 1024 * 1024,
            transcendentals=60 * 2 * rows * rows,
        ),
    )(lists, *operands)


def body(inputs, cotangent, block_ids, positions, attn_in, attn_out, mlp_in, mlp_out, gains):
    low = jnp.bfloat16
    wide = jnp.float32
    token_rows, width = inputs.shape
    block = token_rows // 2
    devices = lax.axis_size(AXES)
    ctx_count, row_parts = lax.axis_size("ctx"), lax.axis_size("fsdp")
    planes = devices // PLANE
    blocks_per_seq = 2 * devices // SEQUENCE_COUNT
    span_blocks = LOOKBACK_SPAN // block
    heads, kv_heads = QUERY_HEADS, KEY_VALUE_HEADS
    score_scale = HEAD_SIZE ** (-0.5)
    me = lax.axis_index(AXES)
    place = me % PLANE
    plane = me // PLANE
    row_share = attn_in.shape[0]
    unit = mlp_out.shape[1] // PLANE
    near = list(range(0, PLANE, 2))
    far = list(range(1, PLANE, 2))

    def whole(weight):
        gathered = lax.all_gather(weight, AXES, axis=0)
        gathered = gathered.reshape((ctx_count, row_parts) + weight.shape)
        return gathered.transpose(1, 2, 0, 3).reshape(width, ctx_count * weight.shape[1])

    attn_whole = whole(attn_in)
    gain_whole = lax.all_gather(gains, "fsdp", axis=0, tiled=True)
    out_whole = whole(attn_out)
    scales = gain_whole.astype(wide)

    mlp_pieces = jnp.concatenate(
        [
            mlp_in.T.reshape(2, PLANE, unit, row_share).transpose(1, 0, 2, 3),
            mlp_out.T.reshape(PLANE, 1, unit, row_share),
        ],
        axis=1,
    )
    mlp_share = ordered(scatter_plane(mlp_pieces, place), place)
    mlp_share = (
        mlp_share.reshape(2, row_parts, 3, unit, row_share)
        .transpose(0, 2, 3, 1, 4)
        .reshape(2, 3 * unit, width)
    )
    in_share = mlp_share[:, : 2 * unit].reshape(4 * unit, width)
    out_share = mlp_share[:, 2 * unit :].reshape(2 * unit, width)
    in_all = jnp.zeros((planes, 4 * unit, width), low)
    out_all = jnp.zeros((planes, 2 * unit, width), low)
    for step in range(planes):
        if step:
            in_share = shift(in_share)
            out_share = shift(out_share)
        at = (plane - step) % planes
        in_all = lax.dynamic_update_index_in_dim(in_all, in_share, at, 0)
        out_all = lax.dynamic_update_index_in_dim(out_all, out_share, at, 0)
    in_all = in_all.reshape(planes * 4 * unit, width)
    out_all = out_all.reshape(planes * 2 * unit, width)
    hidden_width = out_all.shape[0]

    source = inputs.astype(wide)
    inverse_in = inverse_rms(source)
    lowered_in = (source * inverse_in * scales[:, 0]).astype(low)
    projected = dot(lowered_in, attn_whole, 1, 0)
    cosine, sine = rotary_tables(positions)
    by_head = projected.reshape(token_rows, heads + 2 * kv_heads, HEAD_SIZE).transpose(1, 0, 2)
    turned = rotate(by_head[: heads + kv_heads], cosine, sine).astype(low)
    query_heads = turned[:heads]
    key_values = jnp.concatenate([turned[heads:], by_head[heads + kv_heads :].astype(low)], axis=-1)

    def ids_of(which_plane, members):
        slots = [
            lax.dynamic_slice_in_dim(block_ids, 2 * (which_plane * PLANE + (place ^ m)), 2, 0)
            for m in members
        ]
        return jnp.concatenate(slots)

    query_ids = ids_of(plane, range(PLANE))
    lists = []
    for step in range(planes):
        at = (plane - step) % planes
        lists.append(
            jnp.stack(
                [
                    pair_lists(query_ids, ids_of(at, members), blocks_per_seq, span_blocks)
                    for members in (near, far)
                ]
            )
        )

    def pick_kv(mask):
        return pick(key_values, (place ^ mask) // 2)

    own_kv = [pick_kv(0)] + [swap(pick_kv(m), m) for m in near[1:]]
    own_kv = jnp.stack(own_kv).reshape(PLANE, block, 2 * HEAD_SIZE)
    query = jnp.stack(scatter_plane(query_heads, place)).reshape(2 * PLANE, block, HEAD_SIZE)
    kv_stages = []
    state = None
    for step in range(planes):
        if step:
            own_kv = shift(own_kv)
        other_kv = swap(own_kv, CORE)
        kv_stages.append((own_kv, other_kv))
        state = attend(lists[step], query, own_kv, other_kv, state)
    totals = jnp.sum(state[:, :, HEAD_SIZE:], axis=-1, keepdims=True)
    attended = state[:, :, :HEAD_SIZE] / totals
    by_member = attended.astype(low).reshape(PLANE, token_rows, HEAD_SIZE)
    attended_low = ordered(
        [by_member[0]] + [swap(by_member[m], m) for m in range(1, PLANE)], place
    )
    attended_low = attended_low.transpose(1, 0, 2).reshape(token_rows, heads * HEAD_SIZE)

    branch = dot(attended_low, out_whole, 1, 1)
    inverse_branch = inverse_rms(branch)
    middle = source + branch * inverse_branch * scales[:, 1]
    inverse_mid = inverse_rms(middle)
    lowered_mid = (middle * inverse_mid * scales[:, 2]).astype(low)
    mid_groups = gather_plane(lowered_mid)
    gate_ups = [dot(group, in_all, 1, 1).astype(low) for group in mid_groups]

    def activate(gate_up):
        gate = gate_up[:, :hidden_width].astype(wide)
        up = gate_up[:, hidden_width:].astype(wide)
        return jax.nn.gelu(gate, approximate=True) * up

    hiddens = [activate(gate_up).astype(low) for gate_up in gate_ups]
    down_branch = reduce_plane([dot(hidden, out_all, 1, 0) for hidden in hiddens])
    inverse_down = inverse_rms(down_branch)
    result = middle + down_branch * inverse_down * scales[:, 3]
    upstream = cotangent.astype(wide)
    grad_down, grad_gain_post = norm_back(down_branch, inverse_down, scales[:, 3], upstream)
    grad_down_low = grad_down.astype(low)
    down_groups = gather_plane(grad_down_low)

    def activate_back(gate_up, grad_hidden):
        gate = gate_up[:, :hidden_width].astype(wide)
        up = gate_up[:, hidden_width:].astype(wide)
        _, back = jax.vjp(lambda g, u: jax.nn.gelu(g, approximate=True) * u, gate, up)
        grad_gate, grad_up = back(grad_hidden)
        return jnp.concatenate([grad_gate, grad_up], axis=1).astype(low)

    grad_gate_ups = [
        activate_back(gate_up, dot(group, out_all, 1, 1))
        for gate_up, group in zip(gate_ups, down_groups)
    ]
    grad_lowered_mid = reduce_plane([dot(group, in_all, 1, 0) for group in grad_gate_ups])

    down_rows = jnp.concatenate(down_groups)
    grad_out_all = dot(jnp.concatenate(hiddens), down_rows, 0, 0).astype(low)
    grad_in_all = dot(
        jnp.concatenate(grad_gate_ups), jnp.concatenate(mid_groups), 0, 0
    ).astype(low)

    def ring_sum(parts):
        parts = parts.reshape((planes, -1) + parts.shape[1:])
        total = pick(parts, (plane + planes - 1) % planes)
        for step in range(1, planes):
            total = shift(total.astype(low)).astype(wide) + pick(
                parts, (plane + 2 * planes - 1 - step) % planes
            ).astype(wide)
        return total

    out_sum = ring_sum(grad_out_all).astype(low)
    in_sum = ring_sum(grad_in_all).astype(low)
    grad_pieces = jnp.concatenate(
        [
            in_sum.reshape(2, 2, unit, row_parts, row_share),
            out_sum.reshape(2, 1, unit, row_parts, row_share),
        ],
        axis=1,
    )
    grad_pieces = grad_pieces.transpose(0, 3, 1, 2, 4).reshape(PLANE, 3, unit, row_share)
    grad_pieces = ordered(scatter_plane(grad_pieces, place), place).astype(wide)
    grad_mlp_in = grad_pieces[:, :2].transpose(3, 1, 0, 2).reshape(mlp_in.shape)
    grad_mlp_out = grad_pieces[:, 2].transpose(2, 0, 1).reshape(mlp_out.shape)

    grad_through_mid, grad_gain_pre_mlp = norm_back(
        middle, inverse_mid, scales[:, 2], grad_lowered_mid
    )
    grad_middle = upstream + grad_through_mid
    grad_branch, grad_gain_post_attn = norm_back(branch, inverse_branch, scales[:, 1], grad_middle)
    grad_branch_low = grad_branch.astype(low)
    grad_attended = dot(grad_branch_low, out_whole, 1, 0).astype(low)
    grad_by_head = grad_attended.reshape(token_rows, heads, HEAD_SIZE).transpose(1, 0, 2)
    grad_rows = jnp.stack(scatter_plane(grad_by_head, place)).reshape(query.shape).astype(wide)
    row_terms = -jnp.sum(grad_rows * attended, axis=-1) / totals[..., 0]
    grad_summed = (grad_rows / totals).astype(low)
    row_terms = row_terms[:, None, :]
    grad_query = None
    kv_total = None
    for step in range(planes):
        stage = (step + 1) % planes
        own_kv, other_kv = kv_stages[stage]
        grad_query, own_grad, other_grad = attend_back(
            lists[stage], query, grad_summed, row_terms, own_kv, other_kv, grad_query
        )
        part = own_grad.astype(wide) + swap(other_grad, CORE).astype(wide)
        if kv_total is not None:
            part = part + shift(kv_total).astype(wide)
        kv_total = part.astype(low)
    kv_by_member = kv_total.reshape(len(near), token_rows, 2 * HEAD_SIZE)
    grad_kv = ordered(
        [kv_by_member[0]] + [swap(kv_by_member[m // 2], m) for m in near[1:]], place // 2
    ).astype(wide)
    grad_query = grad_query.astype(low).reshape(PLANE, token_rows, HEAD_SIZE)
    grad_queries = ordered(
        [grad_query[0]] + [swap(grad_query[m], m) for m in range(1, PLANE)], place
    ).astype(wide)
    turned_back = rotate(
        jnp.concatenate([grad_queries, grad_kv[:, :, :HEAD_SIZE]]) * score_scale, cosine, -sine
    )
    grad_projected = (
        jnp.concatenate([turned_back, grad_kv[:, :, HEAD_SIZE:]])
        .astype(low)
        .transpose(1, 0, 2)
        .reshape(token_rows, (heads + 2 * kv_heads) * HEAD_SIZE)
    )
    grad_lowered_in = dot(grad_projected, attn_whole, 1, 1)
    grad_source, grad_gain_in = norm_back(source, inverse_in, scales[:, 0], grad_lowered_in)
    grad_input = grad_middle + grad_source

    def spread(left, right, shape):
        parts = dot(left, right, 0, 0).astype(low)
        parts = parts.reshape(row_parts, row_share, ctx_count, shape[1]).transpose(2, 0, 1, 3)
        parts = parts.reshape((devices * row_share, shape[1]))
        return lax.psum_scatter(parts, AXES, scatter_dimension=0, tiled=True).astype(wide)

    grad_attn_out = spread(grad_branch_low, attended_low, attn_out.shape)
    grad_attn_in = spread(lowered_in, grad_projected, attn_in.shape)
    gain_terms = jnp.stack(
        [grad_gain_in, grad_gain_post_attn, grad_gain_pre_mlp, grad_gain_post], axis=1
    )
    gain_total = lax.psum(gain_terms, AXES)
    grad_gains = lax.dynamic_slice_in_dim(
        gain_total, lax.axis_index("fsdp") * row_share, row_share, 0
    )
    return (
        result.astype(low),
        grad_input,
        grad_attn_in,
        grad_attn_out,
        grad_mlp_in,
        grad_mlp_out,
        grad_gains,
    )


def solution(mesh):
    placed = (
        P(("ctx", "fsdp"), None),
        P(("ctx", "fsdp"), None),
        P(),
        P(("ctx", "fsdp")),
        P("fsdp", "ctx"),
        P("fsdp", "ctx"),
        P("fsdp", "ctx"),
        P("fsdp", "ctx"),
        P("fsdp", None),
    )
    return jax.shard_map(
        body,
        mesh=mesh,
        in_specs=placed,
        out_specs=(
            P(("ctx", "fsdp"), None),
            P(("ctx", "fsdp"), None),
            P("fsdp", "ctx"),
            P("fsdp", "ctx"),
            P("fsdp", "ctx"),
            P("fsdp", "ctx"),
            P("fsdp", None),
        ),
        check_vma=False,
    )
```

```python
import functools
import math

import jax
import jax.numpy as jnp
from jax import lax
from jax.experimental import pallas as pl
from jax.experimental.pallas import tpu as pltpu
from jax.sharding import PartitionSpec as P

QUERY_HEADS = 8
KEY_VALUE_HEADS = 4
HEAD_SIZE = 256
LOOKBACK_SPAN = 4096
SEQUENCE_COUNT = 2


EPSILON = 1e-06
SOFT_CAP = 50.0
ROPE_BASE = 10000.0
AXES = ("ctx", "fsdp")
PLANE = 8
CORE, SIDE, ACROSS = 1, 2, 4
TANH_SCALE = HEAD_SIZE ** (-0.5) / SOFT_CAP
EXP2_SCALE = SOFT_CAP * math.log2(math.e)
VMEM_BYTES = 56 * 1024 * 1024


def inverse_rms(values):
    return lax.rsqrt(jnp.mean(values * values, axis=-1, keepdims=True) + EPSILON)


def norm_back(values, inverse, scale, upstream):
    scaled = upstream * scale
    through = inverse * scaled - values * inverse**3 * jnp.mean(
        scaled * values, axis=-1, keepdims=True
    )
    return (through, jnp.sum(upstream * values * inverse, axis=0))


def rotate(values, cosine, sine):
    half_width = values.shape[-1] // 2
    first_half = values[..., :half_width]
    second_half = values[..., half_width:]
    return jnp.concatenate(
        [
            first_half * cosine - second_half * sine,
            second_half * cosine + first_half * sine,
        ],
        axis=-1,
    )


def dot(left, right, left_axis, right_axis):
    return lax.dot_general(
        left,
        right,
        (((left_axis,), (right_axis,)), ((), ())),
        preferred_element_type=jnp.float32,
    )


def after(value, *others):
    return lax.optimization_barrier((value,) + others)[0]


def wide(values):
    return values.astype(jnp.float32)


def narrow(values):
    return values.astype(jnp.bfloat16)


def swap(values, mask):
    count = lax.axis_size(AXES)
    return lax.ppermute(values, AXES, [(i, i ^ mask) for i in range(count)])


def shift(values, steps=1):
    count = lax.axis_size(AXES)
    return lax.ppermute(values, AXES, [(i, (i + steps * PLANE) % count) for i in range(count)])


def route(values, targets):
    count = lax.axis_size(AXES)
    return lax.ppermute(
        values, AXES, [(i, i - i % PLANE + targets[i % PLANE]) for i in range(count)]
    )


def pick(stacked, index):
    return lax.dynamic_index_in_dim(stacked, index, 0, keepdims=False)


def look_up(table, place):
    return pick(jnp.asarray(table, jnp.int32), place)


def exchange(stacked, place, masks=tuple(range(PLANE))):
    return [
        swap(pick(stacked, place ^ mask), mask) if mask else pick(stacked, place) for mask in masks
    ]


def ordered(received, place):
    stacked = jnp.stack(received)
    return jnp.stack([pick(stacked, place ^ j) for j in range(len(received))])


NEAR = [(0, 0), (0, 1), (4, 0), (2, 1), (2, 0), (6, 0), (4, 1), (6, 1)]
FAR = [(mask ^ CORE, half) for mask, half in NEAR]


def gather_plane(rows, work, tied=True):
    half = rows.shape[0] // 2
    low, high = rows[:half], rows[half:]
    other = swap(rows, CORE)
    across_low = swap(low, ACROSS)
    side_high = swap(high, SIDE)
    own = jnp.concatenate([rows, other])
    done = [work(own)] if tied else []
    first = jnp.concatenate([across_low, side_high])
    if tied:
        first = after(first, done[0])
    first_other = swap(first, CORE)
    side_lows = swap(jnp.concatenate([low, first[:half]]), SIDE)
    across_highs = swap(jnp.concatenate([high, first[half:]]), ACROSS)
    first = jnp.concatenate([first, first_other])
    second = jnp.concatenate([side_lows, across_highs])
    if tied:
        done.append(work(first))
        second = after(second, done[1])
    second_other = swap(second, CORE)
    groups = [own, first, second, second_other]
    return groups, done + [work(group) for group in groups[len(done) :]]


def reduce_plane(work):
    second_far = narrow(work(3, None)[1])
    second_got = swap(second_far, CORE)
    second_near = lax.optimization_barrier(narrow(work(2, second_far)[0]))
    second_sum = narrow(wide(second_near) + wide(second_got))
    rows = second_sum.shape[0] // 2
    half = rows // 2
    from_side = swap(second_sum[:rows], SIDE)
    from_across = swap(second_sum[rows:], ACROSS)
    first_near, first_far = work(1, second_sum)
    own_near, own_far = work(0, second_sum)
    first_near, first_far, own_near, own_far = lax.optimization_barrier(
        (narrow(first_near), narrow(first_far), narrow(own_near), narrow(own_far))
    )
    first_sum = wide(first_near) + wide(swap(first_far, CORE))
    own_sum = wide(own_near) + wide(swap(own_far, CORE))
    across_low = narrow(first_sum[:half] + wide(from_side[half:]))
    side_high = narrow(first_sum[half:] + wide(from_across[half:]))
    got_low = swap(across_low, ACROSS)
    got_high = swap(side_high, SIDE)
    return jnp.concatenate(
        [
            own_sum[:half] + wide(from_side[:half]) + wide(got_low),
            own_sum[half:] + wide(from_across[:half]) + wide(got_high),
        ]
    )


def sum_devices(values):
    for mask in (CORE, SIDE, ACROSS):
        values = values + swap(values, mask)
    total = values
    for steps in range(1, lax.axis_size(AXES) // PLANE):
        total = total + shift(values, steps)
    return total


class RingSum:
    def __init__(self, parts, plane):
        self.parts, self.plane, self.planes = parts, plane, parts.shape[0]
        self.hops, self.moving = 0, None
        self.total = self.part(0)

    def part(self, step):
        return pick(self.parts, (self.plane + 2 * self.planes - 1 - step) % self.planes)

    def start(self, *others):
        if self.hops < self.planes - 1:
            self.moving = shift(after(self.total, *others) if others else self.total)

    def finish(self):
        if self.moving is not None:
            self.hops += 1
            self.total = narrow(wide(self.moving) + wide(self.part(self.hops)))
            self.moving = None
        return self.total

    def finish_all(self):
        self.finish()
        while self.hops < self.planes - 1:
            self.start()
            self.finish()
        return self.total


def matchings(edges):
    left, rounds = list(edges), []
    while left:
        owner = {}

        def settle(source, seen):
            for edge in left:
                if edge[0] == source and edge[1] not in seen:
                    seen.add(edge[1])
                    if edge[1] not in owner or settle(owner[edge[1]][0], seen):
                        owner[edge[1]] = edge
                        return True
            return False

        for source in range(PLANE):
            settle(source, set())
        found = sorted(owner.values())
        rounds.append(found)
        left = [edge for edge in left if edge not in found]
    return rounds


def chunk_edges(plane_count, columns, chunk, share):
    edges = []
    for source in range(PLANE):
        for at in range(plane_count):
            column = (2 * at + source // 4) * columns + source % 4 * chunk
            head = column // HEAD_SIZE
            for target in range(head * share, (head + 1) * share):
                edges.append((source, target, at, column % HEAD_SIZE // chunk))
    return edges


def chunks_to_heads(stored, rounds, place):
    spots = len(rounds)
    got = []
    for found in rounds:
        sent = pick(stored, look_up([edge[2] for edge in found], place))
        got.append(route(sent, [edge[1] for edge in found]))
    stacked = jnp.stack(got)
    order = []
    for spot in range(spots):
        table = [0] * PLANE
        for step, found in enumerate(rounds):
            for edge in found:
                if edge[3] == spot:
                    table[edge[1]] = step
        order.append(pick(stacked, look_up(table, place)))
    return order


def heads_to_chunks(heads, rounds, place, plane_count):
    got = []
    for found in rounds:
        back, spot = [0] * PLANE, [0] * PLANE
        for source, target, _, position in found:
            back[target], spot[target] = source, position
        got.append(route(pick(heads, look_up(spot, place)), back))
    stacked = jnp.stack(got)
    chunks = []
    for at in range(plane_count):
        tables = []
        for source in range(PLANE):
            tables.append(
                [
                    step
                    for step, found in enumerate(rounds)
                    for edge in found
                    if edge[0] == source and edge[2] == at
                ]
            )
        terms = [
            pick(stacked, look_up([table[i] for table in tables], place))
            for i in range(len(tables[0]))
        ]
        total = terms[0]
        if len(terms) > 1:
            total = narrow(sum(wide(term) for term in terms))
        chunks.append(total)
    return jnp.stack(chunks)


def row_product_kernel(count, *refs):
    out, total = refs[-2:]
    total[...] = dot(refs[0][...], refs[count][...], 0, 0)
    for i in range(1, count):
        total[...] += dot(refs[i][...], refs[count + i][...], 0, 0)
    out[...] = total[...].astype(out.dtype)


def row_product(lefts, rights, left_tile, right_tile):
    count = len(lefts)
    height, width = lefts[0].shape[1], rights[0].shape[1]
    depths = [left.shape[0] for left in lefts]
    return pl.pallas_call(
        functools.partial(row_product_kernel, count),
        out_shape=jax.ShapeDtypeStruct((height, width), jnp.bfloat16),
        grid=(height // left_tile, width // right_tile),
        in_specs=[pl.BlockSpec((depth, left_tile), lambda i, j: (0, i)) for depth in depths]
        + [pl.BlockSpec((depth, right_tile), lambda i, j: (0, j)) for depth in depths],
        out_specs=pl.BlockSpec((left_tile, right_tile), lambda i, j: (i, j)),
        scratch_shapes=[pltpu.VMEM((left_tile, right_tile), jnp.float32)],
        compiler_params=pltpu.CompilerParams(vmem_limit_bytes=VMEM_BYTES),
        cost_estimate=pl.CostEstimate(
            flops=2 * sum(depths) * height * width,
            bytes_accessed=2 * sum(depths) * (height + width) + 2 * height * width,
            transcendentals=0,
        ),
    )(*lefts, *rights)


def out_kernel(part, rows_ref, weight_ref, out_ref):
    at = pl.program_id(0)
    total = dot(rows_ref[0], weight_ref[0, 0], 1, 1)
    for head in range(1, rows_ref.shape[0]):
        total += dot(rows_ref[head], weight_ref[head, 0], 1, 1)
    for i in range(out_ref.shape[1] // part):

        @pl.when(at == i)
        def _():
            out_ref[:, i * part : (i + 1) * part] = total


def out_product(rows, weight):
    heads, count, size = rows.shape
    _, parts, part, _ = weight.shape
    return pl.pallas_call(
        functools.partial(out_kernel, part),
        out_shape=jax.ShapeDtypeStruct((count, parts * part), jnp.float32),
        grid=(parts,),
        in_specs=[
            pl.BlockSpec((heads, count, size), lambda i: (0, 0, 0)),
            pl.BlockSpec((heads, 1, part, size), lambda i: (0, i, 0, 0)),
        ],
        out_specs=pl.BlockSpec((count, parts * part), lambda i: (0, 0)),
        compiler_params=pltpu.CompilerParams(vmem_limit_bytes=VMEM_BYTES),
        cost_estimate=pl.CostEstimate(
            flops=2 * count * heads * size * parts * part,
            bytes_accessed=2 * heads * size * (count + parts * part) + 4 * count * parts * part,
            transcendentals=0,
        ),
    )(rows, weight)


def out_back_kernel(rows_ref, weight_ref, out_ref):
    part = weight_ref.shape[2]
    total = dot(rows_ref[:, :part], weight_ref[0, 0], 1, 0)
    for i in range(1, weight_ref.shape[1]):
        total += dot(rows_ref[:, i * part : (i + 1) * part], weight_ref[0, i], 1, 0)
    out_ref[0] = total.astype(out_ref.dtype)


def out_back_product(rows, weight):
    count, width = rows.shape
    heads, parts, part, size = weight.shape
    return pl.pallas_call(
        out_back_kernel,
        out_shape=jax.ShapeDtypeStruct((heads, count, size), jnp.bfloat16),
        grid=(heads,),
        in_specs=[
            pl.BlockSpec((count, width), lambda i: (0, 0)),
            pl.BlockSpec((1, parts, part, size), lambda i: (i, 0, 0, 0)),
        ],
        out_specs=pl.BlockSpec((1, count, size), lambda i: (i, 0, 0)),
        compiler_params=pltpu.CompilerParams(vmem_limit_bytes=VMEM_BYTES),
        cost_estimate=pl.CostEstimate(
            flops=2 * count * heads * size * width,
            bytes_accessed=2 * heads * size * (count + width) + 2 * count * width,
            transcendentals=0,
        ),
    )(rows, weight)


def out_grad_kernel(rows_ref, heads_ref, out_ref):
    out_ref[0] = dot(rows_ref[...], heads_ref[0], 0, 0).astype(out_ref.dtype)


def out_grad_product(rows, by_head):
    count, width = rows.shape
    heads, _, size = by_head.shape
    return pl.pallas_call(
        out_grad_kernel,
        out_shape=jax.ShapeDtypeStruct((heads, width, size), jnp.bfloat16),
        grid=(heads,),
        in_specs=[
            pl.BlockSpec((count, width), lambda i: (0, 0)),
            pl.BlockSpec((1, count, size), lambda i: (i, 0, 0)),
        ],
        out_specs=pl.BlockSpec((1, width, size), lambda i: (i, 0, 0)),
        compiler_params=pltpu.CompilerParams(vmem_limit_bytes=VMEM_BYTES),
        cost_estimate=pl.CostEstimate(
            flops=2 * count * heads * size * width,
            bytes_accessed=2 * heads * size * (count + width) + 2 * count * width,
            transcendentals=0,
        ),
    )(rows, by_head)


def pair_lists(query_ids, key_ids, blocks_per_seq, span_blocks):
    query_seq, query_at = query_ids // blocks_per_seq, query_ids % blocks_per_seq
    key_seq, key_at = key_ids // blocks_per_seq, key_ids % blocks_per_seq
    distance = (query_at[:, None] - key_at[None, :]).reshape(-1)
    same = (query_seq[:, None] == key_seq[None, :]).reshape(-1)
    whole = same & (distance > 0) & (distance < span_blocks)
    edged = same & ((distance == 0) | (distance == span_blocks))
    count_whole = jnp.sum(whole.astype(jnp.int32))
    count_edged = jnp.sum(edged.astype(jnp.int32))
    place = jnp.where(
        whole,
        jnp.cumsum(whole.astype(jnp.int32)) - 1,
        jnp.where(edged, count_whole + jnp.cumsum(edged.astype(jnp.int32)) - 1, -1),
    )
    total = distance.shape[0]
    code = jnp.arange(total, dtype=jnp.int32) * 2 + (distance == span_blocks).astype(jnp.int32)
    hit = place[:, None] == jnp.arange(total, dtype=jnp.int32)[None, :]
    entries = jnp.sum(jnp.where(hit, code[:, None], 0), axis=0)
    return jnp.concatenate([jnp.stack([count_whole, count_edged]), entries]).astype(jnp.int32)


def run_pairs(list_ref, row, key_count, unroll, visit):
    whole = list_ref[row, 0]
    edged = list_ref[row, 1]

    def decode(position):
        code = list_ref[row, 2 + position]
        pair = code // 2
        return pair // key_count, pair % key_count, code % 2

    def several(step, carry):
        found = [decode(step * unroll + i) for i in range(unroll)]
        visit([f[0] for f in found], [f[1] for f in found], None)
        return carry

    def single(position, carry):
        i, j, _ = decode(position)
        visit([i], [j], None)
        return carry

    def masked(position, carry):
        i, j, far = decode(position)
        visit([i], [j], far)
        return carry

    groups = whole // unroll
    lax.fori_loop(0, groups, several, 0)
    lax.fori_loop(groups * unroll, whole, single, 0)
    lax.fori_loop(whole, whole + edged, masked, 0)


def attend_kernel(first, unroll, list_ref, query_hbm, own_hbm, other_hbm, *rest):
    if first:
        state_hbm = None
        out_hbm, query, own, other, state, sems = rest
    else:
        state_hbm, out_hbm, query, own, other, state, sems = rest
    copies = [
        pltpu.make_async_copy(query_hbm, query, sems.at[0]),
        pltpu.make_async_copy(own_hbm, own, sems.at[1]),
        pltpu.make_async_copy(other_hbm, other, sems.at[2]),
    ]
    if not first:
        copies.append(pltpu.make_async_copy(state_hbm, state, sems.at[3]))
    for copy in copies:
        copy.start()
    if first:
        state[...] = jnp.zeros_like(state)
    for copy in copies:
        copy.wait()
    rows = query.shape[1]
    lane = lax.broadcasted_iota(jnp.int32, (rows, 128), 1)

    def visit_in(keys):
        def visit(query_at, key_at, far):
            scores = [
                dot(query[i], keys[j, :, :HEAD_SIZE], 1, 1) for i, j in zip(query_at, key_at)
            ]
            for i, j, score in zip(query_at, key_at, scores):
                weights = jnp.exp2(EXP2_SCALE * jnp.tanh(score * TANH_SCALE))
                if far is not None:
                    spacing = (
                        lax.broadcasted_iota(jnp.int32, weights.shape, 0)
                        - lax.broadcasted_iota(jnp.int32, weights.shape, 1)
                        + far * LOOKBACK_SPAN
                    )
                    live = (spacing >= 0) & (spacing < LOOKBACK_SPAN)
                    weights = jnp.where(live, weights, 0.0)
                if rows % 128 == 0:
                    part = weights[:, :128]
                    for k in range(1, rows // 128):
                        part = part + weights[:, k * 128 : (k + 1) * 128]
                else:
                    part = jnp.where(lane == 0, jnp.sum(weights, axis=1, keepdims=True), 0.0)
                state[i, :, HEAD_SIZE:] += part
                state[i, :, :HEAD_SIZE] += dot(
                    weights.astype(jnp.bfloat16), keys[j, :, HEAD_SIZE:], 1, 0
                )

        return visit

    key_count = own.shape[0]
    run_pairs(list_ref, 0, key_count, unroll, visit_in(own))
    run_pairs(list_ref, 1, key_count, unroll, visit_in(other))
    out = pltpu.make_async_copy(state, out_hbm, sems.at[4])
    out.start()
    out.wait()


def attend(lists, query, own, other, state):
    first = state is None
    blocks, rows, _ = query.shape
    shape = (blocks, rows, HEAD_SIZE + 128)
    operands = (query, own, other) if first else (query, own, other, state)
    return pl.pallas_call(
        functools.partial(attend_kernel, first, 4),
        out_shape=jax.ShapeDtypeStruct(shape, jnp.float32),
        grid_spec=pltpu.PrefetchScalarGridSpec(
            num_scalar_prefetch=1,
            grid=(1,),
            in_specs=[pl.BlockSpec(memory_space=pl.ANY)] * len(operands),
            out_specs=pl.BlockSpec(memory_space=pl.ANY),
            scratch_shapes=[
                pltpu.VMEM(query.shape, jnp.bfloat16),
                pltpu.VMEM(own.shape, jnp.bfloat16),
                pltpu.VMEM(other.shape, jnp.bfloat16),
                pltpu.VMEM(shape, jnp.float32),
                pltpu.SemaphoreType.DMA((5,)),
            ],
        ),
        compiler_params=pltpu.CompilerParams(vmem_limit_bytes=VMEM_BYTES),
        cost_estimate=pl.CostEstimate(
            flops=60 * 4 * rows * rows * HEAD_SIZE,
            bytes_accessed=14 * 1024 * 1024,
            transcendentals=60 * 2 * rows * rows,
        ),
    )(lists, *operands)


def attend_back_kernel(
    first,
    unroll,
    list_ref,
    query_hbm,
    grad_hbm,
    term_hbm,
    own_hbm,
    other_hbm,
    *rest,
):
    if first:
        state_hbm = None
    else:
        state_hbm, *rest = rest
    (
        out_hbm,
        own_out_hbm,
        other_out_hbm,
        query,
        grad,
        term,
        own,
        other,
        state,
        own_grad,
        other_grad,
        own_low,
        other_low,
        sems,
    ) = rest
    copies = [
        pltpu.make_async_copy(query_hbm, query, sems.at[0]),
        pltpu.make_async_copy(grad_hbm, grad, sems.at[1]),
        pltpu.make_async_copy(term_hbm, term, sems.at[2]),
        pltpu.make_async_copy(own_hbm, own, sems.at[3]),
        pltpu.make_async_copy(other_hbm, other, sems.at[4]),
    ]
    if not first:
        copies.append(pltpu.make_async_copy(state_hbm, state, sems.at[5]))
    for copy in copies:
        copy.start()
    if first:
        state[...] = jnp.zeros_like(state)
    own_grad[...] = jnp.zeros_like(own_grad)
    other_grad[...] = jnp.zeros_like(other_grad)
    for copy in copies:
        copy.wait()

    def visit_in(keys, key_grad):
        def visit(query_at, key_at, far):
            scores = []
            slopes = []
            for i, j in zip(query_at, key_at):
                scores.append(dot(keys[j, :, :HEAD_SIZE], query[i], 1, 1))
                slopes.append(dot(keys[j, :, HEAD_SIZE:], grad[i], 1, 1))
            for i, j, score, slope in zip(query_at, key_at, scores, slopes):
                bent = jnp.tanh(score * TANH_SCALE)
                weights = jnp.exp2(EXP2_SCALE * bent)
                if far is not None:
                    spacing = (
                        lax.broadcasted_iota(jnp.int32, weights.shape, 1)
                        - lax.broadcasted_iota(jnp.int32, weights.shape, 0)
                        + far * LOOKBACK_SPAN
                    )
                    live = (spacing >= 0) & (spacing < LOOKBACK_SPAN)
                    weights = jnp.where(live, weights, 0.0)
                grad_scores = (
                    (slope + term[i]) * (weights * (1.0 - bent * bent))
                ).astype(jnp.bfloat16)
                key_grad[j, :, :HEAD_SIZE] += dot(grad_scores, query[i], 1, 0)
                key_grad[j, :, HEAD_SIZE:] += dot(weights.astype(jnp.bfloat16), grad[i], 1, 0)
                state[i] += dot(grad_scores, keys[j, :, :HEAD_SIZE], 0, 0)

        return visit

    key_count = own.shape[0]
    run_pairs(list_ref, 1, key_count, unroll, visit_in(other, other_grad))
    other_low[...] = other_grad[...].astype(jnp.bfloat16)
    other_out = pltpu.make_async_copy(other_low, other_out_hbm, sems.at[6])
    other_out.start()
    run_pairs(list_ref, 0, key_count, unroll, visit_in(own, own_grad))
    own_low[...] = own_grad[...].astype(jnp.bfloat16)
    own_out = pltpu.make_async_copy(own_low, own_out_hbm, sems.at[7])
    own_out.start()
    out = pltpu.make_async_copy(state, out_hbm, sems.at[8])
    out.start()
    other_out.wait()
    own_out.wait()
    out.wait()


def attend_back(lists, query, grad, term, own, other, state):
    first = state is None
    blocks, rows, _ = query.shape
    operands = (query, grad, term, own, other)
    if not first:
        operands = operands + (state,)
    return pl.pallas_call(
        functools.partial(attend_back_kernel, first, 2),
        out_shape=[
            jax.ShapeDtypeStruct(query.shape, jnp.float32),
            jax.ShapeDtypeStruct(own.shape, jnp.bfloat16),
            jax.ShapeDtypeStruct(other.shape, jnp.bfloat16),
        ],
        grid_spec=pltpu.PrefetchScalarGridSpec(
            num_scalar_prefetch=1,
            grid=(1,),
            in_specs=[pl.BlockSpec(memory_space=pl.ANY)] * len(operands),
            out_specs=[pl.BlockSpec(memory_space=pl.ANY)] * 3,
            scratch_shapes=[
                pltpu.VMEM(query.shape, jnp.bfloat16),
                pltpu.VMEM(query.shape, jnp.bfloat16),
                pltpu.VMEM(term.shape, jnp.float32),
                pltpu.VMEM(own.shape, jnp.bfloat16),
                pltpu.VMEM(other.shape, jnp.bfloat16),
                pltpu.VMEM(query.shape, jnp.float32),
                pltpu.VMEM(own.shape, jnp.float32),
                pltpu.VMEM(other.shape, jnp.float32),
                pltpu.VMEM(own.shape, jnp.bfloat16),
                pltpu.VMEM(other.shape, jnp.bfloat16),
                pltpu.SemaphoreType.DMA((9,)),
            ],
        ),
        compiler_params=pltpu.CompilerParams(vmem_limit_bytes=VMEM_BYTES),
        cost_estimate=pl.CostEstimate(
            flops=60 * 10 * rows * rows * HEAD_SIZE,
            bytes_accessed=24 * 1024 * 1024,
            transcendentals=60 * 2 * rows * rows,
        ),
    )(lists, *operands)


def body(inputs, cotangent, block_ids, positions, attn_in, attn_out, mlp_in, mlp_out, gains):
    token_rows, width = inputs.shape
    block = token_rows // 2
    devices = lax.axis_size(AXES)
    ctx_count, row_parts = lax.axis_size("ctx"), lax.axis_size("fsdp")
    planes = devices // PLANE
    blocks_per_seq = 2 * devices // SEQUENCE_COUNT
    span_blocks = LOOKBACK_SPAN // block
    score_scale = HEAD_SIZE ** (-0.5)
    me = lax.axis_index(AXES)
    place, plane = me % PLANE, me // PLANE
    part = place % row_parts
    row_share = attn_in.shape[0]
    unit = mlp_out.shape[1] // PLANE
    chunk = attn_in.shape[1] // row_parts
    order = NEAR + FAR

    gain_parts = ordered([gains.T] + [swap(gains.T, mask) for mask in range(1, row_parts)], part)
    scales = wide(gain_parts.transpose(1, 0, 2).reshape(gains.shape[1], width))
    source = wide(inputs)
    inverse_in = inverse_rms(source)
    lowered_in = narrow(source * inverse_in * scales[0])

    in_pieces = exchange(
        attn_in.T.reshape(row_parts, chunk, row_share), part, tuple(range(row_parts))
    )
    in_chunk = ordered(in_pieces, part).transpose(1, 0, 2).reshape(chunk, width)
    stored = jnp.zeros((planes, chunk, width), jnp.bfloat16)
    for step in range(planes):
        if step:
            in_chunk = shift(in_chunk)
        stored = lax.dynamic_update_index_in_dim(stored, in_chunk, (plane - step) % planes, 0)
    query_planes, kv_planes = planes // 2, planes // 4
    query_rounds = matchings(chunk_edges(query_planes, attn_in.shape[1], chunk, 1))
    kv_rounds = matchings(
        chunk_edges(kv_planes, attn_in.shape[1], chunk, QUERY_HEADS // KEY_VALUE_HEADS)
    )
    query_chunks = chunks_to_heads(stored[:query_planes], query_rounds, place)
    kv_chunks = chunks_to_heads(
        jnp.concatenate(
            [stored[query_planes : query_planes + kv_planes], stored[query_planes + kv_planes :]],
            axis=1,
        ),
        kv_rounds,
        place,
    )
    attn_weight = jnp.concatenate(
        query_chunks + [both[:chunk] for both in kv_chunks] + [both[chunk:] for both in kv_chunks]
    )

    mlp_pieces = jnp.concatenate(
        [
            mlp_in.T.reshape(2, PLANE, unit, row_share).transpose(1, 0, 2, 3),
            mlp_out.T.reshape(PLANE, 1, unit, row_share),
        ],
        axis=1,
    )
    mlp_share = ordered(exchange(mlp_pieces, place), place)
    mlp_share = (
        mlp_share.reshape(2, row_parts, 3, unit, row_share)
        .transpose(0, 2, 3, 1, 4)
        .reshape(2, 3 * unit, width)
    )
    in_share = mlp_share[:, : 2 * unit].reshape(4 * unit, width)
    out_share = mlp_share[:, 2 * unit :].reshape(2 * unit, width)
    in_all = jnp.zeros((planes, 4 * unit, width), jnp.bfloat16)
    out_all = jnp.zeros((planes, 2 * unit, width), jnp.bfloat16)

    def place_in(whole, share, step):
        return lax.dynamic_update_index_in_dim(whole, share, (plane - step) % planes, 0)

    in_all = place_in(in_all, in_share, 0)
    out_all = place_in(out_all, out_share, 0)
    in_share = shift(in_share)

    def ids_of(which_plane, slots):
        return jnp.stack(
            [
                lax.dynamic_index_in_dim(
                    block_ids, 2 * (which_plane * PLANE + (place ^ mask)) + half, keepdims=False
                )
                for mask, half in slots
            ]
        )

    query_ids = ids_of(plane, order)
    half_width = HEAD_SIZE // 2
    frequency = ROPE_BASE ** (-2.0 * jnp.arange(half_width, dtype=jnp.float32) / HEAD_SIZE)
    base_angle = wide(query_ids % blocks_per_seq * block)[:, None, None] * frequency
    step_angle = jnp.arange(block, dtype=jnp.float32)[:, None] * frequency
    base_cosine, base_sine = jnp.cos(base_angle), jnp.sin(base_angle)
    step_cosine, step_sine = jnp.cos(step_angle), jnp.sin(step_angle)
    cosine = base_cosine * step_cosine - base_sine * step_sine
    sine = base_sine * step_cosine + base_cosine * step_sine

    in_groups, projected = gather_plane(
        lowered_in, lambda group: dot(group, attn_weight, 1, 1), tied=False
    )

    def split_groups(groups):
        near = jnp.concatenate([groups[0][:token_rows], groups[1][:token_rows], groups[2]])
        far = jnp.concatenate([groups[0][token_rows:], groups[1][token_rows:], groups[3]])
        return [rows.reshape(len(NEAR), block, rows.shape[1]) for rows in (near, far)]

    near_rows, far_rows = split_groups(projected)
    query_parts, kv_parts = [], []
    for rows, low, high in ((near_rows, 0, len(NEAR)), (far_rows, len(NEAR), 2 * len(NEAR))):
        turns = (cosine[low:high], sine[low:high])
        query_parts.append(narrow(rotate(rows[:, :, :HEAD_SIZE], *turns)))
        kv_parts.append(
            jnp.concatenate(
                [
                    narrow(rotate(rows[:, :, HEAD_SIZE : 2 * HEAD_SIZE], *turns)),
                    narrow(rows[:, :, 2 * HEAD_SIZE :]),
                ],
                axis=-1,
            )
        )
    own_kv, other_kv = kv_parts
    query = jnp.concatenate(query_parts)

    lists = []
    for step in range(planes):
        at = (plane - step) % planes
        lists.append(
            jnp.stack(
                [
                    pair_lists(query_ids, ids_of(at, slots), blocks_per_seq, span_blocks)
                    for slots in (NEAR, FAR)
                ]
            )
        )
    gathered_out = lax.all_gather(after(attn_out, own_kv), AXES, axis=0)
    kv_stages = [(own_kv, other_kv)]
    moving = shift(own_kv)
    state = attend(lists[0], query, own_kv, other_kv, None)
    in_arrived = 1
    for step in range(1, planes):
        own_kv = after(moving, state)
        if step < planes - 1:
            moving = shift(own_kv)
        elif planes > 1:
            in_next = shift(after(in_share, own_kv))
        other_kv = swap(own_kv, CORE)
        kv_stages.append((own_kv, other_kv))
        state = attend(lists[step], query, own_kv, other_kv, state)
    in_all = place_in(in_all, in_share, 1)
    totals = jnp.sum(state[:, :, HEAD_SIZE:], axis=-1, keepdims=True)
    attended = state[:, :, :HEAD_SIZE] / totals
    attended_rows = narrow(attended)

    def member_rows(blocks, mask):
        return jnp.concatenate([blocks[order.index((mask, 0))], blocks[order.index((mask, 1))]])

    def blocks_of(received):
        return jnp.stack(
            [received[mask][half * block : (half + 1) * block] for mask, half in order]
        )

    attended_heads = ordered(
        [member_rows(attended_rows, 0)]
        + [swap(member_rows(attended_rows, mask), mask) for mask in range(1, PLANE)],
        place,
    )
    gathered_out = (
        gathered_out.reshape((QUERY_HEADS, -1, row_parts) + attn_out.shape)
        .transpose(0, 2, 3, 1, 4)
        .reshape(QUERY_HEADS, row_parts, row_share, HEAD_SIZE)
    )

    attended_heads = after(attended_heads, in_next)
    in_all = place_in(in_all, in_next, 2)
    for step in range(3, planes):
        in_next = shift(in_next)
        in_all = place_in(in_all, in_next, step)
    branch = out_product(attended_heads, gathered_out)
    inverse_branch = inverse_rms(branch)
    middle = source + branch * inverse_branch * scales[1]
    inverse_mid = inverse_rms(middle)
    lowered_mid = narrow(middle * inverse_mid * scales[2])
    in_all = in_all.reshape(planes * 4 * unit, width)
    hidden_width = planes * 2 * unit
    out_next = shift(after(out_share, in_next))

    def gate_up_of(group):
        return narrow(dot(group, in_all, 1, 1))

    mid_groups, gate_ups = gather_plane(lowered_mid, gate_up_of)
    for step in range(1, planes):
        if step > 1:
            out_next = shift(out_next)
        if step < 3:
            out_next = after(out_next, gate_ups[step - 1])
        out_all = place_in(out_all, out_next, step)
    out_all = out_all.reshape(hidden_width, width)

    def activate(gate_up):
        gate = wide(gate_up[:, :hidden_width])
        up = wide(gate_up[:, hidden_width:])
        return jax.nn.gelu(gate, approximate=True) * up

    hiddens = [narrow(activate(gate_up)) for gate_up in gate_ups]

    def reduce_groups(groups, weight):
        def work(index, token):
            group = groups[index] if token is None else after(groups[index], token)
            partial = narrow(dot(group, weight, 1, 0))
            if index > 1:
                return partial, partial
            return partial[:token_rows], partial[token_rows:]

        return reduce_plane(work)

    down_branch = reduce_groups(hiddens, out_all)
    inverse_down = inverse_rms(down_branch)
    result = middle + down_branch * inverse_down * scales[3]
    upstream = wide(cotangent)
    grad_down, grad_gain_post = norm_back(down_branch, inverse_down, scales[3], upstream)
    grad_down_low = narrow(grad_down)

    def activate_back(gate_up, grad_hidden):
        gate = wide(gate_up[:, :hidden_width])
        up = wide(gate_up[:, hidden_width:])
        _, back = jax.vjp(lambda g, u: jax.nn.gelu(g, approximate=True) * u, gate, up)
        grad_gate, grad_up = back(grad_hidden)
        return narrow(jnp.concatenate([grad_gate, grad_up], axis=1))

    remaining = list(gate_ups)

    def grad_gate_up_of(group):
        return activate_back(remaining.pop(0), dot(group, out_all, 1, 1))

    down_groups, grad_gate_ups = gather_plane(grad_down_low, grad_gate_up_of)

    tile = 768 if width % 768 == 0 and hidden_width % 384 == 0 else width
    grad_out_all = row_product(hiddens, down_groups, 384 if tile == 768 else hidden_width, tile)
    grad_in_all = row_product(grad_gate_ups, mid_groups, tile, tile)
    out_ring = RingSum(grad_out_all.reshape(planes, 2 * unit, width), plane)
    in_ring = RingSum(grad_in_all.reshape(planes, 4 * unit, width), plane)
    out_ring.start()
    in_ring.start()
    grad_lowered_mid = reduce_groups(grad_gate_ups, in_all)
    grad_lowered_mid = after(grad_lowered_mid, grad_in_all, out_ring.finish())
    out_ring.start()

    grad_through_mid, grad_gain_pre_mlp = norm_back(
        middle, inverse_mid, scales[2], grad_lowered_mid
    )
    grad_middle = upstream + grad_through_mid
    grad_branch, grad_gain_post_attn = norm_back(branch, inverse_branch, scales[1], grad_middle)
    grad_branch_low = narrow(grad_branch)
    grad_heads = out_back_product(grad_branch_low, gathered_out)
    grad_rows = wide(blocks_of(exchange(grad_heads, place)))
    row_terms = -jnp.sum(grad_rows * attended, axis=-1) / totals[..., 0]
    grad_summed = narrow(grad_rows / totals)
    grad_summed = after(grad_summed, out_ring.finish())
    out_ring.start()
    row_terms = row_terms[:, None, :]

    out_parts = out_grad_product(after(grad_branch_low, grad_summed), attended_heads)
    out_parts = (
        out_parts.reshape(QUERY_HEADS, width, -1, attn_out.shape[1])
        .transpose(0, 2, 1, 3)
        .reshape(devices * row_share, attn_out.shape[1])
    )
    grad_attn_out = wide(lax.psum_scatter(out_parts, AXES, scatter_dimension=0, tiled=True))
    gain_sums = sum_devices(jnp.stack([grad_gain_post_attn, grad_gain_pre_mlp, grad_gain_post]))

    grad_query, kv_total, moving = None, None, None
    for step in range(planes):
        stage = (step + 1) % planes
        own_kv, other_kv = kv_stages[stage]
        grad_query, own_grad, other_grad = attend_back(
            lists[stage], query, grad_summed, row_terms, own_kv, other_kv, grad_query
        )
        total = wide(own_grad) + wide(swap(other_grad, CORE))
        if step:
            total = total + wide(moving)
        kv_total = narrow(total)
        if step < planes - 1:
            moving = shift(kv_total)
            if step == 0:
                grad_query = after(grad_query, out_ring.finish(), in_ring.finish())
    in_ring.start(kv_total)

    turned_query = narrow(rotate(grad_query * score_scale, cosine, -sine))
    kv_grad = wide(kv_total)
    turned_key = narrow(
        rotate(
            kv_grad[:, :, :HEAD_SIZE] * score_scale, cosine[: len(NEAR)], -sine[: len(NEAR)]
        )
    )
    flat = lambda blocks: blocks.reshape(-1, blocks.shape[-1])
    near_grads = flat(
        jnp.concatenate(
            [turned_query[: len(NEAR)], turned_key, kv_total[:, :, HEAD_SIZE:]], axis=-1
        )
    )
    query_grads = flat(turned_query)
    near_count = len(NEAR) * block
    cuts = (0, token_rows, 2 * token_rows, near_count)
    near_cuts = [near_grads[a:b] for a, b in zip(cuts, cuts[1:])]
    far_cuts = [query_grads[near_count + a : near_count + b] for a, b in zip(cuts, cuts[1:])]
    query_weight = attn_weight[:HEAD_SIZE]

    query_groups = [
        jnp.concatenate([near_cuts[0][:, :HEAD_SIZE], far_cuts[0]]),
        jnp.concatenate([near_cuts[1][:, :HEAD_SIZE], far_cuts[1]]),
        near_cuts[2][:, :HEAD_SIZE],
        far_cuts[2],
    ]
    grad_query_weight = row_product(query_groups, in_groups, HEAD_SIZE, tile)
    grad_kv_weight = row_product(
        [cut[:, HEAD_SIZE:] for cut in near_cuts], in_groups[:3], 2 * HEAD_SIZE, tile
    )
    query_stored = heads_to_chunks(
        grad_query_weight.reshape(HEAD_SIZE // chunk, chunk, width),
        query_rounds,
        place,
        query_planes,
    )
    kv_stored = heads_to_chunks(
        jnp.concatenate(
            [
                grad_kv_weight[:HEAD_SIZE].reshape(HEAD_SIZE // chunk, chunk, width),
                grad_kv_weight[HEAD_SIZE:].reshape(HEAD_SIZE // chunk, chunk, width),
            ],
            axis=1,
        ),
        kv_rounds,
        place,
        kv_planes,
    )
    attn_ring = RingSum(
        jnp.concatenate([query_stored, kv_stored[:, :chunk], kv_stored[:, chunk:]]), plane
    )

    def project_back(index, token):
        near = None if index == 3 else near_cuts[index]
        far = None if index == 2 else far_cuts[min(index, 2)]
        if token is not None:
            near = near if near is None else after(near, token)
            far = far if far is None else after(far, token)
        return (
            near if near is None else dot(near, attn_weight, 1, 0),
            far if far is None else dot(far, query_weight, 1, 0),
        )

    grad_lowered_in = reduce_plane(project_back)
    attn_sum = attn_ring.finish_all()
    in_ring.finish()
    grad_source, grad_gain_in = norm_back(source, inverse_in, scales[0], grad_lowered_in)
    grad_input = grad_middle + grad_source

    attn_pieces = attn_sum.reshape(chunk, row_parts, row_share).transpose(1, 0, 2)
    attn_pieces = ordered(exchange(attn_pieces, part, tuple(range(row_parts))), part)
    grad_attn_in = wide(attn_pieces.reshape(attn_in.shape[1], row_share).T)
    out_sum = out_ring.finish_all()
    in_sum = in_ring.finish_all()
    grad_pieces = jnp.concatenate(
        [
            in_sum.reshape(2, 2, unit, row_parts, row_share),
            out_sum.reshape(2, 1, unit, row_parts, row_share),
        ],
        axis=1,
    )
    grad_pieces = grad_pieces.transpose(0, 3, 1, 2, 4).reshape(PLANE, 3, unit, row_share)
    grad_pieces = wide(ordered(exchange(grad_pieces, place), place))
    grad_mlp_in = grad_pieces[:, :2].transpose(3, 1, 0, 2).reshape(mlp_in.shape)
    grad_mlp_out = grad_pieces[:, 2].transpose(2, 0, 1).reshape(mlp_out.shape)
    gain_total = jnp.concatenate([sum_devices(grad_gain_in[None]), gain_sums])
    grad_gains = pick(
        gain_total.reshape(gains.shape[1], row_parts, row_share).transpose(1, 2, 0), part
    )
    return (
        narrow(result),
        grad_input,
        grad_attn_in,
        grad_attn_out,
        grad_mlp_in,
        grad_mlp_out,
        grad_gains,
    )


def solution(mesh):
    placed = (
        P(("ctx", "fsdp"), None),
        P(("ctx", "fsdp"), None),
        P(),
        P(("ctx", "fsdp")),
        P("fsdp", "ctx"),
        P("fsdp", "ctx"),
        P("fsdp", "ctx"),
        P("fsdp", "ctx"),
        P("fsdp", None),
    )
    return jax.shard_map(
        body,
        mesh=mesh,
        in_specs=placed,
        out_specs=(
            P(("ctx", "fsdp"), None),
            P(("ctx", "fsdp"), None),
            P("fsdp", "ctx"),
            P("fsdp", "ctx"),
            P("fsdp", "ctx"),
            P("fsdp", "ctx"),
            P("fsdp", None),
        ),
        check_vma=False,
    )
```

```python
import functools
import math

import jax
import jax.numpy as jnp
from jax import lax
from jax.experimental import pallas as pl
from jax.experimental.pallas import tpu as pltpu
from jax.sharding import PartitionSpec as P

QUERY_HEADS = 8
KEY_VALUE_HEADS = 4
HEAD_SIZE = 256
LOOKBACK_SPAN = 4096
SEQUENCE_COUNT = 2


EPSILON = 1e-06
SOFT_CAP = 50.0
ROPE_BASE = 10000.0
AXES = ("ctx", "fsdp")
PLANE = 8
CORE, SIDE, ACROSS = 1, 2, 4
TANH_SCALE = HEAD_SIZE ** (-0.5) / SOFT_CAP
EXP2_SCALE = SOFT_CAP * math.log2(math.e)
VMEM_BYTES = 56 * 1024 * 1024


def inverse_rms(values):
    return lax.rsqrt(jnp.mean(values * values, axis=-1, keepdims=True) + EPSILON)


def norm_back(values, inverse, scale, upstream):
    scaled = upstream * scale
    through = inverse * scaled - values * inverse**3 * jnp.mean(
        scaled * values, axis=-1, keepdims=True
    )
    return (through, jnp.sum(upstream * values * inverse, axis=0))


def rotate(values, cosine, sine):
    half_width = values.shape[-1] // 2
    first_half = values[..., :half_width]
    second_half = values[..., half_width:]
    return jnp.concatenate(
        [
            first_half * cosine - second_half * sine,
            second_half * cosine + first_half * sine,
        ],
        axis=-1,
    )


def dot(left, right, left_axis, right_axis):
    return lax.dot_general(
        left,
        right,
        (((left_axis,), (right_axis,)), ((), ())),
        preferred_element_type=jnp.float32,
    )


def after(value, *others):
    return lax.optimization_barrier((value,) + others)[0]


def wide(values):
    return values.astype(jnp.float32)


def narrow(values):
    return values.astype(jnp.bfloat16)


def swap(values, mask):
    count = lax.axis_size(AXES)
    return lax.ppermute(values, AXES, [(i, i ^ mask) for i in range(count)])


def shift(values, steps=1):
    count = lax.axis_size(AXES)
    return lax.ppermute(values, AXES, [(i, (i + steps * PLANE) % count) for i in range(count)])


def route(values, targets):
    count = lax.axis_size(AXES)
    return lax.ppermute(
        values, AXES, [(i, i - i % PLANE + targets[i % PLANE]) for i in range(count)]
    )


def pick(stacked, index):
    return lax.dynamic_index_in_dim(stacked, index, 0, keepdims=False)


def look_up(table, place):
    return pick(jnp.asarray(table, jnp.int32), place)


def exchange(stacked, place, masks=tuple(range(PLANE))):
    return [
        swap(pick(stacked, place ^ mask), mask) if mask else pick(stacked, place) for mask in masks
    ]


def ordered(received, place):
    stacked = jnp.stack(received)
    return jnp.stack([pick(stacked, place ^ j) for j in range(len(received))])


NEAR = [(0, 0), (0, 1), (4, 0), (2, 1), (2, 0), (4, 1), (6, 0), (6, 1)]
FAR = [(mask ^ CORE, half) for mask, half in NEAR]


def together(*values):
    return lax.optimization_barrier(values)


def no_transfers(token):
    return ()


def gather_plane(rows, work, beside=(no_transfers,) * 3, between=None):
    half = rows.shape[0] // 2
    low, high = rows[:half], rows[half:]
    groups, done, extras = [], [], []

    def add_group(near, far):
        groups.append(jnp.concatenate([near, far]))
        done.append(work(groups[-1]))

    other = swap(rows, CORE)
    first_low, first_high = swap(low, ACROSS), swap(high, SIDE)
    extra = beside[0](rows)
    if between is None:
        add_group(rows, other)
        done[0], first_low, first_high, *extra = together(done[0], first_low, first_high, *extra)
    else:
        other, first_low, first_high, *extra = together(other, first_low, first_high, *extra)
    extras.append(extra)
    if between is not None:
        first_low, first_high = together(first_low, first_high, between(first_low))[:2]
    low, high = together(low, high, first_low)[:2]
    first = jnp.concatenate([first_low, first_high])
    first_other = swap(first, CORE)
    second_low, second_high = swap(low, SIDE), swap(high, ACROSS)
    extra = beside[1](first_low)
    if between is not None:
        add_group(rows, other)
    add_group(first, first_other)
    *ready, first_low, first_high, second_low, second_high = together(
        *done, *extra, first_low, first_high, second_low, second_high
    )
    done[:], extra = ready[: len(done)], ready[len(done) :]
    extras.append(extra)
    second = jnp.concatenate([second_low, second_high])
    second_other = swap(second, CORE)
    third_low, third_high = swap(first_low, SIDE), swap(first_high, ACROSS)
    extra = beside[2](second_low)
    add_group(second, second_other)
    done[2], third_low, third_high, *extra = together(done[2], third_low, third_high, *extra)
    extras.append(extra)
    third = jnp.concatenate([third_low, third_high])
    add_group(third, swap(third, CORE))
    return groups, done, extras


def reduce_plane(work, beside=(no_transfers,) * 3):
    extras = []

    def both(group, token):
        far = narrow(work(group, True, token))
        got = swap(far, CORE)
        near = together(narrow(work(group, False, far)))[0]
        return wide(near) + wide(got)

    third = narrow(both(3, None))
    half = third.shape[0] // 2
    got_low, got_high = swap(third[:half], SIDE), swap(third[half:], ACROSS)
    second = narrow(both(2, third))
    got_low, got_high, second, *extra = together(got_low, got_high, second, *beside[0](third))
    extras.append(extra)
    own_low, own_high = swap(second[:half], SIDE), swap(second[half:], ACROSS)
    first = both(1, second)
    first = narrow(first + wide(jnp.concatenate([got_low, got_high])))
    own_low, own_high, first, *extra = together(own_low, own_high, first, *beside[1](second))
    extras.append(extra)
    more_low, more_high = swap(first[:half], ACROSS), swap(first[half:], SIDE)
    own = both(0, first) + wide(jnp.concatenate([own_low, own_high]))
    more_low, more_high, own, *extra = together(more_low, more_high, own, *beside[2](first))
    extras.append(extra)
    return own + wide(jnp.concatenate([more_low, more_high])), extras


def sum_devices(values):
    for mask in (CORE, SIDE, ACROSS):
        values = values + swap(values, mask)
    total = values
    for steps in range(1, lax.axis_size(AXES) // PLANE):
        total = total + shift(values, steps)
    return total


class RingSum:
    def __init__(self, parts, plane):
        self.parts, self.plane, self.planes = parts, plane, parts.shape[0]
        self.hops, self.moving = 0, None
        self.total = self.part(0)

    def part(self, step):
        return pick(self.parts, (self.plane + 2 * self.planes - 1 - step) % self.planes)

    def start(self, *others):
        if self.hops < self.planes - 1:
            self.moving = shift(after(self.total, *others) if others else self.total)

    def finish(self):
        if self.moving is not None:
            self.hops += 1
            self.total = narrow(wide(self.moving) + wide(self.part(self.hops)))
            self.moving = None
        return self.total

    def finish_all(self):
        self.finish()
        while self.hops < self.planes - 1:
            self.start()
            self.finish()
        return self.total


def matchings(edges):
    left, rounds = list(edges), []
    while left:
        owner = {}

        def settle(source, seen):
            for edge in left:
                if edge[0] == source and edge[1] not in seen:
                    seen.add(edge[1])
                    if edge[1] not in owner or settle(owner[edge[1]][0], seen):
                        owner[edge[1]] = edge
                        return True
            return False

        for source in range(PLANE):
            settle(source, set())
        found = sorted(owner.values())
        rounds.append(found)
        left = [edge for edge in left if edge not in found]
    return rounds


def chunk_edges(plane_count, columns, chunk, share):
    edges = []
    for source in range(PLANE):
        for at in range(plane_count):
            column = (2 * at + source // 4) * columns + source % 4 * chunk
            head = column // HEAD_SIZE
            for target in range(head * share, (head + 1) * share):
                edges.append((source, target, at, column % HEAD_SIZE // chunk))
    return edges


def chunks_to_heads(stored, rounds, place):
    spots = len(rounds)
    got = []
    for found in rounds:
        sent = pick(stored, look_up([edge[2] for edge in found], place))
        got.append(route(sent, [edge[1] for edge in found]))
    stacked = jnp.stack(got)
    order = []
    for spot in range(spots):
        table = [0] * PLANE
        for step, found in enumerate(rounds):
            for edge in found:
                if edge[3] == spot:
                    table[edge[1]] = step
        order.append(pick(stacked, look_up(table, place)))
    return order


def heads_to_chunks(heads, rounds, place, plane_count):
    got = []
    for found in rounds:
        back, spot = [0] * PLANE, [0] * PLANE
        for source, target, _, position in found:
            back[target], spot[target] = source, position
        got.append(route(pick(heads, look_up(spot, place)), back))
    stacked = jnp.stack(got)
    chunks = []
    for at in range(plane_count):
        tables = []
        for source in range(PLANE):
            tables.append(
                [
                    step
                    for step, found in enumerate(rounds)
                    for edge in found
                    if edge[0] == source and edge[2] == at
                ]
            )
        terms = [
            pick(stacked, look_up([table[i] for table in tables], place))
            for i in range(len(tables[0]))
        ]
        total = terms[0]
        if len(terms) > 1:
            total = narrow(sum(wide(term) for term in terms))
        chunks.append(total)
    return jnp.stack(chunks)


def row_product_kernel(count, *refs):
    out, total = refs[-2:]
    total[...] = dot(refs[0][...], refs[count][...], 0, 0)
    for i in range(1, count):
        total[...] += dot(refs[i][...], refs[count + i][...], 0, 0)
    out[...] = total[...].astype(out.dtype)


def row_product(lefts, rights, left_tile, right_tile):
    count = len(lefts)
    height, width = lefts[0].shape[1], rights[0].shape[1]
    depths = [left.shape[0] for left in lefts]
    return pl.pallas_call(
        functools.partial(row_product_kernel, count),
        out_shape=jax.ShapeDtypeStruct((height, width), jnp.bfloat16),
        grid=(height // left_tile, width // right_tile),
        in_specs=[pl.BlockSpec((depth, left_tile), lambda i, j: (0, i)) for depth in depths]
        + [pl.BlockSpec((depth, right_tile), lambda i, j: (0, j)) for depth in depths],
        out_specs=pl.BlockSpec((left_tile, right_tile), lambda i, j: (i, j)),
        scratch_shapes=[pltpu.VMEM((left_tile, right_tile), jnp.float32)],
        compiler_params=pltpu.CompilerParams(vmem_limit_bytes=VMEM_BYTES),
        cost_estimate=pl.CostEstimate(
            flops=2 * sum(depths) * height * width,
            bytes_accessed=2 * sum(depths) * (height + width) + 2 * height * width,
            transcendentals=0,
        ),
    )(*lefts, *rights)


def out_kernel(part, rows_ref, weight_ref, out_ref):
    at = pl.program_id(0)
    total = dot(rows_ref[0], weight_ref[0, 0], 1, 1)
    for head in range(1, rows_ref.shape[0]):
        total += dot(rows_ref[head], weight_ref[head, 0], 1, 1)
    for i in range(out_ref.shape[1] // part):

        @pl.when(at == i)
        def _():
            out_ref[:, i * part : (i + 1) * part] = total


def out_product(rows, weight):
    heads, count, size = rows.shape
    _, parts, part, _ = weight.shape
    return pl.pallas_call(
        functools.partial(out_kernel, part),
        out_shape=jax.ShapeDtypeStruct((count, parts * part), jnp.float32),
        grid=(parts,),
        in_specs=[
            pl.BlockSpec((heads, count, size), lambda i: (0, 0, 0)),
            pl.BlockSpec((heads, 1, part, size), lambda i: (0, i, 0, 0)),
        ],
        out_specs=pl.BlockSpec((count, parts * part), lambda i: (0, 0)),
        compiler_params=pltpu.CompilerParams(vmem_limit_bytes=VMEM_BYTES),
        cost_estimate=pl.CostEstimate(
            flops=2 * count * heads * size * parts * part,
            bytes_accessed=2 * heads * size * (count + parts * part) + 4 * count * parts * part,
            transcendentals=0,
        ),
    )(rows, weight)


def out_back_kernel(rows_ref, weight_ref, out_ref):
    part = weight_ref.shape[2]
    total = dot(rows_ref[:, :part], weight_ref[0, 0], 1, 0)
    for i in range(1, weight_ref.shape[1]):
        total += dot(rows_ref[:, i * part : (i + 1) * part], weight_ref[0, i], 1, 0)
    out_ref[0] = total.astype(out_ref.dtype)


def out_back_product(rows, weight):
    count, width = rows.shape
    heads, parts, part, size = weight.shape
    return pl.pallas_call(
        out_back_kernel,
        out_shape=jax.ShapeDtypeStruct((heads, count, size), jnp.bfloat16),
        grid=(heads,),
        in_specs=[
            pl.BlockSpec((count, width), lambda i: (0, 0)),
            pl.BlockSpec((1, parts, part, size), lambda i: (i, 0, 0, 0)),
        ],
        out_specs=pl.BlockSpec((1, count, size), lambda i: (i, 0, 0)),
        compiler_params=pltpu.CompilerParams(vmem_limit_bytes=VMEM_BYTES),
        cost_estimate=pl.CostEstimate(
            flops=2 * count * heads * size * width,
            bytes_accessed=2 * heads * size * (count + width) + 2 * count * width,
            transcendentals=0,
        ),
    )(rows, weight)


def out_grad_kernel(rows_ref, heads_ref, out_ref):
    out_ref[0] = dot(rows_ref[...], heads_ref[0], 0, 0).astype(out_ref.dtype)


def out_grad_product(rows, by_head):
    count, width = rows.shape
    heads, _, size = by_head.shape
    return pl.pallas_call(
        out_grad_kernel,
        out_shape=jax.ShapeDtypeStruct((heads, width, size), jnp.bfloat16),
        grid=(heads,),
        in_specs=[
            pl.BlockSpec((count, width), lambda i: (0, 0)),
            pl.BlockSpec((1, count, size), lambda i: (i, 0, 0)),
        ],
        out_specs=pl.BlockSpec((1, width, size), lambda i: (i, 0, 0)),
        compiler_params=pltpu.CompilerParams(vmem_limit_bytes=VMEM_BYTES),
        cost_estimate=pl.CostEstimate(
            flops=2 * count * heads * size * width,
            bytes_accessed=2 * heads * size * (count + width) + 2 * count * width,
            transcendentals=0,
        ),
    )(rows, by_head)


def pair_lists(query_ids, key_ids, blocks_per_seq, span_blocks):
    query_seq, query_at = query_ids // blocks_per_seq, query_ids % blocks_per_seq
    key_seq, key_at = key_ids // blocks_per_seq, key_ids % blocks_per_seq
    rows = key_ids.shape[0]
    distance = (query_at[None, :, None] - key_at[:, None, :]).reshape(rows, -1)
    same = (query_seq[None, :, None] == key_seq[:, None, :]).reshape(rows, -1)
    whole = same & (distance > 0) & (distance < span_blocks)
    edged = same & ((distance == 0) | (distance == span_blocks))
    kind = whole.astype(jnp.int32) + 2 * edged.astype(jnp.int32)
    total = distance.shape[1]
    index = jnp.arange(total, dtype=jnp.int32)
    earlier = (index[None, :] < index[:, None])[None] & (kind[:, None, :] == kind[:, :, None])
    rank = jnp.sum(earlier.astype(jnp.int32), axis=2)
    count_whole = jnp.sum(whole.astype(jnp.int32), axis=1, keepdims=True)
    count_edged = jnp.sum(edged.astype(jnp.int32), axis=1, keepdims=True)
    spot = jnp.where(kind == 1, rank, jnp.where(kind == 2, count_whole + rank, -1))
    code = index * 2 + (distance == span_blocks).astype(jnp.int32)
    hit = spot[:, :, None] == index[None, None, :]
    entries = jnp.sum(jnp.where(hit, code[:, :, None], 0), axis=1)
    return jnp.concatenate([count_whole, count_edged, entries], axis=1).astype(jnp.int32)


def run_pairs(list_ref, row, key_count, unroll, visit):
    whole = list_ref[row, 0]
    edged = list_ref[row, 1]

    def decode(position):
        code = list_ref[row, 2 + position]
        pair = code // 2
        return pair // key_count, pair % key_count, code % 2

    def several(step, carry):
        found = [decode(step * unroll + i) for i in range(unroll)]
        visit([f[0] for f in found], [f[1] for f in found], None)
        return carry

    def single(position, carry):
        i, j, _ = decode(position)
        visit([i], [j], None)
        return carry

    def masked(position, carry):
        i, j, far = decode(position)
        visit([i], [j], far)
        return carry

    groups = whole // unroll
    lax.fori_loop(0, groups, several, 0)
    lax.fori_loop(groups * unroll, whole, single, 0)
    lax.fori_loop(whole, whole + edged, masked, 0)


def attend_kernel(first, unroll, list_ref, query_hbm, own_hbm, other_hbm, *rest):
    if first:
        state_hbm = None
        out_hbm, query, own, other, state, sems = rest
    else:
        state_hbm, out_hbm, query, own, other, state, sems = rest
    copies = [
        pltpu.make_async_copy(query_hbm, query, sems.at[0]),
        pltpu.make_async_copy(own_hbm, own, sems.at[1]),
        pltpu.make_async_copy(other_hbm, other, sems.at[2]),
    ]
    if not first:
        copies.append(pltpu.make_async_copy(state_hbm, state, sems.at[3]))
    for copy in copies:
        copy.start()
    if first:
        state[...] = jnp.zeros_like(state)
    for copy in copies:
        copy.wait()
    rows = query.shape[1]
    lane = lax.broadcasted_iota(jnp.int32, (rows, 128), 1)

    def visit_in(keys):
        def visit(query_at, key_at, far):
            scores = [
                dot(query[i], keys[j, :, :HEAD_SIZE], 1, 1) for i, j in zip(query_at, key_at)
            ]
            for i, j, score in zip(query_at, key_at, scores):
                weights = jnp.exp2(EXP2_SCALE * jnp.tanh(score * TANH_SCALE))
                if far is not None:
                    spacing = (
                        lax.broadcasted_iota(jnp.int32, weights.shape, 0)
                        - lax.broadcasted_iota(jnp.int32, weights.shape, 1)
                        + far * LOOKBACK_SPAN
                    )
                    live = (spacing >= 0) & (spacing < LOOKBACK_SPAN)
                    weights = jnp.where(live, weights, 0.0)
                if rows % 128 == 0:
                    part = weights[:, :128]
                    for k in range(1, rows // 128):
                        part = part + weights[:, k * 128 : (k + 1) * 128]
                else:
                    part = jnp.where(lane == 0, jnp.sum(weights, axis=1, keepdims=True), 0.0)
                state[i, :, HEAD_SIZE:] += part
                state[i, :, :HEAD_SIZE] += dot(
                    weights.astype(jnp.bfloat16), keys[j, :, HEAD_SIZE:], 1, 0
                )

        return visit

    key_count = own.shape[0]
    run_pairs(list_ref, 0, key_count, unroll, visit_in(own))
    run_pairs(list_ref, 1, key_count, unroll, visit_in(other))
    out = pltpu.make_async_copy(state, out_hbm, sems.at[4])
    out.start()
    out.wait()


def attend(lists, query, own, other, state):
    first = state is None
    blocks, rows, _ = query.shape
    shape = (blocks, rows, HEAD_SIZE + 128)
    operands = (query, own, other) if first else (query, own, other, state)
    return pl.pallas_call(
        functools.partial(attend_kernel, first, 4),
        out_shape=jax.ShapeDtypeStruct(shape, jnp.float32),
        grid_spec=pltpu.PrefetchScalarGridSpec(
            num_scalar_prefetch=1,
            grid=(1,),
            in_specs=[pl.BlockSpec(memory_space=pl.ANY)] * len(operands),
            out_specs=pl.BlockSpec(memory_space=pl.ANY),
            scratch_shapes=[
                pltpu.VMEM(query.shape, jnp.bfloat16),
                pltpu.VMEM(own.shape, jnp.bfloat16),
                pltpu.VMEM(other.shape, jnp.bfloat16),
                pltpu.VMEM(shape, jnp.float32),
                pltpu.SemaphoreType.DMA((5,)),
            ],
        ),
        compiler_params=pltpu.CompilerParams(vmem_limit_bytes=VMEM_BYTES),
        cost_estimate=pl.CostEstimate(
            flops=60 * 4 * rows * rows * HEAD_SIZE,
            bytes_accessed=14 * 1024 * 1024,
            transcendentals=60 * 2 * rows * rows,
        ),
    )(lists, *operands)


def attend_back_kernel(
    first,
    unroll,
    list_ref,
    query_hbm,
    grad_hbm,
    term_hbm,
    own_hbm,
    other_hbm,
    *rest,
):
    if first:
        state_hbm = None
    else:
        state_hbm, *rest = rest
    (
        out_hbm,
        own_out_hbm,
        other_out_hbm,
        query,
        grad,
        term,
        own,
        other,
        state,
        own_grad,
        other_grad,
        own_low,
        other_low,
        sems,
    ) = rest
    copies = [
        pltpu.make_async_copy(query_hbm, query, sems.at[0]),
        pltpu.make_async_copy(grad_hbm, grad, sems.at[1]),
        pltpu.make_async_copy(term_hbm, term, sems.at[2]),
        pltpu.make_async_copy(own_hbm, own, sems.at[3]),
        pltpu.make_async_copy(other_hbm, other, sems.at[4]),
    ]
    if not first:
        copies.append(pltpu.make_async_copy(state_hbm, state, sems.at[5]))
    for copy in copies:
        copy.start()
    if first:
        state[...] = jnp.zeros_like(state)
    own_grad[...] = jnp.zeros_like(own_grad)
    other_grad[...] = jnp.zeros_like(other_grad)
    for copy in copies:
        copy.wait()

    def visit_in(keys, key_grad):
        def visit(query_at, key_at, far):
            scores = []
            slopes = []
            for i, j in zip(query_at, key_at):
                scores.append(dot(keys[j, :, :HEAD_SIZE], query[i], 1, 1))
                slopes.append(dot(keys[j, :, HEAD_SIZE:], grad[i], 1, 1))
            for i, j, score, slope in zip(query_at, key_at, scores, slopes):
                bent = jnp.tanh(score * TANH_SCALE)
                weights = jnp.exp2(EXP2_SCALE * bent)
                if far is not None:
                    spacing = (
                        lax.broadcasted_iota(jnp.int32, weights.shape, 1)
                        - lax.broadcasted_iota(jnp.int32, weights.shape, 0)
                        + far * LOOKBACK_SPAN
                    )
                    live = (spacing >= 0) & (spacing < LOOKBACK_SPAN)
                    weights = jnp.where(live, weights, 0.0)
                grad_scores = (
                    (slope + term[i]) * (weights * (1.0 - bent * bent))
                ).astype(jnp.bfloat16)
                key_grad[j, :, :HEAD_SIZE] += dot(grad_scores, query[i], 1, 0)
                key_grad[j, :, HEAD_SIZE:] += dot(weights.astype(jnp.bfloat16), grad[i], 1, 0)
                state[i] += dot(grad_scores, keys[j, :, :HEAD_SIZE], 0, 0)

        return visit

    key_count = own.shape[0]
    run_pairs(list_ref, 1, key_count, unroll, visit_in(other, other_grad))
    other_low[...] = other_grad[...].astype(jnp.bfloat16)
    other_out = pltpu.make_async_copy(other_low, other_out_hbm, sems.at[6])
    other_out.start()
    run_pairs(list_ref, 0, key_count, unroll, visit_in(own, own_grad))
    own_low[...] = own_grad[...].astype(jnp.bfloat16)
    own_out = pltpu.make_async_copy(own_low, own_out_hbm, sems.at[7])
    own_out.start()
    out = pltpu.make_async_copy(state, out_hbm, sems.at[8])
    out.start()
    other_out.wait()
    own_out.wait()
    out.wait()


def attend_back(lists, query, grad, term, own, other, state):
    first = state is None
    blocks, rows, _ = query.shape
    operands = (query, grad, term, own, other)
    if not first:
        operands = operands + (state,)
    return pl.pallas_call(
        functools.partial(attend_back_kernel, first, 2),
        out_shape=[
            jax.ShapeDtypeStruct(query.shape, jnp.float32),
            jax.ShapeDtypeStruct(own.shape, jnp.bfloat16),
            jax.ShapeDtypeStruct(other.shape, jnp.bfloat16),
        ],
        grid_spec=pltpu.PrefetchScalarGridSpec(
            num_scalar_prefetch=1,
            grid=(1,),
            in_specs=[pl.BlockSpec(memory_space=pl.ANY)] * len(operands),
            out_specs=[pl.BlockSpec(memory_space=pl.ANY)] * 3,
            scratch_shapes=[
                pltpu.VMEM(query.shape, jnp.bfloat16),
                pltpu.VMEM(query.shape, jnp.bfloat16),
                pltpu.VMEM(term.shape, jnp.float32),
                pltpu.VMEM(own.shape, jnp.bfloat16),
                pltpu.VMEM(other.shape, jnp.bfloat16),
                pltpu.VMEM(query.shape, jnp.float32),
                pltpu.VMEM(own.shape, jnp.float32),
                pltpu.VMEM(other.shape, jnp.float32),
                pltpu.VMEM(own.shape, jnp.bfloat16),
                pltpu.VMEM(other.shape, jnp.bfloat16),
                pltpu.SemaphoreType.DMA((9,)),
            ],
        ),
        compiler_params=pltpu.CompilerParams(vmem_limit_bytes=VMEM_BYTES),
        cost_estimate=pl.CostEstimate(
            flops=60 * 10 * rows * rows * HEAD_SIZE,
            bytes_accessed=24 * 1024 * 1024,
            transcendentals=60 * 2 * rows * rows,
        ),
    )(lists, *operands)


def body(inputs, cotangent, block_ids, positions, attn_in, attn_out, mlp_in, mlp_out, gains):
    token_rows, width = inputs.shape
    block = token_rows // 2
    devices = lax.axis_size(AXES)
    ctx_count, row_parts = lax.axis_size("ctx"), lax.axis_size("fsdp")
    planes = devices // PLANE
    blocks_per_seq = 2 * devices // SEQUENCE_COUNT
    span_blocks = LOOKBACK_SPAN // block
    score_scale = HEAD_SIZE ** (-0.5)
    me = lax.axis_index(AXES)
    place, plane = me % PLANE, me // PLANE
    part = place % row_parts
    row_share = attn_in.shape[0]
    unit = mlp_out.shape[1] // PLANE
    chunk = attn_in.shape[1] // row_parts
    order = NEAR + FAR

    gain_parts = ordered([gains.T] + [swap(gains.T, mask) for mask in range(1, row_parts)], part)
    scales = wide(gain_parts.transpose(1, 0, 2).reshape(gains.shape[1], width))
    source = wide(inputs)
    inverse_in = inverse_rms(source)
    lowered_in = narrow(source * inverse_in * scales[0])

    def ids_of(which_plane, slots):
        masks = jnp.asarray([mask for mask, _ in slots], jnp.int32)
        sides = jnp.asarray([half for _, half in slots], jnp.int32)
        at = 2 * (which_plane[:, None] * PLANE + (place ^ masks)[None, :]) + sides[None, :]
        slot = jnp.arange(block_ids.shape[0], dtype=jnp.int32)
        return jnp.sum(jnp.where(at[:, :, None] == slot, block_ids, 0), axis=2)

    stage_planes = (plane + planes - jnp.arange(planes, dtype=jnp.int32)) % planes
    stage_ids = ids_of(stage_planes, order)
    query_ids = stage_ids[0]
    lists = pair_lists(
        query_ids, stage_ids.reshape(2 * planes, len(NEAR)), blocks_per_seq, span_blocks
    ).reshape(planes, 2, -1)
    half_width = HEAD_SIZE // 2
    frequency = ROPE_BASE ** (-2.0 * jnp.arange(half_width, dtype=jnp.float32) / HEAD_SIZE)
    base_angle = wide(query_ids % blocks_per_seq * block)[:, None, None] * frequency
    step_angle = jnp.arange(block, dtype=jnp.float32)[:, None] * frequency
    base_cosine, base_sine = jnp.cos(base_angle), jnp.sin(base_angle)
    step_cosine, step_sine = jnp.cos(step_angle), jnp.sin(step_angle)
    cosine = base_cosine * step_cosine - base_sine * step_sine
    sine = base_sine * step_cosine + base_cosine * step_sine

    in_pieces = exchange(
        attn_in.T.reshape(row_parts, chunk, row_share), part, tuple(range(row_parts))
    )
    in_chunk = ordered(in_pieces, part).transpose(1, 0, 2).reshape(chunk, width)
    stored = [in_chunk]
    for step in range(1, planes):
        stored.append(shift(stored[-1]))

    in_pieces = mlp_in.T.reshape(2, PLANE, unit, row_share).transpose(1, 0, 2, 3)
    in_share = (
        ordered(exchange(in_pieces, place), place)
        .reshape(2, row_parts, 2, unit, row_share)
        .transpose(0, 2, 3, 1, 4)
        .reshape(4 * unit, width)
    )
    in_share, lowered_in, lists, cosine, sine, *stored = together(
        in_share, lowered_in, lists, cosine, sine, *stored
    )
    cut = 2 * unit
    in_halves = [[in_share[:cut], in_share[cut:]]]
    stored = jnp.stack([pick(jnp.stack(stored), (plane - p) % planes) for p in range(planes)])

    query_planes, kv_planes = planes // 2, planes // 4
    query_rounds = matchings(chunk_edges(query_planes, attn_in.shape[1], chunk, 1))
    kv_rounds = matchings(
        chunk_edges(kv_planes, attn_in.shape[1], chunk, QUERY_HEADS // KEY_VALUE_HEADS)
    )
    attn_weights = []

    def attn_weights_of(token):
        chunks = after(stored, token)
        query_chunks = chunks_to_heads(chunks[:query_planes], query_rounds, place)
        kv_chunks = chunks_to_heads(
            jnp.concatenate(
                [
                    chunks[query_planes : query_planes + kv_planes],
                    chunks[query_planes + kv_planes :],
                ],
                axis=1,
            ),
            kv_rounds,
            place,
        )
        weight = jnp.concatenate(
            query_chunks + [both[:chunk] for both in kv_chunks] + [both[chunk:] for both in kv_chunks]
        )
        attn_weights.append(weight)
        return weight

    def shift_after(values):
        return lambda token: (shift(after(values, token)),)

    in_groups, projected, extras = gather_plane(
        lowered_in,
        lambda group: dot(group, attn_weights[0], 1, 1),
        (shift_after(in_halves[0][0]), shift_after(in_halves[0][1]), no_transfers),
        attn_weights_of,
    )
    attn_weight = attn_weights[0]
    in_halves.append([extras[0][0], extras[1][0]])

    def split_groups(groups):
        near = jnp.concatenate([group[:token_rows] for group in groups])
        far = jnp.concatenate([group[token_rows:] for group in groups])
        return [rows.reshape(len(NEAR), block, rows.shape[1]) for rows in (near, far)]

    near_rows, far_rows = split_groups(projected)
    query_parts, kv_parts = [], []
    for rows, low, high in ((near_rows, 0, len(NEAR)), (far_rows, len(NEAR), 2 * len(NEAR))):
        turns = (cosine[low:high], sine[low:high])
        query_parts.append(narrow(rotate(rows[:, :, :HEAD_SIZE], *turns)))
        kv_parts.append(
            jnp.concatenate(
                [
                    narrow(rotate(rows[:, :, HEAD_SIZE : 2 * HEAD_SIZE], *turns)),
                    narrow(rows[:, :, 2 * HEAD_SIZE :]),
                ],
                axis=-1,
            )
        )
    own_kv, other_kv = kv_parts
    query = jnp.concatenate(query_parts)

    gathered_out = lax.all_gather(after(attn_out, own_kv), AXES, axis=0)
    out_pieces = after(mlp_out.T, own_kv).reshape(PLANE, unit, row_share)
    out_share = (
        ordered(exchange(out_pieces, place), place)
        .reshape(2, row_parts, unit, row_share)
        .transpose(0, 2, 1, 3)
        .reshape(2 * unit, width)
    )
    kv_stages = [(own_kv, other_kv)]
    state = None
    for step in range(planes):
        own_kv, other_kv = kv_stages[step]
        state_next = attend(lists[step], query, own_kv, other_kv, state)
        if step < planes - 1:
            moving = shift(own_kv)
            if step == 0:
                state_next, moving, out_share = together(state_next, moving, out_share)
            else:
                state_next, moving = together(state_next, moving)
            kv_stages.append((moving, swap(moving, CORE)))
        else:
            low_next = shift(after(in_halves[1][0], own_kv))
            state_next, low_next = together(state_next, low_next)
        state = state_next
    totals = jnp.sum(state[:, :, HEAD_SIZE:], axis=-1, keepdims=True)
    attended = state[:, :, :HEAD_SIZE] / totals
    attended_rows = narrow(attended)

    def member_rows(blocks, mask):
        return jnp.concatenate([blocks[order.index((mask, 0))], blocks[order.index((mask, 1))]])

    def blocks_of(received):
        return jnp.stack(
            [received[mask][half * block : (half + 1) * block] for mask, half in order]
        )

    high_next = shift(after(in_halves[1][1], low_next))
    attended_heads = ordered(
        [member_rows(attended_rows, 0)]
        + [swap(member_rows(attended_rows, mask), mask) for mask in range(1, PLANE)],
        place,
    )
    attended_heads, high_next = together(attended_heads, high_next)
    in_halves.append([low_next, high_next])
    gathered_out = (
        gathered_out.reshape((QUERY_HEADS, -1, row_parts) + attn_out.shape)
        .transpose(0, 2, 3, 1, 4)
        .reshape(QUERY_HEADS, row_parts, row_share, HEAD_SIZE)
    )

    low_next = shift(after(in_halves[2][0], attended_heads))
    branch = out_product(attended_heads, gathered_out)
    inverse_branch = inverse_rms(branch)
    middle = source + branch * inverse_branch * scales[1]
    inverse_mid = inverse_rms(middle)
    lowered_mid = narrow(middle * inverse_mid * scales[2])
    lowered_mid, low_next = together(lowered_mid, low_next)
    in_halves.append([low_next, None])
    hidden_width = planes * 2 * unit
    in_alls, out_shares = [], [out_share]

    def in_all_of(token):
        for step in range(4, planes):
            in_halves.append([shift(half) for half in in_halves[-1]])
        shares = jnp.stack([jnp.concatenate(halves) for halves in in_halves])
        in_alls.append(
            jnp.concatenate([pick(shares, (plane - p) % planes) for p in range(planes)])
        )
        return in_alls[0]

    def last_half(token):
        in_halves[3][1] = shift(after(in_halves[2][1], token))
        return (in_halves[3][1],)

    def next_out(token):
        out_shares.append(shift(after(out_shares[-1], token)))
        return (out_shares[-1],)

    def gate_up_of(group):
        return narrow(dot(group, in_alls[0], 1, 1))

    mid_groups, gate_ups, extras = gather_plane(
        lowered_mid, gate_up_of, (last_half, next_out, next_out), in_all_of
    )
    in_all = in_alls[0]
    out_shares[1], out_shares[2] = extras[1][0], extras[2][0]
    for step in range(3, planes):
        out_shares.append(shift(out_shares[-1]))
    gate_ups[3], out_shares[3] = together(gate_ups[3], out_shares[3])
    shares = jnp.stack(out_shares)
    out_all = jnp.concatenate([pick(shares, (plane - p) % planes) for p in range(planes)])

    def activate(gate_up):
        gate = wide(gate_up[:, :hidden_width])
        up = wide(gate_up[:, hidden_width:])
        return jax.nn.gelu(gate, approximate=True) * up

    hiddens = [narrow(activate(gate_up)) for gate_up in gate_ups]

    def reduce_groups(groups, weight, *rest):
        def work(index, far, token):
            group = groups[index]
            group = group[token_rows:] if far else group[:token_rows]
            if token is not None:
                group = after(group, token)
            return dot(group, weight, 1, 0)

        return reduce_plane(work, *rest)

    down_branch, _ = reduce_groups(hiddens, out_all)
    inverse_down = inverse_rms(down_branch)
    result = middle + down_branch * inverse_down * scales[3]
    upstream = wide(cotangent)
    grad_down, grad_gain_post = norm_back(down_branch, inverse_down, scales[3], upstream)
    grad_down_low = narrow(grad_down)

    def activate_back(gate_up, grad_hidden):
        gate = wide(gate_up[:, :hidden_width])
        up = wide(gate_up[:, hidden_width:])
        _, back = jax.vjp(lambda g, u: jax.nn.gelu(g, approximate=True) * u, gate, up)
        grad_gate, grad_up = back(grad_hidden)
        return narrow(jnp.concatenate([grad_gate, grad_up], axis=1))

    remaining = list(gate_ups)

    def grad_gate_up_of(group):
        return activate_back(remaining.pop(0), dot(group, out_all, 1, 1))

    down_groups, grad_gate_ups, _ = gather_plane(grad_down_low, grad_gate_up_of)

    tile = 768 if width % 768 == 0 else width
    rings = {}

    def out_grads(token):
        grads = row_product([after(hiddens[0], token)] + hiddens[1:], down_groups, 384, tile)
        rings["out"] = RingSum(grads.reshape(planes, 2 * unit, width), plane)
        return (grads,)

    def in_grads(token):
        rings["out"].start(token)
        grads = row_product(
            [after(grad_gate_ups[0], token)] + grad_gate_ups[1:], mid_groups, tile, tile
        )
        rings["in"] = RingSum(grads.reshape(planes, 4 * unit, width), plane)
        return (grads, rings["out"].finish())

    def second_out(token):
        rings["out"].start(token)
        return (rings["out"].moving,)

    grad_lowered_mid, _ = reduce_groups(
        grad_gate_ups, in_all, (out_grads, in_grads, second_out)
    )

    out_ring, in_ring = rings["out"], rings["in"]
    in_ring.start(grad_lowered_mid)
    grad_through_mid, grad_gain_pre_mlp = norm_back(
        middle, inverse_mid, scales[2], grad_lowered_mid
    )
    grad_middle = upstream + grad_through_mid
    grad_branch, grad_gain_post_attn = norm_back(branch, inverse_branch, scales[1], grad_middle)
    grad_branch_low = narrow(grad_branch)
    grad_heads = out_back_product(grad_branch_low, gathered_out)
    grad_rows = wide(blocks_of(exchange(grad_heads, place)))
    row_terms = -jnp.sum(grad_rows * attended, axis=-1) / totals[..., 0]
    grad_summed = narrow(grad_rows / totals)
    grad_summed, _, _ = together(grad_summed, in_ring.finish(), out_ring.finish())
    row_terms = row_terms[:, None, :]

    grad_query, kv_total, moving = None, None, None
    for step in range(planes):
        stage = (step + 1) % planes
        own_kv, other_kv = kv_stages[stage]
        if step == 0:
            out_ring.start(grad_summed)
        grad_query, own_grad, other_grad = attend_back(
            lists[stage], query, grad_summed, row_terms, own_kv, other_kv, grad_query
        )
        total = wide(own_grad) + wide(swap(other_grad, CORE))
        if step == 0:
            kv_total = narrow(total)
            kv_total, _ = together(kv_total, out_ring.finish())
            moving = shift(kv_total)
            out_parts = out_grad_product(after(grad_branch_low, kv_total), attended_heads)
            out_parts = (
                out_parts.reshape(QUERY_HEADS, width, -1, attn_out.shape[1])
                .transpose(0, 2, 1, 3)
                .reshape(devices * row_share, attn_out.shape[1])
            )
            grad_attn_out = wide(
                lax.psum_scatter(out_parts, AXES, scatter_dimension=0, tiled=True)
            )
        else:
            kv_total = narrow(total + wide(moving))
            if step < planes - 1:
                moving = shift(kv_total)
    gain_sums = sum_devices(jnp.stack([grad_gain_post_attn, grad_gain_pre_mlp, grad_gain_post]))
    in_ring.start(kv_total)

    turned_query = narrow(rotate(grad_query * score_scale, cosine, -sine))
    kv_grad = wide(kv_total)
    turned_key = narrow(
        rotate(
            kv_grad[:, :, :HEAD_SIZE] * score_scale, cosine[: len(NEAR)], -sine[: len(NEAR)]
        )
    )
    near_grads = jnp.concatenate(
        [turned_query[: len(NEAR)], turned_key, kv_total[:, :, HEAD_SIZE:]], axis=-1
    ).reshape(4, token_rows, 3 * HEAD_SIZE)
    far_grads = turned_query[len(NEAR) :].reshape(4, token_rows, HEAD_SIZE)
    query_groups = jnp.concatenate([near_grads[:, :, :HEAD_SIZE], far_grads], axis=1)
    query_weight = attn_weight[:HEAD_SIZE]

    def weight_grads(token):
        query_lefts = [after(query_groups[0], token)] + [query_groups[i] for i in range(1, 4)]
        grad_query_weight = row_product(query_lefts, in_groups, HEAD_SIZE, tile)
        grad_kv_weight = row_product(
            [after(near_grads[i, :, HEAD_SIZE:], grad_query_weight) for i in range(4)],
            in_groups,
            2 * HEAD_SIZE,
            tile,
        )
        return grad_query_weight, grad_kv_weight

    def project_back(index, far, token):
        cut, weight = (far_grads, query_weight) if far else (near_grads, attn_weight)
        cut = cut[index]
        return dot(cut if token is None else after(cut, token), weight, 1, 0)

    def third_in(token):
        return (in_ring.finish(),)

    grad_lowered_in, extras = reduce_plane(project_back, (weight_grads, no_transfers, third_in))
    grad_query_weight, grad_kv_weight = extras[0]
    query_stored = heads_to_chunks(
        grad_query_weight.reshape(HEAD_SIZE // chunk, chunk, width),
        query_rounds,
        place,
        query_planes,
    )
    kv_stored = heads_to_chunks(
        jnp.concatenate(
            [
                grad_kv_weight[:HEAD_SIZE].reshape(HEAD_SIZE // chunk, chunk, width),
                grad_kv_weight[HEAD_SIZE:].reshape(HEAD_SIZE // chunk, chunk, width),
            ],
            axis=1,
        ),
        kv_rounds,
        place,
        kv_planes,
    )
    attn_ring = RingSum(
        jnp.concatenate([query_stored, kv_stored[:, :chunk], kv_stored[:, chunk:]]), plane
    )
    in_sum = in_ring.finish_all()
    attn_sum = attn_ring.finish_all()
    out_sum = out_ring.finish_all()
    grad_source, grad_gain_in = norm_back(source, inverse_in, scales[0], grad_lowered_in)
    grad_input = grad_middle + grad_source

    out_pieces = out_sum.reshape(2, unit, row_parts, row_share)
    out_pieces = out_pieces.transpose(0, 2, 1, 3).reshape(PLANE, unit, row_share)
    out_pieces = wide(ordered(exchange(out_pieces, place), place))
    grad_mlp_out = out_pieces.transpose(2, 0, 1).reshape(mlp_out.shape)
    in_pieces = in_sum.reshape(2, 2, unit, row_parts, row_share)
    in_pieces = in_pieces.transpose(0, 3, 1, 2, 4).reshape(PLANE, 2, unit, row_share)
    in_pieces = wide(ordered(exchange(in_pieces, place), place))
    grad_mlp_in = in_pieces.transpose(3, 1, 0, 2).reshape(mlp_in.shape)
    attn_pieces = attn_sum.reshape(chunk, row_parts, row_share).transpose(1, 0, 2)
    attn_pieces = ordered(exchange(attn_pieces, part, tuple(range(row_parts))), part)
    grad_attn_in = wide(attn_pieces.reshape(attn_in.shape[1], row_share).T)
    gain_total = jnp.concatenate([sum_devices(grad_gain_in[None]), gain_sums])
    grad_gains = pick(
        gain_total.reshape(gains.shape[1], row_parts, row_share).transpose(1, 2, 0), part
    )
    return (
        narrow(result),
        grad_input,
        grad_attn_in,
        grad_attn_out,
        grad_mlp_in,
        grad_mlp_out,
        grad_gains,
    )


def solution(mesh):
    placed = (
        P(("ctx", "fsdp"), None),
        P(("ctx", "fsdp"), None),
        P(),
        P(("ctx", "fsdp")),
        P("fsdp", "ctx"),
        P("fsdp", "ctx"),
        P("fsdp", "ctx"),
        P("fsdp", "ctx"),
        P("fsdp", None),
    )
    return jax.shard_map(
        body,
        mesh=mesh,
        in_specs=placed,
        out_specs=(
            P(("ctx", "fsdp"), None),
            P(("ctx", "fsdp"), None),
            P("fsdp", "ctx"),
            P("fsdp", "ctx"),
            P("fsdp", "ctx"),
            P("fsdp", "ctx"),
            P("fsdp", None),
        ),
        check_vma=False,
    )
```

```python
import functools
import math

import jax
import jax.numpy as jnp
from jax import lax
from jax.experimental import pallas as pl
from jax.experimental.pallas import tpu as pltpu
from jax.sharding import PartitionSpec as P

QUERY_HEADS = 8
KEY_VALUE_HEADS = 4
HEAD_SIZE = 256
LOOKBACK_SPAN = 4096
SEQUENCE_COUNT = 2


EPSILON = 1e-06
SOFT_CAP = 50.0
ROPE_BASE = 10000.0
AXES = ("ctx", "fsdp")
PLANE = 8
CORE, SIDE, ACROSS = 1, 2, 4
TANH_SCALE = HEAD_SIZE ** (-0.5) / SOFT_CAP
EXP2_SCALE = SOFT_CAP * math.log2(math.e)
VMEM_BYTES = 56 * 1024 * 1024


def inverse_rms(values):
    return lax.rsqrt(jnp.mean(values * values, axis=-1, keepdims=True) + EPSILON)


def norm_back(values, inverse, scale, upstream):
    scaled = upstream * scale
    through = inverse * scaled - values * inverse**3 * jnp.mean(
        scaled * values, axis=-1, keepdims=True
    )
    return (through, jnp.sum(upstream * values * inverse, axis=0))


def rotate(values, cosine, sine):
    half_width = values.shape[-1] // 2
    first_half = values[..., :half_width]
    second_half = values[..., half_width:]
    return jnp.concatenate(
        [
            first_half * cosine - second_half * sine,
            second_half * cosine + first_half * sine,
        ],
        axis=-1,
    )


def dot(left, right, left_axis, right_axis):
    return lax.dot_general(
        left,
        right,
        (((left_axis,), (right_axis,)), ((), ())),
        preferred_element_type=jnp.float32,
    )


def after(value, *others):
    return lax.optimization_barrier((value,) + others)[0]


def wide(values):
    return values.astype(jnp.float32)


def narrow(values):
    return values.astype(jnp.bfloat16)


def swap(values, mask):
    count = lax.axis_size(AXES)
    return lax.ppermute(values, AXES, [(i, i ^ mask) for i in range(count)])


def shift(values, steps=1):
    count = lax.axis_size(AXES)
    return lax.ppermute(values, AXES, [(i, (i + steps * PLANE) % count) for i in range(count)])


def route(values, targets):
    count = lax.axis_size(AXES)
    return lax.ppermute(
        values, AXES, [(i, i - i % PLANE + targets[i % PLANE]) for i in range(count)]
    )


def pick(stacked, index):
    return lax.dynamic_index_in_dim(stacked, index, 0, keepdims=False)


def look_up(table, place):
    return pick(jnp.asarray(table, jnp.int32), place)


def exchange(pieces):
    far = swap(jnp.stack([pieces[mask ^ CORE] for mask in range(0, len(pieces), 2)]), CORE)
    received = []
    for i, mask in enumerate(range(0, len(pieces), 2)):
        both = jnp.stack([pieces[mask], far[i]])
        if mask:
            both = swap(both, mask)
        received.extend([both[0], both[1]])
    return received


def exchange_members(stacked, place):
    return exchange([pick(stacked, place ^ mask) for mask in range(stacked.shape[0])])


def ordered(received, place):
    whole = jnp.zeros((len(received),) + received[0].shape, received[0].dtype)
    for mask, rows in enumerate(received):
        whole = lax.dynamic_update_index_in_dim(whole, rows, place ^ mask, 0)
    return whole


NEAR = [(0, 0), (0, 1), (4, 0), (2, 1), (2, 0), (4, 1), (6, 0), (6, 1)]
FAR = [(mask ^ CORE, half) for mask, half in NEAR]


def together(*values):
    return lax.optimization_barrier(values)


def no_transfers(token):
    return ()


def gather_plane(rows, work, beside=(no_transfers,) * 3):
    half = rows.shape[0] // 2
    low, high = rows[:half], rows[half:]
    groups, done, extras = [], [], []

    def add_group(near, far):
        groups.append(jnp.concatenate([near, far]))
        done.append(work(groups[-1]))

    other = swap(rows, CORE)
    first_low, first_high = swap(low, ACROSS), swap(high, SIDE)
    extra = beside[0](rows)
    add_group(rows, other)
    done[0], first_low, first_high, *extra = together(done[0], first_low, first_high, *extra)
    extras.append(extra)
    low, high = together(low, high, first_low)[:2]
    first_other = swap(jnp.concatenate([first_low, first_high]), CORE)
    second_low, second_high = swap(low, SIDE), swap(high, ACROSS)
    extra = beside[1](first_low)
    add_group(jnp.concatenate([first_low, first_high]), first_other)
    done[1], first_low, first_high, second_low, second_high, *extra = together(
        done[1], first_low, first_high, second_low, second_high, *extra
    )
    extras.append(extra)
    second_other = swap(jnp.concatenate([second_low, second_high]), CORE)
    third_low, third_high = swap(first_low, SIDE), swap(first_high, ACROSS)
    extra = beside[2](second_low)
    add_group(jnp.concatenate([second_low, second_high]), second_other)
    done[2], third_low, third_high, *extra = together(done[2], third_low, third_high, *extra)
    extras.append(extra)
    third = jnp.concatenate([third_low, third_high])
    add_group(third, swap(third, CORE))
    return groups, done, extras


def reduce_plane(work, beside=(no_transfers,) * 3, middle=None):
    extras = []

    def both(group, token):
        near, far = work(group, token)
        return wide(near) + wide(swap(far, CORE))

    third = narrow(both(3, None))
    half = third.shape[0] // 2
    got_low, got_high = swap(third[:half], SIDE), swap(third[half:], ACROSS)
    second = narrow(both(2, third))
    got_low, got_high, second, *extra = together(got_low, got_high, second, *beside[0](third))
    extras.append(extra)
    if middle is not None:
        second, *extra = together(second, *middle(extras))
        extras.append(extra)
    own_low, own_high = swap(second[:half], SIDE), swap(second[half:], ACROSS)
    first = both(1, second)
    first = narrow(first + wide(jnp.concatenate([got_low, got_high])))
    own_low, own_high, first, *extra = together(own_low, own_high, first, *beside[1](second))
    extras.append(extra)
    more_low, more_high = swap(first[:half], ACROSS), swap(first[half:], SIDE)
    own = both(0, first) + wide(jnp.concatenate([own_low, own_high]))
    more_low, more_high, own, *extra = together(more_low, more_high, own, *beside[2](first))
    extras.append(extra)
    return own + wide(jnp.concatenate([more_low, more_high])), extras


def sum_devices(values):
    for mask in (CORE, SIDE, ACROSS):
        values = values + swap(values, mask)
    total = values
    for steps in range(1, lax.axis_size(AXES) // PLANE):
        total = total + shift(values, steps)
    return total


class RingSum:
    def __init__(self, parts, plane, first=0, rows=None):
        self.parts, self.plane, self.planes = parts, plane, parts.shape[0]
        self.first, self.rows = first, rows or parts.shape[1]
        self.hops, self.moving = 0, None
        self.total = self.part(0)

    def part(self, step):
        at = (self.plane + 2 * self.planes - 1 - step) % self.planes
        size = (1, self.rows, self.parts.shape[2])
        return lax.dynamic_slice(self.parts, (at, self.first, 0), size)[0]

    def start(self, *others):
        if self.hops < self.planes - 1:
            self.moving = shift(after(self.total, *others) if others else self.total)

    def finish(self):
        if self.moving is not None:
            self.hops += 1
            self.total = narrow(wide(self.moving) + wide(self.part(self.hops)))
            self.moving = None
        return self.total

    def finish_all(self):
        self.finish()
        while self.hops < self.planes - 1:
            self.start()
            self.finish()
        return self.total


def matchings(edges):
    left, rounds = list(edges), []
    while left:
        owner = {}

        def settle(source, seen):
            for edge in left:
                if edge[0] == source and edge[1] not in seen:
                    seen.add(edge[1])
                    if edge[1] not in owner or settle(owner[edge[1]][0], seen):
                        owner[edge[1]] = edge
                        return True
            return False

        for source in range(PLANE):
            settle(source, set())
        found = sorted(owner.values())
        rounds.append(found)
        left = [edge for edge in left if edge not in found]
    return rounds


def chunk_edges(plane_count, columns, chunk, share):
    edges = []
    for source in range(PLANE):
        for at in range(plane_count):
            column = (2 * at + source // 4) * columns + source % 4 * chunk
            head = column // HEAD_SIZE
            for target in range(head * share, (head + 1) * share):
                edges.append((source, target, at, column % HEAD_SIZE // chunk))
    return edges


def chunks_to_heads(stored, rounds, place):
    spots = len(rounds)
    got = []
    for found in rounds:
        sent = pick(stored, look_up([edge[2] for edge in found], place))
        got.append(route(sent, [edge[1] for edge in found]))
    stacked = jnp.stack(got)
    order = []
    for spot in range(spots):
        table = [0] * PLANE
        for step, found in enumerate(rounds):
            for edge in found:
                if edge[3] == spot:
                    table[edge[1]] = step
        order.append(pick(stacked, look_up(table, place)))
    return order


def heads_to_chunks(heads, rounds, place, plane_count):
    got = []
    for found in rounds:
        back, spot = [0] * PLANE, [0] * PLANE
        for source, target, _, position in found:
            back[target], spot[target] = source, position
        got.append(route(pick(heads, look_up(spot, place)), back))
    stacked = jnp.stack(got)
    chunks = []
    for at in range(plane_count):
        tables = []
        for source in range(PLANE):
            tables.append(
                [
                    step
                    for step, found in enumerate(rounds)
                    for edge in found
                    if edge[0] == source and edge[2] == at
                ]
            )
        terms = [
            pick(stacked, look_up([table[i] for table in tables], place))
            for i in range(len(tables[0]))
        ]
        total = terms[0]
        if len(terms) > 1:
            total = narrow(sum(wide(term) for term in terms))
        chunks.append(total)
    return jnp.stack(chunks)


def row_product_kernel(count, *refs):
    out, total = refs[-2:]
    total[...] = dot(refs[0][...], refs[count][...], 0, 0)
    for i in range(1, count):
        total[...] += dot(refs[i][...], refs[count + i][...], 0, 0)
    out[...] = total[...].astype(out.dtype)


def row_product(lefts, rights, left_tile, right_tile):
    count = len(lefts)
    height, width = lefts[0].shape[1], rights[0].shape[1]
    depths = [left.shape[0] for left in lefts]
    return pl.pallas_call(
        functools.partial(row_product_kernel, count),
        out_shape=jax.ShapeDtypeStruct((height, width), jnp.bfloat16),
        grid=(height // left_tile, width // right_tile),
        in_specs=[pl.BlockSpec((depth, left_tile), lambda i, j: (0, i)) for depth in depths]
        + [pl.BlockSpec((depth, right_tile), lambda i, j: (0, j)) for depth in depths],
        out_specs=pl.BlockSpec((left_tile, right_tile), lambda i, j: (i, j)),
        scratch_shapes=[pltpu.VMEM((left_tile, right_tile), jnp.float32)],
        compiler_params=pltpu.CompilerParams(vmem_limit_bytes=VMEM_BYTES),
        cost_estimate=pl.CostEstimate(
            flops=2 * sum(depths) * height * width,
            bytes_accessed=2 * sum(depths) * (height + width) + 2 * height * width,
            transcendentals=0,
        ),
    )(*lefts, *rights)


def out_kernel(part, rows_ref, weight_ref, out_ref):
    at = pl.program_id(0)
    total = dot(rows_ref[0], weight_ref[0, 0], 1, 1)
    for head in range(1, rows_ref.shape[0]):
        total += dot(rows_ref[head], weight_ref[head, 0], 1, 1)
    for i in range(out_ref.shape[1] // part):

        @pl.when(at == i)
        def _():
            out_ref[:, i * part : (i + 1) * part] = total


def out_product(rows, weight):
    heads, count, size = rows.shape
    _, parts, part, _ = weight.shape
    return pl.pallas_call(
        functools.partial(out_kernel, part),
        out_shape=jax.ShapeDtypeStruct((count, parts * part), jnp.float32),
        grid=(parts,),
        in_specs=[
            pl.BlockSpec((heads, count, size), lambda i: (0, 0, 0)),
            pl.BlockSpec((heads, 1, part, size), lambda i: (0, i, 0, 0)),
        ],
        out_specs=pl.BlockSpec((count, parts * part), lambda i: (0, 0)),
        compiler_params=pltpu.CompilerParams(vmem_limit_bytes=VMEM_BYTES),
        cost_estimate=pl.CostEstimate(
            flops=2 * count * heads * size * parts * part,
            bytes_accessed=2 * heads * size * (count + parts * part) + 4 * count * parts * part,
            transcendentals=0,
        ),
    )(rows, weight)


def out_back_kernel(rows_ref, weight_ref, out_ref):
    part = weight_ref.shape[2]
    total = dot(rows_ref[:, :part], weight_ref[0, 0], 1, 0)
    for i in range(1, weight_ref.shape[1]):
        total += dot(rows_ref[:, i * part : (i + 1) * part], weight_ref[0, i], 1, 0)
    out_ref[0] = total.astype(out_ref.dtype)


def out_back_product(rows, weight):
    count, width = rows.shape
    heads, parts, part, size = weight.shape
    return pl.pallas_call(
        out_back_kernel,
        out_shape=jax.ShapeDtypeStruct((heads, count, size), jnp.bfloat16),
        grid=(heads,),
        in_specs=[
            pl.BlockSpec((count, width), lambda i: (0, 0)),
            pl.BlockSpec((1, parts, part, size), lambda i: (i, 0, 0, 0)),
        ],
        out_specs=pl.BlockSpec((1, count, size), lambda i: (i, 0, 0)),
        compiler_params=pltpu.CompilerParams(vmem_limit_bytes=VMEM_BYTES),
        cost_estimate=pl.CostEstimate(
            flops=2 * count * heads * size * width,
            bytes_accessed=2 * heads * size * (count + width) + 2 * count * width,
            transcendentals=0,
        ),
    )(rows, weight)


def out_grad_kernel(rows_ref, heads_ref, out_ref):
    out_ref[0] = dot(rows_ref[...], heads_ref[0], 0, 0).astype(out_ref.dtype)


def out_grad_product(rows, by_head):
    count, width = rows.shape
    heads, _, size = by_head.shape
    return pl.pallas_call(
        out_grad_kernel,
        out_shape=jax.ShapeDtypeStruct((heads, width, size), jnp.bfloat16),
        grid=(heads,),
        in_specs=[
            pl.BlockSpec((count, width), lambda i: (0, 0)),
            pl.BlockSpec((1, count, size), lambda i: (i, 0, 0)),
        ],
        out_specs=pl.BlockSpec((1, width, size), lambda i: (i, 0, 0)),
        compiler_params=pltpu.CompilerParams(vmem_limit_bytes=VMEM_BYTES),
        cost_estimate=pl.CostEstimate(
            flops=2 * count * heads * size * width,
            bytes_accessed=2 * heads * size * (count + width) + 2 * count * width,
            transcendentals=0,
        ),
    )(rows, by_head)


def pair_lists(query_ids, key_ids, blocks_per_seq, span_blocks):
    query_seq, query_at = query_ids // blocks_per_seq, query_ids % blocks_per_seq
    key_seq, key_at = key_ids // blocks_per_seq, key_ids % blocks_per_seq
    rows = key_ids.shape[0]
    distance = (query_at[None, :, None] - key_at[:, None, :]).reshape(rows, -1)
    same = (query_seq[None, :, None] == key_seq[:, None, :]).reshape(rows, -1)
    whole = same & (distance > 0) & (distance < span_blocks)
    edged = same & ((distance == 0) | (distance == span_blocks))
    kind = whole.astype(jnp.int32) + 2 * edged.astype(jnp.int32)
    total = distance.shape[1]
    index = jnp.arange(total, dtype=jnp.int32)
    earlier = (index[None, :] < index[:, None])[None] & (kind[:, None, :] == kind[:, :, None])
    rank = jnp.sum(earlier.astype(jnp.int32), axis=2)
    count_whole = jnp.sum(whole.astype(jnp.int32), axis=1, keepdims=True)
    count_edged = jnp.sum(edged.astype(jnp.int32), axis=1, keepdims=True)
    spot = jnp.where(kind == 1, rank, jnp.where(kind == 2, count_whole + rank, -1))
    code = index * 2 + (distance == span_blocks).astype(jnp.int32)
    hit = spot[:, :, None] == index[None, None, :]
    entries = jnp.sum(jnp.where(hit, code[:, :, None], 0), axis=1)
    return jnp.concatenate([count_whole, count_edged, entries], axis=1).astype(jnp.int32)


def run_pairs(list_ref, row, key_count, unroll, visit):
    whole = list_ref[row, 0]
    edged = list_ref[row, 1]

    def decode(position):
        code = list_ref[row, 2 + position]
        pair = code // 2
        return pair // key_count, pair % key_count, code % 2

    def several(step, carry):
        found = [decode(step * unroll + i) for i in range(unroll)]
        visit([f[0] for f in found], [f[1] for f in found], None)
        return carry

    def single(position, carry):
        i, j, _ = decode(position)
        visit([i], [j], None)
        return carry

    def masked(position, carry):
        i, j, far = decode(position)
        visit([i], [j], far)
        return carry

    groups = whole // unroll
    lax.fori_loop(0, groups, several, 0)
    lax.fori_loop(groups * unroll, whole, single, 0)
    lax.fori_loop(whole, whole + edged, masked, 0)


def attend_kernel(first, unroll, list_ref, query_hbm, own_hbm, other_hbm, *rest):
    if first:
        state_hbm = None
        out_hbm, query, own, other, state, sems = rest
    else:
        state_hbm, out_hbm, query, own, other, state, sems = rest
    copies = [
        pltpu.make_async_copy(query_hbm, query, sems.at[0]),
        pltpu.make_async_copy(own_hbm, own, sems.at[1]),
        pltpu.make_async_copy(other_hbm, other, sems.at[2]),
    ]
    if not first:
        copies.append(pltpu.make_async_copy(state_hbm, state, sems.at[3]))
    for copy in copies:
        copy.start()
    if first:
        state[...] = jnp.zeros_like(state)
    for copy in copies:
        copy.wait()
    rows = query.shape[1]
    lane = lax.broadcasted_iota(jnp.int32, (rows, 128), 1)

    def visit_in(keys):
        def visit(query_at, key_at, far):
            scores = [
                dot(query[i], keys[j, :, :HEAD_SIZE], 1, 1) for i, j in zip(query_at, key_at)
            ]
            for i, j, score in zip(query_at, key_at, scores):
                weights = jnp.exp2(EXP2_SCALE * jnp.tanh(score * TANH_SCALE))
                if far is not None:
                    spacing = (
                        lax.broadcasted_iota(jnp.int32, weights.shape, 0)
                        - lax.broadcasted_iota(jnp.int32, weights.shape, 1)
                        + far * LOOKBACK_SPAN
                    )
                    live = (spacing >= 0) & (spacing < LOOKBACK_SPAN)
                    weights = jnp.where(live, weights, 0.0)
                if rows % 128 == 0:
                    part = weights[:, :128]
                    for k in range(1, rows // 128):
                        part = part + weights[:, k * 128 : (k + 1) * 128]
                else:
                    part = jnp.where(lane == 0, jnp.sum(weights, axis=1, keepdims=True), 0.0)
                state[i, :, HEAD_SIZE:] += part
                state[i, :, :HEAD_SIZE] += dot(
                    weights.astype(jnp.bfloat16), keys[j, :, HEAD_SIZE:], 1, 0
                )

        return visit

    key_count = own.shape[0]
    run_pairs(list_ref, 0, key_count, unroll, visit_in(own))
    run_pairs(list_ref, 1, key_count, unroll, visit_in(other))
    out = pltpu.make_async_copy(state, out_hbm, sems.at[4])
    out.start()
    out.wait()


def attend(lists, query, own, other, state):
    first = state is None
    blocks, rows, _ = query.shape
    shape = (blocks, rows, HEAD_SIZE + 128)
    operands = (query, own, other) if first else (query, own, other, state)
    return pl.pallas_call(
        functools.partial(attend_kernel, first, 4),
        out_shape=jax.ShapeDtypeStruct(shape, jnp.float32),
        grid_spec=pltpu.PrefetchScalarGridSpec(
            num_scalar_prefetch=1,
            grid=(1,),
            in_specs=[pl.BlockSpec(memory_space=pl.ANY)] * len(operands),
            out_specs=pl.BlockSpec(memory_space=pl.ANY),
            scratch_shapes=[
                pltpu.VMEM(query.shape, jnp.bfloat16),
                pltpu.VMEM(own.shape, jnp.bfloat16),
                pltpu.VMEM(other.shape, jnp.bfloat16),
                pltpu.VMEM(shape, jnp.float32),
                pltpu.SemaphoreType.DMA((5,)),
            ],
        ),
        compiler_params=pltpu.CompilerParams(vmem_limit_bytes=VMEM_BYTES),
        cost_estimate=pl.CostEstimate(
            flops=60 * 4 * rows * rows * HEAD_SIZE,
            bytes_accessed=14 * 1024 * 1024,
            transcendentals=60 * 2 * rows * rows,
        ),
    )(lists, *operands)


def attend_back_kernel(
    first,
    unroll,
    list_ref,
    query_hbm,
    grad_hbm,
    term_hbm,
    own_hbm,
    other_hbm,
    *rest,
):
    if first:
        state_hbm = None
    else:
        state_hbm, *rest = rest
    (
        out_hbm,
        own_out_hbm,
        other_out_hbm,
        query,
        grad,
        term,
        own,
        other,
        state,
        own_grad,
        other_grad,
        own_low,
        other_low,
        sems,
    ) = rest
    copies = [
        pltpu.make_async_copy(query_hbm, query, sems.at[0]),
        pltpu.make_async_copy(grad_hbm, grad, sems.at[1]),
        pltpu.make_async_copy(term_hbm, term, sems.at[2]),
        pltpu.make_async_copy(own_hbm, own, sems.at[3]),
        pltpu.make_async_copy(other_hbm, other, sems.at[4]),
    ]
    if not first:
        copies.append(pltpu.make_async_copy(state_hbm, state, sems.at[5]))
    for copy in copies:
        copy.start()
    if first:
        state[...] = jnp.zeros_like(state)
    own_grad[...] = jnp.zeros_like(own_grad)
    other_grad[...] = jnp.zeros_like(other_grad)
    for copy in copies:
        copy.wait()

    def visit_in(keys, key_grad):
        def visit(query_at, key_at, far):
            scores = []
            slopes = []
            for i, j in zip(query_at, key_at):
                scores.append(dot(keys[j, :, :HEAD_SIZE], query[i], 1, 1))
                slopes.append(dot(keys[j, :, HEAD_SIZE:], grad[i], 1, 1))
            for i, j, score, slope in zip(query_at, key_at, scores, slopes):
                bent = jnp.tanh(score * TANH_SCALE)
                weights = jnp.exp2(EXP2_SCALE * bent)
                if far is not None:
                    spacing = (
                        lax.broadcasted_iota(jnp.int32, weights.shape, 1)
                        - lax.broadcasted_iota(jnp.int32, weights.shape, 0)
                        + far * LOOKBACK_SPAN
                    )
                    live = (spacing >= 0) & (spacing < LOOKBACK_SPAN)
                    weights = jnp.where(live, weights, 0.0)
                grad_scores = (
                    (slope + term[i]) * (weights * (1.0 - bent * bent))
                ).astype(jnp.bfloat16)
                key_grad[j, :, :HEAD_SIZE] += dot(grad_scores, query[i], 1, 0)
                key_grad[j, :, HEAD_SIZE:] += dot(weights.astype(jnp.bfloat16), grad[i], 1, 0)
                state[i] += dot(grad_scores, keys[j, :, :HEAD_SIZE], 0, 0)

        return visit

    key_count = own.shape[0]
    run_pairs(list_ref, 1, key_count, unroll, visit_in(other, other_grad))
    other_low[...] = other_grad[...].astype(jnp.bfloat16)
    other_out = pltpu.make_async_copy(other_low, other_out_hbm, sems.at[6])
    other_out.start()
    run_pairs(list_ref, 0, key_count, unroll, visit_in(own, own_grad))
    own_low[...] = own_grad[...].astype(jnp.bfloat16)
    own_out = pltpu.make_async_copy(own_low, own_out_hbm, sems.at[7])
    own_out.start()
    out = pltpu.make_async_copy(state, out_hbm, sems.at[8])
    out.start()
    other_out.wait()
    own_out.wait()
    out.wait()


def attend_back(lists, query, grad, term, own, other, state):
    first = state is None
    blocks, rows, _ = query.shape
    operands = (query, grad, term, own, other)
    if not first:
        operands = operands + (state,)
    return pl.pallas_call(
        functools.partial(attend_back_kernel, first, 2),
        out_shape=[
            jax.ShapeDtypeStruct(query.shape, jnp.float32),
            jax.ShapeDtypeStruct(own.shape, jnp.bfloat16),
            jax.ShapeDtypeStruct(other.shape, jnp.bfloat16),
        ],
        grid_spec=pltpu.PrefetchScalarGridSpec(
            num_scalar_prefetch=1,
            grid=(1,),
            in_specs=[pl.BlockSpec(memory_space=pl.ANY)] * len(operands),
            out_specs=[pl.BlockSpec(memory_space=pl.ANY)] * 3,
            scratch_shapes=[
                pltpu.VMEM(query.shape, jnp.bfloat16),
                pltpu.VMEM(query.shape, jnp.bfloat16),
                pltpu.VMEM(term.shape, jnp.float32),
                pltpu.VMEM(own.shape, jnp.bfloat16),
                pltpu.VMEM(other.shape, jnp.bfloat16),
                pltpu.VMEM(query.shape, jnp.float32),
                pltpu.VMEM(own.shape, jnp.float32),
                pltpu.VMEM(other.shape, jnp.float32),
                pltpu.VMEM(own.shape, jnp.bfloat16),
                pltpu.VMEM(other.shape, jnp.bfloat16),
                pltpu.SemaphoreType.DMA((9,)),
            ],
        ),
        compiler_params=pltpu.CompilerParams(vmem_limit_bytes=VMEM_BYTES),
        cost_estimate=pl.CostEstimate(
            flops=60 * 10 * rows * rows * HEAD_SIZE,
            bytes_accessed=24 * 1024 * 1024,
            transcendentals=60 * 2 * rows * rows,
        ),
    )(lists, *operands)


def body(inputs, cotangent, block_ids, positions, attn_in, attn_out, mlp_in, mlp_out, gains):
    token_rows, width = inputs.shape
    block = token_rows // 2
    devices = lax.axis_size(AXES)
    ctx_count, row_parts = lax.axis_size("ctx"), lax.axis_size("fsdp")
    planes = devices // PLANE
    blocks_per_seq = 2 * devices // SEQUENCE_COUNT
    span_blocks = LOOKBACK_SPAN // block
    score_scale = HEAD_SIZE ** (-0.5)
    me = lax.axis_index(AXES)
    place, plane = me % PLANE, me // PLANE
    part = place % row_parts
    row_share = attn_in.shape[0]
    unit = mlp_out.shape[1] // PLANE
    chunk = attn_in.shape[1] // row_parts
    order = NEAR + FAR

    gain_parts = ordered([gains.T] + [swap(gains.T, mask) for mask in range(1, row_parts)], part)
    scales = wide(gain_parts.transpose(1, 0, 2).reshape(gains.shape[1], width))
    source = wide(inputs)
    inverse_in = inverse_rms(source)
    lowered_in = narrow(source * inverse_in * scales[0])

    gathered_out = lax.all_gather(attn_out, AXES, axis=0)
    in_pieces = mlp_in.T.reshape(2, PLANE, unit, row_share).transpose(1, 0, 2, 3)
    in_received = exchange_members(in_pieces, place)
    attn_pieces = exchange_members(attn_in.T.reshape(row_parts, chunk, row_share), part)
    in_chunk = ordered(attn_pieces, part).transpose(1, 0, 2).reshape(chunk, width)
    stored = [in_chunk]
    for step in range(1, planes):
        stored.append(shift(stored[-1]))
    *in_received, in_chunk = together(*in_received, stored[1])
    in_share = (
        ordered(in_received, place)
        .reshape(2, row_parts, 2, unit, row_share)
        .transpose(0, 2, 3, 1, 4)
        .reshape(4 * unit, width)
    )
    lowered_in = after(lowered_in, in_chunk)
    block_ids = after(block_ids, in_chunk)

    def ids_of(which_plane, slots):
        masks = jnp.asarray([mask for mask, _ in slots], jnp.int32)
        sides = jnp.asarray([half for _, half in slots], jnp.int32)
        at = 2 * (which_plane[:, None] * PLANE + (place ^ masks)[None, :]) + sides[None, :]
        slot = jnp.arange(block_ids.shape[0], dtype=jnp.int32)
        return jnp.sum(jnp.where(at[:, :, None] == slot, block_ids, 0), axis=2)

    stage_planes = (plane + planes - jnp.arange(planes, dtype=jnp.int32)) % planes
    stage_ids = ids_of(stage_planes, order)
    query_ids = stage_ids[0]
    lists = pair_lists(
        query_ids, stage_ids.reshape(2 * planes, len(NEAR)), blocks_per_seq, span_blocks
    ).reshape(planes, 2, -1)
    half_width = HEAD_SIZE // 2
    frequency = ROPE_BASE ** (-2.0 * jnp.arange(half_width, dtype=jnp.float32) / HEAD_SIZE)
    base_angle = wide(query_ids % blocks_per_seq * block)[:, None, None] * frequency
    step_angle = jnp.arange(block, dtype=jnp.float32)[:, None] * frequency
    base_cosine, base_sine = jnp.cos(base_angle), jnp.sin(base_angle)
    step_cosine, step_sine = jnp.cos(step_angle), jnp.sin(step_angle)
    cosine = base_cosine * step_cosine - base_sine * step_sine
    sine = base_sine * step_cosine + base_cosine * step_sine

    in_share = after(in_share, stored[-1])
    stored = jnp.stack([pick(jnp.stack(stored), (plane - p) % planes) for p in range(planes)])
    cut = 2 * unit
    in_halves = [[in_share[:cut]], [in_share[cut:]]]
    out_shares = []
    in_all = jnp.zeros((planes * 4 * unit, width), jnp.bfloat16)
    out_all = jnp.zeros((planes * 2 * unit, width), jnp.bfloat16)

    def next_in(which):
        def start(token):
            in_halves[which].append(shift(after(in_halves[which][-1], token)))
            return (in_halves[which][-1],)

        return start

    def next_out(token):
        out_shares.append(shift(after(out_shares[-1], token)))
        return (out_shares[-1],)

    query_planes, kv_planes = planes // 2, planes // 4
    query_rounds = matchings(chunk_edges(query_planes, attn_in.shape[1], chunk, 1))
    kv_rounds = matchings(
        chunk_edges(kv_planes, attn_in.shape[1], chunk, QUERY_HEADS // KEY_VALUE_HEADS)
    )
    query_chunks = chunks_to_heads(stored[:query_planes], query_rounds, place)
    kv_chunks = chunks_to_heads(
        jnp.concatenate(
            [stored[query_planes : query_planes + kv_planes], stored[query_planes + kv_planes :]],
            axis=1,
        ),
        kv_rounds,
        place,
    )
    attn_weight = jnp.concatenate(
        query_chunks + [both[:chunk] for both in kv_chunks] + [both[chunk:] for both in kv_chunks]
    )

    def first_in(token):
        return next_in(0)(token) + (lists, cosine, sine)

    in_groups, projected, extras = gather_plane(
        lowered_in,
        lambda group: dot(group, attn_weight, 1, 1),
        (first_in, next_in(1), next_in(0)),
    )
    lists, cosine, sine = extras[0][1:]

    def split_groups(groups):
        near = jnp.concatenate([group[:token_rows] for group in groups])
        far = jnp.concatenate([group[token_rows:] for group in groups])
        return [rows.reshape(len(NEAR), block, rows.shape[1]) for rows in (near, far)]

    near_rows, far_rows = split_groups(projected)
    query_parts, kv_parts = [], []
    for rows, low, high in ((near_rows, 0, len(NEAR)), (far_rows, len(NEAR), 2 * len(NEAR))):
        turns = (cosine[low:high], sine[low:high])
        query_parts.append(narrow(rotate(rows[:, :, :HEAD_SIZE], *turns)))
        kv_parts.append(
            jnp.concatenate(
                [
                    narrow(rotate(rows[:, :, HEAD_SIZE : 2 * HEAD_SIZE], *turns)),
                    narrow(rows[:, :, 2 * HEAD_SIZE :]),
                ],
                axis=-1,
            )
        )
    own_kv, other_kv = kv_parts
    query = jnp.concatenate(query_parts)

    out_pieces = after(mlp_out.T, own_kv).reshape(PLANE, unit, row_share)
    out_shares.append(
        ordered(exchange_members(out_pieces, place), place)
        .reshape(2, row_parts, unit, row_share)
        .transpose(0, 2, 1, 3)
        .reshape(2 * unit, width)
    )
    kv_stages = [(own_kv, other_kv)]
    state = None
    for step in range(planes):
        own_kv, other_kv = kv_stages[step]
        state_next = attend(lists[step], query, own_kv, other_kv, state)
        if step < planes - 1:
            moving = shift(own_kv)
            if step == 0:
                state_next, moving, out_shares[0] = together(state_next, moving, out_shares[0])
            else:
                state_next, moving = together(state_next, moving)
            kv_stages.append((moving, swap(moving, CORE)))
        else:
            state_next, _ = together(state_next, *next_in(1)(own_kv))
        state = state_next
    totals = jnp.sum(state[:, :, HEAD_SIZE:], axis=-1, keepdims=True)
    attended = state[:, :, :HEAD_SIZE] / totals
    attended_rows = narrow(attended)

    def member_rows(blocks, mask):
        return jnp.concatenate([blocks[order.index((mask, 0))], blocks[order.index((mask, 1))]])

    def blocks_of(received):
        return jnp.stack(
            [received[mask][half * block : (half + 1) * block] for mask, half in order]
        )

    next_in(0)(attended_rows)
    attended_heads = ordered(
        exchange([member_rows(attended_rows, mask) for mask in range(PLANE)]), place
    )
    attended_heads = after(attended_heads, in_halves[0][-1])
    gathered_out = (
        gathered_out.reshape((QUERY_HEADS, -1, row_parts) + attn_out.shape)
        .transpose(0, 2, 3, 1, 4)
        .reshape(QUERY_HEADS, row_parts, row_share, HEAD_SIZE)
    )

    next_in(1)(attended_heads)
    branch = out_product(attended_heads, gathered_out)
    inverse_branch = inverse_rms(branch)
    middle = source + branch * inverse_branch * scales[1]
    inverse_mid = inverse_rms(middle)
    lowered_mid = narrow(middle * inverse_mid * scales[2])
    lowered_mid = after(lowered_mid, in_halves[1][-1])
    hidden_width = planes * 2 * unit
    for which, shares in enumerate(in_halves):
        while len(shares) < planes:
            shares.append(shift(shares[-1]))
        for step, share in enumerate(shares):
            at = (plane - step) % planes * 4 * unit + which * cut
            in_all = lax.dynamic_update_slice_in_dim(in_all, share, at, 0)

    def gate_up_of(group):
        return narrow(dot(group, in_all, 1, 1))

    mid_groups, gate_ups, _ = gather_plane(lowered_mid, gate_up_of, (next_out,) * 3)
    while len(out_shares) < planes:
        out_shares.append(shift(out_shares[-1]))
    for step, share in enumerate(out_shares):
        at = (plane - step) % planes * 2 * unit
        out_all = lax.dynamic_update_slice_in_dim(out_all, share, at, 0)

    def activate(gate_up):
        gate = wide(gate_up[:, :hidden_width])
        up = wide(gate_up[:, hidden_width:])
        return jax.nn.gelu(gate, approximate=True) * up

    hiddens = [narrow(activate(gate_up)) for gate_up in gate_ups]

    def reduce_groups(groups, weight, *rest):
        def work(index, token):
            group = groups[index] if token is None else after(groups[index], token)
            partial = together(narrow(dot(group, weight, 1, 0)))[0]
            return partial[:token_rows], partial[token_rows:]

        return reduce_plane(work, *rest)

    down_branch, _ = reduce_groups(hiddens, out_all)
    inverse_down = inverse_rms(down_branch)
    result = middle + down_branch * inverse_down * scales[3]
    upstream = wide(cotangent)
    grad_down, grad_gain_post = norm_back(down_branch, inverse_down, scales[3], upstream)
    grad_down_low = narrow(grad_down)

    def activate_back(gate_up, grad_hidden):
        gate = wide(gate_up[:, :hidden_width])
        up = wide(gate_up[:, hidden_width:])
        _, back = jax.vjp(lambda g, u: jax.nn.gelu(g, approximate=True) * u, gate, up)
        grad_gate, grad_up = back(grad_hidden)
        return narrow(jnp.concatenate([grad_gate, grad_up], axis=1))

    remaining = list(gate_ups)

    def grad_gate_up_of(group):
        return activate_back(remaining.pop(0), dot(group, out_all, 1, 1))

    down_groups, grad_gate_ups, _ = gather_plane(grad_down_low, grad_gate_up_of)

    tile = 768 if width % 768 == 0 else width
    rings = {}

    def in_grads(token):
        grads = row_product(
            [after(grad_gate_ups[0], token)] + grad_gate_ups[1:], mid_groups, tile, tile
        )
        parts = grads.reshape(planes, 4 * unit, width)
        rings["low"] = RingSum(parts, plane, 0, cut)
        rings["high"] = RingSum(parts, plane, cut, cut)
        return (grads,)

    def first_low(token):
        rings["low"].start(token)
        return (rings["low"].finish(),)

    def first_high(token):
        rings["high"].start(token)
        return (rings["high"].finish(),)

    grad_lowered_mid, _ = reduce_groups(
        grad_gate_ups, in_all, (in_grads, first_low, first_high)
    )
    low_ring, high_ring = rings["low"], rings["high"]

    low_ring.start(grad_lowered_mid)
    grad_through_mid, grad_gain_pre_mlp = norm_back(
        middle, inverse_mid, scales[2], grad_lowered_mid
    )
    grad_middle = upstream + grad_through_mid
    grad_branch, grad_gain_post_attn = norm_back(branch, inverse_branch, scales[1], grad_middle)
    grad_branch_low = narrow(grad_branch)
    grad_heads = out_back_product(grad_branch_low, gathered_out)
    grad_heads = after(grad_heads, low_ring.finish())
    high_ring.start(grad_heads)
    grad_rows = wide(blocks_of(exchange_members(grad_heads, place)))
    row_terms = -jnp.sum(grad_rows * attended, axis=-1) / totals[..., 0]
    grad_summed = narrow(grad_rows / totals)
    grad_summed = after(grad_summed, high_ring.finish())
    row_terms = row_terms[:, None, :]

    grad_query, kv_total = None, None
    for step in range(planes):
        stage = (step + 1) % planes
        own_kv, other_kv = kv_stages[stage]
        beside = []
        if step == 0:
            low_ring.start(grad_summed)
            out_parts = out_grad_product(after(grad_branch_low, grad_summed), attended_heads)
            beside = [low_ring.finish(), out_parts]
        else:
            beside = [shift(kv_total)]
            grad_query = after(grad_query, kv_total)
        if step == 1:
            high_ring.start(kv_total)
            beside.append(high_ring.finish())
            grads = row_product([after(hiddens[0], kv_total)] + hiddens[1:], down_groups, 384, tile)
            beside.append(grads)
        if step == 2:
            in_sum = jnp.concatenate([low_ring.finish_all(), high_ring.finish_all()])
            in_pieces = after(in_sum, kv_total).reshape(2, 2, unit, row_parts, row_share)
            in_pieces = in_pieces.transpose(0, 3, 1, 2, 4).reshape(PLANE, 2, unit, row_share)
            in_pieces = exchange_members(in_pieces, place)
        if step == planes - 1:
            beside.extend(in_pieces)
        grad_query, own_grad, other_grad, *beside = together(
            *attend_back(
                lists[stage], query, grad_summed, row_terms, own_kv, other_kv, grad_query
            ),
            *beside,
        )
        total = wide(own_grad) + wide(swap(other_grad, CORE))
        if step:
            total = total + wide(beside[0])
        kv_total = narrow(total)
        if step == 1:
            out_ring = RingSum(beside[2].reshape(planes, 2 * unit, width), plane)
        if step == 0:
            out_parts = (
                beside[1].reshape(QUERY_HEADS, width, -1, attn_out.shape[1])
                .transpose(0, 2, 1, 3)
                .reshape(devices * row_share, attn_out.shape[1])
            )
            grad_attn_out = wide(
                lax.psum_scatter(out_parts, AXES, scatter_dimension=0, tiled=True)
            )
    in_received = beside[1:]

    turned_query = narrow(rotate(grad_query * score_scale, cosine, -sine))
    kv_grad = wide(kv_total)
    turned_key = narrow(
        rotate(
            kv_grad[:, :, :HEAD_SIZE] * score_scale, cosine[: len(NEAR)], -sine[: len(NEAR)]
        )
    )
    near_grads = jnp.concatenate(
        [turned_query[: len(NEAR)], turned_key, kv_total[:, :, HEAD_SIZE:]], axis=-1
    ).reshape(4, token_rows, 3 * HEAD_SIZE)
    far_grads = turned_query[len(NEAR) :].reshape(4, token_rows, HEAD_SIZE)
    query_groups = jnp.concatenate([near_grads[:, :, :HEAD_SIZE], far_grads], axis=1)
    query_weight = attn_weight[:HEAD_SIZE]

    out_ring.start(kv_total)

    def weight_grads(token):
        out_ring.finish()
        out_ring.start(token)
        query_lefts = [after(query_groups[0], token)] + [query_groups[i] for i in range(1, 4)]
        grad_query_weight = row_product(query_lefts, in_groups, HEAD_SIZE, tile)
        grad_kv_weight = row_product(
            [after(near_grads[i, :, HEAD_SIZE:], token) for i in range(4)],
            in_groups,
            2 * HEAD_SIZE,
            tile,
        )
        return (grad_query_weight, grad_kv_weight, out_ring.finish())

    def weight_chunks(extras):
        grad_query_weight, grad_kv_weight, out_sum = extras[0]
        query_stored = heads_to_chunks(
            grad_query_weight.reshape(HEAD_SIZE // chunk, chunk, width),
            query_rounds,
            place,
            query_planes,
        )
        kv_stored = heads_to_chunks(
            jnp.concatenate(
                [
                    grad_kv_weight[:HEAD_SIZE].reshape(HEAD_SIZE // chunk, chunk, width),
                    grad_kv_weight[HEAD_SIZE:].reshape(HEAD_SIZE // chunk, chunk, width),
                ],
                axis=1,
            ),
            kv_rounds,
            place,
            kv_planes,
        )
        out_ring.total = out_sum
        out_ring.start()
        stored = jnp.concatenate([query_stored, kv_stored[:, :chunk], kv_stored[:, chunk:]])
        return (stored, out_ring.finish())

    attn_rings = []

    def attn_hop(token):
        if not attn_rings:
            attn_rings.append(RingSum(extras_of[0][1][0], plane))
        attn_rings[0].start(token)
        return (attn_rings[0].finish(),)

    def hop_and_pieces(token):
        pieces = wide(ordered([after(rows, token) for rows in in_received], place))
        grads = pieces.transpose(3, 1, 0, 2).reshape(mlp_in.shape)
        return attn_hop(token) + (grads,)

    def project_back(index, token):
        near, far = near_grads[index], far_grads[index]
        if token is not None:
            near = after(near, token)
        return together(
            narrow(dot(near, attn_weight, 1, 0)), narrow(dot(far, query_weight, 1, 0))
        )

    extras_of = []

    def keep_chunks(extras):
        extras_of.append(extras)
        return weight_chunks(extras)

    grad_lowered_in, extras = reduce_plane(
        project_back, (weight_grads, hop_and_pieces, attn_hop), keep_chunks
    )
    attn_sum = attn_rings[0].finish_all()
    pieces = out_ring.finish_all().reshape(2, unit, row_parts, row_share)
    pieces = pieces.transpose(0, 2, 1, 3).reshape(PLANE, unit, row_share)
    out_received = exchange_members(pieces, place)
    pieces = attn_sum.reshape(chunk, row_parts, row_share).transpose(1, 0, 2)
    attn_received = exchange_members(pieces, part)
    grad_source, grad_gain_in = norm_back(source, inverse_in, scales[0], grad_lowered_in)
    grad_input = grad_middle + grad_source

    grad_mlp_in = extras[2][1]
    attn_pieces = ordered(attn_received, part)
    grad_attn_in = wide(attn_pieces.reshape(attn_in.shape[1], row_share).T)
    out_pieces = wide(ordered(out_received, place))
    grad_mlp_out = out_pieces.transpose(2, 0, 1).reshape(mlp_out.shape)
    gain_total = sum_devices(
        jnp.stack([grad_gain_in, grad_gain_post_attn, grad_gain_pre_mlp, grad_gain_post])
    )
    grad_gains = pick(
        gain_total.reshape(gains.shape[1], row_parts, row_share).transpose(1, 2, 0), part
    )
    return (
        narrow(result),
        grad_input,
        grad_attn_in,
        grad_attn_out,
        grad_mlp_in,
        grad_mlp_out,
        grad_gains,
    )


def solution(mesh):
    placed = (
        P(("ctx", "fsdp"), None),
        P(("ctx", "fsdp"), None),
        P(),
        P(("ctx", "fsdp")),
        P("fsdp", "ctx"),
        P("fsdp", "ctx"),
        P("fsdp", "ctx"),
        P("fsdp", "ctx"),
        P("fsdp", None),
    )
    return jax.shard_map(
        body,
        mesh=mesh,
        in_specs=placed,
        out_specs=(
            P(("ctx", "fsdp"), None),
            P(("ctx", "fsdp"), None),
            P("fsdp", "ctx"),
            P("fsdp", "ctx"),
            P("fsdp", "ctx"),
            P("fsdp", "ctx"),
            P("fsdp", None),
        ),
        check_vma=False,
    )
```

```python
import functools
import math

import jax
import jax.numpy as jnp
from jax import lax
from jax.experimental import pallas as pl
from jax.experimental.pallas import tpu as pltpu
from jax.sharding import PartitionSpec as P

QUERY_HEADS = 8
KEY_VALUE_HEADS = 4
HEAD_SIZE = 256
LOOKBACK_SPAN = 4096
SEQUENCE_COUNT = 2


EPSILON = 1e-06
SOFT_CAP = 50.0
ROPE_BASE = 10000.0
AXES = ("ctx", "fsdp")
PLANE = 8
CORE, SIDE, ACROSS = 1, 2, 4
TANH_SCALE = HEAD_SIZE ** (-0.5) / SOFT_CAP
EXP2_SCALE = SOFT_CAP * math.log2(math.e)
VMEM_BYTES = 56 * 1024 * 1024


def inverse_rms(values):
    return lax.rsqrt(jnp.mean(values * values, axis=-1, keepdims=True) + EPSILON)


def norm_back(values, inverse, scale, upstream):
    scaled = upstream * scale
    through = inverse * scaled - values * inverse**3 * jnp.mean(
        scaled * values, axis=-1, keepdims=True
    )
    return (through, jnp.sum(upstream * values * inverse, axis=0))


def rotate(values, cosine, sine):
    half_width = values.shape[-1] // 2
    first_half = values[..., :half_width]
    second_half = values[..., half_width:]
    return jnp.concatenate(
        [
            first_half * cosine - second_half * sine,
            second_half * cosine + first_half * sine,
        ],
        axis=-1,
    )


def dot(left, right, left_axis, right_axis):
    return lax.dot_general(
        left,
        right,
        (((left_axis,), (right_axis,)), ((), ())),
        preferred_element_type=jnp.float32,
    )


def after(value, *others):
    return lax.optimization_barrier((value,) + others)[0]


def wide(values):
    return values.astype(jnp.float32)


def narrow(values):
    return values.astype(jnp.bfloat16)


def swap(values, mask):
    count = lax.axis_size(AXES)
    return lax.ppermute(values, AXES, [(i, i ^ mask) for i in range(count)])


def shift(values, steps=1):
    count = lax.axis_size(AXES)
    return lax.ppermute(values, AXES, [(i, (i + steps * PLANE) % count) for i in range(count)])


def route(values, targets):
    count = lax.axis_size(AXES)
    return lax.ppermute(
        values, AXES, [(i, i - i % PLANE + targets[i % PLANE]) for i in range(count)]
    )


def pick(stacked, index):
    return lax.dynamic_index_in_dim(stacked, index, 0, keepdims=False)


def look_up(table, place):
    return pick(jnp.asarray(table, jnp.int32), place)


def exchange(pieces):
    far = swap(jnp.stack([pieces[mask ^ CORE] for mask in range(0, len(pieces), 2)]), CORE)
    received = []
    for i, mask in enumerate(range(0, len(pieces), 2)):
        both = jnp.stack([pieces[mask], far[i]])
        if mask:
            both = swap(both, mask)
        received.extend([both[0], both[1]])
    return received


def exchange_members(stacked, place):
    return exchange([pick(stacked, place ^ mask) for mask in range(stacked.shape[0])])


def ordered(received, place):
    whole = jnp.zeros((len(received),) + received[0].shape, received[0].dtype)
    for mask, rows in enumerate(received):
        whole = lax.dynamic_update_index_in_dim(whole, rows, place ^ mask, 0)
    return whole


NEAR = [(0, 0), (0, 1), (4, 0), (2, 1), (2, 0), (4, 1), (6, 0), (6, 1)]
FAR = [(mask ^ CORE, half) for mask, half in NEAR]


def together(*values):
    return lax.optimization_barrier(values)


def no_transfers(token):
    return ()


def gather_plane(rows, work, beside=(no_transfers,) * 3):
    half = rows.shape[0] // 2
    low, high = rows[:half], rows[half:]
    groups, done, extras = [], [], []

    def add_group(near, far):
        groups.append(jnp.concatenate([near, far]))
        done.append(work(groups[-1], len(done)))

    other = swap(rows, CORE)
    first_low, first_high = swap(low, ACROSS), swap(high, SIDE)
    extra = beside[0](rows)
    add_group(rows, other)
    done[0], first_low, first_high, *extra = together(done[0], first_low, first_high, *extra)
    extras.append(extra)
    low, high = together(low, high, first_low)[:2]
    first_other = swap(jnp.concatenate([first_low, first_high]), CORE)
    second_low, second_high = swap(low, SIDE), swap(high, ACROSS)
    extra = beside[1](first_low)
    add_group(jnp.concatenate([first_low, first_high]), first_other)
    done[1], first_low, first_high, second_low, second_high, *extra = together(
        done[1], first_low, first_high, second_low, second_high, *extra
    )
    extras.append(extra)
    second_other = swap(jnp.concatenate([second_low, second_high]), CORE)
    third_low, third_high = swap(first_low, SIDE), swap(first_high, ACROSS)
    extra = beside[2](second_low)
    add_group(jnp.concatenate([second_low, second_high]), second_other)
    done[2], third_low, third_high, *extra = together(done[2], third_low, third_high, *extra)
    extras.append(extra)
    third = jnp.concatenate([third_low, third_high])
    add_group(third, swap(third, CORE))
    return groups, done, extras


def reduce_plane(work, beside=(no_transfers,) * 3, middle=None):
    extras = []

    def both(group, token):
        near, far = work(group, token)
        return wide(near) + wide(swap(far, CORE))

    third = narrow(both(3, None))
    half = third.shape[0] // 2
    got_low, got_high = swap(third[:half], SIDE), swap(third[half:], ACROSS)
    second = narrow(both(2, third))
    got_low, got_high, second, *extra = together(got_low, got_high, second, *beside[0](third))
    extras.append(extra)
    if middle is not None:
        second, *extra = together(second, *middle(extras))
        extras.append(extra)
    own_low, own_high = swap(second[:half], SIDE), swap(second[half:], ACROSS)
    first = both(1, second)
    first = narrow(first + wide(jnp.concatenate([got_low, got_high])))
    own_low, own_high, first, *extra = together(own_low, own_high, first, *beside[1](second))
    extras.append(extra)
    more_low, more_high = swap(first[:half], ACROSS), swap(first[half:], SIDE)
    own = both(0, first) + wide(jnp.concatenate([own_low, own_high]))
    more_low, more_high, own, *extra = together(more_low, more_high, own, *beside[2](first))
    extras.append(extra)
    return own + wide(jnp.concatenate([more_low, more_high])), extras


def sum_devices(values):
    for mask in (CORE, SIDE, ACROSS):
        values = values + swap(values, mask)
    total = values
    for steps in range(1, lax.axis_size(AXES) // PLANE):
        total = total + shift(values, steps)
    return total


class RingSum:
    def __init__(self, parts, plane, first=0, rows=None):
        self.parts, self.plane, self.planes = parts, plane, parts.shape[0]
        self.first, self.rows = first, rows or parts.shape[1]
        self.hops, self.moving = 0, None
        self.total = self.part(0)

    def part(self, step):
        at = (self.plane + 2 * self.planes - 1 - step) % self.planes
        size = (1, self.rows, self.parts.shape[2])
        return lax.dynamic_slice(self.parts, (at, self.first, 0), size)[0]

    def start(self, *others):
        if self.hops < self.planes - 1:
            self.moving = shift(after(self.total, *others) if others else self.total)

    def finish(self):
        if self.moving is not None:
            self.hops += 1
            self.total = narrow(wide(self.moving) + wide(self.part(self.hops)))
            self.moving = None
        return self.total

    def finish_all(self):
        self.finish()
        while self.hops < self.planes - 1:
            self.start()
            self.finish()
        return self.total


def matchings(edges):
    left, rounds = list(edges), []
    while left:
        owner = {}

        def settle(source, seen):
            for edge in left:
                if edge[0] == source and edge[1] not in seen:
                    seen.add(edge[1])
                    if edge[1] not in owner or settle(owner[edge[1]][0], seen):
                        owner[edge[1]] = edge
                        return True
            return False

        for source in range(PLANE):
            settle(source, set())
        found = sorted(owner.values())
        rounds.append(found)
        left = [edge for edge in left if edge not in found]
    return rounds


def chunk_edges(plane_count, columns, chunk, share):
    edges = []
    for source in range(PLANE):
        for at in range(plane_count):
            column = (2 * at + source // 4) * columns + source % 4 * chunk
            head = column // HEAD_SIZE
            for target in range(head * share, (head + 1) * share):
                edges.append((source, target, at, column % HEAD_SIZE // chunk))
    return edges


def chunks_to_heads(stored, rounds, place):
    spots = len(rounds)
    got = []
    for found in rounds:
        sent = pick(stored, look_up([edge[2] for edge in found], place))
        got.append(route(sent, [edge[1] for edge in found]))
    stacked = jnp.stack(got)
    order = []
    for spot in range(spots):
        table = [0] * PLANE
        for step, found in enumerate(rounds):
            for edge in found:
                if edge[3] == spot:
                    table[edge[1]] = step
        order.append(pick(stacked, look_up(table, place)))
    return order


def heads_to_chunks(heads, rounds, place, plane_count):
    got = []
    for found in rounds:
        back, spot = [0] * PLANE, [0] * PLANE
        for source, target, _, position in found:
            back[target], spot[target] = source, position
        got.append(route(pick(heads, look_up(spot, place)), back))
    stacked = jnp.stack(got)
    chunks = []
    for at in range(plane_count):
        tables = []
        for source in range(PLANE):
            tables.append(
                [
                    step
                    for step, found in enumerate(rounds)
                    for edge in found
                    if edge[0] == source and edge[2] == at
                ]
            )
        terms = [
            pick(stacked, look_up([table[i] for table in tables], place))
            for i in range(len(tables[0]))
        ]
        total = terms[0]
        if len(terms) > 1:
            total = narrow(sum(wide(term) for term in terms))
        chunks.append(total)
    return jnp.stack(chunks)


def row_product_kernel(count, *refs):
    out, total = refs[-2:]
    total[...] = dot(refs[0][...], refs[count][...], 0, 0)
    for i in range(1, count):
        total[...] += dot(refs[i][...], refs[count + i][...], 0, 0)
    out[...] = total[...].astype(out.dtype)


def row_product(lefts, rights, left_tile, right_tile):
    count = len(lefts)
    height, width = lefts[0].shape[1], rights[0].shape[1]
    depths = [left.shape[0] for left in lefts]
    return pl.pallas_call(
        functools.partial(row_product_kernel, count),
        out_shape=jax.ShapeDtypeStruct((height, width), jnp.bfloat16),
        grid=(height // left_tile, width // right_tile),
        in_specs=[pl.BlockSpec((depth, left_tile), lambda i, j: (0, i)) for depth in depths]
        + [pl.BlockSpec((depth, right_tile), lambda i, j: (0, j)) for depth in depths],
        out_specs=pl.BlockSpec((left_tile, right_tile), lambda i, j: (i, j)),
        scratch_shapes=[pltpu.VMEM((left_tile, right_tile), jnp.float32)],
        compiler_params=pltpu.CompilerParams(vmem_limit_bytes=VMEM_BYTES),
        cost_estimate=pl.CostEstimate(
            flops=2 * sum(depths) * height * width,
            bytes_accessed=2 * sum(depths) * (height + width) + 2 * height * width,
            transcendentals=0,
        ),
    )(*lefts, *rights)


def out_kernel(part, rows_ref, weight_ref, out_ref):
    at = pl.program_id(0)
    total = dot(rows_ref[0], weight_ref[0, 0], 1, 1)
    for head in range(1, rows_ref.shape[0]):
        total += dot(rows_ref[head], weight_ref[head, 0], 1, 1)
    for i in range(out_ref.shape[1] // part):

        @pl.when(at == i)
        def _():
            out_ref[:, i * part : (i + 1) * part] = total


def out_product(rows, weight):
    heads, count, size = rows.shape
    _, parts, part, _ = weight.shape
    return pl.pallas_call(
        functools.partial(out_kernel, part),
        out_shape=jax.ShapeDtypeStruct((count, parts * part), jnp.float32),
        grid=(parts,),
        in_specs=[
            pl.BlockSpec((heads, count, size), lambda i: (0, 0, 0)),
            pl.BlockSpec((heads, 1, part, size), lambda i: (0, i, 0, 0)),
        ],
        out_specs=pl.BlockSpec((count, parts * part), lambda i: (0, 0)),
        compiler_params=pltpu.CompilerParams(vmem_limit_bytes=VMEM_BYTES),
        cost_estimate=pl.CostEstimate(
            flops=2 * count * heads * size * parts * part,
            bytes_accessed=2 * heads * size * (count + parts * part) + 4 * count * parts * part,
            transcendentals=0,
        ),
    )(rows, weight)


def out_back_kernel(rows_ref, weight_ref, out_ref):
    part = weight_ref.shape[2]
    total = dot(rows_ref[:, :part], weight_ref[0, 0], 1, 0)
    for i in range(1, weight_ref.shape[1]):
        total += dot(rows_ref[:, i * part : (i + 1) * part], weight_ref[0, i], 1, 0)
    out_ref[0] = total.astype(out_ref.dtype)


def out_back_product(rows, weight):
    count, width = rows.shape
    heads, parts, part, size = weight.shape
    return pl.pallas_call(
        out_back_kernel,
        out_shape=jax.ShapeDtypeStruct((heads, count, size), jnp.bfloat16),
        grid=(heads,),
        in_specs=[
            pl.BlockSpec((count, width), lambda i: (0, 0)),
            pl.BlockSpec((1, parts, part, size), lambda i: (i, 0, 0, 0)),
        ],
        out_specs=pl.BlockSpec((1, count, size), lambda i: (i, 0, 0)),
        compiler_params=pltpu.CompilerParams(vmem_limit_bytes=VMEM_BYTES),
        cost_estimate=pl.CostEstimate(
            flops=2 * count * heads * size * width,
            bytes_accessed=2 * heads * size * (count + width) + 2 * count * width,
            transcendentals=0,
        ),
    )(rows, weight)


def out_grad_kernel(rows_ref, heads_ref, out_ref):
    out_ref[0] = dot(rows_ref[...], heads_ref[0], 0, 0).astype(out_ref.dtype)


def out_grad_product(rows, by_head):
    count, width = rows.shape
    heads, _, size = by_head.shape
    return pl.pallas_call(
        out_grad_kernel,
        out_shape=jax.ShapeDtypeStruct((heads, width, size), jnp.bfloat16),
        grid=(heads,),
        in_specs=[
            pl.BlockSpec((count, width), lambda i: (0, 0)),
            pl.BlockSpec((1, count, size), lambda i: (i, 0, 0)),
        ],
        out_specs=pl.BlockSpec((1, width, size), lambda i: (i, 0, 0)),
        compiler_params=pltpu.CompilerParams(vmem_limit_bytes=VMEM_BYTES),
        cost_estimate=pl.CostEstimate(
            flops=2 * count * heads * size * width,
            bytes_accessed=2 * heads * size * (count + width) + 2 * count * width,
            transcendentals=0,
        ),
    )(rows, by_head)


def pair_lists(query_ids, key_ids, blocks_per_seq, span_blocks):
    query_seq, query_at = query_ids // blocks_per_seq, query_ids % blocks_per_seq
    key_seq, key_at = key_ids // blocks_per_seq, key_ids % blocks_per_seq
    rows = key_ids.shape[0]
    distance = (query_at[None, :, None] - key_at[:, None, :]).reshape(rows, -1)
    same = (query_seq[None, :, None] == key_seq[:, None, :]).reshape(rows, -1)
    whole = same & (distance > 0) & (distance < span_blocks)
    edged = same & ((distance == 0) | (distance == span_blocks))
    kind = whole.astype(jnp.int32) + 2 * edged.astype(jnp.int32)
    total = distance.shape[1]
    index = jnp.arange(total, dtype=jnp.int32)
    earlier = (index[None, :] < index[:, None])[None] & (kind[:, None, :] == kind[:, :, None])
    rank = jnp.sum(earlier.astype(jnp.int32), axis=2)
    count_whole = jnp.sum(whole.astype(jnp.int32), axis=1, keepdims=True)
    count_edged = jnp.sum(edged.astype(jnp.int32), axis=1, keepdims=True)
    spot = jnp.where(kind == 1, rank, jnp.where(kind == 2, count_whole + rank, -1))
    code = index * 2 + (distance == span_blocks).astype(jnp.int32)
    hit = spot[:, :, None] == index[None, None, :]
    entries = jnp.sum(jnp.where(hit, code[:, :, None], 0), axis=1)
    return jnp.concatenate([count_whole, count_edged, entries], axis=1).astype(jnp.int32)


def run_pairs(list_ref, row, key_count, unroll, visit):
    whole = list_ref[row, 0]
    edged = list_ref[row, 1]

    def decode(position):
        code = list_ref[row, 2 + position]
        pair = code // 2
        return pair // key_count, pair % key_count, code % 2

    def several(step, carry):
        found = [decode(step * unroll + i) for i in range(unroll)]
        visit([f[0] for f in found], [f[1] for f in found], None)
        return carry

    def single(position, carry):
        i, j, _ = decode(position)
        visit([i], [j], None)
        return carry

    def masked(position, carry):
        i, j, far = decode(position)
        visit([i], [j], far)
        return carry

    groups = whole // unroll
    lax.fori_loop(0, groups, several, 0)
    lax.fori_loop(groups * unroll, whole, single, 0)
    lax.fori_loop(whole, whole + edged, masked, 0)


def attend_kernel(first, unroll, list_ref, query_hbm, own_hbm, other_hbm, *rest):
    if first:
        state_hbm = None
        out_hbm, query, own, other, state, sems = rest
    else:
        state_hbm, out_hbm, query, own, other, state, sems = rest
    copies = [
        pltpu.make_async_copy(query_hbm, query, sems.at[0]),
        pltpu.make_async_copy(own_hbm, own, sems.at[1]),
        pltpu.make_async_copy(other_hbm, other, sems.at[2]),
    ]
    if not first:
        copies.append(pltpu.make_async_copy(state_hbm, state, sems.at[3]))
    for copy in copies:
        copy.start()
    if first:
        state[...] = jnp.zeros_like(state)
    for copy in copies:
        copy.wait()
    rows = query.shape[1]
    lane = lax.broadcasted_iota(jnp.int32, (rows, 128), 1)

    def visit_in(keys):
        def visit(query_at, key_at, far):
            scores = [
                dot(query[i], keys[j, :, :HEAD_SIZE], 1, 1) for i, j in zip(query_at, key_at)
            ]
            for i, j, score in zip(query_at, key_at, scores):
                weights = jnp.exp2(EXP2_SCALE * jnp.tanh(score * TANH_SCALE))
                if far is not None:
                    spacing = (
                        lax.broadcasted_iota(jnp.int32, weights.shape, 0)
                        - lax.broadcasted_iota(jnp.int32, weights.shape, 1)
                        + far * LOOKBACK_SPAN
                    )
                    live = (spacing >= 0) & (spacing < LOOKBACK_SPAN)
                    weights = jnp.where(live, weights, 0.0)
                if rows % 128 == 0:
                    part = weights[:, :128]
                    for k in range(1, rows // 128):
                        part = part + weights[:, k * 128 : (k + 1) * 128]
                else:
                    part = jnp.where(lane == 0, jnp.sum(weights, axis=1, keepdims=True), 0.0)
                state[i, :, HEAD_SIZE:] += part
                state[i, :, :HEAD_SIZE] += dot(
                    weights.astype(jnp.bfloat16), keys[j, :, HEAD_SIZE:], 1, 0
                )

        return visit

    key_count = own.shape[0]
    run_pairs(list_ref, 0, key_count, unroll, visit_in(own))
    run_pairs(list_ref, 1, key_count, unroll, visit_in(other))
    out = pltpu.make_async_copy(state, out_hbm, sems.at[4])
    out.start()
    out.wait()


def attend(lists, query, own, other, state):
    first = state is None
    blocks, rows, _ = query.shape
    shape = (blocks, rows, HEAD_SIZE + 128)
    operands = (query, own, other) if first else (query, own, other, state)
    return pl.pallas_call(
        functools.partial(attend_kernel, first, 4),
        out_shape=jax.ShapeDtypeStruct(shape, jnp.float32),
        grid_spec=pltpu.PrefetchScalarGridSpec(
            num_scalar_prefetch=1,
            grid=(1,),
            in_specs=[pl.BlockSpec(memory_space=pl.ANY)] * len(operands),
            out_specs=pl.BlockSpec(memory_space=pl.ANY),
            scratch_shapes=[
                pltpu.VMEM(query.shape, jnp.bfloat16),
                pltpu.VMEM(own.shape, jnp.bfloat16),
                pltpu.VMEM(other.shape, jnp.bfloat16),
                pltpu.VMEM(shape, jnp.float32),
                pltpu.SemaphoreType.DMA((5,)),
            ],
        ),
        compiler_params=pltpu.CompilerParams(vmem_limit_bytes=VMEM_BYTES),
        cost_estimate=pl.CostEstimate(
            flops=60 * 4 * rows * rows * HEAD_SIZE,
            bytes_accessed=14 * 1024 * 1024,
            transcendentals=60 * 2 * rows * rows,
        ),
    )(lists, *operands)


def attend_back_kernel(
    first,
    unroll,
    list_ref,
    query_hbm,
    grad_hbm,
    term_hbm,
    own_hbm,
    other_hbm,
    *rest,
):
    if first:
        state_hbm = None
    else:
        state_hbm, *rest = rest
    (
        out_hbm,
        own_out_hbm,
        other_out_hbm,
        query,
        grad,
        term,
        own,
        other,
        state,
        own_grad,
        other_grad,
        own_low,
        other_low,
        sems,
    ) = rest
    copies = [
        pltpu.make_async_copy(query_hbm, query, sems.at[0]),
        pltpu.make_async_copy(grad_hbm, grad, sems.at[1]),
        pltpu.make_async_copy(term_hbm, term, sems.at[2]),
        pltpu.make_async_copy(own_hbm, own, sems.at[3]),
        pltpu.make_async_copy(other_hbm, other, sems.at[4]),
    ]
    if not first:
        copies.append(pltpu.make_async_copy(state_hbm, state, sems.at[5]))
    for copy in copies:
        copy.start()
    if first:
        state[...] = jnp.zeros_like(state)
    own_grad[...] = jnp.zeros_like(own_grad)
    other_grad[...] = jnp.zeros_like(other_grad)
    for copy in copies:
        copy.wait()

    def visit_in(keys, key_grad):
        def visit(query_at, key_at, far):
            scores = []
            slopes = []
            for i, j in zip(query_at, key_at):
                scores.append(dot(keys[j, :, :HEAD_SIZE], query[i], 1, 1))
                slopes.append(dot(keys[j, :, HEAD_SIZE:], grad[i], 1, 1))
            for i, j, score, slope in zip(query_at, key_at, scores, slopes):
                bent = jnp.tanh(score * TANH_SCALE)
                weights = jnp.exp2(EXP2_SCALE * bent)
                if far is not None:
                    spacing = (
                        lax.broadcasted_iota(jnp.int32, weights.shape, 1)
                        - lax.broadcasted_iota(jnp.int32, weights.shape, 0)
                        + far * LOOKBACK_SPAN
                    )
                    live = (spacing >= 0) & (spacing < LOOKBACK_SPAN)
                    weights = jnp.where(live, weights, 0.0)
                grad_scores = (
                    (slope + term[i]) * (weights * (1.0 - bent * bent))
                ).astype(jnp.bfloat16)
                key_grad[j, :, :HEAD_SIZE] += dot(grad_scores, query[i], 1, 0)
                key_grad[j, :, HEAD_SIZE:] += dot(weights.astype(jnp.bfloat16), grad[i], 1, 0)
                state[i] += dot(grad_scores, keys[j, :, :HEAD_SIZE], 0, 0)

        return visit

    key_count = own.shape[0]
    run_pairs(list_ref, 1, key_count, unroll, visit_in(other, other_grad))
    other_low[...] = other_grad[...].astype(jnp.bfloat16)
    other_out = pltpu.make_async_copy(other_low, other_out_hbm, sems.at[6])
    other_out.start()
    run_pairs(list_ref, 0, key_count, unroll, visit_in(own, own_grad))
    own_low[...] = own_grad[...].astype(jnp.bfloat16)
    own_out = pltpu.make_async_copy(own_low, own_out_hbm, sems.at[7])
    own_out.start()
    out = pltpu.make_async_copy(state, out_hbm, sems.at[8])
    out.start()
    other_out.wait()
    own_out.wait()
    out.wait()


def attend_back(lists, query, grad, term, own, other, state):
    first = state is None
    blocks, rows, _ = query.shape
    operands = (query, grad, term, own, other)
    if not first:
        operands = operands + (state,)
    return pl.pallas_call(
        functools.partial(attend_back_kernel, first, 2),
        out_shape=[
            jax.ShapeDtypeStruct(query.shape, jnp.float32),
            jax.ShapeDtypeStruct(own.shape, jnp.bfloat16),
            jax.ShapeDtypeStruct(other.shape, jnp.bfloat16),
        ],
        grid_spec=pltpu.PrefetchScalarGridSpec(
            num_scalar_prefetch=1,
            grid=(1,),
            in_specs=[pl.BlockSpec(memory_space=pl.ANY)] * len(operands),
            out_specs=[pl.BlockSpec(memory_space=pl.ANY)] * 3,
            scratch_shapes=[
                pltpu.VMEM(query.shape, jnp.bfloat16),
                pltpu.VMEM(query.shape, jnp.bfloat16),
                pltpu.VMEM(term.shape, jnp.float32),
                pltpu.VMEM(own.shape, jnp.bfloat16),
                pltpu.VMEM(other.shape, jnp.bfloat16),
                pltpu.VMEM(query.shape, jnp.float32),
                pltpu.VMEM(own.shape, jnp.float32),
                pltpu.VMEM(other.shape, jnp.float32),
                pltpu.VMEM(own.shape, jnp.bfloat16),
                pltpu.VMEM(other.shape, jnp.bfloat16),
                pltpu.SemaphoreType.DMA((9,)),
            ],
        ),
        compiler_params=pltpu.CompilerParams(vmem_limit_bytes=VMEM_BYTES),
        cost_estimate=pl.CostEstimate(
            flops=60 * 10 * rows * rows * HEAD_SIZE,
            bytes_accessed=24 * 1024 * 1024,
            transcendentals=60 * 2 * rows * rows,
        ),
    )(lists, *operands)


def body(inputs, cotangent, block_ids, positions, attn_in, attn_out, mlp_in, mlp_out, gains):
    token_rows, width = inputs.shape
    block = token_rows // 2
    devices = lax.axis_size(AXES)
    ctx_count, row_parts = lax.axis_size("ctx"), lax.axis_size("fsdp")
    planes = devices // PLANE
    blocks_per_seq = 2 * devices // SEQUENCE_COUNT
    span_blocks = LOOKBACK_SPAN // block
    score_scale = HEAD_SIZE ** (-0.5)
    me = lax.axis_index(AXES)
    place, plane = me % PLANE, me // PLANE
    part = place % row_parts
    row_share = attn_in.shape[0]
    unit = mlp_out.shape[1] // PLANE
    chunk = attn_in.shape[1] // row_parts
    order = NEAR + FAR

    gain_parts = ordered([gains.T] + [swap(gains.T, mask) for mask in range(1, row_parts)], part)
    scales = wide(gain_parts.transpose(1, 0, 2).reshape(gains.shape[1], width))
    source = wide(inputs)
    inverse_in = inverse_rms(source)
    lowered_in = narrow(source * inverse_in * scales[0])

    gathered_out = lax.all_gather(attn_out, AXES, axis=0)
    in_pieces = mlp_in.T.reshape(2, PLANE, unit, row_share).transpose(1, 0, 2, 3)
    in_received = exchange_members(in_pieces, place)
    attn_pieces = exchange_members(attn_in.T.reshape(row_parts, chunk, row_share), part)
    in_chunk = ordered(attn_pieces, part).transpose(1, 0, 2).reshape(chunk, width)
    stored = [in_chunk]
    for step in range(1, planes):
        stored.append(shift(stored[-1]))
    *in_received, in_chunk = together(*in_received, stored[1])
    in_share = (
        ordered(in_received, place)
        .reshape(2, row_parts, 2, unit, row_share)
        .transpose(0, 2, 3, 1, 4)
        .reshape(4 * unit, width)
    )
    lowered_in = after(lowered_in, in_chunk, gathered_out)
    block_ids = after(block_ids, in_chunk)

    def ids_of(which_plane, slots):
        masks = jnp.asarray([mask for mask, _ in slots], jnp.int32)
        sides = jnp.asarray([half for _, half in slots], jnp.int32)
        at = 2 * (which_plane[:, None] * PLANE + (place ^ masks)[None, :]) + sides[None, :]
        slot = jnp.arange(block_ids.shape[0], dtype=jnp.int32)
        return jnp.sum(jnp.where(at[:, :, None] == slot, block_ids, 0), axis=2)

    stage_planes = (plane + planes - jnp.arange(planes, dtype=jnp.int32)) % planes
    stage_ids = ids_of(stage_planes, order)
    query_ids = stage_ids[0]
    lists = pair_lists(
        query_ids, stage_ids.reshape(2 * planes, len(NEAR)), blocks_per_seq, span_blocks
    ).reshape(planes, 2, -1)
    half_width = HEAD_SIZE // 2
    frequency = ROPE_BASE ** (-2.0 * jnp.arange(half_width, dtype=jnp.float32) / HEAD_SIZE)
    base_angle = wide(query_ids % blocks_per_seq * block)[:, None, None] * frequency
    step_angle = jnp.arange(block, dtype=jnp.float32)[:, None] * frequency
    base_cosine, base_sine = jnp.cos(base_angle), jnp.sin(base_angle)
    step_cosine, step_sine = jnp.cos(step_angle), jnp.sin(step_angle)
    cosine = base_cosine * step_cosine - base_sine * step_sine
    sine = base_sine * step_cosine + base_cosine * step_sine

    in_share, lists, cosine, sine = together(in_share, lists, cosine, sine, stored[-1])[:4]
    stored = jnp.stack([pick(jnp.stack(stored), (plane - p) % planes) for p in range(planes)])
    cut = 2 * unit
    in_halves = [[in_share[:cut]], [in_share[cut:]]]
    out_shares = []
    in_all = jnp.zeros((planes * 4 * unit, width), jnp.bfloat16)
    out_all = jnp.zeros((planes * 2 * unit, width), jnp.bfloat16)

    def next_in(which):
        def start(token):
            in_halves[which].append(shift(after(in_halves[which][-1], token)))
            return (in_halves[which][-1],)

        return start

    def next_out(token):
        out_shares.append(shift(after(out_shares[-1], token)))
        return (out_shares[-1],)

    query_planes, kv_planes = planes // 2, planes // 4
    query_rounds = matchings(chunk_edges(query_planes, attn_in.shape[1], chunk, 1))
    kv_rounds = matchings(
        chunk_edges(kv_planes, attn_in.shape[1], chunk, QUERY_HEADS // KEY_VALUE_HEADS)
    )
    query_chunks = chunks_to_heads(stored[:query_planes], query_rounds, place)
    kv_chunks = chunks_to_heads(
        jnp.concatenate(
            [stored[query_planes : query_planes + kv_planes], stored[query_planes + kv_planes :]],
            axis=1,
        ),
        kv_rounds,
        place,
    )
    attn_weight = jnp.concatenate(
        query_chunks + [both[:chunk] for both in kv_chunks] + [both[chunk:] for both in kv_chunks]
    )

    key_values = []

    def heads_of(group, index):
        rows = dot(group, attn_weight, 1, 1)
        turns = []
        for table in (cosine, sine):
            near, far = table[2 * index : 2 * index + 2], table[8 + 2 * index : 10 + 2 * index]
            turns.append(jnp.concatenate([near, far]).reshape(2 * token_rows, half_width))
        query = narrow(rotate(rows[:, :HEAD_SIZE], *turns))
        key = narrow(rotate(rows[:, HEAD_SIZE : 2 * HEAD_SIZE], *turns))
        key_values.append(jnp.concatenate([key, narrow(rows[:, 2 * HEAD_SIZE :])], axis=1))
        return query

    in_groups, projected, extras = gather_plane(
        lowered_in, heads_of, (next_in(0), next_in(1), next_in(0))
    )

    def near_and_far(groups):
        near = jnp.concatenate([rows[:token_rows] for rows in groups])
        far = jnp.concatenate([rows[token_rows:] for rows in groups])
        return [rows.reshape(len(NEAR), block, rows.shape[1]) for rows in (near, far)]

    own_kv, other_kv = near_and_far(key_values)
    query = jnp.concatenate(near_and_far(projected))

    out_pieces = after(mlp_out.T, own_kv).reshape(PLANE, unit, row_share)
    out_shares.append(
        ordered(exchange_members(out_pieces, place), place)
        .reshape(2, row_parts, unit, row_share)
        .transpose(0, 2, 1, 3)
        .reshape(2 * unit, width)
    )
    kv_stages = [(own_kv, other_kv)]
    state = None
    for step in range(planes):
        own_kv, other_kv = kv_stages[step]
        state_next = attend(lists[step], query, own_kv, other_kv, state)
        if step < planes - 1:
            moving = shift(own_kv)
            if step == 0:
                state_next, moving, out_shares[0] = together(state_next, moving, out_shares[0])
            else:
                state_next, moving = together(state_next, moving)
            kv_stages.append((moving, swap(moving, CORE)))
        else:
            state_next, _ = together(state_next, *next_in(1)(own_kv))
        state = state_next
    totals = jnp.sum(state[:, :, HEAD_SIZE:], axis=-1, keepdims=True)
    attended = state[:, :, :HEAD_SIZE] / totals
    attended_rows = narrow(attended)

    def member_rows(blocks, mask):
        return jnp.concatenate([blocks[order.index((mask, 0))], blocks[order.index((mask, 1))]])

    def blocks_of(received):
        return jnp.stack(
            [received[mask][half * block : (half + 1) * block] for mask, half in order]
        )

    next_in(0)(attended_rows)
    attended_heads = ordered(
        exchange([member_rows(attended_rows, mask) for mask in range(PLANE)]), place
    )
    attended_heads = after(attended_heads, in_halves[0][-1])
    gathered_out = (
        gathered_out.reshape((QUERY_HEADS, -1, row_parts) + attn_out.shape)
        .transpose(0, 2, 3, 1, 4)
        .reshape(QUERY_HEADS, row_parts, row_share, HEAD_SIZE)
    )

    next_in(1)(attended_heads)
    branch = out_product(attended_heads, gathered_out)
    inverse_branch = inverse_rms(branch)
    middle = source + branch * inverse_branch * scales[1]
    inverse_mid = inverse_rms(middle)
    lowered_mid = narrow(middle * inverse_mid * scales[2])
    lowered_mid = after(lowered_mid, in_halves[1][-1])
    hidden_width = planes * 2 * unit
    for which, shares in enumerate(in_halves):
        while len(shares) < planes:
            shares.append(shift(shares[-1]))
        for step, share in enumerate(shares):
            at = (plane - step) % planes * 4 * unit + which * cut
            in_all = lax.dynamic_update_slice_in_dim(in_all, share, at, 0)

    def gate_up_of(group, index):
        return narrow(dot(group, in_all, 1, 1))

    mid_groups, gate_ups, _ = gather_plane(lowered_mid, gate_up_of, (next_out,) * 3)
    while len(out_shares) < planes:
        out_shares.append(shift(out_shares[-1]))
    for step, share in enumerate(out_shares):
        at = (plane - step) % planes * 2 * unit
        out_all = lax.dynamic_update_slice_in_dim(out_all, share, at, 0)

    def activate(gate_up):
        gate = wide(gate_up[:, :hidden_width])
        up = wide(gate_up[:, hidden_width:])
        return jax.nn.gelu(gate, approximate=True) * up

    hiddens = [narrow(activate(gate_up)) for gate_up in gate_ups]

    def reduce_groups(groups, weight, *rest):
        def work(index, token):
            group = groups[index] if token is None else after(groups[index], token)
            partial = together(narrow(dot(group, weight, 1, 0)))[0]
            return partial[:token_rows], partial[token_rows:]

        return reduce_plane(work, *rest)

    down_branch, _ = reduce_groups(hiddens, out_all)
    inverse_down = inverse_rms(down_branch)
    result = middle + down_branch * inverse_down * scales[3]
    upstream = wide(cotangent)
    grad_down, grad_gain_post = norm_back(down_branch, inverse_down, scales[3], upstream)
    grad_down_low = narrow(grad_down)

    def activate_back(gate_up, grad_hidden):
        gate = wide(gate_up[:, :hidden_width])
        up = wide(gate_up[:, hidden_width:])
        _, back = jax.vjp(lambda g, u: jax.nn.gelu(g, approximate=True) * u, gate, up)
        grad_gate, grad_up = back(grad_hidden)
        return narrow(jnp.concatenate([grad_gate, grad_up], axis=1))

    def grad_gate_up_of(group, index):
        return activate_back(gate_ups[index], dot(group, out_all, 1, 1))

    down_groups, grad_gate_ups, _ = gather_plane(grad_down_low, grad_gate_up_of)

    tile = 768 if width % 768 == 0 else width
    rings = {}

    def in_grads(token):
        grads = row_product(
            [after(grad_gate_ups[0], token)] + grad_gate_ups[1:], mid_groups, tile, tile
        )
        parts = grads.reshape(planes, 4 * unit, width)
        rings["low"] = RingSum(parts, plane, 0, cut)
        rings["high"] = RingSum(parts, plane, cut, cut)
        return (grads,)

    def first_low(token):
        rings["low"].start(token)
        return (rings["low"].finish(),)

    def first_high(token):
        rings["high"].start(token)
        return (rings["high"].finish(),)

    grad_lowered_mid, _ = reduce_groups(
        grad_gate_ups, in_all, (in_grads, first_low, first_high)
    )
    low_ring, high_ring = rings["low"], rings["high"]

    low_ring.start(grad_lowered_mid)
    grad_through_mid, grad_gain_pre_mlp = norm_back(
        middle, inverse_mid, scales[2], grad_lowered_mid
    )
    grad_middle = upstream + grad_through_mid
    grad_branch, grad_gain_post_attn = norm_back(branch, inverse_branch, scales[1], grad_middle)
    grad_branch_low = narrow(grad_branch)
    grad_heads = out_back_product(grad_branch_low, gathered_out)
    grad_heads = after(grad_heads, low_ring.finish())
    high_ring.start(grad_heads)
    grad_rows = wide(blocks_of(exchange_members(grad_heads, place)))
    row_terms = -jnp.sum(grad_rows * attended, axis=-1) / totals[..., 0]
    grad_summed = narrow(grad_rows / totals)
    grad_summed = after(grad_summed, high_ring.finish())
    row_terms = row_terms[:, None, :]

    grad_query, kv_total = None, None
    for step in range(planes):
        stage = (step + 1) % planes
        own_kv, other_kv = kv_stages[stage]
        beside = []
        if step == 0:
            low_ring.start(grad_summed)
            out_parts = out_grad_product(after(grad_branch_low, grad_summed), attended_heads)
            beside = [low_ring.finish(), out_parts]
        else:
            beside = [shift(kv_total)]
            grad_query = after(grad_query, kv_total)
        if step == 1:
            high_ring.start(kv_total)
            beside.append(high_ring.finish())
            grads = row_product([after(hiddens[0], kv_total)] + hiddens[1:], down_groups, 384, tile)
            beside.append(grads)
        if step == 2:
            in_sum = jnp.concatenate([low_ring.finish_all(), high_ring.finish_all()])
            in_pieces = after(in_sum, kv_total).reshape(2, 2, unit, row_parts, row_share)
            in_pieces = in_pieces.transpose(0, 3, 1, 2, 4).reshape(PLANE, 2, unit, row_share)
            in_pieces = exchange_members(in_pieces, place)
        if step == planes - 1:
            beside.append(out_reduced)
            beside.extend(in_pieces)
        grad_query, own_grad, other_grad, *beside = together(
            *attend_back(
                lists[stage], query, grad_summed, row_terms, own_kv, other_kv, grad_query
            ),
            *beside,
        )
        total = wide(own_grad) + wide(swap(other_grad, CORE))
        if step:
            total = total + wide(beside[0])
        kv_total = narrow(total)
        if step == 1:
            out_ring = RingSum(beside[2].reshape(planes, 2 * unit, width), plane)
        if step == 0:
            out_parts = (
                beside[1].reshape(QUERY_HEADS, width, -1, attn_out.shape[1])
                .transpose(0, 2, 1, 3)
                .reshape(devices * row_share, attn_out.shape[1])
            )
            out_reduced = lax.psum_scatter(out_parts, AXES, scatter_dimension=0, tiled=True)
    grad_attn_out = wide(beside[1])
    in_received = beside[2:]

    turned_query = narrow(rotate(grad_query * score_scale, cosine, -sine))
    kv_grad = wide(kv_total)
    turned_key = narrow(
        rotate(
            kv_grad[:, :, :HEAD_SIZE] * score_scale, cosine[: len(NEAR)], -sine[: len(NEAR)]
        )
    )
    near_grads = jnp.concatenate(
        [turned_query[: len(NEAR)], turned_key, kv_total[:, :, HEAD_SIZE:]], axis=-1
    ).reshape(4, token_rows, 3 * HEAD_SIZE)
    far_grads = turned_query[len(NEAR) :].reshape(4, token_rows, HEAD_SIZE)
    query_groups = jnp.concatenate([near_grads[:, :, :HEAD_SIZE], far_grads], axis=1)
    query_weight = attn_weight[:HEAD_SIZE]

    out_ring.start(kv_total)

    def weight_grads(token):
        out_ring.finish()
        out_ring.start(token)
        query_lefts = [after(query_groups[0], token)] + [query_groups[i] for i in range(1, 4)]
        grad_query_weight = row_product(query_lefts, in_groups, HEAD_SIZE, tile)
        grad_kv_weight = row_product(
            [after(near_grads[i, :, HEAD_SIZE:], token) for i in range(4)],
            in_groups,
            2 * HEAD_SIZE,
            tile,
        )
        return (grad_query_weight, grad_kv_weight, out_ring.finish())

    def weight_chunks(extras):
        grad_query_weight, grad_kv_weight, out_sum = extras[0]
        query_stored = heads_to_chunks(
            grad_query_weight.reshape(HEAD_SIZE // chunk, chunk, width),
            query_rounds,
            place,
            query_planes,
        )
        kv_stored = heads_to_chunks(
            jnp.concatenate(
                [
                    grad_kv_weight[:HEAD_SIZE].reshape(HEAD_SIZE // chunk, chunk, width),
                    grad_kv_weight[HEAD_SIZE:].reshape(HEAD_SIZE // chunk, chunk, width),
                ],
                axis=1,
            ),
            kv_rounds,
            place,
            kv_planes,
        )
        out_ring.total = out_sum
        out_ring.start()
        stored = jnp.concatenate([query_stored, kv_stored[:, :chunk], kv_stored[:, chunk:]])
        return (stored, out_ring.finish())

    attn_rings = []

    def attn_hop(token):
        if not attn_rings:
            attn_rings.append(RingSum(extras_of[0][1][0], plane))
        attn_rings[0].start(token)
        return (attn_rings[0].finish(),)

    def hop_and_pieces(token):
        pieces = wide(ordered([after(rows, token) for rows in in_received], place))
        grads = pieces.transpose(3, 1, 0, 2).reshape(mlp_in.shape)
        return attn_hop(token) + (grads,)

    def project_back(index, token):
        near, far = near_grads[index], far_grads[index]
        if token is not None:
            near = after(near, token)
        return together(
            narrow(dot(near, attn_weight, 1, 0)), narrow(dot(far, query_weight, 1, 0))
        )

    extras_of = []

    def keep_chunks(extras):
        extras_of.append(extras)
        return weight_chunks(extras)

    grad_lowered_in, extras = reduce_plane(
        project_back, (weight_grads, hop_and_pieces, attn_hop), keep_chunks
    )
    attn_sum = attn_rings[0].finish_all()
    pieces = out_ring.finish_all().reshape(2, unit, row_parts, row_share)
    pieces = pieces.transpose(0, 2, 1, 3).reshape(PLANE, unit, row_share)
    out_received = exchange_members(pieces, place)
    pieces = attn_sum.reshape(chunk, row_parts, row_share).transpose(1, 0, 2)
    attn_received = exchange_members(pieces, part)
    grad_source, grad_gain_in = norm_back(source, inverse_in, scales[0], grad_lowered_in)
    grad_input = grad_middle + grad_source

    grad_mlp_in = extras[2][1]
    attn_pieces = ordered(attn_received, part)
    grad_attn_in = wide(attn_pieces.reshape(attn_in.shape[1], row_share).T)
    out_pieces = wide(ordered(out_received, place))
    grad_mlp_out = out_pieces.transpose(2, 0, 1).reshape(mlp_out.shape)
    gain_total = sum_devices(
        jnp.stack([grad_gain_in, grad_gain_post_attn, grad_gain_pre_mlp, grad_gain_post])
    )
    grad_gains = pick(
        gain_total.reshape(gains.shape[1], row_parts, row_share).transpose(1, 2, 0), part
    )
    return (
        narrow(result),
        grad_input,
        grad_attn_in,
        grad_attn_out,
        grad_mlp_in,
        grad_mlp_out,
        grad_gains,
    )


def solution(mesh):
    placed = (
        P(("ctx", "fsdp"), None),
        P(("ctx", "fsdp"), None),
        P(),
        P(("ctx", "fsdp")),
        P("fsdp", "ctx"),
        P("fsdp", "ctx"),
        P("fsdp", "ctx"),
        P("fsdp", "ctx"),
        P("fsdp", None),
    )
    return jax.shard_map(
        body,
        mesh=mesh,
        in_specs=placed,
        out_specs=(
            P(("ctx", "fsdp"), None),
            P(("ctx", "fsdp"), None),
            P("fsdp", "ctx"),
            P("fsdp", "ctx"),
            P("fsdp", "ctx"),
            P("fsdp", "ctx"),
            P("fsdp", None),
        ),
        check_vma=False,
    )
```

```python
import functools
import math

import jax
import jax.numpy as jnp
from jax import lax
from jax.experimental import pallas as pl
from jax.experimental.pallas import tpu as pltpu
from jax.sharding import PartitionSpec as P

QUERY_HEADS = 8
KEY_VALUE_HEADS = 4
HEAD_SIZE = 256
LOOKBACK_SPAN = 4096
SEQUENCE_COUNT = 2


EPSILON = 1e-06
SOFT_CAP = 50.0
ROPE_BASE = 10000.0
AXES = ("ctx", "fsdp")
PLANE = 8
CORE, SIDE, ACROSS = 1, 2, 4
TANH_SCALE = HEAD_SIZE ** (-0.5) / SOFT_CAP
EXP2_SCALE = SOFT_CAP * math.log2(math.e)
VMEM_BYTES = 56 * 1024 * 1024


def inverse_rms(values):
    return lax.rsqrt(jnp.mean(values * values, axis=-1, keepdims=True) + EPSILON)


def norm_back(values, inverse, scale, upstream):
    scaled = upstream * scale
    through = inverse * scaled - values * inverse**3 * jnp.mean(
        scaled * values, axis=-1, keepdims=True
    )
    return (through, jnp.sum(upstream * values * inverse, axis=0))


def rotate(values, cosine, sine):
    half_width = values.shape[-1] // 2
    first_half = values[..., :half_width]
    second_half = values[..., half_width:]
    return jnp.concatenate(
        [
            first_half * cosine - second_half * sine,
            second_half * cosine + first_half * sine,
        ],
        axis=-1,
    )


def dot(left, right, left_axis, right_axis):
    return lax.dot_general(
        left,
        right,
        (((left_axis,), (right_axis,)), ((), ())),
        preferred_element_type=jnp.float32,
    )


def after(value, *others):
    return lax.optimization_barrier((value,) + others)[0]


def wide(values):
    return values.astype(jnp.float32)


def narrow(values):
    return values.astype(jnp.bfloat16)


def swap(values, mask):
    count = lax.axis_size(AXES)
    return lax.ppermute(values, AXES, [(i, i ^ mask) for i in range(count)])


def shift(values, steps=1):
    count = lax.axis_size(AXES)
    return lax.ppermute(values, AXES, [(i, (i + steps * PLANE) % count) for i in range(count)])


def route(values, targets):
    count = lax.axis_size(AXES)
    return lax.ppermute(
        values, AXES, [(i, i - i % PLANE + targets[i % PLANE]) for i in range(count)]
    )


def pick(stacked, index, axis=0):
    return lax.dynamic_index_in_dim(stacked, index, axis, keepdims=False)


def look_up(table, place):
    return pick(jnp.asarray(table, jnp.int32), place)


def exchange(pieces):
    far = swap(jnp.stack([pieces[mask ^ CORE] for mask in range(0, len(pieces), 2)]), CORE)
    received = []
    for i, mask in enumerate(range(0, len(pieces), 2)):
        both = jnp.stack([pieces[mask], far[i]])
        if mask:
            both = swap(both, mask)
        received.extend([both[0], both[1]])
    return received


def exchange_members(stacked, place):
    return exchange([pick(stacked, place ^ mask) for mask in range(stacked.shape[0])])


def ordered(received, place):
    whole = jnp.zeros((len(received),) + received[0].shape, received[0].dtype)
    for mask, rows in enumerate(received):
        whole = lax.dynamic_update_index_in_dim(whole, rows, place ^ mask, 0)
    return whole


NEAR = [(0, 0), (0, 1), (4, 0), (2, 1), (2, 0), (4, 1), (6, 0), (6, 1)]
FAR = [(mask ^ CORE, half) for mask, half in NEAR]


def together(*values):
    return lax.optimization_barrier(values)


def no_transfers(token, extras=None):
    return ()


def gather_plane(rows, work, beside=(no_transfers,) * 3, late=False):
    half = rows.shape[0] // 2
    low, high = rows[:half], rows[half:]
    groups, done, extras = [], [], []

    def add_group(near, far):
        groups.append(jnp.concatenate([near, far]))
        done.append(work(groups[-1], len(done)))

    other = swap(rows, CORE)
    first_low, first_high = swap(low, ACROSS), swap(high, SIDE)
    extra = beside[0](rows, extras)
    if late:
        first_low, first_high, *extra = together(first_low, first_high, *extra)
    else:
        add_group(rows, other)
        done[0], first_low, first_high, *extra = together(done[0], first_low, first_high, *extra)
    extras.append(extra)
    low, high = together(low, high, first_low)[:2]
    first_other = swap(jnp.concatenate([first_low, first_high]), CORE)
    second_low, second_high = swap(low, SIDE), swap(high, ACROSS)
    extra = beside[1](first_low, extras)
    if late:
        add_group(rows, other)
    add_group(jnp.concatenate([first_low, first_high]), first_other)
    done[1], first_low, first_high, second_low, second_high, *extra = together(
        done[1], first_low, first_high, second_low, second_high, *extra
    )
    extras.append(extra)
    second_other = swap(jnp.concatenate([second_low, second_high]), CORE)
    third_low, third_high = swap(first_low, SIDE), swap(first_high, ACROSS)
    extra = beside[2](second_low, extras)
    add_group(jnp.concatenate([second_low, second_high]), second_other)
    done[2], third_low, third_high, *extra = together(done[2], third_low, third_high, *extra)
    extras.append(extra)
    third = jnp.concatenate([third_low, third_high])
    add_group(third, swap(third, CORE))
    return groups, done, extras


def reduce_plane(work, beside=(no_transfers,) * 3, middle=None, kept=None):
    extras = []
    kept = {} if kept is None else kept

    def both(group, token):
        near, far = work(group, token)
        return wide(near) + wide(swap(far, CORE))

    third = narrow(both(3, None))
    half = third.shape[0] // 2
    got_low, got_high = swap(third[:half], SIDE), swap(third[half:], ACROSS)
    second = narrow(both(2, third))
    got_low, got_high, second, *extra = together(got_low, got_high, second, *beside[0](third))
    extras.append(extra)
    kept["down"] = extra[0] if extra else None
    if middle is not None:
        second, *extra = together(second, *middle(extras))
        extras.append(extra)
    own_low, own_high = swap(second[:half], SIDE), swap(second[half:], ACROSS)
    first = both(1, second)
    first = narrow(first + wide(jnp.concatenate([got_low, got_high])))
    own_low, own_high, first, *extra = together(own_low, own_high, first, *beside[1](second))
    extras.append(extra)
    kept["in"] = extra[0] if extra else None
    more_low, more_high = swap(first[:half], ACROSS), swap(first[half:], SIDE)
    own = both(0, first) + wide(jnp.concatenate([own_low, own_high]))
    more_low, more_high, own, *extra = together(more_low, more_high, own, *beside[2](first))
    extras.append(extra)
    return own + wide(jnp.concatenate([more_low, more_high])), extras


def sum_devices(values):
    for mask in (CORE, SIDE, ACROSS):
        values = values + swap(values, mask)
    total = values
    for steps in range(1, lax.axis_size(AXES) // PLANE):
        total = total + shift(values, steps)
    return total


class RingSum:
    def __init__(self, parts, plane, first=0, rows=None):
        self.parts, self.plane, self.planes = parts, plane, parts.shape[0]
        self.first, self.rows = first, rows or parts.shape[1]
        self.hops, self.moving = 0, None
        self.total = self.part(0)

    def part(self, step):
        at = (self.plane + 2 * self.planes - 1 - step) % self.planes
        size = (1, self.rows, self.parts.shape[2])
        return lax.dynamic_slice(self.parts, (at, self.first, 0), size)[0]

    def start(self, *others):
        if self.hops < self.planes - 1:
            self.moving = shift(after(self.total, *others) if others else self.total)

    def finish(self):
        if self.moving is not None:
            self.hops += 1
            self.total = narrow(wide(self.moving) + wide(self.part(self.hops)))
            self.moving = None
        return self.total

    def finish_all(self):
        self.finish()
        while self.hops < self.planes - 1:
            self.start()
            self.finish()
        return self.total


def matchings(edges):
    left, rounds = list(edges), []
    while left:
        owner = {}

        def settle(source, seen):
            for edge in left:
                if edge[0] == source and edge[1] not in seen:
                    seen.add(edge[1])
                    if edge[1] not in owner or settle(owner[edge[1]][0], seen):
                        owner[edge[1]] = edge
                        return True
            return False

        for source in range(PLANE):
            settle(source, set())
        found = sorted(owner.values())
        rounds.append(found)
        left = [edge for edge in left if edge not in found]
    return rounds


def chunk_edges(plane_count, columns, chunk, share):
    edges = []
    for source in range(PLANE):
        for at in range(plane_count):
            column = (2 * at + source // 4) * columns + source % 4 * chunk
            head = column // HEAD_SIZE
            for target in range(head * share, (head + 1) * share):
                edges.append((source, target, at, column % HEAD_SIZE // chunk))
    return edges


def chunks_to_heads(stored, rounds, place):
    spots = len(rounds)
    got = []
    for found in rounds:
        sent = pick(stored, look_up([edge[2] for edge in found], place))
        got.append(route(sent, [edge[1] for edge in found]))
    stacked = jnp.stack(got)
    order = []
    for spot in range(spots):
        table = [0] * PLANE
        for step, found in enumerate(rounds):
            for edge in found:
                if edge[3] == spot:
                    table[edge[1]] = step
        order.append(pick(stacked, look_up(table, place)))
    return order


def heads_to_chunks(heads, rounds, place, plane_count):
    got = []
    for found in rounds:
        back, spot = [0] * PLANE, [0] * PLANE
        for source, target, _, position in found:
            back[target], spot[target] = source, position
        got.append(route(pick(heads, look_up(spot, place)), back))
    stacked = jnp.stack(got)
    chunks = []
    for at in range(plane_count):
        tables = []
        for source in range(PLANE):
            tables.append(
                [
                    step
                    for step, found in enumerate(rounds)
                    for edge in found
                    if edge[0] == source and edge[2] == at
                ]
            )
        terms = [
            pick(stacked, look_up([table[i] for table in tables], place))
            for i in range(len(tables[0]))
        ]
        total = terms[0]
        if len(terms) > 1:
            total = narrow(sum(wide(term) for term in terms))
        chunks.append(total)
    return jnp.stack(chunks)


def row_product_kernel(count, *refs):
    out, total = refs[-2:]
    total[...] = dot(refs[0][...], refs[count][...], 0, 0)
    for i in range(1, count):
        total[...] += dot(refs[i][...], refs[count + i][...], 0, 0)
    out[...] = total[...].astype(out.dtype)


def row_product(lefts, rights, left_tile, right_tile):
    count = len(lefts)
    height, width = lefts[0].shape[1], rights[0].shape[1]
    depths = [left.shape[0] for left in lefts]
    return pl.pallas_call(
        functools.partial(row_product_kernel, count),
        out_shape=jax.ShapeDtypeStruct((height, width), jnp.bfloat16),
        grid=(height // left_tile, width // right_tile),
        in_specs=[pl.BlockSpec((depth, left_tile), lambda i, j: (0, i)) for depth in depths]
        + [pl.BlockSpec((depth, right_tile), lambda i, j: (0, j)) for depth in depths],
        out_specs=pl.BlockSpec((left_tile, right_tile), lambda i, j: (i, j)),
        scratch_shapes=[pltpu.VMEM((left_tile, right_tile), jnp.float32)],
        compiler_params=pltpu.CompilerParams(vmem_limit_bytes=VMEM_BYTES),
        cost_estimate=pl.CostEstimate(
            flops=2 * sum(depths) * height * width,
            bytes_accessed=2 * sum(depths) * (height + width) + 2 * height * width,
            transcendentals=0,
        ),
    )(*lefts, *rights)


def out_kernel(part, rows_ref, weight_ref, out_ref):
    at = pl.program_id(0)
    total = dot(rows_ref[0], weight_ref[0, 0], 1, 1)
    for head in range(1, rows_ref.shape[0]):
        total += dot(rows_ref[head], weight_ref[head, 0], 1, 1)
    for i in range(out_ref.shape[1] // part):

        @pl.when(at == i)
        def _():
            out_ref[:, i * part : (i + 1) * part] = total


def out_product(rows, weight):
    heads, count, size = rows.shape
    _, parts, part, _ = weight.shape
    return pl.pallas_call(
        functools.partial(out_kernel, part),
        out_shape=jax.ShapeDtypeStruct((count, parts * part), jnp.float32),
        grid=(parts,),
        in_specs=[
            pl.BlockSpec((heads, count, size), lambda i: (0, 0, 0)),
            pl.BlockSpec((heads, 1, part, size), lambda i: (0, i, 0, 0)),
        ],
        out_specs=pl.BlockSpec((count, parts * part), lambda i: (0, 0)),
        compiler_params=pltpu.CompilerParams(vmem_limit_bytes=VMEM_BYTES),
        cost_estimate=pl.CostEstimate(
            flops=2 * count * heads * size * parts * part,
            bytes_accessed=2 * heads * size * (count + parts * part) + 4 * count * parts * part,
            transcendentals=0,
        ),
    )(rows, weight)


def out_back_kernel(rows_ref, weight_ref, out_ref):
    part = weight_ref.shape[2]
    total = dot(rows_ref[:, :part], weight_ref[0, 0], 1, 0)
    for i in range(1, weight_ref.shape[1]):
        total += dot(rows_ref[:, i * part : (i + 1) * part], weight_ref[0, i], 1, 0)
    out_ref[0] = total.astype(out_ref.dtype)


def out_back_product(rows, weight):
    count, width = rows.shape
    heads, parts, part, size = weight.shape
    return pl.pallas_call(
        out_back_kernel,
        out_shape=jax.ShapeDtypeStruct((heads, count, size), jnp.bfloat16),
        grid=(heads,),
        in_specs=[
            pl.BlockSpec((count, width), lambda i: (0, 0)),
            pl.BlockSpec((1, parts, part, size), lambda i: (i, 0, 0, 0)),
        ],
        out_specs=pl.BlockSpec((1, count, size), lambda i: (i, 0, 0)),
        compiler_params=pltpu.CompilerParams(vmem_limit_bytes=VMEM_BYTES),
        cost_estimate=pl.CostEstimate(
            flops=2 * count * heads * size * width,
            bytes_accessed=2 * heads * size * (count + width) + 2 * count * width,
            transcendentals=0,
        ),
    )(rows, weight)


def out_grad_kernel(rows_ref, heads_ref, out_ref):
    total = dot(rows_ref[...], heads_ref[0], 0, 0).astype(out_ref.dtype)
    part = out_ref.shape[3]
    for side in range(2):
        for core in range(2):
            at = (2 * side + core) * part
            out_ref[core, side, 0] = total[at : at + part]


def out_grad_product(rows, by_head):
    count, width = rows.shape
    heads, _, size = by_head.shape
    part = width // 4
    return pl.pallas_call(
        out_grad_kernel,
        out_shape=jax.ShapeDtypeStruct((2, 2, heads, part, size), jnp.bfloat16),
        grid=(heads,),
        in_specs=[
            pl.BlockSpec((count, width), lambda i: (0, 0)),
            pl.BlockSpec((1, count, size), lambda i: (i, 0, 0)),
        ],
        out_specs=pl.BlockSpec((2, 2, 1, part, size), lambda i: (0, 0, i, 0, 0)),
        compiler_params=pltpu.CompilerParams(vmem_limit_bytes=VMEM_BYTES),
        cost_estimate=pl.CostEstimate(
            flops=2 * count * heads * size * width,
            bytes_accessed=2 * heads * size * (count + width) + 2 * count * width,
            transcendentals=0,
        ),
    )(rows, by_head)


def pair_lists(query_ids, key_ids, blocks_per_seq, span_blocks):
    query_seq, query_at = query_ids // blocks_per_seq, query_ids % blocks_per_seq
    key_seq, key_at = key_ids // blocks_per_seq, key_ids % blocks_per_seq
    rows = key_ids.shape[0]
    distance = (query_at[None, :, None] - key_at[:, None, :]).reshape(rows, -1)
    same = (query_seq[None, :, None] == key_seq[:, None, :]).reshape(rows, -1)
    whole = same & (distance > 0) & (distance < span_blocks)
    edged = same & ((distance == 0) | (distance == span_blocks))
    kind = whole.astype(jnp.int32) + 2 * edged.astype(jnp.int32)
    total = distance.shape[1]
    index = jnp.arange(total, dtype=jnp.int32)
    earlier = (index[None, :] < index[:, None])[None] & (kind[:, None, :] == kind[:, :, None])
    rank = jnp.sum(earlier.astype(jnp.int32), axis=2)
    count_whole = jnp.sum(whole.astype(jnp.int32), axis=1, keepdims=True)
    count_edged = jnp.sum(edged.astype(jnp.int32), axis=1, keepdims=True)
    spot = jnp.where(kind == 1, rank, jnp.where(kind == 2, count_whole + rank, -1))
    code = index * 2 + (distance == span_blocks).astype(jnp.int32)
    hit = spot[:, :, None] == index[None, None, :]
    entries = jnp.sum(jnp.where(hit, code[:, :, None], 0), axis=1)
    return jnp.concatenate([count_whole, count_edged, entries], axis=1).astype(jnp.int32)


def run_pairs(list_ref, row, key_count, unroll, visit):
    whole = list_ref[row, 0]
    edged = list_ref[row, 1]

    def decode(position):
        code = list_ref[row, 2 + position]
        pair = code // 2
        return pair // key_count, pair % key_count, code % 2

    def several(step, carry):
        found = [decode(step * unroll + i) for i in range(unroll)]
        visit([f[0] for f in found], [f[1] for f in found], None)
        return carry

    def single(position, carry):
        i, j, _ = decode(position)
        visit([i], [j], None)
        return carry

    def masked(position, carry):
        i, j, far = decode(position)
        visit([i], [j], far)
        return carry

    groups = whole // unroll
    lax.fori_loop(0, groups, several, 0)
    lax.fori_loop(groups * unroll, whole, single, 0)
    lax.fori_loop(whole, whole + edged, masked, 0)


def attend_kernel(first, unroll, list_ref, query_hbm, own_hbm, other_hbm, *rest):
    if first:
        state_hbm = None
        out_hbm, query, own, other, state, sems = rest
    else:
        state_hbm, out_hbm, query, own, other, state, sems = rest
    copies = [
        pltpu.make_async_copy(query_hbm, query, sems.at[0]),
        pltpu.make_async_copy(own_hbm, own, sems.at[1]),
        pltpu.make_async_copy(other_hbm, other, sems.at[2]),
    ]
    if not first:
        copies.append(pltpu.make_async_copy(state_hbm, state, sems.at[3]))
    for copy in copies:
        copy.start()
    if first:
        state[...] = jnp.zeros_like(state)
    for copy in copies:
        copy.wait()
    rows = query.shape[1]
    lane = lax.broadcasted_iota(jnp.int32, (rows, 128), 1)

    def visit_in(keys):
        def visit(query_at, key_at, far):
            scores = [
                dot(query[i], keys[j, :, :HEAD_SIZE], 1, 1) for i, j in zip(query_at, key_at)
            ]
            for i, j, score in zip(query_at, key_at, scores):
                weights = jnp.exp2(EXP2_SCALE * jnp.tanh(score * TANH_SCALE))
                if far is not None:
                    spacing = (
                        lax.broadcasted_iota(jnp.int32, weights.shape, 0)
                        - lax.broadcasted_iota(jnp.int32, weights.shape, 1)
                        + far * LOOKBACK_SPAN
                    )
                    live = (spacing >= 0) & (spacing < LOOKBACK_SPAN)
                    weights = jnp.where(live, weights, 0.0)
                if rows % 128 == 0:
                    part = weights[:, :128]
                    for k in range(1, rows // 128):
                        part = part + weights[:, k * 128 : (k + 1) * 128]
                else:
                    part = jnp.where(lane == 0, jnp.sum(weights, axis=1, keepdims=True), 0.0)
                state[i, :, HEAD_SIZE:] += part
                state[i, :, :HEAD_SIZE] += dot(
                    weights.astype(jnp.bfloat16), keys[j, :, HEAD_SIZE:], 1, 0
                )

        return visit

    key_count = own.shape[0]
    run_pairs(list_ref, 0, key_count, unroll, visit_in(own))
    run_pairs(list_ref, 1, key_count, unroll, visit_in(other))
    out = pltpu.make_async_copy(state, out_hbm, sems.at[4])
    out.start()
    out.wait()


def attend(lists, query, own, other, state):
    first = state is None
    blocks, rows, _ = query.shape
    shape = (blocks, rows, HEAD_SIZE + 128)
    operands = (query, own, other) if first else (query, own, other, state)
    return pl.pallas_call(
        functools.partial(attend_kernel, first, 4),
        out_shape=jax.ShapeDtypeStruct(shape, jnp.float32),
        grid_spec=pltpu.PrefetchScalarGridSpec(
            num_scalar_prefetch=1,
            grid=(1,),
            in_specs=[pl.BlockSpec(memory_space=pl.ANY)] * len(operands),
            out_specs=pl.BlockSpec(memory_space=pl.ANY),
            scratch_shapes=[
                pltpu.VMEM(query.shape, jnp.bfloat16),
                pltpu.VMEM(own.shape, jnp.bfloat16),
                pltpu.VMEM(other.shape, jnp.bfloat16),
                pltpu.VMEM(shape, jnp.float32),
                pltpu.SemaphoreType.DMA((5,)),
            ],
        ),
        compiler_params=pltpu.CompilerParams(vmem_limit_bytes=VMEM_BYTES),
        cost_estimate=pl.CostEstimate(
            flops=60 * 4 * rows * rows * HEAD_SIZE,
            bytes_accessed=14 * 1024 * 1024,
            transcendentals=60 * 2 * rows * rows,
        ),
    )(lists, *operands)


def attend_back_kernel(
    first,
    unroll,
    list_ref,
    query_hbm,
    grad_hbm,
    term_hbm,
    own_hbm,
    other_hbm,
    *rest,
):
    if first:
        state_hbm = None
    else:
        state_hbm, *rest = rest
    (
        out_hbm,
        own_out_hbm,
        other_out_hbm,
        query,
        grad,
        term,
        own,
        other,
        state,
        own_grad,
        other_grad,
        own_low,
        other_low,
        sems,
    ) = rest
    copies = [
        pltpu.make_async_copy(query_hbm, query, sems.at[0]),
        pltpu.make_async_copy(grad_hbm, grad, sems.at[1]),
        pltpu.make_async_copy(term_hbm, term, sems.at[2]),
        pltpu.make_async_copy(own_hbm, own, sems.at[3]),
        pltpu.make_async_copy(other_hbm, other, sems.at[4]),
    ]
    if not first:
        copies.append(pltpu.make_async_copy(state_hbm, state, sems.at[5]))
    for copy in copies:
        copy.start()
    if first:
        state[...] = jnp.zeros_like(state)
    own_grad[...] = jnp.zeros_like(own_grad)
    other_grad[...] = jnp.zeros_like(other_grad)
    for copy in copies:
        copy.wait()

    def visit_in(keys, key_grad):
        def visit(query_at, key_at, far):
            scores = []
            slopes = []
            for i, j in zip(query_at, key_at):
                scores.append(dot(keys[j, :, :HEAD_SIZE], query[i], 1, 1))
                slopes.append(dot(keys[j, :, HEAD_SIZE:], grad[i], 1, 1))
            for i, j, score, slope in zip(query_at, key_at, scores, slopes):
                bent = jnp.tanh(score * TANH_SCALE)
                weights = jnp.exp2(EXP2_SCALE * bent)
                if far is not None:
                    spacing = (
                        lax.broadcasted_iota(jnp.int32, weights.shape, 1)
                        - lax.broadcasted_iota(jnp.int32, weights.shape, 0)
                        + far * LOOKBACK_SPAN
                    )
                    live = (spacing >= 0) & (spacing < LOOKBACK_SPAN)
                    weights = jnp.where(live, weights, 0.0)
                grad_scores = (
                    (slope + term[i]) * (weights * (1.0 - bent * bent))
                ).astype(jnp.bfloat16)
                key_grad[j, :, :HEAD_SIZE] += dot(grad_scores, query[i], 1, 0)
                key_grad[j, :, HEAD_SIZE:] += dot(weights.astype(jnp.bfloat16), grad[i], 1, 0)
                state[i] += dot(grad_scores, keys[j, :, :HEAD_SIZE], 0, 0)

        return visit

    key_count = own.shape[0]
    run_pairs(list_ref, 1, key_count, unroll, visit_in(other, other_grad))
    other_low[...] = other_grad[...].astype(jnp.bfloat16)
    other_out = pltpu.make_async_copy(other_low, other_out_hbm, sems.at[6])
    other_out.start()
    run_pairs(list_ref, 0, key_count, unroll, visit_in(own, own_grad))
    own_low[...] = own_grad[...].astype(jnp.bfloat16)
    own_out = pltpu.make_async_copy(own_low, own_out_hbm, sems.at[7])
    own_out.start()
    out = pltpu.make_async_copy(state, out_hbm, sems.at[8])
    out.start()
    other_out.wait()
    own_out.wait()
    out.wait()


def attend_back(lists, query, grad, term, own, other, state):
    first = state is None
    blocks, rows, _ = query.shape
    operands = (query, grad, term, own, other)
    if not first:
        operands = operands + (state,)
    return pl.pallas_call(
        functools.partial(attend_back_kernel, first, 2),
        out_shape=[
            jax.ShapeDtypeStruct(query.shape, jnp.float32),
            jax.ShapeDtypeStruct(own.shape, jnp.bfloat16),
            jax.ShapeDtypeStruct(other.shape, jnp.bfloat16),
        ],
        grid_spec=pltpu.PrefetchScalarGridSpec(
            num_scalar_prefetch=1,
            grid=(1,),
            in_specs=[pl.BlockSpec(memory_space=pl.ANY)] * len(operands),
            out_specs=[pl.BlockSpec(memory_space=pl.ANY)] * 3,
            scratch_shapes=[
                pltpu.VMEM(query.shape, jnp.bfloat16),
                pltpu.VMEM(query.shape, jnp.bfloat16),
                pltpu.VMEM(term.shape, jnp.float32),
                pltpu.VMEM(own.shape, jnp.bfloat16),
                pltpu.VMEM(other.shape, jnp.bfloat16),
                pltpu.VMEM(query.shape, jnp.float32),
                pltpu.VMEM(own.shape, jnp.float32),
                pltpu.VMEM(other.shape, jnp.float32),
                pltpu.VMEM(own.shape, jnp.bfloat16),
                pltpu.VMEM(other.shape, jnp.bfloat16),
                pltpu.SemaphoreType.DMA((9,)),
            ],
        ),
        compiler_params=pltpu.CompilerParams(vmem_limit_bytes=VMEM_BYTES),
        cost_estimate=pl.CostEstimate(
            flops=60 * 10 * rows * rows * HEAD_SIZE,
            bytes_accessed=24 * 1024 * 1024,
            transcendentals=60 * 2 * rows * rows,
        ),
    )(lists, *operands)


def body(inputs, cotangent, block_ids, positions, attn_in, attn_out, mlp_in, mlp_out, gains):
    token_rows, width = inputs.shape
    block = token_rows // 2
    devices = lax.axis_size(AXES)
    ctx_count, row_parts = lax.axis_size("ctx"), lax.axis_size("fsdp")
    planes = devices // PLANE
    blocks_per_seq = 2 * devices // SEQUENCE_COUNT
    span_blocks = LOOKBACK_SPAN // block
    score_scale = HEAD_SIZE ** (-0.5)
    me = lax.axis_index(AXES)
    place, plane = me % PLANE, me // PLANE
    part = place % row_parts
    row_share = attn_in.shape[0]
    unit = mlp_out.shape[1] // PLANE
    chunk = attn_in.shape[1] // row_parts
    order = NEAR + FAR

    gain_parts = ordered([gains.T] + [swap(gains.T, mask) for mask in range(1, row_parts)], part)
    scales = wide(gain_parts.transpose(1, 0, 2).reshape(gains.shape[1], width))
    source = wide(inputs)
    inverse_in = inverse_rms(source)
    lowered_in = narrow(source * inverse_in * scales[0])

    gathered_out = lax.all_gather(attn_out, AXES, axis=0)
    in_pieces = mlp_in.T.reshape(2, PLANE, unit, row_share).transpose(1, 0, 2, 3)
    in_received = exchange_members(in_pieces, place)
    attn_pieces = exchange_members(attn_in.T.reshape(row_parts, chunk, row_share), part)
    in_chunk = ordered(attn_pieces, part).transpose(1, 0, 2).reshape(chunk, width)
    *in_received, first_stored = together(*in_received, shift(in_chunk))
    stored = [in_chunk, first_stored]
    for step in range(2, planes):
        stored.append(shift(stored[-1]))
    in_share = (
        ordered(in_received, place)
        .reshape(2, row_parts, 2, unit, row_share)
        .transpose(0, 2, 3, 1, 4)
        .reshape(4 * unit, width)
    )
    lowered_in = after(lowered_in, first_stored)
    block_ids = after(block_ids, in_chunk)

    def ids_of(which_plane, slots):
        masks = jnp.asarray([mask for mask, _ in slots], jnp.int32)
        sides = jnp.asarray([half for _, half in slots], jnp.int32)
        at = 2 * (which_plane[:, None] * PLANE + (place ^ masks)[None, :]) + sides[None, :]
        slot = jnp.arange(block_ids.shape[0], dtype=jnp.int32)
        return jnp.sum(jnp.where(at[:, :, None] == slot, block_ids, 0), axis=2)

    stage_planes = (plane + planes - jnp.arange(planes, dtype=jnp.int32)) % planes
    stage_ids = ids_of(stage_planes, order)
    query_ids = stage_ids[0]
    lists = pair_lists(
        query_ids, stage_ids.reshape(2 * planes, len(NEAR)), blocks_per_seq, span_blocks
    ).reshape(planes, 2, -1)
    half_width = HEAD_SIZE // 2
    frequency = ROPE_BASE ** (-2.0 * jnp.arange(half_width, dtype=jnp.float32) / HEAD_SIZE)
    base_angle = wide(query_ids % blocks_per_seq * block)[:, None, None] * frequency
    step_angle = jnp.arange(block, dtype=jnp.float32)[:, None] * frequency
    base_cosine, base_sine = jnp.cos(base_angle), jnp.sin(base_angle)
    step_cosine, step_sine = jnp.cos(step_angle), jnp.sin(step_angle)
    cosine = base_cosine * step_cosine - base_sine * step_sine
    sine = base_sine * step_cosine + base_cosine * step_sine

    cut = 2 * unit
    in_halves = [[], []]
    out_shares = []
    in_all = jnp.zeros((planes * 4 * unit, width), jnp.bfloat16)
    out_all = jnp.zeros((planes * 2 * unit, width), jnp.bfloat16)

    def next_in(which):
        def start(token, extras=None):
            in_halves[which].append(shift(after(in_halves[which][-1], token)))
            return (in_halves[which][-1],)

        return start

    def next_out(token, extras=None):
        out_shares.append(shift(after(out_shares[-1], token)))
        return (out_shares[-1],)

    query_planes, kv_planes = planes // 2, planes // 4
    query_rounds = matchings(chunk_edges(query_planes, attn_in.shape[1], chunk, 1))
    kv_rounds = matchings(
        chunk_edges(kv_planes, attn_in.shape[1], chunk, QUERY_HEADS // KEY_VALUE_HEADS)
    )

    def weights_together(token, extras):
        whole = jnp.zeros((planes, chunk, width), jnp.bfloat16)
        for step, rows in enumerate(stored):
            whole = lax.dynamic_update_index_in_dim(whole, rows, (plane - step) % planes, 0)
        return (whole, in_share)

    attn_weights = []

    def weights_to_heads(token, extras):
        whole, share = extras[0]
        in_halves[0].append(share[:cut])
        in_halves[1].append(share[cut:])
        query_chunks = chunks_to_heads(whole[:query_planes], query_rounds, place)
        kv_chunks = chunks_to_heads(
            jnp.concatenate(
                [whole[query_planes : query_planes + kv_planes], whole[query_planes + kv_planes :]],
                axis=1,
            ),
            kv_rounds,
            place,
        )
        attn_weights.append(
            jnp.concatenate(
                query_chunks
                + [both[:chunk] for both in kv_chunks]
                + [both[chunk:] for both in kv_chunks]
            )
        )
        return next_in(0)(token) + next_in(1)(token) + (gathered_out, lists, cosine, sine)

    in_groups, projected, extras = gather_plane(
        lowered_in,
        lambda group, index: dot(group, attn_weights[0], 1, 1),
        (weights_together, weights_to_heads, next_in(0)),
        late=True,
    )
    attn_weight = attn_weights[0]
    gathered_out, lists, cosine, sine = extras[1][2:]

    def split_groups(groups):
        near = jnp.concatenate([group[:token_rows] for group in groups])
        far = jnp.concatenate([group[token_rows:] for group in groups])
        return [rows.reshape(len(NEAR), block, rows.shape[1]) for rows in (near, far)]

    near_rows, far_rows = split_groups(projected)
    query_parts, kv_parts = [], []
    for rows, low, high in ((near_rows, 0, len(NEAR)), (far_rows, len(NEAR), 2 * len(NEAR))):
        turns = (cosine[low:high], sine[low:high])
        query_parts.append(narrow(rotate(rows[:, :, :HEAD_SIZE], *turns)))
        kv_parts.append(
            jnp.concatenate(
                [
                    narrow(rotate(rows[:, :, HEAD_SIZE : 2 * HEAD_SIZE], *turns)),
                    narrow(rows[:, :, 2 * HEAD_SIZE :]),
                ],
                axis=-1,
            )
        )
    own_kv, other_kv = kv_parts
    query = jnp.concatenate(query_parts)

    kv_stages = [(own_kv, other_kv)]
    state = None
    for step in range(planes):
        own_kv, other_kv = kv_stages[step]
        state_next = attend(lists[step], query, own_kv, other_kv, state)
        if step < planes - 1:
            moving = shift(own_kv)
            beside = []
            if step == 1:
                out_pieces = after(mlp_out.T, own_kv).reshape(PLANE, unit, row_share)
                beside = exchange_members(out_pieces, place)
            state_next, moving, *beside = together(state_next, moving, *beside)
            if step == 1:
                out_shares.append(
                    ordered(beside, place)
                    .reshape(2, row_parts, unit, row_share)
                    .transpose(0, 2, 1, 3)
                    .reshape(2 * unit, width)
                )
            kv_stages.append((moving, swap(moving, CORE)))
        else:
            state_next, _ = together(state_next, *next_in(1)(own_kv))
        state = state_next
    totals = jnp.sum(state[:, :, HEAD_SIZE:], axis=-1, keepdims=True)
    attended = state[:, :, :HEAD_SIZE] / totals
    attended_rows = narrow(attended)

    def member_rows(blocks, mask):
        return jnp.concatenate([blocks[order.index((mask, 0))], blocks[order.index((mask, 1))]])

    def blocks_of(received):
        return jnp.stack(
            [received[mask][half * block : (half + 1) * block] for mask, half in order]
        )

    next_in(0)(attended_rows)
    attended_heads = ordered(
        exchange([member_rows(attended_rows, mask) for mask in range(PLANE)]), place
    )
    attended_heads = after(attended_heads, in_halves[0][-1])
    gathered_out = (
        gathered_out.reshape((QUERY_HEADS, -1, row_parts) + attn_out.shape)
        .transpose(0, 2, 3, 1, 4)
        .reshape(QUERY_HEADS, row_parts, row_share, HEAD_SIZE)
    )

    next_in(1)(attended_heads)
    branch = out_product(attended_heads, gathered_out)
    inverse_branch = inverse_rms(branch)
    middle = source + branch * inverse_branch * scales[1]
    inverse_mid = inverse_rms(middle)
    lowered_mid = narrow(middle * inverse_mid * scales[2])
    lowered_mid = after(lowered_mid, in_halves[1][-1])
    hidden_width = planes * 2 * unit
    for which, shares in enumerate(in_halves):
        while len(shares) < planes:
            shares.append(shift(shares[-1]))
        for step, share in enumerate(shares):
            at = (plane - step) % planes * 4 * unit + which * cut
            in_all = lax.dynamic_update_slice_in_dim(in_all, share, at, 0)

    def gate_up_of(group, index):
        return narrow(dot(group, in_all, 1, 1))

    mid_groups, gate_ups, _ = gather_plane(lowered_mid, gate_up_of, (next_out,) * 3)
    while len(out_shares) < planes:
        out_shares.append(shift(out_shares[-1]))
    for step, share in enumerate(out_shares):
        at = (plane - step) % planes * 2 * unit
        out_all = lax.dynamic_update_slice_in_dim(out_all, share, at, 0)

    def activate(gate_up):
        gate = wide(gate_up[:, :hidden_width])
        up = wide(gate_up[:, hidden_width:])
        return jax.nn.gelu(gate, approximate=True) * up

    hiddens = [narrow(activate(gate_up)) for gate_up in gate_ups]

    def reduce_groups(groups, weight, *rest):
        def work(index, token):
            group = groups[index] if token is None else after(groups[index], token)
            partial = together(narrow(dot(group, weight, 1, 0)))[0]
            return partial[:token_rows], partial[token_rows:]

        return reduce_plane(work, *rest)

    down_branch, _ = reduce_groups(hiddens, out_all)
    inverse_down = inverse_rms(down_branch)
    result = middle + down_branch * inverse_down * scales[3]
    upstream = wide(cotangent)
    grad_down, grad_gain_post = norm_back(down_branch, inverse_down, scales[3], upstream)
    grad_down_low = narrow(grad_down)

    def activate_back(gate_up, grad_hidden):
        gate = wide(gate_up[:, :hidden_width])
        up = wide(gate_up[:, hidden_width:])
        _, back = jax.vjp(lambda g, u: jax.nn.gelu(g, approximate=True) * u, gate, up)
        grad_gate, grad_up = back(grad_hidden)
        return narrow(jnp.concatenate([grad_gate, grad_up], axis=1))

    def grad_gate_up_of(group, index):
        return activate_back(gate_ups[index], dot(group, out_all, 1, 1))

    down_groups, grad_gate_ups, _ = gather_plane(grad_down_low, grad_gate_up_of)

    tile = 768 if width % 768 == 0 else width
    rings = {}

    def out_grads(token):
        grads = row_product([after(hiddens[0], token)] + hiddens[1:], down_groups, 384, tile)
        return (grads,)

    def in_grads(token):
        rings["out"] = RingSum(rings["down"].reshape(planes, 2 * unit, width), plane)
        rings["out"].start(token)
        rings["out"].finish()
        rings["out"].start()
        grads = row_product(
            [after(grad_gate_ups[0], token)] + grad_gate_ups[1:], mid_groups, tile, tile
        )
        return (grads, rings["out"].finish())

    def first_low(token):
        parts = rings["in"].reshape(planes, 4 * unit, width)
        rings["low"] = RingSum(parts, plane, 0, cut)
        rings["high"] = RingSum(parts, plane, cut, cut)
        rings["low"].start(token)
        return (rings["low"].finish(),)

    grad_lowered_mid, _ = reduce_groups(
        grad_gate_ups, in_all, (out_grads, in_grads, first_low), None, rings
    )
    out_ring, low_ring, high_ring = rings["out"], rings["low"], rings["high"]

    high_ring.start(grad_lowered_mid)
    grad_through_mid, grad_gain_pre_mlp = norm_back(
        middle, inverse_mid, scales[2], grad_lowered_mid
    )
    grad_middle = upstream + grad_through_mid
    grad_branch, grad_gain_post_attn = norm_back(branch, inverse_branch, scales[1], grad_middle)
    grad_branch_low = narrow(grad_branch)
    grad_heads = out_back_product(grad_branch_low, gathered_out)
    grad_heads = after(grad_heads, high_ring.finish())
    low_ring.start(grad_heads)
    grad_heads = list(exchange_members(grad_heads, place))
    grad_heads[0] = after(grad_heads[0], low_ring.finish())
    high_ring.start(grad_heads[0])
    grad_rows = wide(blocks_of(grad_heads))
    row_terms = -jnp.sum(grad_rows * attended, axis=-1) / totals[..., 0]
    grad_summed = narrow(grad_rows / totals)
    grad_summed = after(grad_summed, high_ring.finish())
    row_terms = row_terms[:, None, :]

    grad_query, kv_total = None, None
    core, side, across = place % 2, place // 2 % 2, place // 4
    for step in range(planes):
        stage = (step + 1) % planes
        own_kv, other_kv = kv_stages[stage]
        if step == 0:
            low_ring.start(grad_summed)
            out_parts = out_grad_product(after(grad_branch_low, grad_summed), attended_heads)
            beside = [low_ring.finish(), out_parts]
        else:
            beside = [shift(kv_total)]
            grad_query = after(grad_query, kv_total)
        if step == 1:
            high_ring.start(kv_total)
            beside.append(high_ring.finish())
            beside.append(swap(pick(out_parts, 1 - core), CORE))
        if step == 2:
            beside.append(swap(pick(out_lows, 1 - across, 2), ACROSS))
            beside.append(swap(pick(out_highs, 1 - side), SIDE))
        if step == planes - 1:
            in_sum = jnp.concatenate([low_ring.finish_all(), high_ring.finish_all()])
            in_pieces = after(in_sum, kv_total).reshape(2, 2, unit, row_parts, row_share)
            in_pieces = in_pieces.transpose(0, 3, 1, 2, 4).reshape(PLANE, 2, unit, row_share)
            beside.extend(exchange_members(in_pieces, place))
        grad_query, own_grad, other_grad, *beside = together(
            *attend_back(
                lists[stage], query, grad_summed, row_terms, own_kv, other_kv, grad_query
            ),
            *beside,
        )
        total = wide(own_grad) + wide(swap(other_grad, CORE))
        if step:
            total = total + wide(beside[0])
        kv_total = narrow(total)
        if step == 0:
            out_parts = beside[1].reshape(2, 2, QUERY_HEADS, row_share, -1, attn_out.shape[1])
            out_parts = out_parts.transpose(0, 1, 2, 4, 3, 5)
            out_parts = out_parts.reshape(2, 2, planes, 2, row_share, attn_out.shape[1])
        if step == 1:
            out_sums = narrow(wide(pick(out_parts, core)) + wide(beside[2]))
            out_lows = out_sums[:, :, :, : row_share // 2]
            out_highs = out_sums[:, :, :, row_share // 2 :]
        if step == 2:
            out_lows = narrow(wide(pick(out_lows, across, 2)) + wide(beside[1]))
            out_highs = narrow(wide(pick(out_highs, side)) + wide(beside[2]))
    in_received = beside[1:]
    out_ring.start(beside[0])
    got_low = swap(pick(after(out_lows, beside[0]), 1 - side), SIDE)
    got_high = swap(pick(after(out_highs, beside[0]), 1 - across, 1), ACROSS)

    turned_query = narrow(rotate(grad_query * score_scale, cosine, -sine))
    kv_grad = wide(kv_total)
    turned_key = narrow(
        rotate(
            kv_grad[:, :, :HEAD_SIZE] * score_scale, cosine[: len(NEAR)], -sine[: len(NEAR)]
        )
    )
    near_grads = jnp.concatenate(
        [turned_query[: len(NEAR)], turned_key, kv_total[:, :, HEAD_SIZE:]], axis=-1
    ).reshape(4, token_rows, 3 * HEAD_SIZE)
    far_grads = turned_query[len(NEAR) :].reshape(4, token_rows, HEAD_SIZE)
    query_groups = jnp.concatenate([near_grads[:, :, :HEAD_SIZE], far_grads], axis=1)
    query_weight = attn_weight[:HEAD_SIZE]

    attn_out_rings = []

    def weight_grads(token):
        query_lefts = [after(query_groups[0], token)] + [query_groups[i] for i in range(1, 4)]
        grad_query_weight = row_product(query_lefts, in_groups, HEAD_SIZE, tile)
        grad_kv_weight = row_product(
            [after(near_grads[i, :, HEAD_SIZE:], token) for i in range(4)],
            in_groups,
            2 * HEAD_SIZE,
            tile,
        )
        return (grad_query_weight, grad_kv_weight, out_ring.finish())

    def weight_chunks(extras):
        grad_query_weight, grad_kv_weight, out_ring.total = extras[0]
        out_lows_last = wide(pick(out_lows, side)) + wide(got_low)
        out_highs_last = wide(pick(out_highs, across, 1)) + wide(got_high)
        parts = jnp.concatenate([narrow(out_lows_last), narrow(out_highs_last)], axis=1)
        attn_out_rings.append(RingSum(parts, plane))
        query_stored = heads_to_chunks(
            grad_query_weight.reshape(HEAD_SIZE // chunk, chunk, width),
            query_rounds,
            place,
            query_planes,
        )
        kv_stored = heads_to_chunks(
            jnp.concatenate(
                [
                    grad_kv_weight[:HEAD_SIZE].reshape(HEAD_SIZE // chunk, chunk, width),
                    grad_kv_weight[HEAD_SIZE:].reshape(HEAD_SIZE // chunk, chunk, width),
                ],
                axis=1,
            ),
            kv_rounds,
            place,
            kv_planes,
        )
        attn_out_rings[0].start()
        stored = jnp.concatenate([query_stored, kv_stored[:, :chunk], kv_stored[:, chunk:]])
        return (stored, attn_out_rings[0].finish())

    attn_rings = []

    def attn_hop(token):
        if not attn_rings:
            attn_rings.append(RingSum(extras_of[0][1][0], plane))
        attn_rings[0].start(token)
        return (attn_rings[0].finish(),)

    def hop_and_pieces(token):
        pieces = wide(ordered([after(rows, token) for rows in in_received], place))
        grads = pieces.transpose(3, 1, 0, 2).reshape(mlp_in.shape)
        attn_out_rings[0].start(token)
        return attn_hop(token) + (grads, attn_out_rings[0].finish())

    def project_back(index, token):
        near, far = near_grads[index], far_grads[index]
        if token is not None:
            near = after(near, token)
        return together(
            narrow(dot(near, attn_weight, 1, 0)), narrow(dot(far, query_weight, 1, 0))
        )

    extras_of = []

    def keep_chunks(extras):
        extras_of.append(extras)
        return weight_chunks(extras)

    grad_lowered_in, extras = reduce_plane(
        project_back, (weight_grads, hop_and_pieces, attn_hop), keep_chunks
    )
    attn_rings[0].total = after(attn_rings[0].total, grad_lowered_in)
    pieces = after(out_ring.finish_all(), grad_lowered_in).reshape(2, unit, row_parts, row_share)
    pieces = pieces.transpose(0, 2, 1, 3).reshape(PLANE, unit, row_share)
    out_received = exchange_members(pieces, place)
    attn_sum = attn_rings[0].finish_all()
    pieces = attn_sum.reshape(chunk, row_parts, row_share).transpose(1, 0, 2)
    attn_received = exchange_members(pieces, part)
    grad_source, grad_gain_in = norm_back(source, inverse_in, scales[0], grad_lowered_in)
    grad_input = grad_middle + grad_source

    grad_mlp_in = extras[2][1]
    attn_pieces = ordered(attn_received, part)
    grad_attn_out = wide(attn_out_rings[0].finish_all())
    grad_attn_in = wide(attn_pieces.reshape(attn_in.shape[1], row_share).T)
    out_pieces = wide(ordered(out_received, place))
    grad_mlp_out = out_pieces.transpose(2, 0, 1).reshape(mlp_out.shape)
    gain_total = sum_devices(
        jnp.stack([grad_gain_in, grad_gain_post_attn, grad_gain_pre_mlp, grad_gain_post])
    )
    grad_gains = pick(
        gain_total.reshape(gains.shape[1], row_parts, row_share).transpose(1, 2, 0), part
    )
    return (
        narrow(result),
        grad_input,
        grad_attn_in,
        grad_attn_out,
        grad_mlp_in,
        grad_mlp_out,
        grad_gains,
    )


def solution(mesh):
    placed = (
        P(("ctx", "fsdp"), None),
        P(("ctx", "fsdp"), None),
        P(),
        P(("ctx", "fsdp")),
        P("fsdp", "ctx"),
        P("fsdp", "ctx"),
        P("fsdp", "ctx"),
        P("fsdp", "ctx"),
        P("fsdp", None),
    )
    return jax.shard_map(
        body,
        mesh=mesh,
        in_specs=placed,
        out_specs=(
            P(("ctx", "fsdp"), None),
            P(("ctx", "fsdp"), None),
            P("fsdp", "ctx"),
            P("fsdp", "ctx"),
            P("fsdp", "ctx"),
            P("fsdp", "ctx"),
            P("fsdp", None),
        ),
        check_vma=False,
    )
```

```python
import functools
import math

import jax
import jax.numpy as jnp
from jax import lax
from jax.experimental import pallas as pl
from jax.experimental.pallas import tpu as pltpu
from jax.sharding import PartitionSpec as P

QUERY_HEADS = 8
KEY_VALUE_HEADS = 4
HEAD_SIZE = 256
LOOKBACK_SPAN = 4096
SEQUENCE_COUNT = 2


EPSILON = 1e-06
SOFT_CAP = 50.0
ROPE_BASE = 10000.0
AXES = ("ctx", "fsdp")
PLANE = 8
CORE, SIDE, ACROSS = 1, 2, 4
TANH_SCALE = HEAD_SIZE ** (-0.5) / SOFT_CAP
EXP2_SCALE = SOFT_CAP * math.log2(math.e)
VMEM_BYTES = 56 * 1024 * 1024


def inverse_rms(values):
    return lax.rsqrt(jnp.mean(values * values, axis=-1, keepdims=True) + EPSILON)


def norm_back(values, inverse, scale, upstream):
    scaled = upstream * scale
    through = inverse * scaled - values * inverse**3 * jnp.mean(
        scaled * values, axis=-1, keepdims=True
    )
    return (through, jnp.sum(upstream * values * inverse, axis=0))


def rotate(values, cosine, sine):
    half_width = values.shape[-1] // 2
    first_half = values[..., :half_width]
    second_half = values[..., half_width:]
    return jnp.concatenate(
        [
            first_half * cosine - second_half * sine,
            second_half * cosine + first_half * sine,
        ],
        axis=-1,
    )


def dot(left, right, left_axis, right_axis):
    return lax.dot_general(
        left,
        right,
        (((left_axis,), (right_axis,)), ((), ())),
        preferred_element_type=jnp.float32,
    )


def after(value, *others):
    return lax.optimization_barrier((value,) + others)[0]


def wide(values):
    return values.astype(jnp.float32)


def narrow(values):
    return values.astype(jnp.bfloat16)


def swap(values, mask):
    count = lax.axis_size(AXES)
    return lax.ppermute(values, AXES, [(i, i ^ mask) for i in range(count)])


def shift(values, steps=1):
    count = lax.axis_size(AXES)
    return lax.ppermute(values, AXES, [(i, (i + steps * PLANE) % count) for i in range(count)])


def route(values, targets):
    count = lax.axis_size(AXES)
    return lax.ppermute(
        values, AXES, [(i, i - i % PLANE + targets[i % PLANE]) for i in range(count)]
    )


def pick(stacked, index, axis=0):
    return lax.dynamic_index_in_dim(stacked, index, axis, keepdims=False)


def look_up(table, place):
    return pick(jnp.asarray(table, jnp.int32), place)


def exchange(pieces):
    far = swap(jnp.stack([pieces[mask ^ CORE] for mask in range(0, len(pieces), 2)]), CORE)
    received = []
    for i, mask in enumerate(range(0, len(pieces), 2)):
        both = jnp.stack([pieces[mask], far[i]])
        if mask:
            both = swap(both, mask)
        received.extend([both[0], both[1]])
    return received


def exchange_members(stacked, place):
    return exchange([pick(stacked, place ^ mask) for mask in range(stacked.shape[0])])


def ordered(received, place):
    whole = jnp.zeros((len(received),) + received[0].shape, received[0].dtype)
    for mask, rows in enumerate(received):
        whole = lax.dynamic_update_index_in_dim(whole, rows, place ^ mask, 0)
    return whole


NEAR = [(0, 0), (0, 1), (4, 0), (2, 1), (2, 0), (4, 1), (6, 0), (6, 1)]
FAR = [(mask ^ CORE, half) for mask, half in NEAR]


def together(*values):
    return lax.optimization_barrier(values)


def no_transfers(token, extras=None):
    return ()


def gather_plane(rows, work, beside=(no_transfers,) * 3, late=False):
    half = rows.shape[0] // 2
    low, high = rows[:half], rows[half:]
    groups, done, extras = [], [], []

    def add_group(near, far):
        groups.append(jnp.concatenate([near, far]))
        done.append(work(groups[-1], len(done)))

    other = swap(rows, CORE)
    first_low, first_high = swap(low, ACROSS), swap(high, SIDE)
    extra = beside[0](rows, extras)
    if late:
        first_low, first_high, *extra = together(first_low, first_high, *extra)
    else:
        add_group(rows, other)
        done[0], first_low, first_high, *extra = together(done[0], first_low, first_high, *extra)
    extras.append(extra)
    low, high = together(low, high, first_low)[:2]
    first_other = swap(jnp.concatenate([first_low, first_high]), CORE)
    second_low, second_high = swap(low, SIDE), swap(high, ACROSS)
    extra = beside[1](first_low, extras)
    if late:
        add_group(rows, other)
    add_group(jnp.concatenate([first_low, first_high]), first_other)
    done[1], first_low, first_high, second_low, second_high, *extra = together(
        done[1], first_low, first_high, second_low, second_high, *extra
    )
    extras.append(extra)
    second_other = swap(jnp.concatenate([second_low, second_high]), CORE)
    third_low, third_high = swap(first_low, SIDE), swap(first_high, ACROSS)
    extra = beside[2](second_low, extras)
    add_group(jnp.concatenate([second_low, second_high]), second_other)
    done[2], third_low, third_high, *extra = together(done[2], third_low, third_high, *extra)
    extras.append(extra)
    third = jnp.concatenate([third_low, third_high])
    add_group(third, swap(third, CORE))
    return groups, done, extras


def reduce_plane(work, beside=(no_transfers,) * 3, middle=None, kept=None):
    extras = []
    kept = {} if kept is None else kept

    def both(group, token):
        near, far = work(group, token)
        return wide(near) + wide(swap(far, CORE))

    third = narrow(both(3, None))
    half = third.shape[0] // 2
    got_low, got_high = swap(third[:half], SIDE), swap(third[half:], ACROSS)
    second = narrow(both(2, third))
    got_low, got_high, second, *extra = together(got_low, got_high, second, *beside[0](third))
    extras.append(extra)
    kept["down"] = extra[0] if extra else None
    if middle is not None:
        second, *extra = together(second, *middle(extras))
        extras.append(extra)
    own_low, own_high = swap(second[:half], SIDE), swap(second[half:], ACROSS)
    first = both(1, second)
    first = narrow(first + wide(jnp.concatenate([got_low, got_high])))
    own_low, own_high, first, *extra = together(own_low, own_high, first, *beside[1](second))
    extras.append(extra)
    kept["in"] = extra[0] if extra else None
    more_low, more_high = swap(first[:half], ACROSS), swap(first[half:], SIDE)
    own = both(0, first) + wide(jnp.concatenate([own_low, own_high]))
    more_low, more_high, own, *extra = together(more_low, more_high, own, *beside[2](first))
    extras.append(extra)
    return own + wide(jnp.concatenate([more_low, more_high])), extras


def sum_devices(values):
    for mask in (CORE, SIDE, ACROSS):
        values = values + swap(values, mask)
    total = values
    for steps in range(1, lax.axis_size(AXES) // PLANE):
        total = total + shift(values, steps)
    return total


class RingSum:
    def __init__(self, parts, plane, first=0, rows=None):
        self.parts, self.plane, self.planes = parts, plane, parts.shape[0]
        self.first, self.rows = first, rows or parts.shape[1]
        self.hops, self.moving = 0, None
        self.total = self.part(0)

    def part(self, step):
        at = (self.plane + 2 * self.planes - 1 - step) % self.planes
        size = (1, self.rows, self.parts.shape[2])
        return lax.dynamic_slice(self.parts, (at, self.first, 0), size)[0]

    def start(self, *others):
        if self.hops < self.planes - 1:
            self.moving = shift(after(self.total, *others) if others else self.total)

    def finish(self):
        if self.moving is not None:
            self.hops += 1
            self.total = narrow(wide(self.moving) + wide(self.part(self.hops)))
            self.moving = None
        return self.total

    def finish_all(self):
        self.finish()
        while self.hops < self.planes - 1:
            self.start()
            self.finish()
        return self.total


def matchings(edges):
    left, rounds = list(edges), []
    while left:
        owner = {}

        def settle(source, seen):
            for edge in left:
                if edge[0] == source and edge[1] not in seen:
                    seen.add(edge[1])
                    if edge[1] not in owner or settle(owner[edge[1]][0], seen):
                        owner[edge[1]] = edge
                        return True
            return False

        for source in range(PLANE):
            settle(source, set())
        found = sorted(owner.values())
        rounds.append(found)
        left = [edge for edge in left if edge not in found]
    return rounds


def chunk_edges(plane_count, columns, chunk, share):
    edges = []
    for source in range(PLANE):
        for at in range(plane_count):
            column = (2 * at + source // 4) * columns + source % 4 * chunk
            head = column // HEAD_SIZE
            for target in range(head * share, (head + 1) * share):
                edges.append((source, target, at, column % HEAD_SIZE // chunk))
    return edges


def chunks_to_heads(stored, rounds, place):
    spots = len(rounds)
    got = []
    for found in rounds:
        sent = pick(stored, look_up([edge[2] for edge in found], place))
        got.append(route(sent, [edge[1] for edge in found]))
    stacked = jnp.stack(got)
    order = []
    for spot in range(spots):
        table = [0] * PLANE
        for step, found in enumerate(rounds):
            for edge in found:
                if edge[3] == spot:
                    table[edge[1]] = step
        order.append(pick(stacked, look_up(table, place)))
    return order


def heads_to_chunks(heads, rounds, place, plane_count):
    got = []
    for found in rounds:
        back, spot = [0] * PLANE, [0] * PLANE
        for source, target, _, position in found:
            back[target], spot[target] = source, position
        got.append(route(pick(heads, look_up(spot, place)), back))
    stacked = jnp.stack(got)
    chunks = []
    for at in range(plane_count):
        tables = []
        for source in range(PLANE):
            tables.append(
                [
                    step
                    for step, found in enumerate(rounds)
                    for edge in found
                    if edge[0] == source and edge[2] == at
                ]
            )
        terms = [
            pick(stacked, look_up([table[i] for table in tables], place))
            for i in range(len(tables[0]))
        ]
        total = terms[0]
        if len(terms) > 1:
            total = narrow(sum(wide(term) for term in terms))
        chunks.append(total)
    return jnp.stack(chunks)


def row_product_kernel(count, *refs):
    out, total = refs[-2:]
    total[...] = dot(refs[0][...], refs[count][...], 0, 0)
    for i in range(1, count):
        total[...] += dot(refs[i][...], refs[count + i][...], 0, 0)
    out[...] = total[...].astype(out.dtype)


def row_product(lefts, rights, left_tile, right_tile):
    count = len(lefts)
    height, width = lefts[0].shape[1], rights[0].shape[1]
    depths = [left.shape[0] for left in lefts]
    return pl.pallas_call(
        functools.partial(row_product_kernel, count),
        out_shape=jax.ShapeDtypeStruct((height, width), jnp.bfloat16),
        grid=(height // left_tile, width // right_tile),
        in_specs=[pl.BlockSpec((depth, left_tile), lambda i, j: (0, i)) for depth in depths]
        + [pl.BlockSpec((depth, right_tile), lambda i, j: (0, j)) for depth in depths],
        out_specs=pl.BlockSpec((left_tile, right_tile), lambda i, j: (i, j)),
        scratch_shapes=[pltpu.VMEM((left_tile, right_tile), jnp.float32)],
        compiler_params=pltpu.CompilerParams(vmem_limit_bytes=VMEM_BYTES),
        cost_estimate=pl.CostEstimate(
            flops=2 * sum(depths) * height * width,
            bytes_accessed=2 * sum(depths) * (height + width) + 2 * height * width,
            transcendentals=0,
        ),
    )(*lefts, *rights)


def out_kernel(part, rows_ref, weight_ref, out_ref):
    at = pl.program_id(0)
    total = dot(rows_ref[0], weight_ref[0, 0], 1, 1)
    for head in range(1, rows_ref.shape[0]):
        total += dot(rows_ref[head], weight_ref[head, 0], 1, 1)
    for i in range(out_ref.shape[1] // part):

        @pl.when(at == i)
        def _():
            out_ref[:, i * part : (i + 1) * part] = total


def out_product(rows, weight):
    heads, count, size = rows.shape
    _, parts, part, _ = weight.shape
    return pl.pallas_call(
        functools.partial(out_kernel, part),
        out_shape=jax.ShapeDtypeStruct((count, parts * part), jnp.float32),
        grid=(parts,),
        in_specs=[
            pl.BlockSpec((heads, count, size), lambda i: (0, 0, 0)),
            pl.BlockSpec((heads, 1, part, size), lambda i: (0, i, 0, 0)),
        ],
        out_specs=pl.BlockSpec((count, parts * part), lambda i: (0, 0)),
        compiler_params=pltpu.CompilerParams(vmem_limit_bytes=VMEM_BYTES),
        cost_estimate=pl.CostEstimate(
            flops=2 * count * heads * size * parts * part,
            bytes_accessed=2 * heads * size * (count + parts * part) + 4 * count * parts * part,
            transcendentals=0,
        ),
    )(rows, weight)


def out_back_kernel(rows_ref, weight_ref, out_ref):
    part = weight_ref.shape[2]
    total = dot(rows_ref[:, :part], weight_ref[0, 0], 1, 0)
    for i in range(1, weight_ref.shape[1]):
        total += dot(rows_ref[:, i * part : (i + 1) * part], weight_ref[0, i], 1, 0)
    out_ref[0] = total.astype(out_ref.dtype)


def out_back_product(rows, weight):
    count, width = rows.shape
    heads, parts, part, size = weight.shape
    return pl.pallas_call(
        out_back_kernel,
        out_shape=jax.ShapeDtypeStruct((heads, count, size), jnp.bfloat16),
        grid=(heads,),
        in_specs=[
            pl.BlockSpec((count, width), lambda i: (0, 0)),
            pl.BlockSpec((1, parts, part, size), lambda i: (i, 0, 0, 0)),
        ],
        out_specs=pl.BlockSpec((1, count, size), lambda i: (i, 0, 0)),
        compiler_params=pltpu.CompilerParams(vmem_limit_bytes=VMEM_BYTES),
        cost_estimate=pl.CostEstimate(
            flops=2 * count * heads * size * width,
            bytes_accessed=2 * heads * size * (count + width) + 2 * count * width,
            transcendentals=0,
        ),
    )(rows, weight)


def out_grad_kernel(rows_ref, heads_ref, out_ref):
    total = dot(rows_ref[...], heads_ref[0], 0, 0).astype(out_ref.dtype)
    part = out_ref.shape[3]
    for side in range(2):
        for core in range(2):
            at = (2 * side + core) * part
            out_ref[core, side, 0] = total[at : at + part]


def out_grad_product(rows, by_head):
    count, width = rows.shape
    heads, _, size = by_head.shape
    part = width // 4
    return pl.pallas_call(
        out_grad_kernel,
        out_shape=jax.ShapeDtypeStruct((2, 2, heads, part, size), jnp.bfloat16),
        grid=(heads,),
        in_specs=[
            pl.BlockSpec((count, width), lambda i: (0, 0)),
            pl.BlockSpec((1, count, size), lambda i: (i, 0, 0)),
        ],
        out_specs=pl.BlockSpec((2, 2, 1, part, size), lambda i: (0, 0, i, 0, 0)),
        compiler_params=pltpu.CompilerParams(vmem_limit_bytes=VMEM_BYTES),
        cost_estimate=pl.CostEstimate(
            flops=2 * count * heads * size * width,
            bytes_accessed=2 * heads * size * (count + width) + 2 * count * width,
            transcendentals=0,
        ),
    )(rows, by_head)


def pair_lists(query_ids, key_ids, blocks_per_seq, span_blocks):
    query_seq, query_at = query_ids // blocks_per_seq, query_ids % blocks_per_seq
    key_seq, key_at = key_ids // blocks_per_seq, key_ids % blocks_per_seq
    rows = key_ids.shape[0]
    distance = (query_at[None, :, None] - key_at[:, None, :]).reshape(rows, -1)
    same = (query_seq[None, :, None] == key_seq[:, None, :]).reshape(rows, -1)
    whole = same & (distance > 0) & (distance < span_blocks)
    edged = same & ((distance == 0) | (distance == span_blocks))
    kind = whole.astype(jnp.int32) + 2 * edged.astype(jnp.int32)
    total = distance.shape[1]
    index = jnp.arange(total, dtype=jnp.int32)
    earlier = (index[None, :] < index[:, None])[None] & (kind[:, None, :] == kind[:, :, None])
    rank = jnp.sum(earlier.astype(jnp.int32), axis=2)
    count_whole = jnp.sum(whole.astype(jnp.int32), axis=1, keepdims=True)
    count_edged = jnp.sum(edged.astype(jnp.int32), axis=1, keepdims=True)
    spot = jnp.where(kind == 1, rank, jnp.where(kind == 2, count_whole + rank, -1))
    code = index * 2 + (distance == span_blocks).astype(jnp.int32)
    hit = spot[:, :, None] == index[None, None, :]
    entries = jnp.sum(jnp.where(hit, code[:, :, None], 0), axis=1)
    return jnp.concatenate([count_whole, count_edged, entries], axis=1).astype(jnp.int32)


def run_pairs(list_ref, row, key_count, unroll, visit):
    whole = list_ref[row, 0]
    edged = list_ref[row, 1]

    def decode(position):
        code = list_ref[row, 2 + position]
        pair = code // 2
        return pair // key_count, pair % key_count, code % 2

    def several(step, carry):
        found = [decode(step * unroll + i) for i in range(unroll)]
        visit([f[0] for f in found], [f[1] for f in found], None)
        return carry

    def single(position, carry):
        i, j, _ = decode(position)
        visit([i], [j], None)
        return carry

    def masked(position, carry):
        i, j, far = decode(position)
        visit([i], [j], far)
        return carry

    groups = whole // unroll
    lax.fori_loop(0, groups, several, 0)
    lax.fori_loop(groups * unroll, whole, single, 0)
    lax.fori_loop(whole, whole + edged, masked, 0)


def attend_kernel(first, unroll, list_ref, query_hbm, own_hbm, other_hbm, *rest):
    if first:
        state_hbm = None
        out_hbm, query, own, other, state, sems = rest
    else:
        state_hbm, out_hbm, query, own, other, state, sems = rest
    copies = [
        pltpu.make_async_copy(query_hbm, query, sems.at[0]),
        pltpu.make_async_copy(own_hbm, own, sems.at[1]),
        pltpu.make_async_copy(other_hbm, other, sems.at[2]),
    ]
    if not first:
        copies.append(pltpu.make_async_copy(state_hbm, state, sems.at[3]))
    for copy in copies:
        copy.start()
    if first:
        state[...] = jnp.zeros_like(state)
    for copy in copies:
        copy.wait()
    rows = query.shape[1]
    lane = lax.broadcasted_iota(jnp.int32, (rows, 128), 1)

    def visit_in(keys):
        def visit(query_at, key_at, far):
            scores = [
                dot(query[i], keys[j, :, :HEAD_SIZE], 1, 1) for i, j in zip(query_at, key_at)
            ]
            for i, j, score in zip(query_at, key_at, scores):
                weights = jnp.exp2(EXP2_SCALE * jnp.tanh(score * TANH_SCALE))
                if far is not None:
                    spacing = (
                        lax.broadcasted_iota(jnp.int32, weights.shape, 0)
                        - lax.broadcasted_iota(jnp.int32, weights.shape, 1)
                        + far * LOOKBACK_SPAN
                    )
                    live = (spacing >= 0) & (spacing < LOOKBACK_SPAN)
                    weights = jnp.where(live, weights, 0.0)
                if rows % 128 == 0:
                    part = weights[:, :128]
                    for k in range(1, rows // 128):
                        part = part + weights[:, k * 128 : (k + 1) * 128]
                else:
                    part = jnp.where(lane == 0, jnp.sum(weights, axis=1, keepdims=True), 0.0)
                state[i, :, HEAD_SIZE:] += part
                state[i, :, :HEAD_SIZE] += dot(
                    weights.astype(jnp.bfloat16), keys[j, :, HEAD_SIZE:], 1, 0
                )

        return visit

    key_count = own.shape[0]
    run_pairs(list_ref, 0, key_count, unroll, visit_in(own))
    run_pairs(list_ref, 1, key_count, unroll, visit_in(other))
    out = pltpu.make_async_copy(state, out_hbm, sems.at[4])
    out.start()
    out.wait()


def attend(lists, query, own, other, state):
    first = state is None
    blocks, rows, _ = query.shape
    shape = (blocks, rows, HEAD_SIZE + 128)
    operands = (query, own, other) if first else (query, own, other, state)
    return pl.pallas_call(
        functools.partial(attend_kernel, first, 4),
        out_shape=jax.ShapeDtypeStruct(shape, jnp.float32),
        grid_spec=pltpu.PrefetchScalarGridSpec(
            num_scalar_prefetch=1,
            grid=(1,),
            in_specs=[pl.BlockSpec(memory_space=pl.ANY)] * len(operands),
            out_specs=pl.BlockSpec(memory_space=pl.ANY),
            scratch_shapes=[
                pltpu.VMEM(query.shape, jnp.bfloat16),
                pltpu.VMEM(own.shape, jnp.bfloat16),
                pltpu.VMEM(other.shape, jnp.bfloat16),
                pltpu.VMEM(shape, jnp.float32),
                pltpu.SemaphoreType.DMA((5,)),
            ],
        ),
        compiler_params=pltpu.CompilerParams(vmem_limit_bytes=VMEM_BYTES),
        cost_estimate=pl.CostEstimate(
            flops=60 * 4 * rows * rows * HEAD_SIZE,
            bytes_accessed=14 * 1024 * 1024,
            transcendentals=60 * 2 * rows * rows,
        ),
    )(lists, *operands)


def attend_back_kernel(
    first,
    unroll,
    list_ref,
    query_hbm,
    grad_hbm,
    term_hbm,
    own_hbm,
    other_hbm,
    *rest,
):
    if first:
        state_hbm = None
    else:
        state_hbm, *rest = rest
    (
        out_hbm,
        own_out_hbm,
        other_out_hbm,
        query,
        grad,
        term,
        own,
        other,
        state,
        own_grad,
        other_grad,
        own_low,
        other_low,
        sems,
    ) = rest
    copies = [
        pltpu.make_async_copy(query_hbm, query, sems.at[0]),
        pltpu.make_async_copy(grad_hbm, grad, sems.at[1]),
        pltpu.make_async_copy(term_hbm, term, sems.at[2]),
        pltpu.make_async_copy(own_hbm, own, sems.at[3]),
        pltpu.make_async_copy(other_hbm, other, sems.at[4]),
    ]
    if not first:
        copies.append(pltpu.make_async_copy(state_hbm, state, sems.at[5]))
    for copy in copies:
        copy.start()
    if first:
        state[...] = jnp.zeros_like(state)
    own_grad[...] = jnp.zeros_like(own_grad)
    other_grad[...] = jnp.zeros_like(other_grad)
    for copy in copies:
        copy.wait()

    def visit_in(keys, key_grad):
        def visit(query_at, key_at, far):
            scores = []
            slopes = []
            for i, j in zip(query_at, key_at):
                scores.append(dot(keys[j, :, :HEAD_SIZE], query[i], 1, 1))
                slopes.append(dot(keys[j, :, HEAD_SIZE:], grad[i], 1, 1))
            for i, j, score, slope in zip(query_at, key_at, scores, slopes):
                bent = jnp.tanh(score * TANH_SCALE)
                weights = jnp.exp2(EXP2_SCALE * bent)
                if far is not None:
                    spacing = (
                        lax.broadcasted_iota(jnp.int32, weights.shape, 1)
                        - lax.broadcasted_iota(jnp.int32, weights.shape, 0)
                        + far * LOOKBACK_SPAN
                    )
                    live = (spacing >= 0) & (spacing < LOOKBACK_SPAN)
                    weights = jnp.where(live, weights, 0.0)
                grad_scores = (
                    (slope + term[i]) * (weights * (1.0 - bent * bent))
                ).astype(jnp.bfloat16)
                key_grad[j, :, :HEAD_SIZE] += dot(grad_scores, query[i], 1, 0)
                key_grad[j, :, HEAD_SIZE:] += dot(weights.astype(jnp.bfloat16), grad[i], 1, 0)
                state[i] += dot(grad_scores, keys[j, :, :HEAD_SIZE], 0, 0)

        return visit

    key_count = own.shape[0]
    run_pairs(list_ref, 1, key_count, unroll, visit_in(other, other_grad))
    other_low[...] = other_grad[...].astype(jnp.bfloat16)
    other_out = pltpu.make_async_copy(other_low, other_out_hbm, sems.at[6])
    other_out.start()
    run_pairs(list_ref, 0, key_count, unroll, visit_in(own, own_grad))
    own_low[...] = own_grad[...].astype(jnp.bfloat16)
    own_out = pltpu.make_async_copy(own_low, own_out_hbm, sems.at[7])
    own_out.start()
    out = pltpu.make_async_copy(state, out_hbm, sems.at[8])
    out.start()
    other_out.wait()
    own_out.wait()
    out.wait()


def attend_back(lists, query, grad, term, own, other, state):
    first = state is None
    blocks, rows, _ = query.shape
    operands = (query, grad, term, own, other)
    if not first:
        operands = operands + (state,)
    return pl.pallas_call(
        functools.partial(attend_back_kernel, first, 2),
        out_shape=[
            jax.ShapeDtypeStruct(query.shape, jnp.float32),
            jax.ShapeDtypeStruct(own.shape, jnp.bfloat16),
            jax.ShapeDtypeStruct(other.shape, jnp.bfloat16),
        ],
        grid_spec=pltpu.PrefetchScalarGridSpec(
            num_scalar_prefetch=1,
            grid=(1,),
            in_specs=[pl.BlockSpec(memory_space=pl.ANY)] * len(operands),
            out_specs=[pl.BlockSpec(memory_space=pl.ANY)] * 3,
            scratch_shapes=[
                pltpu.VMEM(query.shape, jnp.bfloat16),
                pltpu.VMEM(query.shape, jnp.bfloat16),
                pltpu.VMEM(term.shape, jnp.float32),
                pltpu.VMEM(own.shape, jnp.bfloat16),
                pltpu.VMEM(other.shape, jnp.bfloat16),
                pltpu.VMEM(query.shape, jnp.float32),
                pltpu.VMEM(own.shape, jnp.float32),
                pltpu.VMEM(other.shape, jnp.float32),
                pltpu.VMEM(own.shape, jnp.bfloat16),
                pltpu.VMEM(other.shape, jnp.bfloat16),
                pltpu.SemaphoreType.DMA((9,)),
            ],
        ),
        compiler_params=pltpu.CompilerParams(vmem_limit_bytes=VMEM_BYTES),
        cost_estimate=pl.CostEstimate(
            flops=60 * 10 * rows * rows * HEAD_SIZE,
            bytes_accessed=24 * 1024 * 1024,
            transcendentals=60 * 2 * rows * rows,
        ),
    )(lists, *operands)


def body(inputs, cotangent, block_ids, positions, attn_in, attn_out, mlp_in, mlp_out, gains):
    token_rows, width = inputs.shape
    block = token_rows // 2
    devices = lax.axis_size(AXES)
    ctx_count, row_parts = lax.axis_size("ctx"), lax.axis_size("fsdp")
    planes = devices // PLANE
    blocks_per_seq = 2 * devices // SEQUENCE_COUNT
    span_blocks = LOOKBACK_SPAN // block
    score_scale = HEAD_SIZE ** (-0.5)
    me = lax.axis_index(AXES)
    place, plane = me % PLANE, me // PLANE
    part = place % row_parts
    row_share = attn_in.shape[0]
    unit = mlp_out.shape[1] // PLANE
    chunk = attn_in.shape[1] // row_parts
    order = NEAR + FAR

    gain_parts = ordered([gains.T] + [swap(gains.T, mask) for mask in range(1, row_parts)], part)
    scales = wide(gain_parts.transpose(1, 0, 2).reshape(gains.shape[1], width))
    source = wide(inputs)
    inverse_in = inverse_rms(source)
    lowered_in = narrow(source * inverse_in * scales[0])

    gathered_out = lax.all_gather(attn_out, AXES, axis=0)
    in_pieces = mlp_in.T.reshape(2, PLANE, unit, row_share).transpose(1, 0, 2, 3)
    in_received = exchange_members(in_pieces, place)
    attn_pieces = exchange_members(attn_in.T.reshape(row_parts, chunk, row_share), part)
    in_chunk = ordered(attn_pieces, part).transpose(1, 0, 2).reshape(chunk, width)
    *in_received, first_stored = together(*in_received, shift(in_chunk))
    stored = [in_chunk, first_stored]
    for step in range(2, planes):
        stored.append(shift(stored[-1]))
    in_share = (
        ordered(in_received, place)
        .reshape(2, row_parts, 2, unit, row_share)
        .transpose(0, 2, 3, 1, 4)
        .reshape(4 * unit, width)
    )
    lowered_in = after(lowered_in, first_stored)
    block_ids = after(block_ids, in_chunk)

    def ids_of(which_plane, slots):
        masks = jnp.asarray([mask for mask, _ in slots], jnp.int32)
        sides = jnp.asarray([half for _, half in slots], jnp.int32)
        at = 2 * (which_plane[:, None] * PLANE + (place ^ masks)[None, :]) + sides[None, :]
        slot = jnp.arange(block_ids.shape[0], dtype=jnp.int32)
        return jnp.sum(jnp.where(at[:, :, None] == slot, block_ids, 0), axis=2)

    stage_planes = (plane + planes - jnp.arange(planes, dtype=jnp.int32)) % planes
    stage_ids = ids_of(stage_planes, order)
    query_ids = stage_ids[0]
    lists = pair_lists(
        query_ids, stage_ids.reshape(2 * planes, len(NEAR)), blocks_per_seq, span_blocks
    ).reshape(planes, 2, -1)
    half_width = HEAD_SIZE // 2
    frequency = ROPE_BASE ** (-2.0 * jnp.arange(half_width, dtype=jnp.float32) / HEAD_SIZE)
    base_angle = wide(query_ids % blocks_per_seq * block)[:, None, None] * frequency
    step_angle = jnp.arange(block, dtype=jnp.float32)[:, None] * frequency
    base_cosine, base_sine = jnp.cos(base_angle), jnp.sin(base_angle)
    step_cosine, step_sine = jnp.cos(step_angle), jnp.sin(step_angle)
    cosine = base_cosine * step_cosine - base_sine * step_sine
    sine = base_sine * step_cosine + base_cosine * step_sine

    cut = 2 * unit
    in_halves = [[], []]
    out_shares = []
    in_all = jnp.zeros((planes * 4 * unit, width), jnp.bfloat16)
    out_all = jnp.zeros((planes * 2 * unit, width), jnp.bfloat16)

    def next_in(which):
        def start(token, extras=None):
            in_halves[which].append(shift(after(in_halves[which][-1], token)))
            return (in_halves[which][-1],)

        return start

    def next_out(token, extras=None):
        out_shares.append(shift(after(out_shares[-1], token)))
        return (out_shares[-1],)

    query_planes, kv_planes = planes // 2, planes // 4
    query_rounds = matchings(chunk_edges(query_planes, attn_in.shape[1], chunk, 1))
    kv_rounds = matchings(
        chunk_edges(kv_planes, attn_in.shape[1], chunk, QUERY_HEADS // KEY_VALUE_HEADS)
    )

    def weights_together(token, extras):
        whole = jnp.zeros((planes, chunk, width), jnp.bfloat16)
        for step, rows in enumerate(stored):
            whole = lax.dynamic_update_index_in_dim(whole, rows, (plane - step) % planes, 0)
        return (whole, in_share)

    attn_weights = []

    def weights_to_heads(token, extras):
        whole, share = extras[0]
        in_halves[0].append(share[:cut])
        in_halves[1].append(share[cut:])
        query_chunks = chunks_to_heads(whole[:query_planes], query_rounds, place)
        kv_chunks = chunks_to_heads(
            jnp.concatenate(
                [whole[query_planes : query_planes + kv_planes], whole[query_planes + kv_planes :]],
                axis=1,
            ),
            kv_rounds,
            place,
        )
        attn_weights.append(
            jnp.concatenate(
                query_chunks
                + [both[:chunk] for both in kv_chunks]
                + [both[chunk:] for both in kv_chunks]
            )
        )
        return next_in(0)(token) + next_in(1)(token) + (gathered_out, lists, cosine, sine)

    in_groups, projected, extras = gather_plane(
        lowered_in,
        lambda group, index: dot(group, attn_weights[0], 1, 1),
        (weights_together, weights_to_heads, next_in(0)),
        late=True,
    )
    attn_weight = attn_weights[0]
    gathered_out, lists, cosine, sine = extras[1][2:]

    def split_groups(groups):
        near = jnp.concatenate([group[:token_rows] for group in groups])
        far = jnp.concatenate([group[token_rows:] for group in groups])
        return [rows.reshape(len(NEAR), block, rows.shape[1]) for rows in (near, far)]

    near_rows, far_rows = split_groups(projected)
    query_parts, kv_parts = [], []
    for rows, low, high in ((near_rows, 0, len(NEAR)), (far_rows, len(NEAR), 2 * len(NEAR))):
        turns = (cosine[low:high], sine[low:high])
        query_parts.append(narrow(rotate(rows[:, :, :HEAD_SIZE], *turns)))
        kv_parts.append(
            jnp.concatenate(
                [
                    narrow(rotate(rows[:, :, HEAD_SIZE : 2 * HEAD_SIZE], *turns)),
                    narrow(rows[:, :, 2 * HEAD_SIZE :]),
                ],
                axis=-1,
            )
        )
    own_kv, other_kv = kv_parts
    query = jnp.concatenate(query_parts)

    kv_stages = [(own_kv, other_kv)]
    state = None
    for step in range(planes):
        own_kv, other_kv = kv_stages[step]
        state_next = attend(lists[step], query, own_kv, other_kv, state)
        if step < planes - 1:
            moving = shift(own_kv)
            beside = []
            if step == 1:
                out_pieces = after(mlp_out.T, own_kv).reshape(PLANE, unit, row_share)
                beside = exchange_members(out_pieces, place)
            state_next, moving, *beside = together(state_next, moving, *beside)
            if step == 1:
                out_shares.append(
                    ordered(beside, place)
                    .reshape(2, row_parts, unit, row_share)
                    .transpose(0, 2, 1, 3)
                    .reshape(2 * unit, width)
                )
            kv_stages.append((moving, swap(moving, CORE)))
        else:
            state_next, _ = together(state_next, *next_in(1)(own_kv))
        state = state_next
    totals = jnp.sum(state[:, :, HEAD_SIZE:], axis=-1, keepdims=True)
    attended = state[:, :, :HEAD_SIZE] / totals
    attended_rows = narrow(attended)

    def member_rows(blocks, mask):
        return jnp.concatenate([blocks[order.index((mask, 0))], blocks[order.index((mask, 1))]])

    def blocks_of(received):
        return jnp.stack(
            [received[mask][half * block : (half + 1) * block] for mask, half in order]
        )

    next_in(0)(attended_rows)
    attended_heads = ordered(
        exchange([member_rows(attended_rows, mask) for mask in range(PLANE)]), place
    )
    attended_heads = after(attended_heads, in_halves[0][-1])
    gathered_out = (
        gathered_out.reshape((QUERY_HEADS, -1, row_parts) + attn_out.shape)
        .transpose(0, 2, 3, 1, 4)
        .reshape(QUERY_HEADS, row_parts, row_share, HEAD_SIZE)
    )

    next_in(1)(attended_heads)
    branch = out_product(attended_heads, gathered_out)
    inverse_branch = inverse_rms(branch)
    middle = source + branch * inverse_branch * scales[1]
    inverse_mid = inverse_rms(middle)
    lowered_mid = narrow(middle * inverse_mid * scales[2])
    lowered_mid = after(lowered_mid, in_halves[1][-1])
    hidden_width = planes * 2 * unit
    for which, shares in enumerate(in_halves):
        while len(shares) < planes:
            shares.append(shift(shares[-1]))
        for step, share in enumerate(shares):
            at = (plane - step) % planes * 4 * unit + which * cut
            in_all = lax.dynamic_update_slice_in_dim(in_all, share, at, 0)

    def gate_up_of(group, index):
        return narrow(dot(group, in_all, 1, 1))

    mid_groups, gate_ups, _ = gather_plane(lowered_mid, gate_up_of, (next_out,) * 3)
    while len(out_shares) < planes:
        out_shares.append(shift(out_shares[-1]))
    for step, share in enumerate(out_shares):
        at = (plane - step) % planes * 2 * unit
        out_all = lax.dynamic_update_slice_in_dim(out_all, share, at, 0)

    def activate(gate_up):
        gate = wide(gate_up[:, :hidden_width])
        up = wide(gate_up[:, hidden_width:])
        return jax.nn.gelu(gate, approximate=True) * up

    hiddens = [narrow(activate(gate_up)) for gate_up in gate_ups]

    def reduce_groups(groups, weight, *rest):
        def work(index, token):
            group = groups[index] if token is None else after(groups[index], token)
            partial = together(narrow(dot(group, weight, 1, 0)))[0]
            return partial[:token_rows], partial[token_rows:]

        return reduce_plane(work, *rest)

    down_branch, _ = reduce_groups(hiddens, out_all)
    inverse_down = inverse_rms(down_branch)
    result = middle + down_branch * inverse_down * scales[3]
    upstream = wide(cotangent)
    grad_down, grad_gain_post = norm_back(down_branch, inverse_down, scales[3], upstream)
    grad_down_low = narrow(grad_down)

    def activate_back(gate_up, grad_hidden):
        gate = wide(gate_up[:, :hidden_width])
        up = wide(gate_up[:, hidden_width:])
        _, back = jax.vjp(lambda g, u: jax.nn.gelu(g, approximate=True) * u, gate, up)
        grad_gate, grad_up = back(grad_hidden)
        return narrow(jnp.concatenate([grad_gate, grad_up], axis=1))

    def grad_gate_up_of(group, index):
        return activate_back(gate_ups[index], dot(group, out_all, 1, 1))

    down_groups, grad_gate_ups, _ = gather_plane(grad_down_low, grad_gate_up_of)

    tile = 768 if width % 768 == 0 else width
    rings = {}

    def out_grads(token):
        grads = row_product([after(hiddens[0], token)] + hiddens[1:], down_groups, 384, tile)
        return (grads,)

    def in_grads(token):
        rings["out"] = RingSum(rings["down"].reshape(planes, 2 * unit, width), plane)
        rings["out"].start(token)
        rings["out"].finish()
        rings["out"].start()
        grads = row_product(
            [after(grad_gate_ups[0], token)] + grad_gate_ups[1:], mid_groups, tile, tile
        )
        return (grads, rings["out"].finish())

    def first_low(token):
        parts = rings["in"].reshape(planes, 4 * unit, width)
        rings["low"] = RingSum(parts, plane, 0, cut)
        rings["high"] = RingSum(parts, plane, cut, cut)
        rings["low"].start(token)
        return (rings["low"].finish(),)

    grad_lowered_mid, _ = reduce_groups(
        grad_gate_ups, in_all, (out_grads, in_grads, first_low), None, rings
    )
    out_ring, low_ring, high_ring = rings["out"], rings["low"], rings["high"]

    high_ring.start(grad_lowered_mid)
    grad_through_mid, grad_gain_pre_mlp = norm_back(
        middle, inverse_mid, scales[2], grad_lowered_mid
    )
    grad_middle = upstream + grad_through_mid
    grad_branch, grad_gain_post_attn = norm_back(branch, inverse_branch, scales[1], grad_middle)
    grad_branch_low = narrow(grad_branch)
    grad_heads = out_back_product(grad_branch_low, gathered_out)
    grad_heads = after(grad_heads, high_ring.finish())
    low_ring.start(grad_heads)
    grad_heads = list(exchange_members(grad_heads, place))
    grad_heads[0] = after(grad_heads[0], low_ring.finish())
    high_ring.start(grad_heads[0])
    grad_rows = wide(blocks_of(grad_heads))
    row_terms = -jnp.sum(grad_rows * attended, axis=-1) / totals[..., 0]
    grad_summed = narrow(grad_rows / totals)
    grad_summed = after(grad_summed, high_ring.finish())
    row_terms = row_terms[:, None, :]

    grad_query, kv_total = None, None
    core, side, across = place % 2, place // 2 % 2, place // 4
    for step in range(planes):
        stage = (step + 1) % planes
        own_kv, other_kv = kv_stages[stage]
        if step == 0:
            low_ring.start(grad_summed)
            out_parts = out_grad_product(after(grad_branch_low, grad_summed), attended_heads)
            high_ring.start(grad_summed)
            beside = [low_ring.finish(), out_parts, high_ring.finish()]
        else:
            beside = [shift(kv_total)]
            grad_query = after(grad_query, kv_total)
        if step == 1:
            beside.append(swap(pick(out_parts, 1 - core), CORE))
        if step == 2:
            beside.append(swap(pick(out_lows, 1 - across, 2), ACROSS))
            beside.append(swap(pick(out_highs, 1 - side), SIDE))
        if step == planes - 1:
            in_sum = jnp.concatenate([low_ring.finish_all(), high_ring.finish_all()])
            in_pieces = after(in_sum, kv_total).reshape(2, 2, unit, row_parts, row_share)
            in_pieces = in_pieces.transpose(0, 3, 1, 2, 4).reshape(PLANE, 2, unit, row_share)
            beside.extend(exchange_members(in_pieces, place))
        grad_query, own_grad, other_grad, *beside = together(
            *attend_back(
                lists[stage], query, grad_summed, row_terms, own_kv, other_kv, grad_query
            ),
            *beside,
        )
        total = wide(own_grad) + wide(swap(other_grad, CORE))
        if step:
            total = total + wide(beside[0])
        kv_total = narrow(total)
        if step == 0:
            out_parts = beside[1].reshape(2, 2, QUERY_HEADS, row_share, -1, attn_out.shape[1])
            out_parts = out_parts.transpose(0, 1, 2, 4, 3, 5)
            out_parts = out_parts.reshape(2, 2, planes, 2, row_share, attn_out.shape[1])
        if step == 1:
            out_sums = narrow(wide(pick(out_parts, core)) + wide(beside[1]))
            out_lows = out_sums[:, :, :, : row_share // 2]
            out_highs = out_sums[:, :, :, row_share // 2 :]
        if step == 2:
            out_lows = narrow(wide(pick(out_lows, across, 2)) + wide(beside[1]))
            out_highs = narrow(wide(pick(out_highs, side)) + wide(beside[2]))
    in_received = beside[1:]
    out_ring.start(beside[0])
    got_low = swap(pick(after(out_lows, beside[0]), 1 - side), SIDE)
    got_high = swap(pick(after(out_highs, beside[0]), 1 - across, 1), ACROSS)

    turned_query = narrow(rotate(grad_query * score_scale, cosine, -sine))
    kv_grad = wide(kv_total)
    turned_key = narrow(
        rotate(
            kv_grad[:, :, :HEAD_SIZE] * score_scale, cosine[: len(NEAR)], -sine[: len(NEAR)]
        )
    )
    near_grads = jnp.concatenate(
        [turned_query[: len(NEAR)], turned_key, kv_total[:, :, HEAD_SIZE:]], axis=-1
    ).reshape(4, token_rows, 3 * HEAD_SIZE)
    far_grads = turned_query[len(NEAR) :].reshape(4, token_rows, HEAD_SIZE)
    query_groups = jnp.concatenate([near_grads[:, :, :HEAD_SIZE], far_grads], axis=1)
    query_weight = attn_weight[:HEAD_SIZE]

    attn_out_rings = []

    def weight_grads(token):
        query_lefts = [after(query_groups[0], token)] + [query_groups[i] for i in range(1, 4)]
        grad_query_weight = row_product(query_lefts, in_groups, HEAD_SIZE, tile)
        grad_kv_weight = row_product(
            [after(near_grads[i, :, HEAD_SIZE:], token) for i in range(4)],
            in_groups,
            2 * HEAD_SIZE,
            tile,
        )
        return (grad_query_weight, grad_kv_weight)

    def weight_chunks(extras):
        grad_query_weight, grad_kv_weight = extras[0]
        low_rows, high_rows = after(got_low, grad_query_weight), after(got_high, grad_query_weight)
        out_lows_last = wide(pick(out_lows, side)) + wide(low_rows)
        out_highs_last = wide(pick(out_highs, across, 1)) + wide(high_rows)
        parts = jnp.concatenate([narrow(out_lows_last), narrow(out_highs_last)], axis=1)
        attn_out_rings.append(RingSum(parts, plane))
        query_stored = heads_to_chunks(
            grad_query_weight.reshape(HEAD_SIZE // chunk, chunk, width),
            query_rounds,
            place,
            query_planes,
        )
        kv_stored = heads_to_chunks(
            jnp.concatenate(
                [
                    grad_kv_weight[:HEAD_SIZE].reshape(HEAD_SIZE // chunk, chunk, width),
                    grad_kv_weight[HEAD_SIZE:].reshape(HEAD_SIZE // chunk, chunk, width),
                ],
                axis=1,
            ),
            kv_rounds,
            place,
            kv_planes,
        )
        attn_out_rings[0].start()
        stored = jnp.concatenate([query_stored, kv_stored[:, :chunk], kv_stored[:, chunk:]])
        return (stored, attn_out_rings[0].finish(), out_ring.finish())

    attn_rings = []

    def attn_hop(token):
        if not attn_rings:
            attn_rings.append(RingSum(extras_of[0][1][0], plane))
        attn_rings[0].start(token)
        return (attn_rings[0].finish(),)

    def hop_and_pieces(token):
        pieces = wide(ordered([after(rows, token) for rows in in_received], place))
        grads = pieces.transpose(3, 1, 0, 2).reshape(mlp_in.shape)
        attn_out_rings[0].start(token)
        return attn_hop(token) + (grads, attn_out_rings[0].finish())

    def hop_and_exchange(token):
        pieces = after(out_ring.finish_all(), token).reshape(2, unit, row_parts, row_share)
        pieces = pieces.transpose(0, 2, 1, 3).reshape(PLANE, unit, row_share)
        return attn_hop(token) + tuple(exchange_members(pieces, place))

    def project_back(index, token):
        near, far = near_grads[index], far_grads[index]
        if token is not None:
            near = after(near, token)
        return together(
            narrow(dot(near, attn_weight, 1, 0)), narrow(dot(far, query_weight, 1, 0))
        )

    extras_of = []

    def keep_chunks(extras):
        extras_of.append(extras)
        return weight_chunks(extras)

    grad_lowered_in, extras = reduce_plane(
        project_back, (weight_grads, hop_and_pieces, hop_and_exchange), keep_chunks
    )
    attn_rings[0].total = after(attn_rings[0].total, grad_lowered_in)
    attn_sum = attn_rings[0].finish_all()
    pieces = attn_sum.reshape(chunk, row_parts, row_share).transpose(1, 0, 2)
    attn_received = exchange_members(pieces, part)
    grad_source, grad_gain_in = norm_back(source, inverse_in, scales[0], grad_lowered_in)
    grad_input = grad_middle + grad_source

    grad_mlp_in = extras[2][1]
    attn_pieces = ordered(attn_received, part)
    grad_attn_out = wide(attn_out_rings[0].finish_all())
    grad_attn_in = wide(attn_pieces.reshape(attn_in.shape[1], row_share).T)
    out_pieces = wide(ordered(extras[3][1:], place))
    grad_mlp_out = out_pieces.transpose(2, 0, 1).reshape(mlp_out.shape)
    gain_total = sum_devices(
        jnp.stack([grad_gain_in, grad_gain_post_attn, grad_gain_pre_mlp, grad_gain_post])
    )
    grad_gains = pick(
        gain_total.reshape(gains.shape[1], row_parts, row_share).transpose(1, 2, 0), part
    )
    return (
        narrow(result),
        grad_input,
        grad_attn_in,
        grad_attn_out,
        grad_mlp_in,
        grad_mlp_out,
        grad_gains,
    )


def solution(mesh):
    placed = (
        P(("ctx", "fsdp"), None),
        P(("ctx", "fsdp"), None),
        P(),
        P(("ctx", "fsdp")),
        P("fsdp", "ctx"),
        P("fsdp", "ctx"),
        P("fsdp", "ctx"),
        P("fsdp", "ctx"),
        P("fsdp", None),
    )
    return jax.shard_map(
        body,
        mesh=mesh,
        in_specs=placed,
        out_specs=(
            P(("ctx", "fsdp"), None),
            P(("ctx", "fsdp"), None),
            P("fsdp", "ctx"),
            P("fsdp", "ctx"),
            P("fsdp", "ctx"),
            P("fsdp", "ctx"),
            P("fsdp", None),
        ),
        check_vma=False,
    )
```

```python
import functools
import math

import jax
import jax.numpy as jnp
from jax import lax
from jax.experimental import pallas as pl
from jax.experimental.pallas import tpu as pltpu
from jax.sharding import PartitionSpec as P

QUERY_HEADS = 8
KEY_VALUE_HEADS = 4
HEAD_SIZE = 256
LOOKBACK_SPAN = 4096
SEQUENCE_COUNT = 2


EPSILON = 1e-06
SOFT_CAP = 50.0
ROPE_BASE = 10000.0
AXES = ("ctx", "fsdp")
PLANE = 8
CORE, SIDE, ACROSS = 1, 2, 4
TANH_SCALE = HEAD_SIZE ** (-0.5) / SOFT_CAP
EXP2_SCALE = SOFT_CAP * math.log2(math.e)
VMEM_BYTES = 56 * 1024 * 1024


def inverse_rms(values):
    return lax.rsqrt(jnp.mean(values * values, axis=-1, keepdims=True) + EPSILON)


def norm_back(values, inverse, scale, upstream):
    scaled = upstream * scale
    through = inverse * scaled - values * inverse**3 * jnp.mean(
        scaled * values, axis=-1, keepdims=True
    )
    return (through, jnp.sum(upstream * values * inverse, axis=0))


def rotate(values, cosine, sine):
    half_width = values.shape[-1] // 2
    first_half = values[..., :half_width]
    second_half = values[..., half_width:]
    return jnp.concatenate(
        [
            first_half * cosine - second_half * sine,
            second_half * cosine + first_half * sine,
        ],
        axis=-1,
    )


def dot(left, right, left_axis, right_axis):
    return lax.dot_general(
        left,
        right,
        (((left_axis,), (right_axis,)), ((), ())),
        preferred_element_type=jnp.float32,
    )


def after(value, *others):
    return lax.optimization_barrier((value,) + others)[0]


def wide(values):
    return values.astype(jnp.float32)


def narrow(values):
    return values.astype(jnp.bfloat16)


def swap(values, mask):
    count = lax.axis_size(AXES)
    return lax.ppermute(values, AXES, [(i, i ^ mask) for i in range(count)])


def shift(values, steps=1):
    count = lax.axis_size(AXES)
    return lax.ppermute(values, AXES, [(i, (i + steps * PLANE) % count) for i in range(count)])


def route(values, targets):
    count = lax.axis_size(AXES)
    return lax.ppermute(
        values, AXES, [(i, i - i % PLANE + targets[i % PLANE]) for i in range(count)]
    )


def pick(stacked, index, axis=0):
    return lax.dynamic_index_in_dim(stacked, index, axis, keepdims=False)


def look_up(table, place):
    return pick(jnp.asarray(table, jnp.int32), place)


def exchange(pieces):
    far = swap(jnp.stack([pieces[mask ^ CORE] for mask in range(0, len(pieces), 2)]), CORE)
    received = []
    for i, mask in enumerate(range(0, len(pieces), 2)):
        both = jnp.stack([pieces[mask], far[i]])
        if mask:
            both = swap(both, mask)
        received.extend([both[0], both[1]])
    return received


def exchange_members(stacked, place):
    return exchange([pick(stacked, place ^ mask) for mask in range(stacked.shape[0])])


def ordered(received, place):
    whole = jnp.zeros((len(received),) + received[0].shape, received[0].dtype)
    for mask, rows in enumerate(received):
        whole = lax.dynamic_update_index_in_dim(whole, rows, place ^ mask, 0)
    return whole


NEAR = [(0, 0), (0, 1), (4, 0), (2, 1), (2, 0), (4, 1), (6, 0), (6, 1)]
FAR = [(mask ^ CORE, half) for mask, half in NEAR]


def together(*values):
    return lax.optimization_barrier(values)


def no_transfers(token, extras=None):
    return ()


def gather_plane(rows, work, beside=(no_transfers,) * 3, late=False):
    half = rows.shape[0] // 2
    low, high = rows[:half], rows[half:]
    groups, done, extras = [], [], []

    def add_group(near, far):
        groups.append(jnp.concatenate([near, far]))
        done.append(work(groups[-1], len(done)))

    other = swap(rows, CORE)
    first_low, first_high = swap(low, ACROSS), swap(high, SIDE)
    extra = beside[0](rows, extras)
    if late:
        first_low, first_high, *extra = together(first_low, first_high, *extra)
    else:
        add_group(rows, other)
        done[0], first_low, first_high, *extra = together(done[0], first_low, first_high, *extra)
    extras.append(extra)
    low, high = together(low, high, first_low)[:2]
    first_other = swap(jnp.concatenate([first_low, first_high]), CORE)
    second_low, second_high = swap(low, SIDE), swap(high, ACROSS)
    extra = beside[1](first_low, extras)
    if late:
        add_group(rows, other)
    add_group(jnp.concatenate([first_low, first_high]), first_other)
    done[1], first_low, first_high, second_low, second_high, *extra = together(
        done[1], first_low, first_high, second_low, second_high, *extra
    )
    extras.append(extra)
    second_other = swap(jnp.concatenate([second_low, second_high]), CORE)
    third_low, third_high = swap(first_low, SIDE), swap(first_high, ACROSS)
    extra = beside[2](second_low, extras)
    add_group(jnp.concatenate([second_low, second_high]), second_other)
    done[2], third_low, third_high, *extra = together(done[2], third_low, third_high, *extra)
    extras.append(extra)
    third = jnp.concatenate([third_low, third_high])
    add_group(third, swap(third, CORE))
    return groups, done, extras


def reduce_plane(work, beside=(no_transfers,) * 3, middle=None, kept=None):
    extras = []
    kept = {} if kept is None else kept

    def both(group, token):
        near, far = work(group, token)
        return wide(near) + wide(swap(far, CORE))

    third = narrow(both(3, None))
    half = third.shape[0] // 2
    got_low, got_high = swap(third[:half], SIDE), swap(third[half:], ACROSS)
    second = narrow(both(2, third))
    got_low, got_high, second, *extra = together(got_low, got_high, second, *beside[0](third))
    extras.append(extra)
    kept["down"] = extra[0] if extra else None
    if middle is not None:
        second, *extra = together(second, *middle(extras))
        extras.append(extra)
    own_low, own_high = swap(second[:half], SIDE), swap(second[half:], ACROSS)
    first = both(1, second)
    first = narrow(first + wide(jnp.concatenate([got_low, got_high])))
    own_low, own_high, first, *extra = together(own_low, own_high, first, *beside[1](second))
    extras.append(extra)
    kept["in"] = extra[0] if extra else None
    more_low, more_high = swap(first[:half], ACROSS), swap(first[half:], SIDE)
    own = both(0, first) + wide(jnp.concatenate([own_low, own_high]))
    more_low, more_high, own, *extra = together(more_low, more_high, own, *beside[2](first))
    extras.append(extra)
    return own + wide(jnp.concatenate([more_low, more_high])), extras


def sum_devices(values):
    for mask in (CORE, SIDE, ACROSS):
        values = values + swap(values, mask)
    total = values
    for steps in range(1, lax.axis_size(AXES) // PLANE):
        total = total + shift(values, steps)
    return total


class RingSum:
    def __init__(self, parts, plane, first=0, rows=None):
        self.parts, self.plane, self.planes = parts, plane, parts.shape[0]
        self.first, self.rows = first, rows or parts.shape[1]
        self.hops, self.moving = 0, None
        self.total = self.part(0)

    def part(self, step):
        at = (self.plane + 2 * self.planes - 1 - step) % self.planes
        size = (1, self.rows, self.parts.shape[2])
        return lax.dynamic_slice(self.parts, (at, self.first, 0), size)[0]

    def start(self, *others):
        if self.hops < self.planes - 1:
            self.moving = shift(after(self.total, *others) if others else self.total)

    def finish(self):
        if self.moving is not None:
            self.hops += 1
            self.total = narrow(wide(self.moving) + wide(self.part(self.hops)))
            self.moving = None
        return self.total

    def finish_all(self):
        self.finish()
        while self.hops < self.planes - 1:
            self.start()
            self.finish()
        return self.total


def matchings(edges):
    left, rounds = list(edges), []
    while left:
        owner = {}

        def settle(source, seen):
            for edge in left:
                if edge[0] == source and edge[1] not in seen:
                    seen.add(edge[1])
                    if edge[1] not in owner or settle(owner[edge[1]][0], seen):
                        owner[edge[1]] = edge
                        return True
            return False

        for source in range(PLANE):
            settle(source, set())
        found = sorted(owner.values())
        rounds.append(found)
        left = [edge for edge in left if edge not in found]
    return rounds


def chunk_edges(plane_count, columns, chunk, share):
    edges = []
    for source in range(PLANE):
        for at in range(plane_count):
            column = (2 * at + source // 4) * columns + source % 4 * chunk
            head = column // HEAD_SIZE
            for target in range(head * share, (head + 1) * share):
                edges.append((source, target, at, column % HEAD_SIZE // chunk))
    return edges


def chunks_to_heads(stored, rounds, place):
    spots = len(rounds)
    got = []
    for found in rounds:
        sent = pick(stored, look_up([edge[2] for edge in found], place))
        got.append(route(sent, [edge[1] for edge in found]))
    stacked = jnp.stack(got)
    order = []
    for spot in range(spots):
        table = [0] * PLANE
        for step, found in enumerate(rounds):
            for edge in found:
                if edge[3] == spot:
                    table[edge[1]] = step
        order.append(pick(stacked, look_up(table, place)))
    return order


def heads_to_chunks(heads, rounds, place, plane_count):
    got = []
    for found in rounds:
        back, spot = [0] * PLANE, [0] * PLANE
        for source, target, _, position in found:
            back[target], spot[target] = source, position
        got.append(route(pick(heads, look_up(spot, place)), back))
    stacked = jnp.stack(got)
    chunks = []
    for at in range(plane_count):
        tables = []
        for source in range(PLANE):
            tables.append(
                [
                    step
                    for step, found in enumerate(rounds)
                    for edge in found
                    if edge[0] == source and edge[2] == at
                ]
            )
        terms = [
            pick(stacked, look_up([table[i] for table in tables], place))
            for i in range(len(tables[0]))
        ]
        total = terms[0]
        if len(terms) > 1:
            total = narrow(sum(wide(term) for term in terms))
        chunks.append(total)
    return jnp.stack(chunks)


def row_product_kernel(count, *refs):
    out, total = refs[-2:]
    total[...] = dot(refs[0][...], refs[count][...], 0, 0)
    for i in range(1, count):
        total[...] += dot(refs[i][...], refs[count + i][...], 0, 0)
    out[...] = total[...].astype(out.dtype)


def row_product(lefts, rights, left_tile, right_tile):
    count = len(lefts)
    height, width = lefts[0].shape[1], rights[0].shape[1]
    depths = [left.shape[0] for left in lefts]
    return pl.pallas_call(
        functools.partial(row_product_kernel, count),
        out_shape=jax.ShapeDtypeStruct((height, width), jnp.bfloat16),
        grid=(height // left_tile, width // right_tile),
        in_specs=[pl.BlockSpec((depth, left_tile), lambda i, j: (0, i)) for depth in depths]
        + [pl.BlockSpec((depth, right_tile), lambda i, j: (0, j)) for depth in depths],
        out_specs=pl.BlockSpec((left_tile, right_tile), lambda i, j: (i, j)),
        scratch_shapes=[pltpu.VMEM((left_tile, right_tile), jnp.float32)],
        compiler_params=pltpu.CompilerParams(vmem_limit_bytes=VMEM_BYTES),
        cost_estimate=pl.CostEstimate(
            flops=2 * sum(depths) * height * width,
            bytes_accessed=2 * sum(depths) * (height + width) + 2 * height * width,
            transcendentals=0,
        ),
    )(*lefts, *rights)


def out_kernel(part, rows_ref, weight_ref, out_ref):
    at = pl.program_id(0)
    total = dot(rows_ref[0], weight_ref[0, 0], 1, 1)
    for head in range(1, rows_ref.shape[0]):
        total += dot(rows_ref[head], weight_ref[head, 0], 1, 1)
    for i in range(out_ref.shape[1] // part):

        @pl.when(at == i)
        def _():
            out_ref[:, i * part : (i + 1) * part] = total


def out_product(rows, weight):
    heads, count, size = rows.shape
    _, parts, part, _ = weight.shape
    return pl.pallas_call(
        functools.partial(out_kernel, part),
        out_shape=jax.ShapeDtypeStruct((count, parts * part), jnp.float32),
        grid=(parts,),
        in_specs=[
            pl.BlockSpec((heads, count, size), lambda i: (0, 0, 0)),
            pl.BlockSpec((heads, 1, part, size), lambda i: (0, i, 0, 0)),
        ],
        out_specs=pl.BlockSpec((count, parts * part), lambda i: (0, 0)),
        compiler_params=pltpu.CompilerParams(vmem_limit_bytes=VMEM_BYTES),
        cost_estimate=pl.CostEstimate(
            flops=2 * count * heads * size * parts * part,
            bytes_accessed=2 * heads * size * (count + parts * part) + 4 * count * parts * part,
            transcendentals=0,
        ),
    )(rows, weight)


def out_back_kernel(rows_ref, weight_ref, out_ref):
    part = weight_ref.shape[2]
    total = dot(rows_ref[:, :part], weight_ref[0, 0], 1, 0)
    for i in range(1, weight_ref.shape[1]):
        total += dot(rows_ref[:, i * part : (i + 1) * part], weight_ref[0, i], 1, 0)
    out_ref[0] = total.astype(out_ref.dtype)


def out_back_product(rows, weight):
    count, width = rows.shape
    heads, parts, part, size = weight.shape
    return pl.pallas_call(
        out_back_kernel,
        out_shape=jax.ShapeDtypeStruct((heads, count, size), jnp.bfloat16),
        grid=(heads,),
        in_specs=[
            pl.BlockSpec((count, width), lambda i: (0, 0)),
            pl.BlockSpec((1, parts, part, size), lambda i: (i, 0, 0, 0)),
        ],
        out_specs=pl.BlockSpec((1, count, size), lambda i: (i, 0, 0)),
        compiler_params=pltpu.CompilerParams(vmem_limit_bytes=VMEM_BYTES),
        cost_estimate=pl.CostEstimate(
            flops=2 * count * heads * size * width,
            bytes_accessed=2 * heads * size * (count + width) + 2 * count * width,
            transcendentals=0,
        ),
    )(rows, weight)


def out_grad_kernel(rows_ref, heads_ref, out_ref):
    total = dot(rows_ref[...], heads_ref[0], 0, 0).astype(out_ref.dtype)
    part = out_ref.shape[3]
    for side in range(2):
        for core in range(2):
            at = (2 * side + core) * part
            out_ref[core, side, 0] = total[at : at + part]


def out_grad_product(rows, by_head):
    count, width = rows.shape
    heads, _, size = by_head.shape
    part = width // 4
    return pl.pallas_call(
        out_grad_kernel,
        out_shape=jax.ShapeDtypeStruct((2, 2, heads, part, size), jnp.bfloat16),
        grid=(heads,),
        in_specs=[
            pl.BlockSpec((count, width), lambda i: (0, 0)),
            pl.BlockSpec((1, count, size), lambda i: (i, 0, 0)),
        ],
        out_specs=pl.BlockSpec((2, 2, 1, part, size), lambda i: (0, 0, i, 0, 0)),
        compiler_params=pltpu.CompilerParams(vmem_limit_bytes=VMEM_BYTES),
        cost_estimate=pl.CostEstimate(
            flops=2 * count * heads * size * width,
            bytes_accessed=2 * heads * size * (count + width) + 2 * count * width,
            transcendentals=0,
        ),
    )(rows, by_head)


def pair_lists(query_ids, key_ids, blocks_per_seq, span_blocks):
    query_seq, query_at = query_ids // blocks_per_seq, query_ids % blocks_per_seq
    key_seq, key_at = key_ids // blocks_per_seq, key_ids % blocks_per_seq
    rows = key_ids.shape[0]
    distance = (query_at[None, :, None] - key_at[:, None, :]).reshape(rows, -1)
    same = (query_seq[None, :, None] == key_seq[:, None, :]).reshape(rows, -1)
    whole = same & (distance > 0) & (distance < span_blocks)
    edged = same & ((distance == 0) | (distance == span_blocks))
    kind = whole.astype(jnp.int32) + 2 * edged.astype(jnp.int32)
    total = distance.shape[1]
    index = jnp.arange(total, dtype=jnp.int32)
    earlier = (index[None, :] < index[:, None])[None] & (kind[:, None, :] == kind[:, :, None])
    rank = jnp.sum(earlier.astype(jnp.int32), axis=2)
    count_whole = jnp.sum(whole.astype(jnp.int32), axis=1, keepdims=True)
    count_edged = jnp.sum(edged.astype(jnp.int32), axis=1, keepdims=True)
    spot = jnp.where(kind == 1, rank, jnp.where(kind == 2, count_whole + rank, -1))
    code = index * 2 + (distance == span_blocks).astype(jnp.int32)
    hit = spot[:, :, None] == index[None, None, :]
    entries = jnp.sum(jnp.where(hit, code[:, :, None], 0), axis=1)
    return jnp.concatenate([count_whole, count_edged, entries], axis=1).astype(jnp.int32)


def run_pairs(list_ref, row, key_count, unroll, visit):
    whole = list_ref[row, 0]
    edged = list_ref[row, 1]

    def decode(position):
        code = list_ref[row, 2 + position]
        pair = code // 2
        return pair // key_count, pair % key_count, code % 2

    def several(step, carry):
        found = [decode(step * unroll + i) for i in range(unroll)]
        visit([f[0] for f in found], [f[1] for f in found], None)
        return carry

    def single(position, carry):
        i, j, _ = decode(position)
        visit([i], [j], None)
        return carry

    def masked(position, carry):
        i, j, far = decode(position)
        visit([i], [j], far)
        return carry

    groups = whole // unroll
    lax.fori_loop(0, groups, several, 0)
    lax.fori_loop(groups * unroll, whole, single, 0)
    lax.fori_loop(whole, whole + edged, masked, 0)


def attend_kernel(first, unroll, list_ref, query_hbm, own_hbm, other_hbm, *rest):
    if first:
        state_hbm = None
        out_hbm, query, own, other, state, sems = rest
    else:
        state_hbm, out_hbm, query, own, other, state, sems = rest
    copies = [
        pltpu.make_async_copy(query_hbm, query, sems.at[0]),
        pltpu.make_async_copy(own_hbm, own, sems.at[1]),
        pltpu.make_async_copy(other_hbm, other, sems.at[2]),
    ]
    if not first:
        copies.append(pltpu.make_async_copy(state_hbm, state, sems.at[3]))
    for copy in copies:
        copy.start()
    if first:
        state[...] = jnp.zeros_like(state)
    for copy in copies:
        copy.wait()
    rows = query.shape[1]
    lane = lax.broadcasted_iota(jnp.int32, (rows, 128), 1)

    def visit_in(keys):
        def visit(query_at, key_at, far):
            scores = [
                dot(query[i], keys[j, :, :HEAD_SIZE], 1, 1) for i, j in zip(query_at, key_at)
            ]
            for i, j, score in zip(query_at, key_at, scores):
                weights = jnp.exp2(EXP2_SCALE * jnp.tanh(score * TANH_SCALE))
                if far is not None:
                    spacing = (
                        lax.broadcasted_iota(jnp.int32, weights.shape, 0)
                        - lax.broadcasted_iota(jnp.int32, weights.shape, 1)
                        + far * LOOKBACK_SPAN
                    )
                    live = (spacing >= 0) & (spacing < LOOKBACK_SPAN)
                    weights = jnp.where(live, weights, 0.0)
                if rows % 128 == 0:
                    part = weights[:, :128]
                    for k in range(1, rows // 128):
                        part = part + weights[:, k * 128 : (k + 1) * 128]
                else:
                    part = jnp.where(lane == 0, jnp.sum(weights, axis=1, keepdims=True), 0.0)
                state[i, :, HEAD_SIZE:] += part
                state[i, :, :HEAD_SIZE] += dot(
                    weights.astype(jnp.bfloat16), keys[j, :, HEAD_SIZE:], 1, 0
                )

        return visit

    key_count = own.shape[0]
    run_pairs(list_ref, 0, key_count, unroll, visit_in(own))
    run_pairs(list_ref, 1, key_count, unroll, visit_in(other))
    out = pltpu.make_async_copy(state, out_hbm, sems.at[4])
    out.start()
    out.wait()


def attend(lists, query, own, other, state):
    first = state is None
    blocks, rows, _ = query.shape
    shape = (blocks, rows, HEAD_SIZE + 128)
    operands = (query, own, other) if first else (query, own, other, state)
    return pl.pallas_call(
        functools.partial(attend_kernel, first, 4),
        out_shape=jax.ShapeDtypeStruct(shape, jnp.float32),
        grid_spec=pltpu.PrefetchScalarGridSpec(
            num_scalar_prefetch=1,
            grid=(1,),
            in_specs=[pl.BlockSpec(memory_space=pl.ANY)] * len(operands),
            out_specs=pl.BlockSpec(memory_space=pl.ANY),
            scratch_shapes=[
                pltpu.VMEM(query.shape, jnp.bfloat16),
                pltpu.VMEM(own.shape, jnp.bfloat16),
                pltpu.VMEM(other.shape, jnp.bfloat16),
                pltpu.VMEM(shape, jnp.float32),
                pltpu.SemaphoreType.DMA((5,)),
            ],
        ),
        compiler_params=pltpu.CompilerParams(vmem_limit_bytes=VMEM_BYTES),
        cost_estimate=pl.CostEstimate(
            flops=60 * 4 * rows * rows * HEAD_SIZE,
            bytes_accessed=14 * 1024 * 1024,
            transcendentals=60 * 2 * rows * rows,
        ),
    )(lists, *operands)


def attend_back_kernel(
    first,
    unroll,
    list_ref,
    query_hbm,
    grad_hbm,
    term_hbm,
    own_hbm,
    other_hbm,
    *rest,
):
    if first:
        state_hbm = None
    else:
        state_hbm, *rest = rest
    (
        out_hbm,
        own_out_hbm,
        other_out_hbm,
        query,
        grad,
        term,
        own,
        other,
        state,
        own_grad,
        other_grad,
        own_low,
        other_low,
        sems,
    ) = rest
    copies = [
        pltpu.make_async_copy(query_hbm, query, sems.at[0]),
        pltpu.make_async_copy(grad_hbm, grad, sems.at[1]),
        pltpu.make_async_copy(term_hbm, term, sems.at[2]),
        pltpu.make_async_copy(own_hbm, own, sems.at[3]),
        pltpu.make_async_copy(other_hbm, other, sems.at[4]),
    ]
    if not first:
        copies.append(pltpu.make_async_copy(state_hbm, state, sems.at[5]))
    for copy in copies:
        copy.start()
    if first:
        state[...] = jnp.zeros_like(state)
    own_grad[...] = jnp.zeros_like(own_grad)
    other_grad[...] = jnp.zeros_like(other_grad)
    for copy in copies:
        copy.wait()

    def visit_in(keys, key_grad):
        def visit(query_at, key_at, far):
            scores = []
            slopes = []
            for i, j in zip(query_at, key_at):
                scores.append(dot(keys[j, :, :HEAD_SIZE], query[i], 1, 1))
                slopes.append(dot(keys[j, :, HEAD_SIZE:], grad[i], 1, 1))
            for i, j, score, slope in zip(query_at, key_at, scores, slopes):
                bent = jnp.tanh(score * TANH_SCALE)
                weights = jnp.exp2(EXP2_SCALE * bent)
                if far is not None:
                    spacing = (
                        lax.broadcasted_iota(jnp.int32, weights.shape, 1)
                        - lax.broadcasted_iota(jnp.int32, weights.shape, 0)
                        + far * LOOKBACK_SPAN
                    )
                    live = (spacing >= 0) & (spacing < LOOKBACK_SPAN)
                    weights = jnp.where(live, weights, 0.0)
                grad_scores = (
                    (slope + term[i]) * (weights * (1.0 - bent * bent))
                ).astype(jnp.bfloat16)
                key_grad[j, :, :HEAD_SIZE] += dot(grad_scores, query[i], 1, 0)
                key_grad[j, :, HEAD_SIZE:] += dot(weights.astype(jnp.bfloat16), grad[i], 1, 0)
                state[i] += dot(grad_scores, keys[j, :, :HEAD_SIZE], 0, 0)

        return visit

    key_count = own.shape[0]
    run_pairs(list_ref, 1, key_count, unroll, visit_in(other, other_grad))
    other_low[...] = other_grad[...].astype(jnp.bfloat16)
    other_out = pltpu.make_async_copy(other_low, other_out_hbm, sems.at[6])
    other_out.start()
    run_pairs(list_ref, 0, key_count, unroll, visit_in(own, own_grad))
    own_low[...] = own_grad[...].astype(jnp.bfloat16)
    own_out = pltpu.make_async_copy(own_low, own_out_hbm, sems.at[7])
    own_out.start()
    out = pltpu.make_async_copy(state, out_hbm, sems.at[8])
    out.start()
    other_out.wait()
    own_out.wait()
    out.wait()


def attend_back(lists, query, grad, term, own, other, state):
    first = state is None
    blocks, rows, _ = query.shape
    operands = (query, grad, term, own, other)
    if not first:
        operands = operands + (state,)
    return pl.pallas_call(
        functools.partial(attend_back_kernel, first, 2),
        out_shape=[
            jax.ShapeDtypeStruct(query.shape, jnp.float32),
            jax.ShapeDtypeStruct(own.shape, jnp.bfloat16),
            jax.ShapeDtypeStruct(other.shape, jnp.bfloat16),
        ],
        grid_spec=pltpu.PrefetchScalarGridSpec(
            num_scalar_prefetch=1,
            grid=(1,),
            in_specs=[pl.BlockSpec(memory_space=pl.ANY)] * len(operands),
            out_specs=[pl.BlockSpec(memory_space=pl.ANY)] * 3,
            scratch_shapes=[
                pltpu.VMEM(query.shape, jnp.bfloat16),
                pltpu.VMEM(query.shape, jnp.bfloat16),
                pltpu.VMEM(term.shape, jnp.float32),
                pltpu.VMEM(own.shape, jnp.bfloat16),
                pltpu.VMEM(other.shape, jnp.bfloat16),
                pltpu.VMEM(query.shape, jnp.float32),
                pltpu.VMEM(own.shape, jnp.float32),
                pltpu.VMEM(other.shape, jnp.float32),
                pltpu.VMEM(own.shape, jnp.bfloat16),
                pltpu.VMEM(other.shape, jnp.bfloat16),
                pltpu.SemaphoreType.DMA((9,)),
            ],
        ),
        compiler_params=pltpu.CompilerParams(vmem_limit_bytes=VMEM_BYTES),
        cost_estimate=pl.CostEstimate(
            flops=60 * 10 * rows * rows * HEAD_SIZE,
            bytes_accessed=24 * 1024 * 1024,
            transcendentals=60 * 2 * rows * rows,
        ),
    )(lists, *operands)


def body(inputs, cotangent, block_ids, positions, attn_in, attn_out, mlp_in, mlp_out, gains):
    token_rows, width = inputs.shape
    block = token_rows // 2
    devices = lax.axis_size(AXES)
    ctx_count, row_parts = lax.axis_size("ctx"), lax.axis_size("fsdp")
    planes = devices // PLANE
    blocks_per_seq = 2 * devices // SEQUENCE_COUNT
    span_blocks = LOOKBACK_SPAN // block
    score_scale = HEAD_SIZE ** (-0.5)
    me = lax.axis_index(AXES)
    place, plane = me % PLANE, me // PLANE
    part = place % row_parts
    row_share = attn_in.shape[0]
    unit = mlp_out.shape[1] // PLANE
    chunk = attn_in.shape[1] // row_parts
    order = NEAR + FAR

    gain_parts = ordered([gains.T] + [swap(gains.T, mask) for mask in range(1, row_parts)], part)
    scales = wide(gain_parts.transpose(1, 0, 2).reshape(gains.shape[1], width))
    source = wide(inputs)
    inverse_in = inverse_rms(source)
    lowered_in = narrow(source * inverse_in * scales[0])

    gathered_out = lax.all_gather(attn_out, AXES, axis=0)
    in_pieces = mlp_in.T.reshape(2, PLANE, unit, row_share).transpose(1, 0, 2, 3)
    in_received = exchange_members(in_pieces, place)
    attn_pieces = exchange_members(attn_in.T.reshape(row_parts, chunk, row_share), part)
    in_chunk = ordered(attn_pieces, part).transpose(1, 0, 2).reshape(chunk, width)
    *in_received, first_stored = together(*in_received, shift(in_chunk))
    stored = [in_chunk, first_stored]
    for step in range(2, planes):
        stored.append(shift(stored[-1]))
    in_share = (
        ordered(in_received, place)
        .reshape(2, row_parts, 2, unit, row_share)
        .transpose(0, 2, 3, 1, 4)
        .reshape(4 * unit, width)
    )
    lowered_in = after(lowered_in, first_stored)
    block_ids = after(block_ids, in_chunk)

    def ids_of(which_plane, slots):
        masks = jnp.asarray([mask for mask, _ in slots], jnp.int32)
        sides = jnp.asarray([half for _, half in slots], jnp.int32)
        at = 2 * (which_plane[:, None] * PLANE + (place ^ masks)[None, :]) + sides[None, :]
        slot = jnp.arange(block_ids.shape[0], dtype=jnp.int32)
        return jnp.sum(jnp.where(at[:, :, None] == slot, block_ids, 0), axis=2)

    stage_planes = (plane + planes - jnp.arange(planes, dtype=jnp.int32)) % planes
    stage_ids = ids_of(stage_planes, order)
    query_ids = stage_ids[0]
    lists = pair_lists(
        query_ids, stage_ids.reshape(2 * planes, len(NEAR)), blocks_per_seq, span_blocks
    ).reshape(planes, 2, -1)
    half_width = HEAD_SIZE // 2
    frequency = ROPE_BASE ** (-2.0 * jnp.arange(half_width, dtype=jnp.float32) / HEAD_SIZE)
    base_angle = wide(query_ids % blocks_per_seq * block)[:, None, None] * frequency
    step_angle = jnp.arange(block, dtype=jnp.float32)[:, None] * frequency
    base_cosine, base_sine = jnp.cos(base_angle), jnp.sin(base_angle)
    step_cosine, step_sine = jnp.cos(step_angle), jnp.sin(step_angle)
    cosine = base_cosine * step_cosine - base_sine * step_sine
    sine = base_sine * step_cosine + base_cosine * step_sine

    cut = 2 * unit
    in_halves = [[], []]
    out_shares = []
    in_all = jnp.zeros((planes * 4 * unit, width), jnp.bfloat16)
    out_all = jnp.zeros((planes * 2 * unit, width), jnp.bfloat16)

    def next_in(which):
        def start(token, extras=None):
            in_halves[which].append(shift(after(in_halves[which][-1], token)))
            return (in_halves[which][-1],)

        return start

    def next_out(token, extras=None):
        out_shares.append(shift(after(out_shares[-1], token)))
        return (out_shares[-1],)

    query_planes, kv_planes = planes // 2, planes // 4
    query_rounds = matchings(chunk_edges(query_planes, attn_in.shape[1], chunk, 1))
    kv_rounds = matchings(
        chunk_edges(kv_planes, attn_in.shape[1], chunk, QUERY_HEADS // KEY_VALUE_HEADS)
    )

    def weights_together(token, extras):
        whole = jnp.zeros((planes, chunk, width), jnp.bfloat16)
        for step, rows in enumerate(stored):
            whole = lax.dynamic_update_index_in_dim(whole, rows, (plane - step) % planes, 0)
        return (whole, in_share)

    attn_weights = []

    def weights_to_heads(token, extras):
        whole, share = extras[0]
        in_halves[0].append(share[:cut])
        in_halves[1].append(share[cut:])
        query_chunks = chunks_to_heads(whole[:query_planes], query_rounds, place)
        kv_chunks = chunks_to_heads(
            jnp.concatenate(
                [whole[query_planes : query_planes + kv_planes], whole[query_planes + kv_planes :]],
                axis=1,
            ),
            kv_rounds,
            place,
        )
        attn_weights.append(
            jnp.concatenate(
                query_chunks
                + [both[:chunk] for both in kv_chunks]
                + [both[chunk:] for both in kv_chunks]
            )
        )
        return next_in(0)(token) + next_in(1)(token) + (gathered_out, lists, cosine, sine)

    in_groups, projected, extras = gather_plane(
        lowered_in,
        lambda group, index: narrow(dot(group, attn_weights[0], 1, 1)),
        (weights_together, weights_to_heads, next_in(0)),
        late=True,
    )
    projected[3] = together(projected[3], *next_in(1)(extras[2][0]))[0]
    attn_weight = attn_weights[0]
    gathered_out, lists, cosine, sine = extras[1][2:]

    def split_groups(groups):
        near = jnp.concatenate([group[:token_rows] for group in groups])
        far = jnp.concatenate([group[token_rows:] for group in groups])
        return [rows.reshape(len(NEAR), block, rows.shape[1]) for rows in (near, far)]

    near_rows, far_rows = split_groups(projected)
    query_parts, kv_parts = [], []
    for rows, low, high in ((near_rows, 0, len(NEAR)), (far_rows, len(NEAR), 2 * len(NEAR))):
        turns = (cosine[low:high], sine[low:high])
        query_parts.append(narrow(rotate(wide(rows[:, :, :HEAD_SIZE]), *turns)))
        kv_parts.append(
            jnp.concatenate(
                [
                    narrow(rotate(wide(rows[:, :, HEAD_SIZE : 2 * HEAD_SIZE]), *turns)),
                    rows[:, :, 2 * HEAD_SIZE :],
                ],
                axis=-1,
            )
        )
    own_kv, other_kv = kv_parts
    query = jnp.concatenate(query_parts)

    kv_stages = [(own_kv, other_kv)]
    state = None
    for step in range(planes):
        own_kv, other_kv = kv_stages[step]
        state_next = attend(lists[step], query, own_kv, other_kv, state)
        if step < planes - 1:
            moving = shift(own_kv)
            beside = []
            if step == 1:
                out_pieces = after(mlp_out.T, own_kv).reshape(PLANE, unit, row_share)
                beside = exchange_members(out_pieces, place)
            state_next, moving, *beside = together(state_next, moving, *beside)
            if step == 1:
                out_shares.append(
                    ordered(beside, place)
                    .reshape(2, row_parts, unit, row_share)
                    .transpose(0, 2, 1, 3)
                    .reshape(2 * unit, width)
                )
            kv_stages.append((moving, swap(moving, CORE)))
        else:
            state_next, _ = together(state_next, *next_in(0)(own_kv))
        state = state_next
    totals = jnp.sum(state[:, :, HEAD_SIZE:], axis=-1, keepdims=True)
    attended = state[:, :, :HEAD_SIZE] / totals
    attended_rows = narrow(attended)

    def member_rows(blocks, mask):
        return jnp.concatenate([blocks[order.index((mask, 0))], blocks[order.index((mask, 1))]])

    def blocks_of(received):
        return jnp.stack(
            [received[mask][half * block : (half + 1) * block] for mask, half in order]
        )

    next_in(1)(attended_rows)
    attended_heads = ordered(
        exchange([member_rows(attended_rows, mask) for mask in range(PLANE)]), place
    )
    attended_heads = after(attended_heads, in_halves[1][-1])
    gathered_out = (
        gathered_out.reshape((QUERY_HEADS, -1, row_parts) + attn_out.shape)
        .transpose(0, 2, 3, 1, 4)
        .reshape(QUERY_HEADS, row_parts, row_share, HEAD_SIZE)
    )

    branch = out_product(attended_heads, gathered_out)
    inverse_branch = inverse_rms(branch)
    middle = source + branch * inverse_branch * scales[1]
    inverse_mid = inverse_rms(middle)
    lowered_mid = narrow(middle * inverse_mid * scales[2])
    hidden_width = planes * 2 * unit
    for which, shares in enumerate(in_halves):
        while len(shares) < planes:
            shares.append(shift(shares[-1]))
        for step, share in enumerate(shares):
            at = (plane - step) % planes * 4 * unit + which * cut
            in_all = lax.dynamic_update_slice_in_dim(in_all, share, at, 0)

    def gate_up_of(group, index):
        return narrow(dot(group, in_all, 1, 1))

    mid_groups, gate_ups, _ = gather_plane(lowered_mid, gate_up_of, (next_out,) * 3)
    while len(out_shares) < planes:
        out_shares.append(shift(out_shares[-1]))
    for step, share in enumerate(out_shares):
        at = (plane - step) % planes * 2 * unit
        out_all = lax.dynamic_update_slice_in_dim(out_all, share, at, 0)

    def activate(gate_up):
        gate = wide(gate_up[:, :hidden_width])
        up = wide(gate_up[:, hidden_width:])
        return jax.nn.gelu(gate, approximate=True) * up

    hiddens = [narrow(activate(gate_up)) for gate_up in gate_ups]

    def reduce_groups(groups, weight, *rest):
        def work(index, token):
            group = groups[index] if token is None else after(groups[index], token)
            partial = together(narrow(dot(group, weight, 1, 0)))[0]
            return partial[:token_rows], partial[token_rows:]

        return reduce_plane(work, *rest)

    down_branch, _ = reduce_groups(hiddens, out_all)
    inverse_down = inverse_rms(down_branch)
    result = middle + down_branch * inverse_down * scales[3]
    upstream = wide(cotangent)
    grad_down, grad_gain_post = norm_back(down_branch, inverse_down, scales[3], upstream)
    grad_down_low = narrow(grad_down)

    def activate_back(gate_up, grad_hidden):
        gate = wide(gate_up[:, :hidden_width])
        up = wide(gate_up[:, hidden_width:])
        _, back = jax.vjp(lambda g, u: jax.nn.gelu(g, approximate=True) * u, gate, up)
        grad_gate, grad_up = back(grad_hidden)
        return narrow(jnp.concatenate([grad_gate, grad_up], axis=1))

    def grad_gate_up_of(group, index):
        return activate_back(gate_ups[index], dot(group, out_all, 1, 1))

    down_groups, grad_gate_ups, _ = gather_plane(grad_down_low, grad_gate_up_of)

    tile = 768 if width % 768 == 0 else width
    rings = {}

    def out_grads(token):
        grads = row_product([after(hiddens[0], token)] + hiddens[1:], down_groups, 384, tile)
        return (grads,)

    def in_grads(token):
        rings["out"] = RingSum(rings["down"].reshape(planes, 2 * unit, width), plane)
        rings["out"].start(token)
        rings["out"].finish()
        rings["out"].start()
        grads = row_product(
            [after(grad_gate_ups[0], token)] + grad_gate_ups[1:], mid_groups, tile, tile
        )
        return (grads, rings["out"].finish())

    def first_low(token):
        parts = rings["in"].reshape(planes, 4 * unit, width)
        rings["low"] = RingSum(parts, plane, 0, cut)
        rings["high"] = RingSum(parts, plane, cut, cut)
        rings["low"].start(token)
        return (rings["low"].finish(),)

    grad_lowered_mid, _ = reduce_groups(
        grad_gate_ups, in_all, (out_grads, in_grads, first_low), None, rings
    )
    out_ring, low_ring, high_ring = rings["out"], rings["low"], rings["high"]

    high_ring.start(grad_lowered_mid)
    grad_through_mid, grad_gain_pre_mlp = norm_back(
        middle, inverse_mid, scales[2], grad_lowered_mid
    )
    grad_middle = upstream + grad_through_mid
    grad_branch, grad_gain_post_attn = norm_back(branch, inverse_branch, scales[1], grad_middle)
    grad_branch_low = narrow(grad_branch)
    grad_heads = out_back_product(grad_branch_low, gathered_out)
    grad_heads = after(grad_heads, high_ring.finish())
    low_ring.start(grad_heads)
    grad_heads = list(exchange_members(grad_heads, place))
    grad_heads[0] = after(grad_heads[0], low_ring.finish())
    high_ring.start(grad_heads[0])
    grad_rows = wide(blocks_of(grad_heads))
    row_terms = -jnp.sum(grad_rows * attended, axis=-1) / totals[..., 0]
    grad_summed = narrow(grad_rows / totals)
    grad_summed = after(grad_summed, high_ring.finish())
    row_terms = row_terms[:, None, :]

    grad_query, kv_total = None, None
    core, side, across = place % 2, place // 2 % 2, place // 4
    for step in range(planes):
        stage = (step + 1) % planes
        own_kv, other_kv = kv_stages[stage]
        if step == 0:
            low_ring.start(grad_summed)
            out_parts = out_grad_product(after(grad_branch_low, grad_summed), attended_heads)
            high_ring.start(grad_summed)
            beside = [low_ring.finish(), out_parts, high_ring.finish()]
        else:
            beside = [shift(kv_total)]
            grad_query = after(grad_query, kv_total)
        if step == 1:
            beside.append(swap(pick(after(out_parts, kv_total), 1 - core), CORE))
        if step == 2:
            beside.append(swap(pick(out_lows, 1 - across, 2), ACROSS))
            beside.append(swap(pick(out_highs, 1 - side), SIDE))
        if step == planes - 1:
            in_sum = jnp.concatenate([low_ring.finish_all(), high_ring.finish_all()])
            in_pieces = after(in_sum, kv_total).reshape(2, 2, unit, row_parts, row_share)
            in_pieces = in_pieces.transpose(0, 3, 1, 2, 4).reshape(PLANE, 2, unit, row_share)
            beside.extend(exchange_members(in_pieces, place))
        grad_query, own_grad, other_grad, *beside = together(
            *attend_back(
                lists[stage], query, grad_summed, row_terms, own_kv, other_kv, grad_query
            ),
            *beside,
        )
        total = wide(own_grad) + wide(swap(other_grad, CORE))
        if step:
            total = total + wide(beside[0])
        kv_total = narrow(total)
        if step == 0:
            out_parts = beside[1].reshape(2, 2, QUERY_HEADS, row_share, -1, attn_out.shape[1])
            out_parts = out_parts.transpose(0, 1, 2, 4, 3, 5)
            out_parts = out_parts.reshape(2, 2, planes, 2, row_share, attn_out.shape[1])
        if step == 1:
            out_sums = narrow(wide(pick(out_parts, core)) + wide(beside[1]))
            out_lows = out_sums[:, :, :, : row_share // 2]
            out_highs = out_sums[:, :, :, row_share // 2 :]
        if step == 2:
            out_lows = narrow(wide(pick(out_lows, across, 2)) + wide(beside[1]))
            out_highs = narrow(wide(pick(out_highs, side)) + wide(beside[2]))
    in_received = beside[1:]
    out_ring.start(beside[0])
    got_low = swap(pick(after(out_lows, beside[0]), 1 - side), SIDE)
    got_high = swap(pick(after(out_highs, beside[0]), 1 - across, 1), ACROSS)

    turned_query = narrow(rotate(grad_query * score_scale, cosine, -sine))
    kv_grad = wide(kv_total)
    turned_key = narrow(
        rotate(
            kv_grad[:, :, :HEAD_SIZE] * score_scale, cosine[: len(NEAR)], -sine[: len(NEAR)]
        )
    )
    near_grads = jnp.concatenate(
        [turned_query[: len(NEAR)], turned_key, kv_total[:, :, HEAD_SIZE:]], axis=-1
    ).reshape(4, token_rows, 3 * HEAD_SIZE)
    far_grads = turned_query[len(NEAR) :].reshape(4, token_rows, HEAD_SIZE)
    query_groups = jnp.concatenate([near_grads[:, :, :HEAD_SIZE], far_grads], axis=1)
    query_weight = attn_weight[:HEAD_SIZE]

    attn_out_rings = []

    def weight_grads(token):
        query_lefts = [after(query_groups[0], token)] + [query_groups[i] for i in range(1, 4)]
        grad_query_weight = row_product(query_lefts, in_groups, HEAD_SIZE, tile)
        grad_kv_weight = row_product(
            [after(near_grads[i, :, HEAD_SIZE:], token) for i in range(4)],
            in_groups,
            2 * HEAD_SIZE,
            tile,
        )
        return (grad_query_weight, grad_kv_weight)

    def weight_chunks(extras):
        grad_query_weight, grad_kv_weight = extras[0]
        low_rows, high_rows = after(got_low, grad_query_weight), after(got_high, grad_query_weight)
        out_lows_last = wide(pick(out_lows, side)) + wide(low_rows)
        out_highs_last = wide(pick(out_highs, across, 1)) + wide(high_rows)
        parts = jnp.concatenate([narrow(out_lows_last), narrow(out_highs_last)], axis=1)
        attn_out_rings.append(RingSum(parts, plane))
        query_stored = heads_to_chunks(
            grad_query_weight.reshape(HEAD_SIZE // chunk, chunk, width),
            query_rounds,
            place,
            query_planes,
        )
        kv_stored = heads_to_chunks(
            jnp.concatenate(
                [
                    grad_kv_weight[:HEAD_SIZE].reshape(HEAD_SIZE // chunk, chunk, width),
                    grad_kv_weight[HEAD_SIZE:].reshape(HEAD_SIZE // chunk, chunk, width),
                ],
                axis=1,
            ),
            kv_rounds,
            place,
            kv_planes,
        )
        attn_out_rings[0].start()
        stored = jnp.concatenate([query_stored, kv_stored[:, :chunk], kv_stored[:, chunk:]])
        return (stored, attn_out_rings[0].finish(), out_ring.finish())

    attn_rings = []

    def attn_hop(token):
        if not attn_rings:
            attn_rings.append(RingSum(extras_of[0][1][0], plane))
        attn_rings[0].start(token)
        return (attn_rings[0].finish(),)

    def hop_and_pieces(token):
        pieces = wide(ordered([after(rows, token) for rows in in_received], place))
        grads = pieces.transpose(3, 1, 0, 2).reshape(mlp_in.shape)
        attn_out_rings[0].start(token)
        return attn_hop(token) + (grads, attn_out_rings[0].finish())

    def hop_and_exchange(token):
        pieces = after(out_ring.finish_all(), token).reshape(2, unit, row_parts, row_share)
        pieces = pieces.transpose(0, 2, 1, 3).reshape(PLANE, unit, row_share)
        return attn_hop(token) + tuple(exchange_members(pieces, place))

    def project_back(index, token):
        near, far = near_grads[index], far_grads[index]
        if token is not None:
            near = after(near, token)
        return together(
            narrow(dot(near, attn_weight, 1, 0)), narrow(dot(far, query_weight, 1, 0))
        )

    extras_of = []

    def keep_chunks(extras):
        extras_of.append(extras)
        return weight_chunks(extras)

    grad_lowered_in, extras = reduce_plane(
        project_back, (weight_grads, hop_and_pieces, hop_and_exchange), keep_chunks
    )
    attn_rings[0].total = after(attn_rings[0].total, grad_lowered_in)
    attn_sum = attn_rings[0].finish_all()
    pieces = attn_sum.reshape(chunk, row_parts, row_share).transpose(1, 0, 2)
    attn_received = exchange_members(pieces, part)
    grad_source, grad_gain_in = norm_back(source, inverse_in, scales[0], grad_lowered_in)
    grad_input = grad_middle + grad_source

    grad_mlp_in = extras[2][1]
    attn_pieces = ordered(attn_received, part)
    grad_attn_out = wide(attn_out_rings[0].finish_all())
    grad_attn_in = wide(attn_pieces.reshape(attn_in.shape[1], row_share).T)
    out_pieces = wide(ordered(extras[3][1:], place))
    grad_mlp_out = out_pieces.transpose(2, 0, 1).reshape(mlp_out.shape)
    gain_total = sum_devices(
        jnp.stack([grad_gain_in, grad_gain_post_attn, grad_gain_pre_mlp, grad_gain_post])
    )
    grad_gains = pick(
        gain_total.reshape(gains.shape[1], row_parts, row_share).transpose(1, 2, 0), part
    )
    return (
        narrow(result),
        grad_input,
        grad_attn_in,
        grad_attn_out,
        grad_mlp_in,
        grad_mlp_out,
        grad_gains,
    )


def solution(mesh):
    placed = (
        P(("ctx", "fsdp"), None),
        P(("ctx", "fsdp"), None),
        P(),
        P(("ctx", "fsdp")),
        P("fsdp", "ctx"),
        P("fsdp", "ctx"),
        P("fsdp", "ctx"),
        P("fsdp", "ctx"),
        P("fsdp", None),
    )
    return jax.shard_map(
        body,
        mesh=mesh,
        in_specs=placed,
        out_specs=(
            P(("ctx", "fsdp"), None),
            P(("ctx", "fsdp"), None),
            P("fsdp", "ctx"),
            P("fsdp", "ctx"),
            P("fsdp", "ctx"),
            P("fsdp", "ctx"),
            P("fsdp", None),
        ),
        check_vma=False,
    )
```

```python
import functools
import math

import jax
import jax.numpy as jnp
from jax import lax
from jax.experimental import pallas as pl
from jax.experimental.pallas import tpu as pltpu
from jax.sharding import PartitionSpec as P

QUERY_HEADS = 8
KEY_VALUE_HEADS = 4
HEAD_SIZE = 256
LOOKBACK_SPAN = 4096
SEQUENCE_COUNT = 2


EPSILON = 1e-06
SOFT_CAP = 50.0
ROPE_BASE = 10000.0
AXES = ("ctx", "fsdp")
PLANE = 8
CORE, SIDE, ACROSS = 1, 2, 4
TANH_SCALE = HEAD_SIZE ** (-0.5) / SOFT_CAP
EXP2_SCALE = SOFT_CAP * math.log2(math.e)
VMEM_BYTES = 56 * 1024 * 1024


def inverse_rms(values):
    return lax.rsqrt(jnp.mean(values * values, axis=-1, keepdims=True) + EPSILON)


def norm_back(values, inverse, scale, upstream):
    scaled = upstream * scale
    through = inverse * scaled - values * inverse**3 * jnp.mean(
        scaled * values, axis=-1, keepdims=True
    )
    return (through, jnp.sum(upstream * values * inverse, axis=0))


def rotate(values, cosine, sine):
    half_width = values.shape[-1] // 2
    first_half = values[..., :half_width]
    second_half = values[..., half_width:]
    return jnp.concatenate(
        [
            first_half * cosine - second_half * sine,
            second_half * cosine + first_half * sine,
        ],
        axis=-1,
    )


def dot(left, right, left_axis, right_axis):
    return lax.dot_general(
        left,
        right,
        (((left_axis,), (right_axis,)), ((), ())),
        preferred_element_type=jnp.float32,
    )


def after(value, *others):
    return lax.optimization_barrier((value,) + others)[0]


def wide(values):
    return values.astype(jnp.float32)


def narrow(values):
    return values.astype(jnp.bfloat16)


def swap(values, mask):
    count = lax.axis_size(AXES)
    return lax.ppermute(values, AXES, [(i, i ^ mask) for i in range(count)])


def shift(values, steps=1):
    count = lax.axis_size(AXES)
    return lax.ppermute(values, AXES, [(i, (i + steps * PLANE) % count) for i in range(count)])


def route(values, targets):
    count = lax.axis_size(AXES)
    return lax.ppermute(
        values, AXES, [(i, i - i % PLANE + targets[i % PLANE]) for i in range(count)]
    )


def pick(stacked, index, axis=0):
    return lax.dynamic_index_in_dim(stacked, index, axis, keepdims=False)


def look_up(table, place):
    return pick(jnp.asarray(table, jnp.int32), place)


def exchange(pieces):
    far = swap(jnp.stack([pieces[mask ^ CORE] for mask in range(0, len(pieces), 2)]), CORE)
    received = []
    for i, mask in enumerate(range(0, len(pieces), 2)):
        both = jnp.stack([pieces[mask], far[i]])
        if mask:
            both = swap(both, mask)
        received.extend([both[0], both[1]])
    return received


def exchange_members(stacked, place):
    return exchange([pick(stacked, place ^ mask) for mask in range(stacked.shape[0])])


def ordered(received, place):
    whole = jnp.zeros((len(received),) + received[0].shape, received[0].dtype)
    for mask, rows in enumerate(received):
        whole = lax.dynamic_update_index_in_dim(whole, rows, place ^ mask, 0)
    return whole


NEAR = [(0, 0), (0, 1), (4, 0), (2, 1), (2, 0), (4, 1), (6, 0), (6, 1)]
FAR = [(mask ^ CORE, half) for mask, half in NEAR]


def together(*values):
    return lax.optimization_barrier(values)


def no_transfers(token, extras=None):
    return ()


def gather_plane(rows, work, beside=(no_transfers,) * 3, late=False):
    half = rows.shape[0] // 2
    low, high = rows[:half], rows[half:]
    groups, done, extras = [], [], []

    def add_group(near, far):
        groups.append(jnp.concatenate([near, far]))
        done.append(work(groups[-1], len(done)))

    other = swap(rows, CORE)
    first_low, first_high = swap(low, ACROSS), swap(high, SIDE)
    extra = beside[0](rows, extras)
    if late:
        first_low, first_high, *extra = together(first_low, first_high, *extra)
    else:
        add_group(rows, other)
        done[0], first_low, first_high, *extra = together(done[0], first_low, first_high, *extra)
    extras.append(extra)
    low, high = together(low, high, first_low)[:2]
    first_other = swap(jnp.concatenate([first_low, first_high]), CORE)
    second_low, second_high = swap(low, SIDE), swap(high, ACROSS)
    extra = beside[1](first_low, extras)
    if late:
        add_group(rows, other)
    add_group(jnp.concatenate([first_low, first_high]), first_other)
    done[1], first_low, first_high, second_low, second_high, *extra = together(
        done[1], first_low, first_high, second_low, second_high, *extra
    )
    extras.append(extra)
    second_other = swap(jnp.concatenate([second_low, second_high]), CORE)
    third_low, third_high = swap(first_low, SIDE), swap(first_high, ACROSS)
    extra = beside[2](second_low, extras)
    add_group(jnp.concatenate([second_low, second_high]), second_other)
    done[2], third_low, third_high, *extra = together(done[2], third_low, third_high, *extra)
    extras.append(extra)
    third = jnp.concatenate([third_low, third_high])
    add_group(third, swap(third, CORE))
    return groups, done, extras


def reduce_plane(work, beside=(no_transfers,) * 3, middle=None, kept=None):
    extras = []
    kept = {} if kept is None else kept

    def both(group, token):
        near, far = work(group, token)
        return wide(near) + wide(swap(far, CORE))

    third = narrow(both(3, None))
    half = third.shape[0] // 2
    got_low, got_high = swap(third[:half], SIDE), swap(third[half:], ACROSS)
    second = narrow(both(2, third))
    got_low, got_high, second, *extra = together(got_low, got_high, second, *beside[0](third))
    extras.append(extra)
    kept["down"] = extra[0] if extra else None
    if middle is not None:
        second, *extra = together(second, *middle(extras))
        extras.append(extra)
    own_low, own_high = swap(second[:half], SIDE), swap(second[half:], ACROSS)
    first = both(1, second)
    first = narrow(first + wide(jnp.concatenate([got_low, got_high])))
    own_low, own_high, first, *extra = together(own_low, own_high, first, *beside[1](second))
    extras.append(extra)
    kept["in"] = extra[0] if extra else None
    more_low, more_high = swap(first[:half], ACROSS), swap(first[half:], SIDE)
    own = both(0, first) + wide(jnp.concatenate([own_low, own_high]))
    more_low, more_high, own, *extra = together(more_low, more_high, own, *beside[2](first))
    extras.append(extra)
    return own + wide(jnp.concatenate([more_low, more_high])), extras


def sum_devices(values):
    for mask in (CORE, SIDE, ACROSS):
        values = values + swap(values, mask)
    total = values
    for steps in range(1, lax.axis_size(AXES) // PLANE):
        total = total + shift(values, steps)
    return total


class RingSum:
    def __init__(self, parts, plane, first=0, rows=None):
        self.parts, self.plane, self.planes = parts, plane, parts.shape[0]
        self.first, self.rows = first, rows or parts.shape[1]
        self.hops, self.moving = 0, None
        self.total = self.part(0)

    def part(self, step):
        at = (self.plane + 2 * self.planes - 1 - step) % self.planes
        size = (1, self.rows, self.parts.shape[2])
        return lax.dynamic_slice(self.parts, (at, self.first, 0), size)[0]

    def start(self, *others):
        if self.hops < self.planes - 1:
            self.moving = shift(after(self.total, *others) if others else self.total)

    def finish(self):
        if self.moving is not None:
            self.hops += 1
            self.total = narrow(wide(self.moving) + wide(self.part(self.hops)))
            self.moving = None
        return self.total

    def finish_all(self):
        self.finish()
        while self.hops < self.planes - 1:
            self.start()
            self.finish()
        return self.total


def matchings(edges):
    left, rounds = list(edges), []
    while left:
        owner = {}

        def settle(source, seen):
            for edge in left:
                if edge[0] == source and edge[1] not in seen:
                    seen.add(edge[1])
                    if edge[1] not in owner or settle(owner[edge[1]][0], seen):
                        owner[edge[1]] = edge
                        return True
            return False

        for source in range(PLANE):
            settle(source, set())
        found = sorted(owner.values())
        rounds.append(found)
        left = [edge for edge in left if edge not in found]
    return rounds


def chunk_edges(plane_count, columns, chunk, share):
    edges = []
    for source in range(PLANE):
        for at in range(plane_count):
            column = (2 * at + source // 4) * columns + source % 4 * chunk
            head = column // HEAD_SIZE
            for target in range(head * share, (head + 1) * share):
                edges.append((source, target, at, column % HEAD_SIZE // chunk))
    return edges


def chunks_to_heads(stored, rounds, place):
    spots = len(rounds)
    got = []
    for found in rounds:
        sent = pick(stored, look_up([edge[2] for edge in found], place))
        got.append(route(sent, [edge[1] for edge in found]))
    stacked = jnp.stack(got)
    order = []
    for spot in range(spots):
        table = [0] * PLANE
        for step, found in enumerate(rounds):
            for edge in found:
                if edge[3] == spot:
                    table[edge[1]] = step
        order.append(pick(stacked, look_up(table, place)))
    return order


def heads_to_chunks(heads, rounds, place, plane_count):
    got = []
    for found in rounds:
        back, spot = [0] * PLANE, [0] * PLANE
        for source, target, _, position in found:
            back[target], spot[target] = source, position
        got.append(route(pick(heads, look_up(spot, place)), back))
    stacked = jnp.stack(got)
    chunks = []
    for at in range(plane_count):
        tables = []
        for source in range(PLANE):
            tables.append(
                [
                    step
                    for step, found in enumerate(rounds)
                    for edge in found
                    if edge[0] == source and edge[2] == at
                ]
            )
        terms = [
            pick(stacked, look_up([table[i] for table in tables], place))
            for i in range(len(tables[0]))
        ]
        total = terms[0]
        if len(terms) > 1:
            total = narrow(sum(wide(term) for term in terms))
        chunks.append(total)
    return jnp.stack(chunks)


def row_product_kernel(count, *refs):
    out, total = refs[-2:]
    total[...] = dot(refs[0][...], refs[count][...], 0, 0)
    for i in range(1, count):
        total[...] += dot(refs[i][...], refs[count + i][...], 0, 0)
    out[...] = total[...].astype(out.dtype)


def row_product(lefts, rights, left_tile, right_tile):
    count = len(lefts)
    height, width = lefts[0].shape[1], rights[0].shape[1]
    depths = [left.shape[0] for left in lefts]
    return pl.pallas_call(
        functools.partial(row_product_kernel, count),
        out_shape=jax.ShapeDtypeStruct((height, width), jnp.bfloat16),
        grid=(height // left_tile, width // right_tile),
        in_specs=[pl.BlockSpec((depth, left_tile), lambda i, j: (0, i)) for depth in depths]
        + [pl.BlockSpec((depth, right_tile), lambda i, j: (0, j)) for depth in depths],
        out_specs=pl.BlockSpec((left_tile, right_tile), lambda i, j: (i, j)),
        scratch_shapes=[pltpu.VMEM((left_tile, right_tile), jnp.float32)],
        compiler_params=pltpu.CompilerParams(vmem_limit_bytes=VMEM_BYTES),
        cost_estimate=pl.CostEstimate(
            flops=2 * sum(depths) * height * width,
            bytes_accessed=2 * sum(depths) * (height + width) + 2 * height * width,
            transcendentals=0,
        ),
    )(*lefts, *rights)


def out_kernel(part, rows_ref, weight_ref, out_ref):
    at = pl.program_id(0)
    total = dot(rows_ref[0], weight_ref[0, 0], 1, 1)
    for head in range(1, rows_ref.shape[0]):
        total += dot(rows_ref[head], weight_ref[head, 0], 1, 1)
    for i in range(out_ref.shape[1] // part):

        @pl.when(at == i)
        def _():
            out_ref[:, i * part : (i + 1) * part] = total


def out_product(rows, weight):
    heads, count, size = rows.shape
    _, parts, part, _ = weight.shape
    return pl.pallas_call(
        functools.partial(out_kernel, part),
        out_shape=jax.ShapeDtypeStruct((count, parts * part), jnp.float32),
        grid=(parts,),
        in_specs=[
            pl.BlockSpec((heads, count, size), lambda i: (0, 0, 0)),
            pl.BlockSpec((heads, 1, part, size), lambda i: (0, i, 0, 0)),
        ],
        out_specs=pl.BlockSpec((count, parts * part), lambda i: (0, 0)),
        compiler_params=pltpu.CompilerParams(vmem_limit_bytes=VMEM_BYTES),
        cost_estimate=pl.CostEstimate(
            flops=2 * count * heads * size * parts * part,
            bytes_accessed=2 * heads * size * (count + parts * part) + 4 * count * parts * part,
            transcendentals=0,
        ),
    )(rows, weight)


def out_back_kernel(rows_ref, weight_ref, out_ref):
    part = weight_ref.shape[2]
    total = dot(rows_ref[:, :part], weight_ref[0, 0], 1, 0)
    for i in range(1, weight_ref.shape[1]):
        total += dot(rows_ref[:, i * part : (i + 1) * part], weight_ref[0, i], 1, 0)
    out_ref[0] = total.astype(out_ref.dtype)


def out_back_product(rows, weight):
    count, width = rows.shape
    heads, parts, part, size = weight.shape
    return pl.pallas_call(
        out_back_kernel,
        out_shape=jax.ShapeDtypeStruct((heads, count, size), jnp.bfloat16),
        grid=(heads,),
        in_specs=[
            pl.BlockSpec((count, width), lambda i: (0, 0)),
            pl.BlockSpec((1, parts, part, size), lambda i: (i, 0, 0, 0)),
        ],
        out_specs=pl.BlockSpec((1, count, size), lambda i: (i, 0, 0)),
        compiler_params=pltpu.CompilerParams(vmem_limit_bytes=VMEM_BYTES),
        cost_estimate=pl.CostEstimate(
            flops=2 * count * heads * size * width,
            bytes_accessed=2 * heads * size * (count + width) + 2 * count * width,
            transcendentals=0,
        ),
    )(rows, weight)


def out_grad_kernel(rows_ref, heads_ref, out_ref):
    total = dot(rows_ref[...], heads_ref[0], 0, 0).astype(out_ref.dtype)
    part = out_ref.shape[3]
    for side in range(2):
        for core in range(2):
            at = (2 * side + core) * part
            out_ref[core, side, 0] = total[at : at + part]


def out_grad_product(rows, by_head):
    count, width = rows.shape
    heads, _, size = by_head.shape
    part = width // 4
    return pl.pallas_call(
        out_grad_kernel,
        out_shape=jax.ShapeDtypeStruct((2, 2, heads, part, size), jnp.bfloat16),
        grid=(heads,),
        in_specs=[
            pl.BlockSpec((count, width), lambda i: (0, 0)),
            pl.BlockSpec((1, count, size), lambda i: (i, 0, 0)),
        ],
        out_specs=pl.BlockSpec((2, 2, 1, part, size), lambda i: (0, 0, i, 0, 0)),
        compiler_params=pltpu.CompilerParams(vmem_limit_bytes=VMEM_BYTES),
        cost_estimate=pl.CostEstimate(
            flops=2 * count * heads * size * width,
            bytes_accessed=2 * heads * size * (count + width) + 2 * count * width,
            transcendentals=0,
        ),
    )(rows, by_head)


def pair_lists(query_ids, key_ids, blocks_per_seq, span_blocks):
    query_seq, query_at = query_ids // blocks_per_seq, query_ids % blocks_per_seq
    key_seq, key_at = key_ids // blocks_per_seq, key_ids % blocks_per_seq
    rows = key_ids.shape[0]
    distance = (query_at[None, :, None] - key_at[:, None, :]).reshape(rows, -1)
    same = (query_seq[None, :, None] == key_seq[:, None, :]).reshape(rows, -1)
    whole = same & (distance > 0) & (distance < span_blocks)
    edged = same & ((distance == 0) | (distance == span_blocks))
    kind = whole.astype(jnp.int32) + 2 * edged.astype(jnp.int32)
    total = distance.shape[1]
    index = jnp.arange(total, dtype=jnp.int32)
    earlier = (index[None, :] < index[:, None])[None] & (kind[:, None, :] == kind[:, :, None])
    rank = jnp.sum(earlier.astype(jnp.int32), axis=2)
    count_whole = jnp.sum(whole.astype(jnp.int32), axis=1, keepdims=True)
    count_edged = jnp.sum(edged.astype(jnp.int32), axis=1, keepdims=True)
    spot = jnp.where(kind == 1, rank, jnp.where(kind == 2, count_whole + rank, -1))
    code = index * 2 + (distance == span_blocks).astype(jnp.int32)
    hit = spot[:, :, None] == index[None, None, :]
    entries = jnp.sum(jnp.where(hit, code[:, :, None], 0), axis=1)
    return jnp.concatenate([count_whole, count_edged, entries], axis=1).astype(jnp.int32)


def run_pairs(list_ref, row, key_count, unroll, visit):
    whole = list_ref[row, 0]
    edged = list_ref[row, 1]

    def decode(position):
        code = list_ref[row, 2 + position]
        pair = code // 2
        return pair // key_count, pair % key_count, code % 2

    def several(step, carry):
        found = [decode(step * unroll + i) for i in range(unroll)]
        visit([f[0] for f in found], [f[1] for f in found], None)
        return carry

    def single(position, carry):
        i, j, _ = decode(position)
        visit([i], [j], None)
        return carry

    def masked(position, carry):
        i, j, far = decode(position)
        visit([i], [j], far)
        return carry

    groups = whole // unroll
    lax.fori_loop(0, groups, several, 0)
    lax.fori_loop(groups * unroll, whole, single, 0)
    lax.fori_loop(whole, whole + edged, masked, 0)


def attend_kernel(first, unroll, list_ref, query_hbm, own_hbm, other_hbm, *rest):
    if first:
        state_hbm = None
        out_hbm, query, own, other, state, sems = rest
    else:
        state_hbm, out_hbm, query, own, other, state, sems = rest
    copies = [
        pltpu.make_async_copy(query_hbm, query, sems.at[0]),
        pltpu.make_async_copy(own_hbm, own, sems.at[1]),
        pltpu.make_async_copy(other_hbm, other, sems.at[2]),
    ]
    if not first:
        copies.append(pltpu.make_async_copy(state_hbm, state, sems.at[3]))
    for copy in copies:
        copy.start()
    if first:
        state[...] = jnp.zeros_like(state)
    for copy in copies:
        copy.wait()
    rows = query.shape[1]
    lane = lax.broadcasted_iota(jnp.int32, (rows, 128), 1)

    def visit_in(keys):
        def visit(query_at, key_at, far):
            scores = [
                dot(query[i], keys[j, :, :HEAD_SIZE], 1, 1) for i, j in zip(query_at, key_at)
            ]
            for i, j, score in zip(query_at, key_at, scores):
                weights = jnp.exp2(EXP2_SCALE * jnp.tanh(score * TANH_SCALE))
                if far is not None:
                    spacing = (
                        lax.broadcasted_iota(jnp.int32, weights.shape, 0)
                        - lax.broadcasted_iota(jnp.int32, weights.shape, 1)
                        + far * LOOKBACK_SPAN
                    )
                    live = (spacing >= 0) & (spacing < LOOKBACK_SPAN)
                    weights = jnp.where(live, weights, 0.0)
                if rows % 128 == 0:
                    part = weights[:, :128]
                    for k in range(1, rows // 128):
                        part = part + weights[:, k * 128 : (k + 1) * 128]
                else:
                    part = jnp.where(lane == 0, jnp.sum(weights, axis=1, keepdims=True), 0.0)
                state[i, :, HEAD_SIZE:] += part
                state[i, :, :HEAD_SIZE] += dot(
                    weights.astype(jnp.bfloat16), keys[j, :, HEAD_SIZE:], 1, 0
                )

        return visit

    key_count = own.shape[0]
    run_pairs(list_ref, 0, key_count, unroll, visit_in(own))
    run_pairs(list_ref, 1, key_count, unroll, visit_in(other))
    out = pltpu.make_async_copy(state, out_hbm, sems.at[4])
    out.start()
    out.wait()


def attend(lists, query, own, other, state):
    first = state is None
    blocks, rows, _ = query.shape
    shape = (blocks, rows, HEAD_SIZE + 128)
    operands = (query, own, other) if first else (query, own, other, state)
    return pl.pallas_call(
        functools.partial(attend_kernel, first, 4),
        out_shape=jax.ShapeDtypeStruct(shape, jnp.float32),
        grid_spec=pltpu.PrefetchScalarGridSpec(
            num_scalar_prefetch=1,
            grid=(1,),
            in_specs=[pl.BlockSpec(memory_space=pl.ANY)] * len(operands),
            out_specs=pl.BlockSpec(memory_space=pl.ANY),
            scratch_shapes=[
                pltpu.VMEM(query.shape, jnp.bfloat16),
                pltpu.VMEM(own.shape, jnp.bfloat16),
                pltpu.VMEM(other.shape, jnp.bfloat16),
                pltpu.VMEM(shape, jnp.float32),
                pltpu.SemaphoreType.DMA((5,)),
            ],
        ),
        compiler_params=pltpu.CompilerParams(vmem_limit_bytes=VMEM_BYTES),
        cost_estimate=pl.CostEstimate(
            flops=60 * 4 * rows * rows * HEAD_SIZE,
            bytes_accessed=14 * 1024 * 1024,
            transcendentals=60 * 2 * rows * rows,
        ),
    )(lists, *operands)


def attend_back_kernel(
    first,
    unroll,
    list_ref,
    query_hbm,
    grad_hbm,
    term_hbm,
    own_hbm,
    other_hbm,
    *rest,
):
    if first:
        state_hbm = None
    else:
        state_hbm, *rest = rest
    (
        out_hbm,
        own_out_hbm,
        other_out_hbm,
        query,
        grad,
        term,
        own,
        other,
        state,
        own_grad,
        other_grad,
        own_low,
        other_low,
        sems,
    ) = rest
    copies = [
        pltpu.make_async_copy(query_hbm, query, sems.at[0]),
        pltpu.make_async_copy(grad_hbm, grad, sems.at[1]),
        pltpu.make_async_copy(term_hbm, term, sems.at[2]),
        pltpu.make_async_copy(own_hbm, own, sems.at[3]),
        pltpu.make_async_copy(other_hbm, other, sems.at[4]),
    ]
    if not first:
        copies.append(pltpu.make_async_copy(state_hbm, state, sems.at[5]))
    for copy in copies:
        copy.start()
    if first:
        state[...] = jnp.zeros_like(state)
    own_grad[...] = jnp.zeros_like(own_grad)
    other_grad[...] = jnp.zeros_like(other_grad)
    for copy in copies:
        copy.wait()

    def visit_in(keys, key_grad):
        def visit(query_at, key_at, far):
            scores = []
            slopes = []
            for i, j in zip(query_at, key_at):
                scores.append(dot(keys[j, :, :HEAD_SIZE], query[i], 1, 1))
                slopes.append(dot(keys[j, :, HEAD_SIZE:], grad[i], 1, 1))
            for i, j, score, slope in zip(query_at, key_at, scores, slopes):
                bent = jnp.tanh(score * TANH_SCALE)
                weights = jnp.exp2(EXP2_SCALE * bent)
                if far is not None:
                    spacing = (
                        lax.broadcasted_iota(jnp.int32, weights.shape, 1)
                        - lax.broadcasted_iota(jnp.int32, weights.shape, 0)
                        + far * LOOKBACK_SPAN
                    )
                    live = (spacing >= 0) & (spacing < LOOKBACK_SPAN)
                    weights = jnp.where(live, weights, 0.0)
                grad_scores = (
                    (slope + term[i]) * (weights * (1.0 - bent * bent))
                ).astype(jnp.bfloat16)
                key_grad[j, :, :HEAD_SIZE] += dot(grad_scores, query[i], 1, 0)
                key_grad[j, :, HEAD_SIZE:] += dot(weights.astype(jnp.bfloat16), grad[i], 1, 0)
                state[i] += dot(grad_scores, keys[j, :, :HEAD_SIZE], 0, 0)

        return visit

    key_count = own.shape[0]
    run_pairs(list_ref, 1, key_count, unroll, visit_in(other, other_grad))
    other_low[...] = other_grad[...].astype(jnp.bfloat16)
    other_out = pltpu.make_async_copy(other_low, other_out_hbm, sems.at[6])
    other_out.start()
    run_pairs(list_ref, 0, key_count, unroll, visit_in(own, own_grad))
    own_low[...] = own_grad[...].astype(jnp.bfloat16)
    own_out = pltpu.make_async_copy(own_low, own_out_hbm, sems.at[7])
    own_out.start()
    out = pltpu.make_async_copy(state, out_hbm, sems.at[8])
    out.start()
    other_out.wait()
    own_out.wait()
    out.wait()


def attend_back(lists, query, grad, term, own, other, state):
    first = state is None
    blocks, rows, _ = query.shape
    operands = (query, grad, term, own, other)
    if not first:
        operands = operands + (state,)
    return pl.pallas_call(
        functools.partial(attend_back_kernel, first, 2),
        out_shape=[
            jax.ShapeDtypeStruct(query.shape, jnp.float32),
            jax.ShapeDtypeStruct(own.shape, jnp.bfloat16),
            jax.ShapeDtypeStruct(other.shape, jnp.bfloat16),
        ],
        grid_spec=pltpu.PrefetchScalarGridSpec(
            num_scalar_prefetch=1,
            grid=(1,),
            in_specs=[pl.BlockSpec(memory_space=pl.ANY)] * len(operands),
            out_specs=[pl.BlockSpec(memory_space=pl.ANY)] * 3,
            scratch_shapes=[
                pltpu.VMEM(query.shape, jnp.bfloat16),
                pltpu.VMEM(query.shape, jnp.bfloat16),
                pltpu.VMEM(term.shape, jnp.float32),
                pltpu.VMEM(own.shape, jnp.bfloat16),
                pltpu.VMEM(other.shape, jnp.bfloat16),
                pltpu.VMEM(query.shape, jnp.float32),
                pltpu.VMEM(own.shape, jnp.float32),
                pltpu.VMEM(other.shape, jnp.float32),
                pltpu.VMEM(own.shape, jnp.bfloat16),
                pltpu.VMEM(other.shape, jnp.bfloat16),
                pltpu.SemaphoreType.DMA((9,)),
            ],
        ),
        compiler_params=pltpu.CompilerParams(vmem_limit_bytes=VMEM_BYTES),
        cost_estimate=pl.CostEstimate(
            flops=60 * 10 * rows * rows * HEAD_SIZE,
            bytes_accessed=24 * 1024 * 1024,
            transcendentals=60 * 2 * rows * rows,
        ),
    )(lists, *operands)


def body(inputs, cotangent, block_ids, positions, attn_in, attn_out, mlp_in, mlp_out, gains):
    token_rows, width = inputs.shape
    block = token_rows // 2
    devices = lax.axis_size(AXES)
    ctx_count, row_parts = lax.axis_size("ctx"), lax.axis_size("fsdp")
    planes = devices // PLANE
    blocks_per_seq = 2 * devices // SEQUENCE_COUNT
    span_blocks = LOOKBACK_SPAN // block
    score_scale = HEAD_SIZE ** (-0.5)
    me = lax.axis_index(AXES)
    place, plane = me % PLANE, me // PLANE
    part = place % row_parts
    row_share = attn_in.shape[0]
    unit = mlp_out.shape[1] // PLANE
    chunk = attn_in.shape[1] // row_parts
    order = NEAR + FAR

    gain_parts = ordered([gains.T] + [swap(gains.T, mask) for mask in range(1, row_parts)], part)
    scales = wide(gain_parts.transpose(1, 0, 2).reshape(gains.shape[1], width))
    source = wide(inputs)
    inverse_in = inverse_rms(source)
    lowered_in = narrow(source * inverse_in * scales[0])

    gathered_out = lax.all_gather(attn_out, AXES, axis=0)
    in_pieces = mlp_in.T.reshape(2, PLANE, unit, row_share).transpose(1, 0, 2, 3)
    in_received = exchange_members(in_pieces, place)
    attn_pieces = exchange_members(attn_in.T.reshape(row_parts, chunk, row_share), part)
    in_chunk = ordered(attn_pieces, part).transpose(1, 0, 2).reshape(chunk, width)
    *in_received, first_stored = together(*in_received, shift(in_chunk))
    stored = [in_chunk, first_stored]
    for step in range(2, planes):
        stored.append(shift(stored[-1]))
    in_share = (
        ordered(in_received, place)
        .reshape(2, row_parts, 2, unit, row_share)
        .transpose(0, 2, 3, 1, 4)
        .reshape(4 * unit, width)
    )
    lowered_in = after(lowered_in, first_stored)
    block_ids = after(block_ids, in_chunk)

    def ids_of(which_plane, slots):
        masks = jnp.asarray([mask for mask, _ in slots], jnp.int32)
        sides = jnp.asarray([half for _, half in slots], jnp.int32)
        at = 2 * (which_plane[:, None] * PLANE + (place ^ masks)[None, :]) + sides[None, :]
        slot = jnp.arange(block_ids.shape[0], dtype=jnp.int32)
        return jnp.sum(jnp.where(at[:, :, None] == slot, block_ids, 0), axis=2)

    stage_planes = (plane + planes - jnp.arange(planes, dtype=jnp.int32)) % planes
    stage_ids = ids_of(stage_planes, order)
    query_ids = stage_ids[0]
    lists = pair_lists(
        query_ids, stage_ids.reshape(2 * planes, len(NEAR)), blocks_per_seq, span_blocks
    ).reshape(planes, 2, -1)
    half_width = HEAD_SIZE // 2
    frequency = ROPE_BASE ** (-2.0 * jnp.arange(half_width, dtype=jnp.float32) / HEAD_SIZE)
    base_angle = wide(query_ids % blocks_per_seq * block)[:, None, None] * frequency
    step_angle = jnp.arange(block, dtype=jnp.float32)[:, None] * frequency
    base_cosine, base_sine = jnp.cos(base_angle), jnp.sin(base_angle)
    step_cosine, step_sine = jnp.cos(step_angle), jnp.sin(step_angle)
    cosine = base_cosine * step_cosine - base_sine * step_sine
    sine = base_sine * step_cosine + base_cosine * step_sine

    cut = 2 * unit
    in_halves = [[], []]
    out_shares = []
    in_all = jnp.zeros((planes * 4 * unit, width), jnp.bfloat16)
    out_all = jnp.zeros((planes * 2 * unit, width), jnp.bfloat16)

    def next_in(which):
        def start(token, extras=None):
            in_halves[which].append(shift(after(in_halves[which][-1], token)))
            return (in_halves[which][-1],)

        return start

    def next_out(token, extras=None):
        out_shares.append(shift(after(out_shares[-1], token)))
        return (out_shares[-1],)

    query_planes, kv_planes = planes // 2, planes // 4
    query_rounds = matchings(chunk_edges(query_planes, attn_in.shape[1], chunk, 1))
    kv_rounds = matchings(
        chunk_edges(kv_planes, attn_in.shape[1], chunk, QUERY_HEADS // KEY_VALUE_HEADS)
    )

    def weights_together(token, extras):
        whole = jnp.zeros((planes, chunk, width), jnp.bfloat16)
        for step, rows in enumerate(stored):
            whole = lax.dynamic_update_index_in_dim(whole, rows, (plane - step) % planes, 0)
        return (whole, in_share)

    attn_weights = []

    def weights_to_heads(token, extras):
        whole, share = extras[0]
        in_halves[0].append(share[:cut])
        in_halves[1].append(share[cut:])
        query_chunks = chunks_to_heads(whole[:query_planes], query_rounds, place)
        kv_chunks = chunks_to_heads(
            jnp.concatenate(
                [whole[query_planes : query_planes + kv_planes], whole[query_planes + kv_planes :]],
                axis=1,
            ),
            kv_rounds,
            place,
        )
        attn_weights.append(
            jnp.concatenate(
                query_chunks
                + [both[:chunk] for both in kv_chunks]
                + [both[chunk:] for both in kv_chunks]
            )
        )
        return next_in(0)(token) + next_in(1)(token) + (gathered_out, lists, cosine, sine)

    in_groups, projected, extras = gather_plane(
        lowered_in,
        lambda group, index: dot(group, attn_weights[0], 1, 1),
        (weights_together, weights_to_heads, next_in(0)),
        late=True,
    )
    attn_weight = attn_weights[0]
    gathered_out, lists, cosine, sine = extras[1][2:]

    def split_groups(groups):
        near = jnp.concatenate([group[:token_rows] for group in groups])
        far = jnp.concatenate([group[token_rows:] for group in groups])
        return [rows.reshape(len(NEAR), block, rows.shape[1]) for rows in (near, far)]

    near_rows, far_rows = split_groups(projected)
    query_parts, kv_parts = [], []
    for rows, low, high in ((near_rows, 0, len(NEAR)), (far_rows, len(NEAR), 2 * len(NEAR))):
        turns = (cosine[low:high], sine[low:high])
        query_parts.append(narrow(rotate(rows[:, :, :HEAD_SIZE], *turns)))
        kv_parts.append(
            jnp.concatenate(
                [
                    narrow(rotate(rows[:, :, HEAD_SIZE : 2 * HEAD_SIZE], *turns)),
                    narrow(rows[:, :, 2 * HEAD_SIZE :]),
                ],
                axis=-1,
            )
        )
    own_kv, other_kv = kv_parts
    query = jnp.concatenate(query_parts)

    kv_stages = [(own_kv, other_kv)]
    state = None
    for step in range(planes):
        own_kv, other_kv = kv_stages[step]
        state_next = attend(lists[step], query, own_kv, other_kv, state)
        if step < planes - 1:
            moving = shift(own_kv)
            beside = []
            if step == 1:
                out_pieces = after(mlp_out.T, own_kv).reshape(PLANE, unit, row_share)
                beside = exchange_members(out_pieces, place)
            state_next, moving, *beside = together(state_next, moving, *beside)
            if step == 1:
                out_shares.append(
                    ordered(beside, place)
                    .reshape(2, row_parts, unit, row_share)
                    .transpose(0, 2, 1, 3)
                    .reshape(2 * unit, width)
                )
            kv_stages.append((moving, swap(moving, CORE)))
        else:
            state_next, _ = together(state_next, *next_in(1)(own_kv))
        state = state_next
    totals = jnp.sum(state[:, :, HEAD_SIZE:], axis=-1, keepdims=True)
    attended = state[:, :, :HEAD_SIZE] / totals
    attended_rows = narrow(attended)

    def member_rows(blocks, mask):
        return jnp.concatenate([blocks[order.index((mask, 0))], blocks[order.index((mask, 1))]])

    def blocks_of(received):
        return jnp.stack(
            [received[mask][half * block : (half + 1) * block] for mask, half in order]
        )

    next_in(0)(attended_rows)
    attended_heads = ordered(
        exchange([member_rows(attended_rows, mask) for mask in range(PLANE)]), place
    )
    attended_heads = after(attended_heads, in_halves[0][-1])
    gathered_out = (
        gathered_out.reshape((QUERY_HEADS, -1, row_parts) + attn_out.shape)
        .transpose(0, 2, 3, 1, 4)
        .reshape(QUERY_HEADS, row_parts, row_share, HEAD_SIZE)
    )

    next_in(1)(attended_heads)
    branch = out_product(attended_heads, gathered_out)
    inverse_branch = inverse_rms(branch)
    middle = source + branch * inverse_branch * scales[1]
    inverse_mid = inverse_rms(middle)
    lowered_mid = narrow(middle * inverse_mid * scales[2])
    lowered_mid = after(lowered_mid, in_halves[1][-1])
    hidden_width = planes * 2 * unit
    for which, shares in enumerate(in_halves):
        while len(shares) < planes:
            shares.append(shift(shares[-1]))
        for step, share in enumerate(shares):
            at = (plane - step) % planes * 4 * unit + which * cut
            in_all = lax.dynamic_update_slice_in_dim(in_all, share, at, 0)

    def gate_up_of(group, index):
        return narrow(dot(group, in_all, 1, 1))

    mid_groups, gate_ups, _ = gather_plane(lowered_mid, gate_up_of, (next_out,) * 3)
    while len(out_shares) < planes:
        out_shares.append(shift(out_shares[-1]))
    for step, share in enumerate(out_shares):
        at = (plane - step) % planes * 2 * unit
        out_all = lax.dynamic_update_slice_in_dim(out_all, share, at, 0)

    def activate(gate_up):
        gate = wide(gate_up[:, :hidden_width])
        up = wide(gate_up[:, hidden_width:])
        return jax.nn.gelu(gate, approximate=True) * up

    hiddens = [narrow(activate(gate_up)) for gate_up in gate_ups]

    def reduce_groups(groups, weight, *rest):
        def work(index, token):
            group = groups[index] if token is None else after(groups[index], token)
            partial = together(narrow(dot(group, weight, 1, 0)))[0]
            return partial[:token_rows], partial[token_rows:]

        return reduce_plane(work, *rest)

    down_branch, _ = reduce_groups(hiddens, out_all)
    inverse_down = inverse_rms(down_branch)
    result = middle + down_branch * inverse_down * scales[3]
    upstream = wide(cotangent)
    grad_down, grad_gain_post = norm_back(down_branch, inverse_down, scales[3], upstream)
    grad_down_low = narrow(grad_down)

    def activate_back(gate_up, grad_hidden):
        gate = wide(gate_up[:, :hidden_width])
        up = wide(gate_up[:, hidden_width:])
        _, back = jax.vjp(lambda g, u: jax.nn.gelu(g, approximate=True) * u, gate, up)
        grad_gate, grad_up = back(grad_hidden)
        return narrow(jnp.concatenate([grad_gate, grad_up], axis=1))

    def grad_gate_up_of(group, index):
        return activate_back(gate_ups[index], dot(group, out_all, 1, 1))

    down_groups, grad_gate_ups, _ = gather_plane(grad_down_low, grad_gate_up_of)

    tile = 768 if width % 768 == 0 else width
    rings = {}

    def out_grads(token):
        grads = row_product([after(hiddens[0], token)] + hiddens[1:], down_groups, 384, tile)
        return (grads,)

    def in_grads(token):
        rings["out"] = RingSum(rings["down"].reshape(planes, 2 * unit, width), plane)
        rings["out"].start(token)
        rings["out"].finish()
        rings["out"].start()
        grads = row_product(
            [after(grad_gate_ups[0], token)] + grad_gate_ups[1:], mid_groups, tile, tile
        )
        return (grads, rings["out"].finish())

    def first_low(token):
        parts = rings["in"].reshape(planes, 4 * unit, width)
        rings["low"] = RingSum(parts, plane, 0, cut)
        rings["high"] = RingSum(parts, plane, cut, cut)
        rings["low"].start(token)
        return (rings["low"].finish(),)

    grad_lowered_mid, _ = reduce_groups(
        grad_gate_ups, in_all, (out_grads, in_grads, first_low), None, rings
    )
    out_ring, low_ring, high_ring = rings["out"], rings["low"], rings["high"]

    high_ring.start(grad_lowered_mid)
    grad_through_mid, grad_gain_pre_mlp = norm_back(
        middle, inverse_mid, scales[2], grad_lowered_mid
    )
    grad_middle = upstream + grad_through_mid
    grad_branch, grad_gain_post_attn = norm_back(branch, inverse_branch, scales[1], grad_middle)
    grad_branch_low = narrow(grad_branch)
    grad_heads = out_back_product(grad_branch_low, gathered_out)
    grad_heads = after(grad_heads, high_ring.finish())
    low_ring.start(grad_heads)
    grad_heads = list(exchange_members(grad_heads, place))
    grad_heads[0] = after(grad_heads[0], low_ring.finish())
    high_ring.start(grad_heads[0])
    grad_rows = wide(blocks_of(grad_heads))
    row_terms = -jnp.sum(grad_rows * attended, axis=-1) / totals[..., 0]
    grad_summed = narrow(grad_rows / totals)
    grad_summed = after(grad_summed, high_ring.finish())
    row_terms = row_terms[:, None, :]

    grad_query, kv_total = None, None
    core, side, across = place % 2, place // 2 % 2, place // 4
    for step in range(planes):
        stage = (step + 1) % planes
        own_kv, other_kv = kv_stages[stage]
        if step == 0:
            low_ring.start(grad_summed)
            out_parts = out_grad_product(after(grad_branch_low, grad_summed), attended_heads)
            high_ring.start(grad_summed)
            beside = [low_ring.finish(), out_parts, high_ring.finish()]
        else:
            beside = [shift(kv_total)]
            grad_query = after(grad_query, kv_total)
        if step == 1:
            beside.append(swap(pick(after(out_parts, kv_total), 1 - core), CORE))
        if step == 2:
            beside.append(swap(pick(out_lows, 1 - across, 2), ACROSS))
            beside.append(swap(pick(out_highs, 1 - side), SIDE))
        if step == planes - 1:
            in_sum = jnp.concatenate([low_ring.finish_all(), high_ring.finish_all()])
            in_pieces = after(in_sum, kv_total).reshape(2, 2, unit, row_parts, row_share)
            in_pieces = in_pieces.transpose(0, 3, 1, 2, 4).reshape(PLANE, 2, unit, row_share)
            beside.extend(exchange_members(in_pieces, place))
        grad_query, own_grad, other_grad, *beside = together(
            *attend_back(
                lists[stage], query, grad_summed, row_terms, own_kv, other_kv, grad_query
            ),
            *beside,
        )
        total = wide(own_grad) + wide(swap(other_grad, CORE))
        if step:
            total = total + wide(beside[0])
        kv_total = narrow(total)
        if step == 0:
            out_parts = beside[1].reshape(2, 2, QUERY_HEADS, row_share, -1, attn_out.shape[1])
            out_parts = out_parts.transpose(0, 1, 2, 4, 3, 5)
            out_parts = out_parts.reshape(2, 2, planes, 2, row_share, attn_out.shape[1])
        if step == 1:
            out_sums = narrow(wide(pick(out_parts, core)) + wide(beside[1]))
            out_lows = out_sums[:, :, :, : row_share // 2]
            out_highs = out_sums[:, :, :, row_share // 2 :]
        if step == 2:
            out_lows = narrow(wide(pick(out_lows, across, 2)) + wide(beside[1]))
            out_highs = narrow(wide(pick(out_highs, side)) + wide(beside[2]))
    in_received = beside[1:]
    out_ring.start(beside[0])
    got_low = swap(pick(after(out_lows, beside[0]), 1 - side), SIDE)
    got_high = swap(pick(after(out_highs, beside[0]), 1 - across, 1), ACROSS)

    turned_query = narrow(rotate(grad_query * score_scale, cosine, -sine))
    kv_grad = wide(kv_total)
    turned_key = narrow(
        rotate(
            kv_grad[:, :, :HEAD_SIZE] * score_scale, cosine[: len(NEAR)], -sine[: len(NEAR)]
        )
    )
    near_grads = jnp.concatenate(
        [turned_query[: len(NEAR)], turned_key, kv_total[:, :, HEAD_SIZE:]], axis=-1
    ).reshape(4, token_rows, 3 * HEAD_SIZE)
    far_grads = turned_query[len(NEAR) :].reshape(4, token_rows, HEAD_SIZE)
    query_groups = jnp.concatenate([near_grads[:, :, :HEAD_SIZE], far_grads], axis=1)
    query_weight = attn_weight[:HEAD_SIZE]

    attn_out_rings = []

    def weight_grads(token):
        query_lefts = [after(query_groups[0], token)] + [query_groups[i] for i in range(1, 4)]
        grad_query_weight = row_product(query_lefts, in_groups, HEAD_SIZE, tile)
        grad_kv_weight = row_product(
            [after(near_grads[i, :, HEAD_SIZE:], token) for i in range(4)],
            in_groups,
            2 * HEAD_SIZE,
            tile,
        )
        return (grad_query_weight, grad_kv_weight)

    def weight_chunks(extras):
        grad_query_weight, grad_kv_weight = extras[0]
        low_rows, high_rows = after(got_low, grad_query_weight), after(got_high, grad_query_weight)
        out_lows_last = wide(pick(out_lows, side)) + wide(low_rows)
        out_highs_last = wide(pick(out_highs, across, 1)) + wide(high_rows)
        parts = jnp.concatenate([narrow(out_lows_last), narrow(out_highs_last)], axis=1)
        attn_out_rings.append(RingSum(parts, plane))
        query_stored = heads_to_chunks(
            grad_query_weight.reshape(HEAD_SIZE // chunk, chunk, width),
            query_rounds,
            place,
            query_planes,
        )
        kv_stored = heads_to_chunks(
            jnp.concatenate(
                [
                    grad_kv_weight[:HEAD_SIZE].reshape(HEAD_SIZE // chunk, chunk, width),
                    grad_kv_weight[HEAD_SIZE:].reshape(HEAD_SIZE // chunk, chunk, width),
                ],
                axis=1,
            ),
            kv_rounds,
            place,
            kv_planes,
        )
        attn_out_rings[0].start()
        stored = jnp.concatenate([query_stored, kv_stored[:, :chunk], kv_stored[:, chunk:]])
        return (stored, attn_out_rings[0].finish(), out_ring.finish())

    attn_rings = []

    def attn_hop(token):
        if not attn_rings:
            attn_rings.append(RingSum(extras_of[0][1][0], plane))
        attn_rings[0].start(token)
        return (attn_rings[0].finish(),)

    def hop_and_pieces(token):
        pieces = wide(ordered([after(rows, token) for rows in in_received], place))
        grads = pieces.transpose(3, 1, 0, 2).reshape(mlp_in.shape)
        attn_out_rings[0].start(token)
        return attn_hop(token) + (grads, attn_out_rings[0].finish())

    def hop_and_exchange(token):
        pieces = after(out_ring.finish_all(), token).reshape(2, unit, row_parts, row_share)
        pieces = pieces.transpose(0, 2, 1, 3).reshape(PLANE, unit, row_share)
        return attn_hop(token) + tuple(exchange_members(pieces, place))

    def project_back(index, token):
        near, far = near_grads[index], far_grads[index]
        if token is not None:
            near = after(near, token)
        return together(
            narrow(dot(near, attn_weight, 1, 0)), narrow(dot(far, query_weight, 1, 0))
        )

    extras_of = []

    def keep_chunks(extras):
        extras_of.append(extras)
        return weight_chunks(extras)

    grad_lowered_in, extras = reduce_plane(
        project_back, (weight_grads, hop_and_pieces, hop_and_exchange), keep_chunks
    )
    attn_rings[0].total = after(attn_rings[0].total, grad_lowered_in)
    attn_sum = attn_rings[0].finish_all()
    pieces = attn_sum.reshape(chunk, row_parts, row_share).transpose(1, 0, 2)
    attn_received = exchange_members(pieces, part)
    grad_source, grad_gain_in = norm_back(source, inverse_in, scales[0], grad_lowered_in)
    grad_input = grad_middle + grad_source

    grad_mlp_in = extras[2][1]
    attn_pieces = ordered(attn_received, part)
    grad_attn_out = wide(attn_out_rings[0].finish_all())
    grad_attn_in = wide(attn_pieces.reshape(attn_in.shape[1], row_share).T)
    out_pieces = wide(ordered(extras[3][1:], place))
    grad_mlp_out = out_pieces.transpose(2, 0, 1).reshape(mlp_out.shape)
    gain_total = sum_devices(
        jnp.stack([grad_gain_in, grad_gain_post_attn, grad_gain_pre_mlp, grad_gain_post])
    )
    grad_gains = pick(
        gain_total.reshape(gains.shape[1], row_parts, row_share).transpose(1, 2, 0), part
    )
    return (
        narrow(result),
        grad_input,
        grad_attn_in,
        grad_attn_out,
        grad_mlp_in,
        grad_mlp_out,
        grad_gains,
    )


def solution(mesh):
    placed = (
        P(("ctx", "fsdp"), None),
        P(("ctx", "fsdp"), None),
        P(),
        P(("ctx", "fsdp")),
        P("fsdp", "ctx"),
        P("fsdp", "ctx"),
        P("fsdp", "ctx"),
        P("fsdp", "ctx"),
        P("fsdp", None),
    )
    return jax.shard_map(
        body,
        mesh=mesh,
        in_specs=placed,
        out_specs=(
            P(("ctx", "fsdp"), None),
            P(("ctx", "fsdp"), None),
            P("fsdp", "ctx"),
            P("fsdp", "ctx"),
            P("fsdp", "ctx"),
            P("fsdp", "ctx"),
            P("fsdp", None),
        ),
        check_vma=False,
    )
```
